32 devices in a mesh: seq: 8 (over z, core), img: 4 (over y, x).
Axes of the slice: x: 2, y: 2, z: 4, core: 2. Of those that a mesh axis runs over, the one named last changes fastest.
Arguments:
- images: bfloat16 [4, 2048, 1024], P('img', 'seq'), may hold values from -6 to 6
- cotangent: bfloat16 [4, 2048, 1024], P('img', 'seq'), may hold values from -6 to 6
- qkv_weight: float32 [1024, 3072], P(('seq', 'img')), may hold values from -0.1875 to 0.1875
- out_weight: float32 [1024, 1024], P(('seq', 'img')), may hold values from -1 to 1
- up_weight: float32 [1024, 4096], P(('seq', 'img')), may hold values from -0.1875 to 0.1875
- down_weight: float32 [4096, 1024], P(('seq', 'img')), may hold values from -0.09375 to 0.09375
- norm_params: float32 [4, 1024], P(None, ('seq', 'img')), may hold values from -1 to 5, as said below
- qkv_first: float32 [1024, 3072], P(('seq', 'img')), may hold values from -5.6372688e-05 to 5.6372688e-05
- out_first: float32 [1024, 1024], P(('seq', 'img')), may hold values from -5.6372688e-05 to 5.6372688e-05
- up_first: float32 [1024, 4096], P(('seq', 'img')), may hold values from -5.6372688e-05 to 5.6372688e-05
- down_first: float32 [4096, 1024], P(('seq', 'img')), may hold values from -5.6372688e-05 to 5.6372688e-05
- norm_first: float32 [4, 1024], P(None, ('seq', 'img')), may hold values from -0.00022549075 to 0.00022549075
- qkv_second: float32 [1024, 3072], P(('seq', 'img')), may hold values from 7.9447e-11 to 3.17788e-10, as said below
- out_second: float32 [1024, 1024], P(('seq', 'img')), may hold values from 7.9447e-11 to 3.17788e-10, as said below
- up_second: float32 [1024, 4096], P(('seq', 'img')), may hold values from 7.9447e-11 to 3.17788e-10, as said below
- down_second: float32 [4096, 1024], P(('seq', 'img')), may hold values from 7.9447e-11 to 3.17788e-10, as said below
- norm_second: float32 [4, 1024], P(None, ('seq', 'img')), may hold values from 1.271152e-09 to 5.084608e-09, as said below
Outputs:
- activations: bfloat16 [4, 2048, 1024], P('img', 'seq')
- input_grad: bfloat16 [4, 2048, 1024], P('img', 'seq')
- grad_norm: float32 [], replicated
- qkv_new: float32 [1024, 3072], P(('seq', 'img'))
- out_new: float32 [1024, 1024], P(('seq', 'img'))
- up_new: float32 [1024, 4096], P(('seq', 'img'))
- down_new: float32 [4096, 1024], P(('seq', 'img'))
- norm_new: float32 [4, 1024], P(None, ('seq', 'img'))
- qkv_first_new: float32 [1024, 3072], P(('seq', 'img'))
- out_first_new: float32 [1024, 1024], P(('seq', 'img'))
- up_first_new: float32 [1024, 4096], P(('seq', 'img'))
- down_first_new: float32 [4096, 1024], P(('seq', 'img'))
- norm_first_new: float32 [4, 1024], P(None, ('seq', 'img'))
- qkv_second_new: float32 [1024, 3072], P(('seq', 'img'))
- out_second_new: float32 [1024, 1024], P(('seq', 'img'))
- up_second_new: float32 [1024, 4096], P(('seq', 'img'))
- down_second_new: float32 [4096, 1024], P(('seq', 'img'))
- norm_second_new: float32 [4, 1024], P(None, ('seq', 'img'))
The draws below stay inside these ranges and needn't reach their ends.
Inputs may be any that keep to these rules, and one draw needn't show every extreme that they name: `norm_params`: rows 0 and 2 hold positive gains, rows 1 and 3 biases. `qkv_second`: positive. `out_second`: positive. `up_second`: positive. `down_second`: positive. `norm_second`: positive.
All inputs are finite; a program needn't handle non-finite values.
Results may differ from the reference program's by a relative error of at most 0.009.
Values may be sent and summed in bfloat16 or wider, within the bound.
No kernel may reach another device: no remote copies, remote signals or barrier semaphores. Data moves between devices by JAX's collectives and lax.ppermute only.
A program may use at most 256 MiB of HBM per device.

```python
import math
import jax
import jax.numpy as jnp
from jax import lax

D = 1024
HEADS = 16
HEAD_DIM = 64
FF = 4096
GROUP = 256
STEP = 10
LENGTH = 2048
IMAGES = 4
OUT_FAN = 32
PARAMS = 12587008


def first_moment(key, shape, grad_scale):
    return 0.11 * grad_scale * jax.random.uniform(key, shape, jnp.float32, -1.8, 1.8)


def second_moment(key, shape, grad_scale):
    factor = jnp.exp(jax.random.uniform(key, shape, jnp.float32, 0.0, math.log(4.0)))
    return 0.001 * grad_scale * grad_scale * factor


def draw_norm_params(key, part):
    key = jax.random.fold_in(key, 11)
    gain_key, bias_key = jax.random.split(key)
    ramp = jnp.arange(D, dtype=jnp.float32) / (D - 1)
    rise = 1.0 + 2.0 * ramp
    spread = jax.random.uniform(gain_key, (2, D), jnp.float32, 0.8, 1.2)
    gains = rise * spread
    biases = jax.random.uniform(bias_key, (2, D), jnp.float32, -1.0, 1.0)
    return jnp.stack([gains[0], biases[0], gains[1], biases[1]])


def draw_qkv_first(key, part):
    key = jax.random.fold_in(key, 21)
    return first_moment(key, (D, 3 * D), PARAMS ** (-0.5))


def draw_out_first(key, part):
    key = jax.random.fold_in(key, 22)
    return first_moment(key, (D, D), PARAMS ** (-0.5))


def draw_up_first(key, part):
    key = jax.random.fold_in(key, 23)
    return first_moment(key, (D, FF), PARAMS ** (-0.5))


def draw_down_first(key, part):
    key = jax.random.fold_in(key, 24)
    return first_moment(key, (FF, D), PARAMS ** (-0.5))


def draw_norm_first(key, part):
    key = jax.random.fold_in(key, 25)
    return first_moment(key, (4, D), 4.0 * PARAMS ** (-0.5))


def draw_qkv_second(key, part):
    key = jax.random.fold_in(key, 31)
    return second_moment(key, (D, 3 * D), PARAMS ** (-0.5))


def draw_out_second(key, part):
    key = jax.random.fold_in(key, 32)
    return second_moment(key, (D, D), PARAMS ** (-0.5))


def draw_up_second(key, part):
    key = jax.random.fold_in(key, 33)
    return second_moment(key, (D, FF), PARAMS ** (-0.5))


def draw_down_second(key, part):
    key = jax.random.fold_in(key, 34)
    return second_moment(key, (FF, D), PARAMS ** (-0.5))


def draw_norm_second(key, part):
    key = jax.random.fold_in(key, 35)
    return second_moment(key, (4, D), 4.0 * PARAMS ** (-0.5))


def steps_of(own_key, shape, cuts, smallest, top_value):
    def one(dim, shards_of):
        heights = jax.random.uniform(jax.random.fold_in(jax.random.fold_in(own_key, 6), dim), (shards_of,), jnp.float32, smallest / len(cuts), top_value / len(cuts))
        return jnp.repeat(jnp.exp(heights), shape[dim] // shards_of).reshape((-1,) + (1,) * (len(shape) - dim - 1))

    level = one(*cuts[0])
    for cut in cuts[1:]:
        level = level * one(*cut)
    return level


def bell_draw(rng, dims, scale, reach, cuts=(), kind=jnp.bfloat16):
    array = scale * jax.random.normal(rng, dims, jnp.float32)
    if cuts:
        array = array * steps_of(rng, dims, cuts, -0.22, 0.18)
    return jnp.clip(array, -reach, reach).astype(kind)


def setup_inputs(seed: int = 0) -> dict:
    streams_of = jax.random.split(jax.random.key(seed), 18)
    images = bell_draw(streams_of[0], (IMAGES, LENGTH, D), 1.0, 6.0, ((0, 4), (1, 8)))
    cotangent = bell_draw(streams_of[1], (IMAGES, LENGTH, D), 1.0, 6.0, ((0, 4), (1, 8)))
    qkv_weight = bell_draw(streams_of[2], (D, 3 * D), D ** -0.5, 0.1875, ((0, 32),), jnp.float32)
    out_weight = bell_draw(streams_of[3], (D, D), OUT_FAN ** -0.5, 1.0, ((0, 32),), jnp.float32)
    up_weight = bell_draw(streams_of[4], (D, FF), D ** -0.5, 0.1875, ((0, 32),), jnp.float32)
    down_weight = bell_draw(streams_of[5], (FF, D), FF ** -0.5, 0.09375, ((0, 32),), jnp.float32)
    norm_params = draw_norm_params(jax.random.fold_in(streams_of[17], 71), 0)
    qkv_first = draw_qkv_first(jax.random.fold_in(streams_of[17], 71), 0)
    out_first = draw_out_first(jax.random.fold_in(streams_of[17], 71), 0)
    up_first = draw_up_first(jax.random.fold_in(streams_of[17], 71), 0)
    down_first = draw_down_first(jax.random.fold_in(streams_of[17], 71), 0)
    norm_first = draw_norm_first(jax.random.fold_in(streams_of[17], 71), 0)
    qkv_second = draw_qkv_second(jax.random.fold_in(streams_of[17], 71), 0)
    out_second = draw_out_second(jax.random.fold_in(streams_of[17], 71), 0)
    up_second = draw_up_second(jax.random.fold_in(streams_of[17], 71), 0)
    down_second = draw_down_second(jax.random.fold_in(streams_of[17], 71), 0)
    norm_second = draw_norm_second(jax.random.fold_in(streams_of[17], 71), 0)
    return dict(images=images, cotangent=cotangent, qkv_weight=qkv_weight, out_weight=out_weight, up_weight=up_weight, down_weight=down_weight, norm_params=norm_params, qkv_first=qkv_first, out_first=out_first, up_first=up_first, down_first=down_first, norm_first=norm_first, qkv_second=qkv_second, out_second=out_second, up_second=up_second, down_second=down_second, norm_second=norm_second)


HIGH = lax.Precision.HIGHEST
NORM_EPS = 1e-05
BETA_ONE = 0.9
BETA_TWO = 0.999
ADAM_EPS = 1e-08
WEIGHT_DECAY = 0.1
CLIP_LIMIT = 1.0

@jax.custom_vjp
def low(v):
    return lax.optimization_barrier(v.astype(jnp.bfloat16)).astype(jnp.float32)

@jax.custom_vjp
def low_back(v):
    return v

def low_keep(v):
    return (low(v), None)

def low_pass(kept, grad):
    return (grad,)

def back_keep(v):
    return (v, None)

def back_low(kept, grad):
    return (low(grad),)
low.defvjp(low_keep, low_pass)
low_back.defvjp(back_keep, back_low)

def layer_norm(values, gain, bias):
    center = values - lax.optimization_barrier(jnp.mean(values, axis=-1, keepdims=True))
    spread = lax.optimization_barrier(jnp.mean(center * center, axis=-1, keepdims=True))
    return center * lax.rsqrt(spread + NORM_EPS) * gain + bias

def feature_map(values):
    return jax.nn.elu(values) + 1.0

def gelu_tanh(values):
    return jax.nn.gelu(values, approximate=True)

def attend(query_feat, key_feat, value_rows, state_in, keysum_in):
    scores = jnp.einsum('ithe,ishe->ihts', query_feat, key_feat, precision=HIGH)
    length = query_feat.shape[1]
    causal = jnp.tril(jnp.ones((length, length), jnp.float32))
    scores = scores * causal
    numer = jnp.einsum('ihts,ishf->ithf', scores, value_rows, precision=HIGH)
    numer = numer + jnp.einsum('ithe,ihef->ithf', query_feat, state_in, precision=HIGH)
    denom = jnp.transpose(lax.optimization_barrier(jnp.sum(scores, axis=-1)), (0, 2, 1))
    denom = denom + jnp.einsum('ithe,ihe->ith', query_feat, keysum_in, precision=HIGH)
    return numer / denom[..., None]

def group_state(key_feat, value_rows):
    state = jnp.einsum('ishe,ishf->ihef', key_feat, value_rows, precision=HIGH)
    return (state, lax.optimization_barrier(jnp.sum(key_feat, axis=1)))

def image_forward(params, image):
    qkv_w, out_w, up_w, down_w, norm_p = params
    length = image.shape[0]
    normed_one = low(layer_norm(image, norm_p[0], norm_p[1]))
    projected = low_back(jnp.dot(normed_one, qkv_w, precision=HIGH))
    shaped = projected.reshape(length, 3, HEADS, HEAD_DIM)
    query_feat = low(feature_map(shaped[:, 0]))
    key_feat = low(feature_map(shaped[:, 1]))
    value_rows = low(shaped[:, 2])
    blocks = length // GROUP

    def block_step(carry, piece):
        state, keysum = carry
        part_q, part_k, part_v = piece
        mixed_block = attend(part_q[None], part_k[None], part_v[None], state[None], keysum[None])[0]
        add_state, add_sum = group_state(part_k[None], part_v[None])
        return ((state + add_state[0], keysum + add_sum[0]), mixed_block)

    def blocked(values):
        return values.reshape(blocks, GROUP, HEADS, HEAD_DIM)
    start = (jnp.zeros((HEADS, HEAD_DIM, HEAD_DIM), jnp.float32), jnp.zeros((HEADS, HEAD_DIM), jnp.float32))
    _, mixed_all = lax.scan(jax.checkpoint(block_step), start, (blocked(query_feat), blocked(key_feat), blocked(value_rows)))
    mixed = low(mixed_all.reshape(length, D))
    resid = image + low_back(jnp.dot(mixed, out_w, precision=HIGH))
    normed_two = low(layer_norm(resid, norm_p[2], norm_p[3]))
    hidden = low_back(jnp.dot(normed_two, up_w, precision=HIGH))
    activated = low(gelu_tanh(hidden))
    return resid + low_back(jnp.dot(activated, down_w, precision=HIGH))

def adam_update(weight, first, second, grad, rate, decay):
    first_new = BETA_ONE * first + (1.0 - BETA_ONE) * grad
    second_new = BETA_TWO * second + (1.0 - BETA_TWO) * grad * grad
    first_hat = first_new / (1.0 - BETA_ONE ** STEP)
    second_hat = second_new / (1.0 - BETA_TWO ** STEP)
    weight_new = weight - rate * (first_hat / (jnp.sqrt(second_hat) + ADAM_EPS) + decay * weight)
    return (weight_new, first_new, second_new)

def reference(images, cotangent, qkv_weight, out_weight, up_weight, down_weight, norm_params, qkv_first, out_first, up_first, down_first, norm_first, qkv_second, out_second, up_second, down_second, norm_second):
    masters = (qkv_weight, out_weight, up_weight, down_weight, norm_params)
    working = tuple((low(weight) for weight in masters))

    def per_image(totals, pair):
        image, cot = pair
        image_wide = image.astype(jnp.float32)
        result, pullback = jax.vjp(image_forward, working, image_wide)
        param_grads, image_grad = pullback(cot.astype(jnp.float32))
        totals = jax.tree.map(jnp.add, totals, param_grads)
        return (totals, (result.astype(jnp.bfloat16), image_grad.astype(jnp.bfloat16)))
    zeros = tuple((jnp.zeros_like(weight) for weight in working))
    grads, (activations, input_grad) = lax.scan(per_image, zeros, (images, cotangent))
    squares = jnp.float32(0.0)
    for grad in grads:
        squares = squares + jnp.sum(grad * grad)
    grad_norm = jnp.sqrt(squares)
    clip = jnp.minimum(1.0, CLIP_LIMIT / (grad_norm + 1e-06))
    rates = (3.0 * D ** (-0.5), 3.0 * OUT_FAN ** (-0.5), 3.0 * D ** (-0.5), 3.0 * FF ** (-0.5), 1.5)
    decays = (WEIGHT_DECAY, WEIGHT_DECAY, WEIGHT_DECAY, WEIGHT_DECAY, 0.0)
    firsts = (qkv_first, out_first, up_first, down_first, norm_first)
    seconds = (qkv_second, out_second, up_second, down_second, norm_second)
    news = [adam_update(masters[k], firsts[k], seconds[k], clip * grads[k], rates[k], decays[k]) for k in range(5)]
    return (activations, input_grad, grad_norm, news[0][0], news[1][0], news[2][0], news[3][0], news[4][0], news[0][1], news[1][1], news[2][1], news[3][1], news[4][1], news[0][2], news[1][2], news[2][2], news[3][2], news[4][2])
```

```python
import functools

import jax
import jax.numpy as jnp
from jax import lax
from jax.experimental import pallas as pl
from jax.experimental.pallas import tpu as pltpu
from jax.sharding import PartitionSpec as P

HEAD_DIM = 64
STEP = 10
NORM_EPS = 1e-05
BETA_ONE = 0.9
BETA_TWO = 0.999
ADAM_EPS = 1e-08
WEIGHT_DECAY = 0.1
CLIP_LIMIT = 1.0
LANES = 128

LOW = jnp.bfloat16
WIDE = jnp.float32
ALL = ("z", "c", "y", "x")
SWAP = [(0, 1), (1, 0)]


def swap(value, axis):
    return lax.ppermute(value, axis, SWAP)


def shift(value, step, wrap=True):
    size = lax.axis_size("z")
    pairs = [(i, (i + step) % size) for i in range(size) if wrap or 0 <= i + step < size]
    return lax.ppermute(value, "z", pairs)


def mine(pair_axis_first):
    return jnp.where(lax.axis_index("c") == 0, pair_axis_first[0], pair_axis_first[1])


def other(pair_axis_first):
    return jnp.where(lax.axis_index("c") == 0, pair_axis_first[1], pair_axis_first[0])


def in_order(own, mate, axis=0):
    first = lax.axis_index("c") == 0
    return jnp.concatenate([jnp.where(first, own, mate), jnp.where(first, mate, own)], axis)


def gather_chips(shard):
    column = jnp.stack([shard] + [shift(shard, k) for k in range(1, lax.axis_size("z"))])
    half = column.shape[0] // 2
    along_x, along_y = swap(column, "x"), swap(column, "y")
    far = (swap(along_y[:half], "x"), swap(along_x[half:], "y"))
    return (column, along_x, along_y) + far


def gathered_places(depth):
    half = depth // 2
    places = [(0, k, (k, 0, 0)) for k in range(depth)]
    places += [(1, k, (k, 0, 1)) for k in range(depth)]
    places += [(2, k, (k, 1, 0)) for k in range(depth)]
    places += [(3, k, (k, 1, 1)) for k in range(half)]
    places += [(4, k - half, (k, 1, 1)) for k in range(half, depth)]
    return places


def reduce_chips(send_x, keep_x, send_y, keep_y):
    depth = send_x.shape[1]
    got_x, got_y = swap(send_x, "x"), swap(send_y, "y")
    wide = lambda a: a.astype(WIDE)
    on_y = swap((wide(keep_x[1]) + wide(got_x[1])).astype(LOW), "y")
    on_x = swap((wide(keep_y[1]) + wide(got_y[1])).astype(LOW), "x")
    parts = []
    for k in range(depth):
        one = wide(keep_x[0, k]) + wide(got_x[0, k]) + wide(on_y[k])
        two = wide(keep_y[0, k]) + wide(got_y[0, k]) + wide(on_x[k])
        parts.append(jnp.concatenate([one, two]))
    total = parts[0]
    for k in range(1, depth):
        total = total + wide(shift(parts[k].astype(LOW), k))
    return total


def coordinates():
    return jnp.stack([lax.axis_index("z"), lax.axis_index("y"), lax.axis_index("x")]).astype(jnp.int32)


def chip_of(coords, rel, depth, back):
    dz, dy, dx = rel
    z, y, x = coords[0], coords[1], coords[2]
    zz = lax.rem(z + (depth - dz if back else dz), depth)
    yy = 1 - y if dy else y
    xx = 1 - x if dx else x
    return zz, yy * 2 + xx


def run_copies(copies, sems):
    started = [pltpu.make_async_copy(src, dst, sems.at[i]) for i, (src, dst) in enumerate(copies)]
    for copy in started:
        copy.start()
    for copy in started:
        copy.wait()


def window(ref, lead, row, rows, col, cols):
    rows_at = pl.ds(row if isinstance(row, int) else pl.multiple_of(row, 16), rows)
    return ref.at[(*lead, rows_at, pl.ds(col, cols))]


def place(parts, depth, outs, moves):
    spots = gathered_places(depth)
    count = len(spots) * len(moves(0, 0))

    def kernel(coords, *refs):
        ins, out_refs, sems = refs[: len(parts)], refs[len(parts) : len(parts) + len(outs)], refs[-1]
        copies = []
        for array, slot, rel in spots:
            zz, plane = chip_of(coords, rel, depth, True)
            for o, sr, sc, rows, cols, tr, tc in moves(zz, plane):
                copies.append(
                    (window(ins[array], (slot,), sr, rows, sc, cols), window(out_refs[o], (), tr, rows, tc, cols))
                )
        run_copies(copies, sems)

    return pl.pallas_call(
        kernel,
        out_shape=[jax.ShapeDtypeStruct(s, LOW) for s in outs],
        in_specs=[pl.BlockSpec(memory_space=pltpu.SMEM)] + [pl.BlockSpec(memory_space=pl.ANY)] * len(parts),
        out_specs=[pl.BlockSpec(memory_space=pl.ANY)] * len(outs),
        scratch_shapes=[pltpu.SemaphoreType.DMA((count,))],
    )(coordinates(), *parts)


def unplace(grads, depth, rows_cols, moves):
    spots = []
    for dz in range(depth):
        for d in range(2):
            spots += [(0, d, dz, (dz, d, 1), 0), (1, d, dz, (dz, d, 0), 0)]
            spots += [(2, d, dz, (dz, 1, d), 1), (3, d, dz, (dz, 0, d), 1)]
    count = len(spots) * len(moves(0, 0, 0))

    def kernel(coords, *refs):
        ins, out_refs, sems = refs[: len(grads)], refs[len(grads) : len(grads) + 4], refs[-1]
        copies = []
        for array, d, dz, rel, half in spots:
            zz, plane = chip_of(coords, rel, depth, False)
            for i, sr, sc, rows, cols, tr, tc in moves(zz, plane, half):
                copies.append(
                    (window(ins[i], (), sr, rows, sc, cols), window(out_refs[array], (d, dz), tr, rows, tc, cols))
                )
        run_copies(copies, sems)

    return pl.pallas_call(
        kernel,
        out_shape=[jax.ShapeDtypeStruct((2, depth) + rows_cols, LOW)] * 4,
        in_specs=[pl.BlockSpec(memory_space=pltpu.SMEM)] + [pl.BlockSpec(memory_space=pl.ANY)] * len(grads),
        out_specs=[pl.BlockSpec(memory_space=pl.ANY)] * 4,
        scratch_shapes=[pltpu.SemaphoreType.DMA((count,))],
    )(coordinates(), *grads)


def layer_norm(values, gain, bias):
    center = values - jnp.mean(values, axis=-1, keepdims=True)
    spread = jnp.mean(center * center, axis=-1, keepdims=True)
    return center * lax.rsqrt(spread + NORM_EPS) * gain + bias


def feature_map(values):
    return jax.nn.elu(values) + 1.0


def gelu_tanh(values):
    return jax.nn.gelu(values, approximate=True)


def dot(left, right):
    return jnp.dot(left, right, preferred_element_type=WIDE)


def dot_rows(left, right):
    return lax.dot_general(left, right, (((0,), (0,)), ((), ())), preferred_element_type=WIDE)


def dot_cols(left, right):
    return lax.dot_general(left, right, (((1,), (1,)), ((), ())), preferred_element_type=WIDE)


def mul(spec, left, right):
    return jnp.einsum(spec, left, right, preferred_element_type=WIDE)


def adam_update(weight, first, second, grad, rate, decay):
    first_new = BETA_ONE * first + (1.0 - BETA_ONE) * grad
    second_new = BETA_TWO * second + (1.0 - BETA_TWO) * grad * grad
    first_hat = first_new / (1.0 - BETA_ONE**STEP)
    second_hat = second_new / (1.0 - BETA_TWO**STEP)
    weight_new = weight - rate * (first_hat / (jnp.sqrt(second_hat) + ADAM_EPS) + decay * weight)
    return (weight_new, first_new, second_new)


def from_others(value, step):
    low = value.astype(LOW)
    total = jnp.zeros(value.shape, WIDE)
    for k in range(1, lax.axis_size("z")):
        total = total + shift(low, step * k, wrap=False).astype(WIDE)
    return total


def sum_everywhere(value, direct):
    if not direct:
        return lax.psum(value, ALL)
    value = jnp.broadcast_to(value, (8, LANES))
    value = value + swap(value, "c")
    across = lax.ppermute(value, ("y", "x"), [(i, 3 - i) for i in range(4)])
    value = value + swap(value, "y") + (swap(value, "x") + across)
    near = [shift(value, k) for k in range(1, lax.axis_size("z"))]
    for part in near:
        value = value + part
    return value[0, 0]


def body(
    images,
    cotangent,
    qkv_weight,
    out_weight,
    up_weight,
    down_weight,
    norm_params,
    qkv_first,
    out_first,
    up_first,
    down_first,
    norm_first,
    qkv_second,
    out_second,
    up_second,
    down_second,
    norm_second,
):
    depth, core = lax.axis_size("z"), lax.axis_index("c")
    count, group, width = images.shape
    hidden_units = up_weight.shape[1]
    own_rows = qkv_weight.shape[0]
    own_units = down_weight.shape[0]
    chips = lax.axis_size("y") * lax.axis_size("x")
    block, ff_block = width // (2 * depth), hidden_units // (2 * depth)
    half_qkv, half_ff, half_d = 3 * width // 2, hidden_units // 2, width // 2
    ring = lax.axis_size("y") == 2 and lax.axis_size("x") == 2 and depth % 2 == 0 and own_rows % 32 == 0
    heads = half_d // HEAD_DIM
    tokens = 2 * group

    own_x, own_g = images.reshape(group, width), cotangent.reshape(group, width)
    split_qkv = lambda w: jnp.moveaxis(w.reshape(-1, 3 * depth, 2, block), 2, 0).reshape(2, -1, half_qkv)
    split_up = lambda w: jnp.moveaxis(w.reshape(-1, depth, 2, ff_block), 2, 0).reshape(2, -1, half_ff)

    qkv_low, out_low = qkv_weight.astype(LOW), out_weight.astype(LOW)
    up_low, down_low = up_weight.astype(LOW), down_weight.astype(LOW)
    norm_low = norm_params.astype(LOW)
    if ring:
        pad = jnp.zeros((own_rows, LANES - 4), LOW)
        norm_cols = jnp.concatenate([norm_low.T, pad], axis=1)
        pair = split_qkv(qkv_low)
        qkv_mine = jnp.concatenate([mine(pair), norm_cols], axis=1)
        qkv_mate = swap(jnp.concatenate([other(pair), norm_cols], axis=1), "c")
        pair = split_up(up_low)
        up_mine, up_mate = mine(pair), swap(other(pair), "c")
        out_part = jnp.concatenate([out_low[:, :half_d], out_low[:, half_d:]])
        up_part = jnp.concatenate([in_order(up_mine, up_mate), out_part], axis=1)
        x_mate, g_mate = swap(own_x, "c"), swap(own_g, "c")
        qkv_parts = gather_chips(in_order(qkv_mine, qkv_mate))
        up_parts = gather_chips(up_part)
        down_parts = gather_chips(down_low)

        def qkv_moves(zz, plane):
            row = lambda h: ((zz * 2 + h) * chips + plane) * own_rows
            moves = [(0, h * own_rows, 0, own_rows, half_qkv, row(h), 0) for h in (0, 1)]
            return moves + [(1, h * own_rows, half_qkv, own_rows, LANES, row(h), 0) for h in (0, 1)]

        def up_moves(zz, plane):
            row = lambda h: ((zz * 2 + h) * chips + plane) * own_rows
            moves = [(0, h * own_rows, 0, own_rows, half_ff, row(h), 0) for h in (0, 1)]
            to = zz * block + plane * own_rows
            return moves + [(1, h * own_rows, half_ff, own_rows, half_d, to, h * half_d) for h in (0, 1)]

        def down_moves(zz, plane):
            return [(0, 0, 0, own_units, width, zz * ff_block + plane * own_units, 0)]

        qkv_w, norm_w = place(qkv_parts, depth, [(width, half_qkv), (width, LANES)], qkv_moves)
        up_w, out_w = place(up_parts, depth, [(width, half_ff), (half_d, width)], up_moves)
        (down_w,) = place(down_parts, depth, [(half_ff, width)], down_moves)
        norm_vals = norm_w[:, :4].T.astype(WIDE)
    else:
        x_mate, g_mate = swap(own_x, "c"), swap(own_g, "c")
        whole = lambda w, axis=0: lax.all_gather(w, ALL, axis=axis, tiled=True)
        qkv_w, up_w = mine(split_qkv(whole(qkv_low))), mine(split_up(whole(up_low)))
        rows_half = lambda w, b: mine(jnp.moveaxis(w.reshape(depth, 2, b, width), 1, 0)).reshape(-1, width)
        out_w, down_w = rows_half(whole(out_low), block), rows_half(whole(down_low), ff_block)
        norm_vals = whole(norm_low, 1).astype(WIDE)

    inputs = in_order(own_x, x_mate).astype(WIDE)
    grad_out = in_order(own_g, g_mate)
    normed_one, norm_one_back = jax.vjp(layer_norm, inputs, norm_vals[0], norm_vals[1])
    normed_one_low = normed_one.astype(LOW)
    projected = dot(normed_one_low, qkv_w)
    by_head = lambda a: a.reshape(tokens, heads, HEAD_DIM)
    feats, feat_back = jax.vjp(feature_map, projected[:, : 2 * half_d])
    feats = feats.astype(LOW)
    query_feat, key_feat = by_head(feats[:, :half_d]), by_head(feats[:, half_d:])
    values = by_head(projected[:, 2 * half_d :].astype(LOW))

    state = mul("the,thf->hef", key_feat, values)
    keysum = jnp.sum(key_feat.astype(WIDE), axis=0)
    pack = lambda s, k: jnp.concatenate([s.reshape(-1, LANES), k.reshape(-1, LANES)])
    unpack = lambda a: (
        a[: heads * HEAD_DIM // 2].reshape(heads, HEAD_DIM, HEAD_DIM),
        a[heads * HEAD_DIM // 2 :].reshape(heads, HEAD_DIM),
    )
    state_in, keysum_in = unpack(from_others(pack(state, keysum), 1))
    state_in_low, keysum_in_low = state_in.astype(LOW), keysum_in.astype(LOW)
    causal = jnp.tril(jnp.ones((tokens, tokens), WIDE))
    scores = mul("the,she->hts", query_feat, key_feat) * causal
    scores_low = scores.astype(LOW)
    numer = mul("hts,shf->thf", scores_low, values) + mul("the,hef->thf", query_feat, state_in_low)
    denom = jnp.sum(scores, axis=-1).T + mul("the,he->th", query_feat, keysum_in_low)
    mixed = (numer / denom[..., None]).reshape(tokens, half_d)
    mixed_low = mixed.astype(LOW)

    out_part = dot(mixed_low, out_w)
    resid = inputs + out_part + swap(out_part.astype(LOW), "c").astype(WIDE)
    normed_two, norm_two_back = jax.vjp(layer_norm, resid, norm_vals[2], norm_vals[3])
    normed_two_low = normed_two.astype(LOW)
    hidden = dot(normed_two_low, up_w)
    activated, gelu_back = jax.vjp(gelu_tanh, hidden)
    activated_low = activated.astype(LOW)
    down_grad = dot_rows(activated_low, grad_out).astype(LOW)

    halves = lambda a: a.reshape(2, group, -1)
    down_part = dot(activated_low, down_w)
    got = swap(other(halves(down_part)).astype(LOW), "c").astype(WIDE)
    activations = (mine(halves(resid + down_part)) + got).astype(LOW)

    grad_hidden = gelu_back(dot_cols(grad_out, down_w))[0].astype(LOW)
    up_grad = dot_rows(normed_two_low, grad_hidden).astype(LOW)
    grad_two = dot_cols(grad_hidden, up_w)
    grad_two = grad_two + swap(grad_two.astype(LOW), "c").astype(WIDE)
    grad_resid_norm, gain_two_grad, bias_two_grad = norm_two_back(grad_two)
    grad_resid = grad_out.astype(WIDE) + grad_resid_norm
    grad_resid_low = grad_resid.astype(LOW)
    out_grad = dot_rows(mixed_low, grad_resid_low).astype(LOW)

    grad_mixed = by_head(dot_cols(grad_resid_low, out_w))
    a_rows = grad_mixed / denom[..., None]
    b_rows = -jnp.sum(a_rows * by_head(mixed), axis=-1)
    a_low = a_rows.astype(LOW)
    state_grad = mul("the,thf->hef", query_feat, a_low)
    keysum_grad = jnp.sum(query_feat.astype(WIDE) * b_rows[..., None], axis=0)
    later_state, later_sum = unpack(from_others(pack(state_grad, keysum_grad), -1))
    later_state_low = later_state.astype(LOW)
    pulls = (mul("thf,shf->hts", a_low, values) + b_rows.T[:, :, None]) * causal
    pulls_low = pulls.astype(LOW)
    grad_query = mul("hts,she->the", pulls_low, key_feat)
    grad_query = grad_query + mul("thf,hef->the", a_low, state_in_low)
    grad_query = grad_query + b_rows[..., None] * keysum_in
    grad_key = mul("hts,the->she", pulls_low, query_feat)
    grad_key = grad_key + mul("shf,hef->she", values, later_state_low) + later_sum
    grad_value = mul("hts,thf->shf", scores_low, a_low) + mul("she,hef->shf", key_feat, later_state_low)
    flat = lambda a: a.reshape(tokens, half_d)
    grad_feats = feat_back(jnp.concatenate([flat(grad_query), flat(grad_key)], axis=1))[0]
    grad_projected = jnp.concatenate([grad_feats, flat(grad_value)], axis=1).astype(LOW)
    qkv_grad = dot_rows(normed_one_low, grad_projected).astype(LOW)
    grad_one = dot_cols(grad_projected, qkv_w)
    grad_one = grad_one + swap(grad_one.astype(LOW), "c").astype(WIDE)
    grad_in_norm, gain_one_grad, bias_one_grad = norm_one_back(grad_one)
    input_grad = mine(halves(grad_resid + grad_in_norm)).astype(LOW)
    norm_grad = jnp.stack([gain_one_grad, bias_one_grad, gain_two_grad, bias_two_grad])

    if ring:
        norm_cols = jnp.concatenate([norm_grad.T.astype(LOW), jnp.zeros((width, LANES - 4), LOW)], axis=1)
        thin, small = own_units // 2, own_rows // 2

        def down_cuts(zz, plane, half):
            return [(0, zz * ff_block + plane * own_units + half * thin, 0, thin, width, 0, 0)]

        def up_cuts(zz, plane, half):
            cuts = [(0, ((zz * 2 + half) * chips + plane) * own_rows, 0, own_rows, half_ff, 0, 0)]
            row = zz * block + plane * own_rows + half * small
            return cuts + [(1, row, p * half_d, small, half_d, p * small, half_ff) for p in (0, 1)]

        def qkv_cuts(zz, plane, half):
            row = ((zz * 2 + half) * chips + plane) * own_rows
            return [(0, row, 0, own_rows, half_qkv, 0, 0), (1, row, 0, own_rows, LANES, 0, half_qkv)]

        down_red = reduce_chips(*unplace([down_grad], depth, (thin, width), down_cuts))
        up_red = reduce_chips(*unplace([up_grad, out_grad], depth, (own_rows, half_ff + half_d), up_cuts))
        qkv_red = reduce_chips(*unplace([qkv_grad, norm_cols], depth, (own_rows, half_qkv + LANES), qkv_cuts))
        out_halves = up_red[:, half_ff:].reshape(2, 2, small, half_d)
        out_red = jnp.concatenate([out_halves[:, 0], out_halves[:, 1]], axis=2).reshape(own_rows, width)
        by_rows = lambda a: a.reshape(2, own_rows, -1)
        norm_red = mine(by_rows(qkv_red[:, half_qkv : half_qkv + 4])).T

        def joined(part, blocks):
            part = by_rows(part)
            got = swap(other(part), "c")
            pair = in_order(mine(part)[None], got[None])
            pair = pair.reshape(2, own_rows, blocks, -1)
            return jnp.moveaxis(pair, 0, 2).reshape(own_rows, -1)

        qkv_red = joined(qkv_red[:, :half_qkv], 3 * depth)
        up_red = joined(up_red[:, :half_ff], depth)
    else:
        scatter = lambda g: lax.psum_scatter(g, ALL, scatter_dimension=0, tiled=True)
        both = lambda a, axis: jnp.stack([jnp.where(core == k, a, 0.0) for k in (0, 1)], axis)
        to_all = lambda a: a.astype(WIDE)
        qkv_red = scatter(both(to_all(qkv_grad).reshape(width, 3 * depth, block), 2).reshape(width, -1))
        up_red = scatter(both(to_all(up_grad).reshape(width, depth, ff_block), 2).reshape(width, -1))
        out_red = scatter(both(to_all(out_grad).reshape(depth, block, width), 1).reshape(width, width))
        down_red = scatter(both(to_all(down_grad).reshape(depth, ff_block, width), 1).reshape(hidden_units, width))
        norm_red = scatter(jnp.where(core == 0, norm_grad, 0.0).T).T

    reduced = (qkv_red, out_red, up_red, down_red, norm_red)
    local_squares = sum(jnp.sum(grad * grad) for grad in reduced)
    grad_norm = jnp.sqrt(sum_everywhere(local_squares, ring))
    clip = jnp.minimum(1.0, CLIP_LIMIT / (grad_norm + 1e-06))
    out_fan = max(1, width * 64 // (tokens * depth))
    rates = (3.0 * width**-0.5, 3.0 * out_fan**-0.5, 3.0 * width**-0.5, 3.0 * hidden_units**-0.5, 1.5)
    decays = (WEIGHT_DECAY, WEIGHT_DECAY, WEIGHT_DECAY, WEIGHT_DECAY, 0.0)
    masters = (qkv_weight, out_weight, up_weight, down_weight, norm_params)
    firsts = (qkv_first, out_first, up_first, down_first, norm_first)
    seconds = (qkv_second, out_second, up_second, down_second, norm_second)
    news = [
        adam_update(masters[k], firsts[k], seconds[k], clip * reduced[k], rates[k], decays[k]) for k in range(5)
    ]
    return (
        activations.reshape(count, group, width),
        input_grad.reshape(count, group, width),
        grad_norm,
        *[new[0] for new in news],
        *[new[1] for new in news],
        *[new[2] for new in news],
    )


def solution(mesh):
    depth, planes = mesh.shape["seq"] // 2, mesh.shape["img"]
    across = max(k for k in range(1, planes + 1) if planes % k == 0 and k * k <= planes)
    grid = jax.sharding.Mesh(mesh.devices.reshape(depth, 2, planes // across, across), ALL)
    tokens = P(("y", "x"), ("z", "c"), None)
    matrix, norm = P(ALL, None), P(None, ALL)
    state = (matrix, matrix, matrix, matrix, norm)
    return jax.shard_map(
        body,
        mesh=grid,
        in_specs=(tokens, tokens) + state * 3,
        out_specs=(tokens, tokens, P()) + state * 3,
        check_vma=False,
    )
```

```python
import functools

import jax
import jax.numpy as jnp
from jax import lax
from jax.experimental import pallas as pl
from jax.experimental.pallas import tpu as pltpu
from jax.sharding import PartitionSpec as P

HEAD_DIM = 64
STEP = 10
NORM_EPS = 1e-05
BETA_ONE = 0.9
BETA_TWO = 0.999
ADAM_EPS = 1e-08
WEIGHT_DECAY = 0.1
CLIP_LIMIT = 1.0
LANES = 128

LOW = jnp.bfloat16
WIDE = jnp.float32
ALL = ("z", "c", "y", "x")
SWAP = [(0, 1), (1, 0)]


def swap(value, axis):
    return lax.ppermute(value, axis, SWAP)


def shift(value, step, wrap=True):
    size = lax.axis_size("z")
    pairs = [(i, (i + step) % size) for i in range(size) if wrap or 0 <= i + step < size]
    return lax.ppermute(value, "z", pairs)


def mine(pair_axis_first):
    return jnp.where(lax.axis_index("c") == 0, pair_axis_first[0], pair_axis_first[1])


def other(pair_axis_first):
    return jnp.where(lax.axis_index("c") == 0, pair_axis_first[1], pair_axis_first[0])


def in_order(own, mate, axis=0):
    first = lax.axis_index("c") == 0
    return jnp.concatenate([jnp.where(first, own, mate), jnp.where(first, mate, own)], axis)


def gather_chips(shard):
    column = jnp.stack([shard] + [shift(shard, k) for k in range(1, lax.axis_size("z"))])
    half = column.shape[0] // 2
    along_x, along_y = swap(column, "x"), swap(column, "y")
    far = (swap(along_y[:half], "x"), swap(along_x[half:], "y"))
    return (column, along_x, along_y) + far


def gathered_places(depth):
    half = depth // 2
    places = [(0, k, (k, 0, 0)) for k in range(depth)]
    places += [(1, k, (k, 0, 1)) for k in range(depth)]
    places += [(2, k, (k, 1, 0)) for k in range(depth)]
    places += [(3, k, (k, 1, 1)) for k in range(half)]
    places += [(4, k - half, (k, 1, 1)) for k in range(half, depth)]
    return places


def reduce_chips(send_x, keep_x, send_y, keep_y):
    depth = send_x.shape[1]
    got_x, got_y = swap(send_x, "x"), swap(send_y, "y")
    wide = lambda a: a.astype(WIDE)
    on_y = swap((wide(keep_x[1]) + wide(got_x[1])).astype(LOW), "y")
    on_x = swap((wide(keep_y[1]) + wide(got_y[1])).astype(LOW), "x")
    parts = []
    for k in range(depth):
        one = wide(keep_x[0, k]) + wide(got_x[0, k]) + wide(on_y[k])
        two = wide(keep_y[0, k]) + wide(got_y[0, k]) + wide(on_x[k])
        parts.append(jnp.concatenate([one, two]))
    total = parts[0]
    for k in range(1, depth):
        total = total + wide(shift(parts[k].astype(LOW), k))
    return total


def coordinates():
    return jnp.stack([lax.axis_index("z"), lax.axis_index("y"), lax.axis_index("x")]).astype(jnp.int32)


def chip_of(coords, rel, depth, back):
    dz, dy, dx = rel
    z, y, x = coords[0], coords[1], coords[2]
    zz = lax.rem(z + (depth - dz if back else dz), depth)
    yy = 1 - y if dy else y
    xx = 1 - x if dx else x
    return zz, yy * 2 + xx


def window(row, rows, col, cols):
    rows_at = pl.ds(row if isinstance(row, int) else pl.multiple_of(row, 16), rows)
    return rows_at, pl.ds(col, cols)


VMEM = pl.BlockSpec(memory_space=pltpu.VMEM)
ROOM = pltpu.CompilerParams(vmem_limit_bytes=24 * 1024 * 1024)


def place(parts, depth, outs, moves):
    def kernel(coords, *refs):
        ins, out_refs = refs[: len(parts)], refs[len(parts) :]
        for array, slot, rel in gathered_places(depth):
            zz, plane = chip_of(coords, rel, depth, True)
            for o, sr, sc, rows, cols, tr, tc in moves(zz, plane):
                out_refs[o][window(tr, rows, tc, cols)] = ins[array][(slot, *window(sr, rows, sc, cols))]

    return pl.pallas_call(
        kernel,
        out_shape=[jax.ShapeDtypeStruct(s, LOW) for s in outs],
        in_specs=[pl.BlockSpec(memory_space=pltpu.SMEM)] + [VMEM] * len(parts),
        out_specs=[VMEM] * len(outs),
        compiler_params=ROOM,
    )(coordinates(), *parts)


def unplace(grads, depth, rows_cols, moves):
    spots = []
    for dz in range(depth):
        for d in range(2):
            spots += [(0, d, dz, (dz, d, 1), 0), (1, d, dz, (dz, d, 0), 0)]
            spots += [(2, d, dz, (dz, 1, d), 1), (3, d, dz, (dz, 0, d), 1)]

    def kernel(coords, *refs):
        ins, out_refs = refs[: len(grads)], refs[len(grads) :]
        for array, d, dz, rel, half in spots:
            zz, plane = chip_of(coords, rel, depth, False)
            for i, sr, sc, rows, cols, tr, tc in moves(zz, plane, half):
                out_refs[array][(d, dz, *window(tr, rows, tc, cols))] = ins[i][window(sr, rows, sc, cols)]

    return pl.pallas_call(
        kernel,
        out_shape=[jax.ShapeDtypeStruct((2, depth) + rows_cols, LOW)] * 4,
        in_specs=[pl.BlockSpec(memory_space=pltpu.SMEM)] + [VMEM] * len(grads),
        out_specs=[VMEM] * 4,
        compiler_params=ROOM,
    )(coordinates(), *grads)


def layer_norm(values, gain, bias):
    center = values - jnp.mean(values, axis=-1, keepdims=True)
    spread = jnp.mean(center * center, axis=-1, keepdims=True)
    return center * lax.rsqrt(spread + NORM_EPS) * gain + bias


def feature_map(values):
    return jax.nn.elu(values) + 1.0


def gelu_tanh(values):
    return jax.nn.gelu(values, approximate=True)


def dot(left, right):
    return jnp.dot(left, right, preferred_element_type=WIDE)


def dot_rows(left, right):
    return lax.dot_general(left, right, (((0,), (0,)), ((), ())), preferred_element_type=WIDE)


def dot_cols(left, right):
    return lax.dot_general(left, right, (((1,), (1,)), ((), ())), preferred_element_type=WIDE)


def mul(spec, left, right):
    return jnp.einsum(spec, left, right, preferred_element_type=WIDE)


def adam_update(weight, first, second, grad, rate, decay):
    first_new = BETA_ONE * first + (1.0 - BETA_ONE) * grad
    second_new = BETA_TWO * second + (1.0 - BETA_TWO) * grad * grad
    first_hat = first_new / (1.0 - BETA_ONE**STEP)
    second_hat = second_new / (1.0 - BETA_TWO**STEP)
    weight_new = weight - rate * (first_hat / (jnp.sqrt(second_hat) + ADAM_EPS) + decay * weight)
    return (weight_new, first_new, second_new)


def from_others(value, step):
    low = value.astype(LOW)
    total = jnp.zeros(value.shape, WIDE)
    for k in range(1, lax.axis_size("z")):
        total = total + shift(low, step * k, wrap=False).astype(WIDE)
    return total


def sum_everywhere(value, direct):
    if not direct:
        return lax.psum(value, ALL)
    value = jnp.broadcast_to(value, (8, LANES))
    value = value + swap(value, "c")
    across = lax.ppermute(value, ("y", "x"), [(i, 3 - i) for i in range(4)])
    value = value + swap(value, "y") + (swap(value, "x") + across)
    near = [shift(value, k) for k in range(1, lax.axis_size("z"))]
    for part in near:
        value = value + part
    return value[0, 0]


def body(
    images,
    cotangent,
    qkv_weight,
    out_weight,
    up_weight,
    down_weight,
    norm_params,
    qkv_first,
    out_first,
    up_first,
    down_first,
    norm_first,
    qkv_second,
    out_second,
    up_second,
    down_second,
    norm_second,
):
    depth, core = lax.axis_size("z"), lax.axis_index("c")
    count, group, width = images.shape
    hidden_units = up_weight.shape[1]
    own_rows = qkv_weight.shape[0]
    own_units = down_weight.shape[0]
    chips = lax.axis_size("y") * lax.axis_size("x")
    block, ff_block = width // (2 * depth), hidden_units // (2 * depth)
    half_qkv, half_ff, half_d = 3 * width // 2, hidden_units // 2, width // 2
    ring = lax.axis_size("y") == 2 and lax.axis_size("x") == 2 and depth % 2 == 0 and own_rows % 32 == 0
    heads = half_d // HEAD_DIM
    tokens = 2 * group

    own_x, own_g = images.reshape(group, width), cotangent.reshape(group, width)
    split_qkv = lambda w: jnp.moveaxis(w.reshape(-1, 3 * depth, 2, block), 2, 0).reshape(2, -1, half_qkv)
    split_up = lambda w: jnp.moveaxis(w.reshape(-1, depth, 2, ff_block), 2, 0).reshape(2, -1, half_ff)

    qkv_low, out_low = qkv_weight.astype(LOW), out_weight.astype(LOW)
    up_low, down_low = up_weight.astype(LOW), down_weight.astype(LOW)
    norm_low = norm_params.astype(LOW)
    if ring:
        pad = jnp.zeros((own_rows, LANES - 4), LOW)
        norm_cols = jnp.concatenate([norm_low.T, pad], axis=1)
        pair = split_qkv(qkv_low)
        qkv_mine = jnp.concatenate([mine(pair), norm_cols], axis=1)
        qkv_mate = swap(jnp.concatenate([other(pair), norm_cols], axis=1), "c")
        pair = split_up(up_low)
        up_mine, up_mate = mine(pair), swap(other(pair), "c")
        out_part = jnp.concatenate([out_low[:, :half_d], out_low[:, half_d:]])
        up_part = jnp.concatenate([in_order(up_mine, up_mate), out_part], axis=1)
        x_mate, g_mate = swap(own_x, "c"), swap(own_g, "c")
        qkv_parts = gather_chips(in_order(qkv_mine, qkv_mate))
        up_parts = gather_chips(up_part)
        down_parts = gather_chips(down_low)

        def qkv_moves(zz, plane):
            row = lambda h: ((zz * 2 + h) * chips + plane) * own_rows
            moves = [(0, h * own_rows, 0, own_rows, half_qkv, row(h), 0) for h in (0, 1)]
            return moves + [(1, h * own_rows, half_qkv, own_rows, LANES, row(h), 0) for h in (0, 1)]

        def up_moves(zz, plane):
            row = lambda h: ((zz * 2 + h) * chips + plane) * own_rows
            moves = [(0, h * own_rows, 0, own_rows, half_ff, row(h), 0) for h in (0, 1)]
            to = zz * block + plane * own_rows
            return moves + [(1, h * own_rows, half_ff, own_rows, half_d, to, h * half_d) for h in (0, 1)]

        def down_moves(zz, plane):
            return [(0, 0, 0, own_units, width, zz * ff_block + plane * own_units, 0)]

        qkv_w, norm_w = place(qkv_parts, depth, [(width, half_qkv), (width, LANES)], qkv_moves)
        up_w, out_w = place(up_parts, depth, [(width, half_ff), (half_d, width)], up_moves)
        (down_w,) = place(down_parts, depth, [(half_ff, width)], down_moves)
        norm_vals = norm_w[:, :4].T.astype(WIDE)
    else:
        x_mate, g_mate = swap(own_x, "c"), swap(own_g, "c")
        whole = lambda w, axis=0: lax.all_gather(w, ALL, axis=axis, tiled=True)
        qkv_w, up_w = mine(split_qkv(whole(qkv_low))), mine(split_up(whole(up_low)))
        rows_half = lambda w, b: mine(jnp.moveaxis(w.reshape(depth, 2, b, width), 1, 0)).reshape(-1, width)
        out_w, down_w = rows_half(whole(out_low), block), rows_half(whole(down_low), ff_block)
        norm_vals = whole(norm_low, 1).astype(WIDE)

    inputs = in_order(own_x, x_mate).astype(WIDE)
    grad_out = in_order(own_g, g_mate)
    normed_one, norm_one_back = jax.vjp(layer_norm, inputs, norm_vals[0], norm_vals[1])
    normed_one_low = normed_one.astype(LOW)
    projected = dot(normed_one_low, qkv_w)
    by_head = lambda a: a.reshape(tokens, heads, HEAD_DIM)
    feats, feat_back = jax.vjp(feature_map, projected[:, : 2 * half_d])
    feats = feats.astype(LOW)
    query_feat, key_feat = by_head(feats[:, :half_d]), by_head(feats[:, half_d:])
    values = by_head(projected[:, 2 * half_d :].astype(LOW))

    state = mul("the,thf->hef", key_feat, values)
    keysum = jnp.sum(key_feat.astype(WIDE), axis=0)
    pack = lambda s, k: jnp.concatenate([s.reshape(-1, LANES), k.reshape(-1, LANES)])
    unpack = lambda a: (
        a[: heads * HEAD_DIM // 2].reshape(heads, HEAD_DIM, HEAD_DIM),
        a[heads * HEAD_DIM // 2 :].reshape(heads, HEAD_DIM),
    )
    state_in, keysum_in = unpack(from_others(pack(state, keysum), 1))
    state_in_low, keysum_in_low = state_in.astype(LOW), keysum_in.astype(LOW)
    causal = jnp.tril(jnp.ones((tokens, tokens), WIDE))
    scores = mul("the,she->hts", query_feat, key_feat) * causal
    scores_low = scores.astype(LOW)
    numer = mul("hts,shf->thf", scores_low, values) + mul("the,hef->thf", query_feat, state_in_low)
    denom = jnp.sum(scores, axis=-1).T + mul("the,he->th", query_feat, keysum_in_low)
    mixed = (numer / denom[..., None]).reshape(tokens, half_d)
    mixed_low = mixed.astype(LOW)

    out_part = dot(mixed_low, out_w)
    resid = inputs + out_part + swap(out_part.astype(LOW), "c").astype(WIDE)
    normed_two, norm_two_back = jax.vjp(layer_norm, resid, norm_vals[2], norm_vals[3])
    normed_two_low = normed_two.astype(LOW)
    hidden = dot(normed_two_low, up_w)
    activated, gelu_back = jax.vjp(gelu_tanh, hidden)
    activated_low = activated.astype(LOW)
    down_grad = dot_rows(activated_low, grad_out).astype(LOW)

    halves = lambda a: a.reshape(2, group, -1)
    down_part = dot(activated_low, down_w)
    got = swap(other(halves(down_part)).astype(LOW), "c").astype(WIDE)
    activations = (mine(halves(resid + down_part)) + got).astype(LOW)

    grad_hidden = gelu_back(dot_cols(grad_out, down_w))[0].astype(LOW)
    up_grad = dot_rows(normed_two_low, grad_hidden).astype(LOW)
    grad_two = dot_cols(grad_hidden, up_w)
    grad_two = grad_two + swap(grad_two.astype(LOW), "c").astype(WIDE)
    grad_resid_norm, gain_two_grad, bias_two_grad = norm_two_back(grad_two)
    grad_resid = grad_out.astype(WIDE) + grad_resid_norm
    grad_resid_low = grad_resid.astype(LOW)
    out_grad = dot_rows(mixed_low, grad_resid_low).astype(LOW)

    grad_mixed = by_head(dot_cols(grad_resid_low, out_w))
    a_rows = grad_mixed / denom[..., None]
    b_rows = -jnp.sum(a_rows * by_head(mixed), axis=-1)
    a_low = a_rows.astype(LOW)
    state_grad = mul("the,thf->hef", query_feat, a_low)
    keysum_grad = jnp.sum(query_feat.astype(WIDE) * b_rows[..., None], axis=0)
    later_state, later_sum = unpack(from_others(pack(state_grad, keysum_grad), -1))
    later_state_low = later_state.astype(LOW)
    pulls = (mul("thf,shf->hts", a_low, values) + b_rows.T[:, :, None]) * causal
    pulls_low = pulls.astype(LOW)
    grad_query = mul("hts,she->the", pulls_low, key_feat)
    grad_query = grad_query + mul("thf,hef->the", a_low, state_in_low)
    grad_query = grad_query + b_rows[..., None] * keysum_in
    grad_key = mul("hts,the->she", pulls_low, query_feat)
    grad_key = grad_key + mul("shf,hef->she", values, later_state_low) + later_sum
    grad_value = mul("hts,thf->shf", scores_low, a_low) + mul("she,hef->shf", key_feat, later_state_low)
    flat = lambda a: a.reshape(tokens, half_d)
    grad_feats = feat_back(jnp.concatenate([flat(grad_query), flat(grad_key)], axis=1))[0]
    grad_projected = jnp.concatenate([grad_feats, flat(grad_value)], axis=1).astype(LOW)
    qkv_grad = dot_rows(normed_one_low, grad_projected).astype(LOW)
    grad_one = dot_cols(grad_projected, qkv_w)
    grad_one = grad_one + swap(grad_one.astype(LOW), "c").astype(WIDE)
    grad_in_norm, gain_one_grad, bias_one_grad = norm_one_back(grad_one)
    input_grad = mine(halves(grad_resid + grad_in_norm)).astype(LOW)
    norm_grad = jnp.stack([gain_one_grad, bias_one_grad, gain_two_grad, bias_two_grad])

    if ring:
        norm_cols = jnp.concatenate([norm_grad.T.astype(LOW), jnp.zeros((width, LANES - 4), LOW)], axis=1)
        thin, small = own_units // 2, own_rows // 2

        def down_cuts(zz, plane, half):
            return [(0, zz * ff_block + plane * own_units + half * thin, 0, thin, width, 0, 0)]

        def up_cuts(zz, plane, half):
            cuts = [(0, ((zz * 2 + half) * chips + plane) * own_rows, 0, own_rows, half_ff, 0, 0)]
            row = zz * block + plane * own_rows + half * small
            return cuts + [(1, row, p * half_d, small, half_d, p * small, half_ff) for p in (0, 1)]

        def qkv_cuts(zz, plane, half):
            row = ((zz * 2 + half) * chips + plane) * own_rows
            return [(0, row, 0, own_rows, half_qkv, 0, 0), (1, row, 0, own_rows, LANES, 0, half_qkv)]

        down_red = reduce_chips(*unplace([down_grad], depth, (thin, width), down_cuts))
        up_red = reduce_chips(*unplace([up_grad, out_grad], depth, (own_rows, half_ff + half_d), up_cuts))
        qkv_red = reduce_chips(*unplace([qkv_grad, norm_cols], depth, (own_rows, half_qkv + LANES), qkv_cuts))
        out_halves = up_red[:, half_ff:].reshape(2, 2, small, half_d)
        out_red = jnp.concatenate([out_halves[:, 0], out_halves[:, 1]], axis=2).reshape(own_rows, width)
        by_rows = lambda a: a.reshape(2, own_rows, -1)
        norm_red = mine(by_rows(qkv_red[:, half_qkv : half_qkv + 4])).T

        def joined(part, blocks):
            part = by_rows(part)
            got = swap(other(part), "c")
            pair = in_order(mine(part)[None], got[None])
            pair = pair.reshape(2, own_rows, blocks, -1)
            return jnp.moveaxis(pair, 0, 2).reshape(own_rows, -1)

        qkv_red = joined(qkv_red[:, :half_qkv], 3 * depth)
        up_red = joined(up_red[:, :half_ff], depth)
    else:
        scatter = lambda g: lax.psum_scatter(g, ALL, scatter_dimension=0, tiled=True)
        both = lambda a, axis: jnp.stack([jnp.where(core == k, a, 0.0) for k in (0, 1)], axis)
        to_all = lambda a: a.astype(WIDE)
        qkv_red = scatter(both(to_all(qkv_grad).reshape(width, 3 * depth, block), 2).reshape(width, -1))
        up_red = scatter(both(to_all(up_grad).reshape(width, depth, ff_block), 2).reshape(width, -1))
        out_red = scatter(both(to_all(out_grad).reshape(depth, block, width), 1).reshape(width, width))
        down_red = scatter(both(to_all(down_grad).reshape(depth, ff_block, width), 1).reshape(hidden_units, width))
        norm_red = scatter(jnp.where(core == 0, norm_grad, 0.0).T).T

    reduced = (qkv_red, out_red, up_red, down_red, norm_red)
    local_squares = sum(jnp.sum(grad * grad) for grad in reduced)
    grad_norm = jnp.sqrt(sum_everywhere(local_squares, ring))
    clip = jnp.minimum(1.0, CLIP_LIMIT / (grad_norm + 1e-06))
    out_fan = max(1, width * 64 // (tokens * depth))
    rates = (3.0 * width**-0.5, 3.0 * out_fan**-0.5, 3.0 * width**-0.5, 3.0 * hidden_units**-0.5, 1.5)
    decays = (WEIGHT_DECAY, WEIGHT_DECAY, WEIGHT_DECAY, WEIGHT_DECAY, 0.0)
    masters = (qkv_weight, out_weight, up_weight, down_weight, norm_params)
    firsts = (qkv_first, out_first, up_first, down_first, norm_first)
    seconds = (qkv_second, out_second, up_second, down_second, norm_second)
    news = [
        adam_update(masters[k], firsts[k], seconds[k], clip * reduced[k], rates[k], decays[k]) for k in range(5)
    ]
    return (
        activations.reshape(count, group, width),
        input_grad.reshape(count, group, width),
        grad_norm,
        *[new[0] for new in news],
        *[new[1] for new in news],
        *[new[2] for new in news],
    )


def solution(mesh):
    depth, planes = mesh.shape["seq"] // 2, mesh.shape["img"]
    across = max(k for k in range(1, planes + 1) if planes % k == 0 and k * k <= planes)
    grid = jax.sharding.Mesh(mesh.devices.reshape(depth, 2, planes // across, across), ALL)
    tokens = P(("y", "x"), ("z", "c"), None)
    matrix, norm = P(ALL, None), P(None, ALL)
    state = (matrix, matrix, matrix, matrix, norm)
    return jax.shard_map(
        body,
        mesh=grid,
        in_specs=(tokens, tokens) + state * 3,
        out_specs=(tokens, tokens, P()) + state * 3,
        check_vma=False,
    )
```

```python
import functools

import jax
import jax.numpy as jnp
from jax import lax
from jax.experimental import pallas as pl
from jax.experimental.pallas import tpu as pltpu
from jax.sharding import PartitionSpec as P

HEAD_DIM = 64
STEP = 10
NORM_EPS = 1e-05
BETA_ONE = 0.9
BETA_TWO = 0.999
ADAM_EPS = 1e-08
WEIGHT_DECAY = 0.1
CLIP_LIMIT = 1.0
LANES = 128

LOW = jnp.bfloat16
WIDE = jnp.float32
ALL = ("z", "c", "y", "x")
SWAP = [(0, 1), (1, 0)]


def swap(value, axis):
    return lax.ppermute(value, axis, SWAP)


def shift(value, step, wrap=True):
    size = lax.axis_size("z")
    pairs = [(i, (i + step) % size) for i in range(size) if wrap or 0 <= i + step < size]
    return lax.ppermute(value, "z", pairs)


def mine(pair_axis_first):
    return jnp.where(lax.axis_index("c") == 0, pair_axis_first[0], pair_axis_first[1])


def other(pair_axis_first):
    return jnp.where(lax.axis_index("c") == 0, pair_axis_first[1], pair_axis_first[0])


def in_order(own, mate, axis=0):
    first = lax.axis_index("c") == 0
    return jnp.concatenate([jnp.where(first, own, mate), jnp.where(first, mate, own)], axis)


def after(value, *before):
    return lax.optimization_barrier((value, *before))[0]


def column_first(shard):
    return [shard] + [shift(shard, k) for k in range(1, lax.axis_size("z"))]


def plane_last(column):
    half = column.shape[0] // 2
    along_x, along_y = swap(column, "x"), swap(column, "y")
    far = (swap(along_y[:half], "x"), swap(along_x[half:], "y"))
    return (column, along_x, along_y) + far


def plane_first(shard):
    half = shard.shape[0] // 2
    along_x, along_y = swap(shard, "x"), swap(shard, "y")
    far_low, far_high = swap(along_y[:half], "x"), swap(along_x[half:], "y")
    return jnp.concatenate([shard, along_x, along_y, far_low, far_high])


def column_last(plane):
    parts = [plane]
    for _ in range(1, lax.axis_size("z")):
        parts.append(shift(parts[-1], 1))
    return parts


def column_first_spots(depth):
    half = depth // 2
    spots = [(0, (k,), 0, (k, 0, 0)) for k in range(depth)]
    spots += [(1, (k,), 0, (k, 0, 1)) for k in range(depth)]
    spots += [(2, (k,), 0, (k, 1, 0)) for k in range(depth)]
    spots += [(3, (k,), 0, (k, 1, 1)) for k in range(half)]
    return spots + [(4, (k - half,), 0, (k, 1, 1)) for k in range(half, depth)]


def plane_first_spots(depth, rows):
    return [(k, (), p * rows, (k, p // 2, p % 2)) for k in range(depth) for p in range(4)]


def reduce_chips(send_x, keep_x, send_y, keep_y, gate=()):
    depth = send_x.shape[1]
    send_x, send_y = after(send_x, *gate), after(send_y, *gate)
    got_x, got_y = swap(send_x, "x"), swap(send_y, "y")
    wide = lambda a: a.astype(WIDE)
    on_y = swap((wide(keep_x[1]) + wide(got_x[1])).astype(LOW), "y")
    on_x = swap((wide(keep_y[1]) + wide(got_y[1])).astype(LOW), "x")
    parts = []
    for k in range(depth):
        one = wide(keep_x[0, k]) + wide(got_x[0, k]) + wide(on_y[k])
        two = wide(keep_y[0, k]) + wide(got_y[0, k]) + wide(on_x[k])
        parts.append(jnp.concatenate([one, two]))
    total = parts[0]
    for k in range(1, depth):
        total = total + wide(shift(parts[k].astype(LOW), k))
    return total, (on_x, on_y)


def coordinates():
    return jnp.stack([lax.axis_index(name) for name in ("z", "y", "x", "c")]).astype(jnp.int32)


def chip_of(coords, rel, depth, back):
    dz, dy, dx = rel
    z, y, x = coords[0], coords[1], coords[2]
    zz = lax.rem(z + (depth - dz if back else dz), depth)
    yy = 1 - y if dy else y
    xx = 1 - x if dx else x
    return zz, yy * 2 + xx


def window(row, rows, col, cols):
    rows_at = pl.ds(row if isinstance(row, int) else pl.multiple_of(row, 16), rows)
    return rows_at, pl.ds(col, cols)


VMEM = pl.BlockSpec(memory_space=pltpu.VMEM)
ROOM = pltpu.CompilerParams(vmem_limit_bytes=24 * 1024 * 1024)


def place(parts, depth, outs, spots, moves):
    def kernel(coords, *refs):
        ins, out_refs = refs[: len(parts)], refs[len(parts) :]
        for array, lead, base, rel in spots:
            zz, plane = chip_of(coords, rel, depth, True)
            for o, sr, sc, rows, cols, tr, tc in moves(zz, plane):
                out_refs[o][window(tr, rows, tc, cols)] = ins[array][(*lead, *window(base + sr, rows, sc, cols))]

    return pl.pallas_call(
        kernel,
        out_shape=[jax.ShapeDtypeStruct(s, LOW) for s in outs],
        in_specs=[pl.BlockSpec(memory_space=pltpu.SMEM)] + [VMEM] * len(parts),
        out_specs=[VMEM] * len(outs),
        compiler_params=ROOM,
    )(coordinates(), *parts)


def unplace(grads, depth, rows_cols, moves):
    spots = []
    for dz in range(depth):
        for d in range(2):
            spots += [(0, d, dz, (dz, d, 1), 0), (1, d, dz, (dz, d, 0), 0)]
            spots += [(2, d, dz, (dz, 1, d), 1), (3, d, dz, (dz, 0, d), 1)]

    def kernel(coords, *refs):
        ins, out_refs = refs[: len(grads)], refs[len(grads) :]
        for array, d, dz, rel, half in spots:
            zz, plane = chip_of(coords, rel, depth, False)
            for i, sr, sc, rows, cols, tr, tc in moves(zz, plane, half):
                out_refs[array][(d, dz, *window(tr, rows, tc, cols))] = ins[i][window(sr, rows, sc, cols)]

    return pl.pallas_call(
        kernel,
        out_shape=[jax.ShapeDtypeStruct((2, depth) + rows_cols, LOW)] * 4,
        in_specs=[pl.BlockSpec(memory_space=pltpu.SMEM)] + [VMEM] * len(grads),
        out_specs=[VMEM] * 4,
        compiler_params=ROOM,
    )(coordinates(), *grads)


def cast_qkv(qkv, norm, halves):
    rows, cols = qkv.shape
    wide = cols // 2 + LANES
    block = cols // (2 * halves)

    def kernel(coords, qkv_ref, norm_ref, own_ref, mate_ref, tall):
        first = coords[3] == 0
        for j in range(halves):
            a = qkv_ref[:, 2 * j * block : (2 * j + 1) * block]
            b = qkv_ref[:, (2 * j + 1) * block : (2 * j + 2) * block]
            own_ref[:, j * block : (j + 1) * block] = jnp.where(first, a, b).astype(LOW)
            mate_ref[:, j * block : (j + 1) * block] = jnp.where(first, b, a).astype(LOW)
        tall[...] = jnp.zeros_like(tall)
        tall[0:4, :] = norm_ref[...].astype(LOW).astype(WIDE)
        i = lax.broadcasted_iota(jnp.int32, (rows, rows), 0)
        j = lax.broadcasted_iota(jnp.int32, (rows, rows), 1)
        columns = dot_cols((i == j).astype(LOW), tall[...].astype(LOW)).astype(LOW)
        own_ref[:, cols // 2 :] = columns
        mate_ref[:, cols // 2 :] = columns

    return pl.pallas_call(
        kernel,
        out_shape=[jax.ShapeDtypeStruct((rows, wide), LOW)] * 2,
        in_specs=[pl.BlockSpec(memory_space=pltpu.SMEM), VMEM, VMEM],
        out_specs=[VMEM] * 2,
        scratch_shapes=[pltpu.VMEM((LANES, rows), WIDE)],
        compiler_params=ROOM,
    )(coordinates(), qkv, norm)


def cast_rest(up, out, down, halves):
    rows, cols = up.shape
    block, width = cols // (2 * halves), out.shape[1]

    def kernel(coords, up_ref, out_ref, down_ref, own_ref, mate_ref, part_ref, low_ref):
        first = coords[3] == 0
        for j in range(halves):
            a = up_ref[:, 2 * j * block : (2 * j + 1) * block]
            b = up_ref[:, (2 * j + 1) * block : (2 * j + 2) * block]
            own_ref[:, j * block : (j + 1) * block] = jnp.where(first, a, b).astype(LOW)
            mate_ref[:, j * block : (j + 1) * block] = jnp.where(first, b, a).astype(LOW)
        part_ref[:rows, :] = out_ref[:, : width // 2].astype(LOW)
        part_ref[rows:, :] = out_ref[:, width // 2 :].astype(LOW)
        low_ref[...] = down_ref[...].astype(LOW)

    return pl.pallas_call(
        kernel,
        out_shape=[jax.ShapeDtypeStruct((rows, cols // 2), LOW)] * 2
        + [jax.ShapeDtypeStruct((2 * rows, width // 2), LOW), jax.ShapeDtypeStruct(down.shape, LOW)],
        in_specs=[pl.BlockSpec(memory_space=pltpu.SMEM), VMEM, VMEM, VMEM],
        out_specs=[VMEM] * 4,
        compiler_params=ROOM,
    )(coordinates(), up, out, down)


def join_rows(own, mate, side=None):
    rows, cols = own.shape
    wide = cols + (side.shape[1] if side is not None else 0)

    def kernel(coords, own_ref, mate_ref, *refs):
        out_ref = refs[-1]
        core = coords[3]
        out_ref[pl.ds(pl.multiple_of(core * rows, 16), rows), :cols] = own_ref[...]
        out_ref[pl.ds(pl.multiple_of((1 - core) * rows, 16), rows), :cols] = mate_ref[...]
        if side is not None:
            out_ref[:, cols:] = refs[0][...]

    ins = [own, mate] + ([side] if side is not None else [])
    return pl.pallas_call(
        kernel,
        out_shape=jax.ShapeDtypeStruct((2 * rows, wide), LOW),
        in_specs=[pl.BlockSpec(memory_space=pltpu.SMEM)] + [VMEM] * len(ins),
        out_specs=VMEM,
        compiler_params=ROOM,
    )(coordinates(), *ins)


def layer_norm(values, gain, bias):
    center = values - jnp.mean(values, axis=-1, keepdims=True)
    spread = jnp.mean(center * center, axis=-1, keepdims=True)
    return center * lax.rsqrt(spread + NORM_EPS) * gain + bias


def feature_map(values):
    return jax.nn.elu(values) + 1.0


def gelu_tanh(values):
    return jax.nn.gelu(values, approximate=True)


def dot(left, right):
    return jnp.dot(left, right, preferred_element_type=WIDE)


def dot_rows(left, right):
    return lax.dot_general(left, right, (((0,), (0,)), ((), ())), preferred_element_type=WIDE)


def dot_cols(left, right):
    return lax.dot_general(left, right, (((1,), (1,)), ((), ())), preferred_element_type=WIDE)


def mul(spec, left, right):
    return jnp.einsum(spec, left, right, preferred_element_type=WIDE)


def adam_update(weight, first, second, grad, rate, decay):
    first_new = BETA_ONE * first + (1.0 - BETA_ONE) * grad
    second_new = BETA_TWO * second + (1.0 - BETA_TWO) * grad * grad
    first_hat = first_new / (1.0 - BETA_ONE**STEP)
    second_hat = second_new / (1.0 - BETA_TWO**STEP)
    weight_new = weight - rate * (first_hat / (jnp.sqrt(second_hat) + ADAM_EPS) + decay * weight)
    return (weight_new, first_new, second_new)


def from_others(value, step):
    low = value.astype(LOW)
    total = jnp.zeros(value.shape, WIDE)
    for k in range(1, lax.axis_size("z")):
        total = total + shift(low, step * k, wrap=False).astype(WIDE)
    return total


def sum_everywhere(value, direct):
    if not direct:
        return lax.psum(value, ALL)
    value = jnp.broadcast_to(value, (8, LANES))
    value = value + swap(value, "c")
    across = lax.ppermute(value, ("y", "x"), [(i, 3 - i) for i in range(4)])
    value = value + swap(value, "y") + (swap(value, "x") + across)
    near = [shift(value, k) for k in range(1, lax.axis_size("z"))]
    for part in near:
        value = value + part
    return value[0, 0]


def body(
    images,
    cotangent,
    qkv_weight,
    out_weight,
    up_weight,
    down_weight,
    norm_params,
    qkv_first,
    out_first,
    up_first,
    down_first,
    norm_first,
    qkv_second,
    out_second,
    up_second,
    down_second,
    norm_second,
):
    depth, core = lax.axis_size("z"), lax.axis_index("c")
    count, group, width = images.shape
    hidden_units = up_weight.shape[1]
    own_rows = qkv_weight.shape[0]
    own_units = down_weight.shape[0]
    chips = lax.axis_size("y") * lax.axis_size("x")
    block, ff_block = width // (2 * depth), hidden_units // (2 * depth)
    half_qkv, half_ff, half_d = 3 * width // 2, hidden_units // 2, width // 2
    ring = lax.axis_size("y") == 2 and lax.axis_size("x") == 2 and depth % 2 == 0 and own_rows % 32 == 0
    heads = half_d // HEAD_DIM
    tokens = 2 * group

    own_x, own_g = images.reshape(group, width), cotangent.reshape(group, width)
    split_qkv = lambda w: jnp.moveaxis(w.reshape(-1, 3 * depth, 2, block), 2, 0).reshape(2, -1, half_qkv)
    split_up = lambda w: jnp.moveaxis(w.reshape(-1, depth, 2, ff_block), 2, 0).reshape(2, -1, half_ff)

    if ring:
        qkv_mine, qkv_give = cast_qkv(qkv_weight, norm_params, 3 * depth)
        up_mine, up_give, out_part, down_low = cast_rest(after(up_weight, qkv_give), out_weight, down_weight, depth)
        qkv_mate = swap(qkv_give, "c")
        up_mate = swap(up_give, "c")
        x_mate = swap(own_x, "c")
        qkv_column = column_first(join_rows(qkv_mine, qkv_mate))
        down_plane = plane_first(down_low)
        up_part = join_rows(up_mine, up_mate, out_part)
        up_column = column_first(after(up_part, *qkv_column))
        qkv_parts = plane_last(jnp.stack(qkv_column))
        g_mate = swap(after(own_g, *qkv_column), "c")
        up_parts = plane_last(after(jnp.stack(up_column), *qkv_parts[3:]))
        down_parts = column_last(after(down_plane, *up_column))

        def qkv_moves(zz, plane):
            row = lambda h: ((zz * 2 + h) * chips + plane) * own_rows
            moves = [(0, h * own_rows, 0, own_rows, half_qkv, row(h), 0) for h in (0, 1)]
            return moves + [(1, h * own_rows, half_qkv, own_rows, LANES, row(h), 0) for h in (0, 1)]

        def up_moves(zz, plane):
            row = lambda h: ((zz * 2 + h) * chips + plane) * own_rows
            moves = [(0, h * own_rows, 0, own_rows, half_ff, row(h), 0) for h in (0, 1)]
            to = zz * block + plane * own_rows
            return moves + [(1, h * own_rows, half_ff, own_rows, half_d, to, h * half_d) for h in (0, 1)]

        def down_moves(zz, plane):
            return [(0, 0, 0, own_units, width, zz * ff_block + plane * own_units, 0)]

        spots = column_first_spots(depth)
        qkv_w, norm_w = place(qkv_parts, depth, [(width, half_qkv), (width, LANES)], spots, qkv_moves)
        up_w, out_w = place(up_parts, depth, [(width, half_ff), (half_d, width)], spots, up_moves)
        spots = plane_first_spots(depth, own_units)
        (down_w,) = place(down_parts, depth, [(half_ff, width)], spots, down_moves)
        norm_vals = norm_w[:, :4].T.astype(WIDE)
    else:
        qkv_low, out_low = qkv_weight.astype(LOW), out_weight.astype(LOW)
        up_low, down_low = up_weight.astype(LOW), down_weight.astype(LOW)
        norm_low = norm_params.astype(LOW)
        x_mate, g_mate = swap(own_x, "c"), swap(own_g, "c")
        whole = lambda w, axis=0: lax.all_gather(w, ALL, axis=axis, tiled=True)
        qkv_w, up_w = mine(split_qkv(whole(qkv_low))), mine(split_up(whole(up_low)))
        rows_half = lambda w, b: mine(jnp.moveaxis(w.reshape(depth, 2, b, width), 1, 0)).reshape(-1, width)
        out_w, down_w = rows_half(whole(out_low), block), rows_half(whole(down_low), ff_block)
        norm_vals = whole(norm_low, 1).astype(WIDE)

    inputs = in_order(own_x, x_mate).astype(WIDE)
    grad_out = in_order(own_g, g_mate)
    normed_one, norm_one_back = jax.vjp(layer_norm, inputs, norm_vals[0], norm_vals[1])
    normed_one_low = normed_one.astype(LOW)
    projected = dot(normed_one_low, qkv_w)
    by_head = lambda a: a.reshape(tokens, heads, HEAD_DIM)
    feats, feat_back = jax.vjp(feature_map, projected[:, : 2 * half_d])
    feats = feats.astype(LOW)
    query_feat, key_feat = by_head(feats[:, :half_d]), by_head(feats[:, half_d:])
    values = by_head(projected[:, 2 * half_d :].astype(LOW))

    state = mul("the,thf->hef", key_feat, values)
    keysum = jnp.sum(key_feat.astype(WIDE), axis=0)
    pack = lambda s, k: jnp.concatenate([s.reshape(-1, LANES), k.reshape(-1, LANES)])
    unpack = lambda a: (
        a[: heads * HEAD_DIM // 2].reshape(heads, HEAD_DIM, HEAD_DIM),
        a[heads * HEAD_DIM // 2 :].reshape(heads, HEAD_DIM),
    )
    state_in, keysum_in = unpack(from_others(pack(state, keysum), 1))
    state_in_low, keysum_in_low = state_in.astype(LOW), keysum_in.astype(LOW)
    causal = jnp.tril(jnp.ones((tokens, tokens), WIDE))
    scores = mul("the,she->hts", query_feat, key_feat) * causal
    scores_low = scores.astype(LOW)
    numer = mul("hts,shf->thf", scores_low, values) + mul("the,hef->thf", query_feat, state_in_low)
    denom = jnp.sum(scores, axis=-1).T + mul("the,he->th", query_feat, keysum_in_low)
    mixed = (numer / denom[..., None]).reshape(tokens, half_d)
    mixed_low = mixed.astype(LOW)

    out_part = dot(mixed_low, out_w)
    resid = inputs + out_part + swap(out_part.astype(LOW), "c").astype(WIDE)
    normed_two, norm_two_back = jax.vjp(layer_norm, resid, norm_vals[2], norm_vals[3])
    normed_two_low = normed_two.astype(LOW)
    hidden = dot(normed_two_low, up_w)
    activated, gelu_back = jax.vjp(gelu_tanh, hidden)
    activated_low = activated.astype(LOW)
    down_grad = dot_rows(activated_low, grad_out).astype(LOW)

    halves = lambda a: a.reshape(2, group, -1)
    down_part = dot(activated_low, down_w)
    got = swap(other(halves(down_part)).astype(LOW), "c").astype(WIDE)
    activations = (mine(halves(resid + down_part)) + got).astype(LOW)

    grad_hidden = gelu_back(dot_cols(grad_out, down_w))[0].astype(LOW)
    up_grad = dot_rows(normed_two_low, grad_hidden).astype(LOW)
    grad_two = dot_cols(grad_hidden, up_w)
    grad_two = grad_two + swap(grad_two.astype(LOW), "c").astype(WIDE)
    grad_resid_norm, gain_two_grad, bias_two_grad = norm_two_back(grad_two)
    grad_resid = grad_out.astype(WIDE) + grad_resid_norm
    grad_resid_low = grad_resid.astype(LOW)
    out_grad = dot_rows(mixed_low, grad_resid_low).astype(LOW)

    grad_mixed = by_head(dot_cols(grad_resid_low, out_w))
    a_rows = grad_mixed / denom[..., None]
    b_rows = -jnp.sum(a_rows * by_head(mixed), axis=-1)
    a_low = a_rows.astype(LOW)
    state_grad = mul("the,thf->hef", query_feat, a_low)
    keysum_grad = jnp.sum(query_feat.astype(WIDE) * b_rows[..., None], axis=0)
    later_state, later_sum = unpack(from_others(pack(state_grad, keysum_grad), -1))
    later_state_low = later_state.astype(LOW)
    pulls = (mul("thf,shf->hts", a_low, values) + b_rows.T[:, :, None]) * causal
    pulls_low = pulls.astype(LOW)
    grad_query = mul("hts,she->the", pulls_low, key_feat)
    grad_query = grad_query + mul("thf,hef->the", a_low, state_in_low)
    grad_query = grad_query + b_rows[..., None] * keysum_in
    grad_key = mul("hts,the->she", pulls_low, query_feat)
    grad_key = grad_key + mul("shf,hef->she", values, later_state_low) + later_sum
    grad_value = mul("hts,thf->shf", scores_low, a_low) + mul("she,hef->shf", key_feat, later_state_low)
    flat = lambda a: a.reshape(tokens, half_d)
    grad_feats = feat_back(jnp.concatenate([flat(grad_query), flat(grad_key)], axis=1))[0]
    grad_projected = jnp.concatenate([grad_feats, flat(grad_value)], axis=1).astype(LOW)
    qkv_grad = dot_rows(normed_one_low, grad_projected).astype(LOW)
    grad_one = dot_cols(grad_projected, qkv_w)
    grad_one = grad_one + swap(grad_one.astype(LOW), "c").astype(WIDE)
    grad_in_norm, gain_one_grad, bias_one_grad = norm_one_back(grad_one)
    input_grad = mine(halves(grad_resid + grad_in_norm)).astype(LOW)
    norm_grad = jnp.stack([gain_one_grad, bias_one_grad, gain_two_grad, bias_two_grad])

    if ring:
        norm_cols = jnp.concatenate([norm_grad.T.astype(LOW), jnp.zeros((width, LANES - 4), LOW)], axis=1)
        thin, small = own_units // 2, own_rows // 2

        def down_cuts(zz, plane, half):
            return [(0, zz * ff_block + plane * own_units + half * thin, 0, thin, width, 0, 0)]

        def up_cuts(zz, plane, half):
            cuts = [(0, ((zz * 2 + half) * chips + plane) * own_rows, 0, own_rows, half_ff, 0, 0)]
            row = zz * block + plane * own_rows + half * small
            return cuts + [(1, row, p * half_d, small, half_d, p * small, half_ff) for p in (0, 1)]

        def qkv_cuts(zz, plane, half):
            row = ((zz * 2 + half) * chips + plane) * own_rows
            return [(0, row, 0, own_rows, half_qkv, 0, 0), (1, row, 0, own_rows, LANES, 0, half_qkv)]

        down_red, gate = reduce_chips(*unplace([down_grad], depth, (thin, width), down_cuts))
        cuts = unplace([up_grad, out_grad], depth, (own_rows, half_ff + half_d), up_cuts)
        up_red, gate = reduce_chips(*cuts, gate)
        cuts = unplace([qkv_grad, norm_cols], depth, (own_rows, half_qkv + LANES), qkv_cuts)
        qkv_red, gate = reduce_chips(*cuts, gate)
        out_halves = up_red[:, half_ff:].reshape(2, 2, small, half_d)
        out_red = jnp.concatenate([out_halves[:, 0], out_halves[:, 1]], axis=2).reshape(own_rows, width)
        by_rows = lambda a: a.reshape(2, own_rows, -1)
        norm_red = mine(by_rows(qkv_red[:, half_qkv : half_qkv + 4])).T

        def joined(part, blocks):
            part = by_rows(part)
            got = swap(other(part), "c")
            pair = in_order(mine(part)[None], got[None])
            pair = pair.reshape(2, own_rows, blocks, -1)
            return jnp.moveaxis(pair, 0, 2).reshape(own_rows, -1)

        qkv_red = joined(qkv_red[:, :half_qkv], 3 * depth)
        up_red = joined(up_red[:, :half_ff], depth)
    else:
        scatter = lambda g: lax.psum_scatter(g, ALL, scatter_dimension=0, tiled=True)
        both = lambda a, axis: jnp.stack([jnp.where(core == k, a, 0.0) for k in (0, 1)], axis)
        to_all = lambda a: a.astype(WIDE)
        qkv_red = scatter(both(to_all(qkv_grad).reshape(width, 3 * depth, block), 2).reshape(width, -1))
        up_red = scatter(both(to_all(up_grad).reshape(width, depth, ff_block), 2).reshape(width, -1))
        out_red = scatter(both(to_all(out_grad).reshape(depth, block, width), 1).reshape(width, width))
        down_red = scatter(both(to_all(down_grad).reshape(depth, ff_block, width), 1).reshape(hidden_units, width))
        norm_red = scatter(jnp.where(core == 0, norm_grad, 0.0).T).T

    reduced = (qkv_red, out_red, up_red, down_red, norm_red)
    local_squares = sum(jnp.sum(grad * grad) for grad in reduced)
    grad_norm = jnp.sqrt(sum_everywhere(local_squares, ring))
    clip = jnp.minimum(1.0, CLIP_LIMIT / (grad_norm + 1e-06))
    out_fan = max(1, width * 64 // (tokens * depth))
    rates = (3.0 * width**-0.5, 3.0 * out_fan**-0.5, 3.0 * width**-0.5, 3.0 * hidden_units**-0.5, 1.5)
    decays = (WEIGHT_DECAY, WEIGHT_DECAY, WEIGHT_DECAY, WEIGHT_DECAY, 0.0)
    masters = (qkv_weight, out_weight, up_weight, down_weight, norm_params)
    firsts = (qkv_first, out_first, up_first, down_first, norm_first)
    seconds = (qkv_second, out_second, up_second, down_second, norm_second)
    news = [
        adam_update(masters[k], firsts[k], seconds[k], clip * reduced[k], rates[k], decays[k]) for k in range(5)
    ]
    return (
        activations.reshape(count, group, width),
        input_grad.reshape(count, group, width),
        grad_norm,
        *[new[0] for new in news],
        *[new[1] for new in news],
        *[new[2] for new in news],
    )


def solution(mesh):
    depth, planes = mesh.shape["seq"] // 2, mesh.shape["img"]
    across = max(k for k in range(1, planes + 1) if planes % k == 0 and k * k <= planes)
    grid = jax.sharding.Mesh(mesh.devices.reshape(depth, 2, planes // across, across), ALL)
    tokens = P(("y", "x"), ("z", "c"), None)
    matrix, norm = P(ALL, None), P(None, ALL)
    state = (matrix, matrix, matrix, matrix, norm)
    return jax.shard_map(
        body,
        mesh=grid,
        in_specs=(tokens, tokens) + state * 3,
        out_specs=(tokens, tokens, P()) + state * 3,
        check_vma=False,
    )
```

```python
import functools

import jax
import jax.numpy as jnp
from jax import lax
from jax.experimental import pallas as pl
from jax.experimental.pallas import tpu as pltpu
from jax.sharding import PartitionSpec as P

HEAD_DIM = 64
STEP = 10
NORM_EPS = 1e-05
BETA_ONE = 0.9
BETA_TWO = 0.999
ADAM_EPS = 1e-08
WEIGHT_DECAY = 0.1
CLIP_LIMIT = 1.0
LANES = 128

LOW = jnp.bfloat16
WIDE = jnp.float32
ALL = ("z", "c", "y", "x")
SWAP = [(0, 1), (1, 0)]


def swap(value, axis):
    return lax.ppermute(value, axis, SWAP)


def shift(value, step, wrap=True):
    size = lax.axis_size("z")
    pairs = [(i, (i + step) % size) for i in range(size) if wrap or 0 <= i + step < size]
    return lax.ppermute(value, "z", pairs)


def mine(pair_axis_first):
    return jnp.where(lax.axis_index("c") == 0, pair_axis_first[0], pair_axis_first[1])


def other(pair_axis_first):
    return jnp.where(lax.axis_index("c") == 0, pair_axis_first[1], pair_axis_first[0])


def in_order(own, mate, axis=0):
    first = lax.axis_index("c") == 0
    return jnp.concatenate([jnp.where(first, own, mate), jnp.where(first, mate, own)], axis)


def after(value, *before):
    return lax.optimization_barrier((value, *before))[0]


def column_first(shard):
    return [shard] + [shift(shard, k) for k in range(1, lax.axis_size("z"))]


def plane_last(column):
    half = column.shape[0] // 2
    along_x, along_y = swap(column, "x"), swap(column, "y")
    far = (swap(along_y[:half], "x"), swap(along_x[half:], "y"))
    return (column, along_x, along_y) + far


def plane_first(shard):
    half = shard.shape[0] // 2
    along_x, along_y = swap(shard, "x"), swap(shard, "y")
    far_low, far_high = swap(along_y[:half], "x"), swap(along_x[half:], "y")
    return jnp.concatenate([shard, along_x, along_y, far_low, far_high])


def column_last(plane):
    parts = [plane]
    for _ in range(1, lax.axis_size("z")):
        parts.append(shift(parts[-1], 1))
    return parts


def column_first_spots(depth):
    half = depth // 2
    spots = [(0, (k,), 0, (k, 0, 0)) for k in range(depth)]
    spots += [(1, (k,), 0, (k, 0, 1)) for k in range(depth)]
    spots += [(2, (k,), 0, (k, 1, 0)) for k in range(depth)]
    spots += [(3, (k,), 0, (k, 1, 1)) for k in range(half)]
    return spots + [(4, (k - half,), 0, (k, 1, 1)) for k in range(half, depth)]


def plane_first_spots(depth, rows):
    return [(k, (), p * rows, (k, p // 2, p % 2)) for k in range(depth) for p in range(4)]


def reduce_chips(send_x, keep_x, send_y, keep_y, gate=()):
    depth = send_x.shape[1]
    send_x, send_y = after(send_x, *gate), after(send_y, *gate)
    got_x, got_y = swap(send_x, "x"), swap(send_y, "y")
    wide = lambda a: a.astype(WIDE)
    on_y = swap((wide(keep_x[1]) + wide(got_x[1])).astype(LOW), "y")
    on_x = swap((wide(keep_y[1]) + wide(got_y[1])).astype(LOW), "x")
    parts = []
    for k in range(depth):
        one = wide(keep_x[0, k]) + wide(got_x[0, k]) + wide(on_y[k])
        two = wide(keep_y[0, k]) + wide(got_y[0, k]) + wide(on_x[k])
        parts.append(jnp.concatenate([one, two]))
    total = parts[0]
    for k in range(1, depth):
        total = total + wide(shift(parts[k].astype(LOW), k))
    return total, (on_x, on_y)


def coordinates():
    return jnp.stack([lax.axis_index(name) for name in ("z", "y", "x", "c")]).astype(jnp.int32)


def chip_of(coords, rel, depth, back):
    dz, dy, dx = rel
    z, y, x = coords[0], coords[1], coords[2]
    zz = lax.rem(z + (depth - dz if back else dz), depth)
    yy = 1 - y if dy else y
    xx = 1 - x if dx else x
    return zz, yy * 2 + xx


def window(row, rows, col, cols):
    rows_at = pl.ds(row if isinstance(row, int) else pl.multiple_of(row, 16), rows)
    return rows_at, pl.ds(col, cols)


VMEM = pl.BlockSpec(memory_space=pltpu.VMEM)
ROOM = pltpu.CompilerParams(vmem_limit_bytes=24 * 1024 * 1024)


def place(parts, depth, outs, spots, moves):
    def kernel(coords, *refs):
        ins, out_refs = refs[: len(parts)], refs[len(parts) :]
        for array, lead, base, rel in spots:
            zz, plane = chip_of(coords, rel, depth, True)
            for o, sr, sc, rows, cols, tr, tc in moves(zz, plane):
                out_refs[o][window(tr, rows, tc, cols)] = ins[array][(*lead, *window(base + sr, rows, sc, cols))]

    return pl.pallas_call(
        kernel,
        out_shape=[jax.ShapeDtypeStruct(s, LOW) for s in outs],
        in_specs=[pl.BlockSpec(memory_space=pltpu.SMEM)] + [VMEM] * len(parts),
        out_specs=[VMEM] * len(outs),
        compiler_params=ROOM,
    )(coordinates(), *parts)


def unplace(grads, depth, rows_cols, moves):
    spots = []
    for dz in range(depth):
        for d in range(2):
            spots += [(0, d, dz, (dz, d, 1), 0), (1, d, dz, (dz, d, 0), 0)]
            spots += [(2, d, dz, (dz, 1, d), 1), (3, d, dz, (dz, 0, d), 1)]

    def kernel(coords, *refs):
        ins, out_refs = refs[: len(grads)], refs[len(grads) :]
        for array, d, dz, rel, half in spots:
            zz, plane = chip_of(coords, rel, depth, False)
            for i, sr, sc, rows, cols, tr, tc in moves(zz, plane, half):
                out_refs[array][(d, dz, *window(tr, rows, tc, cols))] = ins[i][window(sr, rows, sc, cols)]

    return pl.pallas_call(
        kernel,
        out_shape=[jax.ShapeDtypeStruct((2, depth) + rows_cols, LOW)] * 4,
        in_specs=[pl.BlockSpec(memory_space=pltpu.SMEM)] + [VMEM] * len(grads),
        out_specs=[VMEM] * 4,
        compiler_params=ROOM,
    )(coordinates(), *grads)


def cast_qkv(qkv, norm, halves):
    rows, cols = qkv.shape
    wide = cols // 2 + LANES
    block = cols // (2 * halves)

    def kernel(coords, qkv_ref, norm_ref, own_ref, mate_ref, tall):
        first = coords[3] == 0
        for j in range(halves):
            a = qkv_ref[:, 2 * j * block : (2 * j + 1) * block]
            b = qkv_ref[:, (2 * j + 1) * block : (2 * j + 2) * block]
            own_ref[:, j * block : (j + 1) * block] = jnp.where(first, a, b).astype(LOW)
            mate_ref[:, j * block : (j + 1) * block] = jnp.where(first, b, a).astype(LOW)
        tall[...] = jnp.zeros_like(tall)
        tall[0:4, :] = norm_ref[...].astype(LOW).astype(WIDE)
        i = lax.broadcasted_iota(jnp.int32, (rows, rows), 0)
        j = lax.broadcasted_iota(jnp.int32, (rows, rows), 1)
        columns = dot_cols((i == j).astype(LOW), tall[...].astype(LOW)).astype(LOW)
        own_ref[:, cols // 2 :] = columns
        mate_ref[:, cols // 2 :] = columns

    return pl.pallas_call(
        kernel,
        out_shape=[jax.ShapeDtypeStruct((rows, wide), LOW)] * 2,
        in_specs=[pl.BlockSpec(memory_space=pltpu.SMEM), VMEM, VMEM],
        out_specs=[VMEM] * 2,
        scratch_shapes=[pltpu.VMEM((LANES, rows), WIDE)],
        compiler_params=ROOM,
    )(coordinates(), qkv, norm)


def cast_rest(up, out, down, halves):
    rows, cols = up.shape
    block, width = cols // (2 * halves), out.shape[1]

    def kernel(coords, up_ref, out_ref, down_ref, own_ref, mate_ref, part_ref, low_ref):
        first = coords[3] == 0
        for j in range(halves):
            a = up_ref[:, 2 * j * block : (2 * j + 1) * block]
            b = up_ref[:, (2 * j + 1) * block : (2 * j + 2) * block]
            own_ref[:, j * block : (j + 1) * block] = jnp.where(first, a, b).astype(LOW)
            mate_ref[:, j * block : (j + 1) * block] = jnp.where(first, b, a).astype(LOW)
        part_ref[:rows, :] = out_ref[:, : width // 2].astype(LOW)
        part_ref[rows:, :] = out_ref[:, width // 2 :].astype(LOW)
        low_ref[...] = down_ref[...].astype(LOW)

    return pl.pallas_call(
        kernel,
        out_shape=[jax.ShapeDtypeStruct((rows, cols // 2), LOW)] * 2
        + [jax.ShapeDtypeStruct((2 * rows, width // 2), LOW), jax.ShapeDtypeStruct(down.shape, LOW)],
        in_specs=[pl.BlockSpec(memory_space=pltpu.SMEM), VMEM, VMEM, VMEM],
        out_specs=[VMEM] * 4,
        compiler_params=ROOM,
    )(coordinates(), up, out, down)


def join_rows(own, mate, side=None):
    rows, cols = own.shape
    wide = cols + (side.shape[1] if side is not None else 0)

    def kernel(coords, own_ref, mate_ref, *refs):
        out_ref = refs[-1]
        core = coords[3]
        out_ref[pl.ds(pl.multiple_of(core * rows, 16), rows), :cols] = own_ref[...]
        out_ref[pl.ds(pl.multiple_of((1 - core) * rows, 16), rows), :cols] = mate_ref[...]
        if side is not None:
            out_ref[:, cols:] = refs[0][...]

    ins = [own, mate] + ([side] if side is not None else [])
    return pl.pallas_call(
        kernel,
        out_shape=jax.ShapeDtypeStruct((2 * rows, wide), LOW),
        in_specs=[pl.BlockSpec(memory_space=pltpu.SMEM)] + [VMEM] * len(ins),
        out_specs=VMEM,
        compiler_params=ROOM,
    )(coordinates(), *ins)


def run(kernel, outs, *ins, scalars=True, scratch=(), flops=10**9, room=40):
    size = sum(a.size * a.dtype.itemsize for a in ins)
    out_shape = [jax.ShapeDtypeStruct(shape, kind) for shape, kind in outs]
    return pl.pallas_call(
        kernel,
        out_shape=out_shape,
        in_specs=([pl.BlockSpec(memory_space=pltpu.SMEM)] if scalars else []) + [VMEM] * len(ins),
        out_specs=[VMEM] * len(outs),
        scratch_shapes=list(scratch),
        compiler_params=pltpu.CompilerParams(vmem_limit_bytes=room * 1024 * 1024),
        cost_estimate=pl.CostEstimate(flops=flops, bytes_accessed=2 * size, transcendentals=0),
    )(*([coordinates()] if scalars else []), *ins)


def dot(left, right):
    return jnp.dot(left, right, preferred_element_type=WIDE)


def dot_rows(left, right):
    return lax.dot_general(left, right, (((0,), (0,)), ((), ())), preferred_element_type=WIDE)


def dot_cols(left, right):
    return lax.dot_general(left, right, (((1,), (1,)), ((), ())), preferred_element_type=WIDE)


def eye(rows, cols):
    i = lax.broadcasted_iota(jnp.int32, (rows, cols), 0)
    return (i == lax.broadcasted_iota(jnp.int32, (rows, cols), 1)).astype(LOW)


def normalise(values):
    center = values - jnp.mean(values, axis=-1, keepdims=True)
    rate = lax.rsqrt(jnp.mean(center * center, axis=-1, keepdims=True) + NORM_EPS)
    return center * rate, rate


def norm_back(normed, rate, grad, gain):
    scaled = grad * gain
    shared = jnp.mean(scaled, axis=-1, keepdims=True)
    along = jnp.mean(scaled * normed, axis=-1, keepdims=True)
    return rate * (scaled - shared - normed * along)


def low_lanes(rows):
    return lax.broadcasted_iota(jnp.int32, (rows, LANES), 1) < HEAD_DIM


def by_head(pair):
    wide = pair.astype(WIDE)
    first = low_lanes(pair.shape[0])
    return jnp.where(first, wide, 0.0).astype(LOW), jnp.where(first, 0.0, wide).astype(LOW)


def pack_state(square):
    first = low_lanes(HEAD_DIM)
    return jnp.where(first, square[:HEAD_DIM], square[HEAD_DIM:])


def open_state(packed):
    first = low_lanes(HEAD_DIM)
    return jnp.concatenate([jnp.where(first, packed, 0.0), jnp.where(first, 0.0, packed)])


def feature(values):
    return jnp.where(values > 0.0, values + 1.0, jnp.exp(jnp.minimum(values, 0.0)))


def project(x, norm_w, qkv_w):
    tokens, width = x.shape
    half = qkv_w.shape[1] // 3
    pairs = half // LANES
    step = tokens // 2

    def kernel(x_ref, norm_ref, w_ref, rows_ref, normed_ref, qk_ref, q_ref, k_ref, v_ref, state_ref, sums):
        rows_ref[...] = dot_cols(eye(8, LANES), norm_ref[...])
        gain, bias = rows_ref[0:1, :], rows_ref[1:2, :]
        for i in range(2):
            at = slice(i * step, (i + 1) * step)
            normed = normalise(x_ref[at, :].astype(WIDE))[0]
            normed_ref[at, :] = (normed * gain + bias).astype(LOW)
            low = normed_ref[at, :]
            for j, out in enumerate((q_ref, k_ref)):
                part = dot(low, w_ref[:, j * half : (j + 1) * half])
                qk_ref[at, j * half : (j + 1) * half] = part
                out[at, :] = feature(part).astype(LOW)
            v_ref[at, :] = dot(low, w_ref[:, 2 * half :]).astype(LOW)
        total = dot_rows(jnp.ones((tokens, 8), LOW), k_ref[...])
        sums[...] = jnp.zeros_like(sums)
        for p in range(pairs):
            lanes = slice(p * LANES, (p + 1) * LANES)
            packed = pack_state(dot_rows(k_ref[:, lanes], v_ref[:, lanes]))
            state_ref[p * HEAD_DIM : (p + 1) * HEAD_DIM, :] = packed.astype(LOW)
            sums[p : p + 1, :] = total[0:1, lanes]
        state_ref[pairs * HEAD_DIM :, :] = sums[...].astype(LOW)

    outs = [((8, width), WIDE), ((tokens, width), LOW), ((tokens, 2 * half), WIDE)] + [((tokens, half), LOW)] * 3
    outs += [((pairs * HEAD_DIM + 16, LANES), LOW)]
    scratch = [pltpu.VMEM((16, LANES), WIDE)]
    return run(kernel, outs, x, norm_w, qkv_w, scalars=False, scratch=scratch, flops=2 * x.size * qkv_w.shape[1])


def total_state(refs):
    total = refs[0][...].astype(WIDE)
    for ref in refs[1:]:
        total = total + ref[...].astype(WIDE)
    return total


def causal_mask(step):
    i = lax.broadcasted_iota(jnp.int32, (step, step), 0)
    return i >= lax.broadcasted_iota(jnp.int32, (step, step), 1)


def attend(query, key, value, parts):
    tokens, half = query.shape
    pairs, step = half // LANES, tokens // 2

    def kernel(q_ref, k_ref, v_ref, *refs):
        mixed_ref, low_ref, denom_ref, state_ref = refs[len(parts) :]
        state_ref[...] = total_state(refs[: len(parts)])
        lower = causal_mask(step)
        first = low_lanes(step)
        top = low_lanes(HEAD_DIM)
        diagonal = eye(LANES, LANES).astype(WIDE)
        for p in range(pairs):
            lanes = slice(p * LANES, (p + 1) * LANES)
            packed = state_ref[p * HEAD_DIM : (p + 1) * HEAD_DIM, :]
            sums = state_ref[pairs * HEAD_DIM + p : pairs * HEAD_DIM + p + 1, :]
            column = jnp.sum(diagonal * sums, axis=1, keepdims=True)
            zero = jnp.zeros((HEAD_DIM, LANES), WIDE)
            ext = (
                jnp.concatenate([jnp.where(top, packed, column[:HEAD_DIM]), zero]).astype(LOW),
                jnp.concatenate([zero, jnp.where(top, column[HEAD_DIM:], packed)]).astype(LOW),
            )
            wide = v_ref[:, lanes].astype(WIDE)
            full = low_lanes(tokens)
            value_ext = (jnp.where(full, wide, 1.0).astype(LOW), jnp.where(full, 1.0, wide).astype(LOW))
            queries = by_head(q_ref[:, lanes])
            for i in range(2):
                at = slice(i * step, (i + 1) * step)
                got = []
                for h in range(2):
                    rows = queries[h][at]
                    total = dot(rows, ext[h])
                    for j in range(i + 1):
                        to = slice(j * step, (j + 1) * step)
                        scores = dot_cols(rows, k_ref[to, lanes])
                        if j == i:
                            scores = jnp.where(lower, scores, 0.0)
                        total = total + dot(scores.astype(LOW), value_ext[h][to])
                    got.append(total)
                denom = pltpu.roll(jnp.where(first, got[1], got[0]), HEAD_DIM, 1)
                mixed = jnp.where(first, got[0], got[1]) / denom
                mixed_ref[at, lanes] = mixed
                low_ref[at, lanes] = mixed.astype(LOW)
                denom_ref[at, lanes] = denom

    outs = [((tokens, half), WIDE), ((tokens, half), LOW), ((tokens, half), WIDE), (parts[0].shape, WIDE)]
    return run(kernel, outs, query, key, value, *parts, scalars=False, flops=8 * tokens * tokens * half)


def feed(x, part, got, rows, up_w):
    tokens, width = x.shape
    units, step, cut = up_w.shape[1], tokens // 2, 512

    def kernel(x_ref, part_ref, got_ref, rows_ref, w_ref, resid_ref, normed_ref, act_ref, slope_ref):
        for i in range(2):
            at = slice(i * step, (i + 1) * step)
            resid = x_ref[at, :].astype(WIDE) + part_ref[at, :] + got_ref[at, :].astype(WIDE)
            resid_ref[at, :] = resid
            normed_ref[at, :] = (normalise(resid)[0] * rows_ref[2:3, :] + rows_ref[3:4, :]).astype(LOW)
            for j in range(units // cut):
                to = slice(j * cut, (j + 1) * cut)
                v = dot(normed_ref[at, :], w_ref[:, to])
                root = (2.0 / 3.141592653589793) ** 0.5
                square = v * v
                bend = jnp.tanh(root * v * (1.0 + 0.044715 * square))
                cdf = 0.5 * (1.0 + bend)
                act_ref[at, to] = (v * cdf).astype(LOW)
                slope_ref[at, to] = cdf + 0.5 * v * (1.0 - bend * bend) * (root * (1.0 + 3.0 * 0.044715 * square))

    outs = [((tokens, width), WIDE), ((tokens, width), LOW), ((tokens, units), LOW), ((tokens, units), WIDE)]
    return run(kernel, outs, x, part, got, rows, up_w, scalars=False, flops=2 * x.size * units)


def feed_back(grad_out, down_w, slope, up_w):
    tokens, width = grad_out.shape
    units, step, cut = up_w.shape[1], tokens // 2, 512

    def kernel(g_ref, down_ref, slope_ref, up_ref, hidden_ref, part_ref, low_ref):
        for i in range(2):
            at = slice(i * step, (i + 1) * step)
            for j in range(units // cut):
                to = slice(j * cut, (j + 1) * cut)
                grad = dot_cols(g_ref[at, :], down_ref[to, :]) * slope_ref[at, to]
                hidden_ref[at, to] = grad.astype(LOW)
            part = dot_cols(hidden_ref[at, :], up_ref[...])
            part_ref[at, :] = part
            low_ref[at, :] = part.astype(LOW)

    outs = [((tokens, units), LOW), ((tokens, width), WIDE), ((tokens, width), LOW)]
    return run(kernel, outs, grad_out, down_w, slope, up_w, scalars=False, flops=4 * tokens * width * units)


def attend_turn(part, got, resid, rows, grad_out, out_w, mixed, denom, query):
    tokens, width = resid.shape
    half = mixed.shape[1]
    pairs, step = half // LANES, tokens // 2

    def kernel(
        part_ref, got_ref, resid_ref, rows_ref, g_ref, w_ref, mixed_ref, denom_ref, q_ref,
        grad_ref, low_ref, a_ref, b_ref, state_ref, norm_ref, sums,
    ):
        gain = rows_ref[2:3, :]
        gain_grad, bias_grad = jnp.zeros((1, width), WIDE), jnp.zeros((1, width), WIDE)
        first = low_lanes(step)
        for i in range(2):
            at = slice(i * step, (i + 1) * step)
            normed, rate = normalise(resid_ref[at, :])
            own = part_ref[at, :]
            gain_grad = gain_grad + jnp.sum(own * normed, axis=0, keepdims=True)
            bias_grad = bias_grad + jnp.sum(own, axis=0, keepdims=True)
            grad = g_ref[at, :].astype(WIDE) + norm_back(normed, rate, own + got_ref[at, :].astype(WIDE), gain)
            grad_ref[at, :] = grad
            low_ref[at, :] = grad.astype(LOW)
            turned = dot_cols(low_ref[at, :], w_ref[...]) / denom_ref[at, :]
            a_ref[at, :] = turned.astype(LOW)
            along = turned * mixed_ref[at, :]
            for p in range(pairs):
                lanes = slice(p * LANES, (p + 1) * LANES)
                piece = along[:, lanes]
                low = jnp.sum(jnp.where(first, piece, 0.0), axis=1, keepdims=True)
                high = jnp.sum(jnp.where(first, 0.0, piece), axis=1, keepdims=True)
                b_ref[at, lanes] = -jnp.where(first, low, high)
        norm_ref[0:1, :] = gain_grad
        norm_ref[1:2, :] = bias_grad
        sums[...] = jnp.zeros_like(sums)
        for p in range(pairs):
            lanes = slice(p * LANES, (p + 1) * LANES)
            packed = pack_state(dot_rows(q_ref[:, lanes], a_ref[:, lanes]))
            state_ref[p * HEAD_DIM : (p + 1) * HEAD_DIM, :] = packed.astype(LOW)
            sums[p : p + 1, :] = jnp.sum(q_ref[:, lanes].astype(WIDE) * b_ref[:, lanes], axis=0, keepdims=True)
        state_ref[pairs * HEAD_DIM :, :] = sums[...].astype(LOW)

    outs = [((tokens, width), WIDE), ((tokens, width), LOW), ((tokens, half), LOW), ((tokens, half), WIDE)]
    outs += [((pairs * HEAD_DIM + 16, LANES), LOW), ((2, width), WIDE)]
    ins = (part, got, resid, rows, grad_out, out_w, mixed, denom, query)
    scratch = [pltpu.VMEM((16, LANES), WIDE)]
    return run(kernel, outs, *ins, scalars=False, scratch=scratch, flops=2 * tokens * width * half)


def attend_back(query, key, value, qk, a_low, b_rows, state, parts):
    tokens, half = query.shape
    pairs, step = half // LANES, tokens // 2

    def kernel(q_ref, k_ref, v_ref, qk_ref, a_ref, b_ref, state_ref, *refs):
        out_ref = refs[len(parts)]
        later = total_state(refs[: len(parts)])
        lower = causal_mask(step)
        for p in range(pairs):
            lanes = slice(p * LANES, (p + 1) * LANES)
            rows = slice(p * HEAD_DIM, (p + 1) * HEAD_DIM)
            sums = slice(pairs * HEAD_DIM + p, pairs * HEAD_DIM + p + 1)
            before, after_it = open_state(state_ref[rows, :]).astype(LOW), open_state(later[rows]).astype(LOW)
            queries, keys, pulls = by_head(q_ref[:, lanes]), by_head(k_ref[:, lanes]), by_head(a_ref[:, lanes])
            cuts = [slice(i * step, (i + 1) * step) for i in range(2)]
            grad_q = [dot_cols(a_ref[c, lanes], before) + b_ref[c, lanes] * state_ref[sums, :] for c in cuts]
            grad_k = [dot_cols(v_ref[c, lanes], after_it) + later[sums] for c in cuts]
            grad_v = [dot(k_ref[c, lanes], after_it) for c in cuts]
            for i in range(2):
                for j in range(i + 1):
                    for h in range(2):
                        q, a = queries[h][cuts[i]], pulls[h][cuts[i]]
                        b = b_ref[cuts[i], p * LANES + h * HEAD_DIM : p * LANES + h * HEAD_DIM + 1]
                        scores = dot_cols(q, k_ref[cuts[j], lanes])
                        pull = dot_cols(a, v_ref[cuts[j], lanes]) + b
                        if j == i:
                            scores, pull = jnp.where(lower, scores, 0.0), jnp.where(lower, pull, 0.0)
                        scores, pull = scores.astype(LOW), pull.astype(LOW)
                        grad_q[i] = grad_q[i] + dot(pull, keys[h][cuts[j]])
                        grad_k[j] = grad_k[j] + dot_rows(pull, q)
                        grad_v[j] = grad_v[j] + dot_rows(scores, a)
            for i, c in enumerate(cuts):
                for n, grad in enumerate((grad_q[i], grad_k[i])):
                    at = slice(n * half + p * LANES, n * half + (p + 1) * LANES)
                    raw = qk_ref[c, at]
                    out_ref[c, at] = (grad * jnp.where(raw > 0.0, 1.0, jnp.exp(jnp.minimum(raw, 0.0)))).astype(LOW)
                out_ref[c, 2 * half + p * LANES : 2 * half + (p + 1) * LANES] = grad_v[i].astype(LOW)

    ins = (query, key, value, qk, a_low, b_rows, state, *parts)
    return run(kernel, [((tokens, 3 * half), LOW)], *ins, scalars=False, flops=20 * tokens * tokens * half)[0]


def project_back(grad, qkv_w, x, norm_two):
    tokens, width = x.shape
    step = tokens // 2

    def kernel(grad_ref, w_ref, x_ref, two_ref, part_ref, low_ref, cols_ref, rows):
        gain_grad, bias_grad = jnp.zeros((1, width), WIDE), jnp.zeros((1, width), WIDE)
        for i in range(2):
            at = slice(i * step, (i + 1) * step)
            part = dot_cols(grad_ref[at, :], w_ref[...])
            part_ref[at, :] = part
            low_ref[at, :] = part.astype(LOW)
            gain_grad = gain_grad + jnp.sum(part * normalise(x_ref[at, :].astype(WIDE))[0], axis=0, keepdims=True)
            bias_grad = bias_grad + jnp.sum(part, axis=0, keepdims=True)
        rows[...] = jnp.zeros_like(rows)
        rows[0:1, :], rows[1:2, :], rows[2:4, :] = gain_grad, bias_grad, two_ref[...]
        cols_ref[...] = dot_rows(rows[...].astype(LOW), eye(8, LANES)).astype(LOW)

    outs = [((tokens, width), WIDE), ((tokens, width), LOW), ((width, LANES), LOW)]
    scratch = [pltpu.VMEM((8, width), WIDE)]
    flops = 2 * x.size * grad.shape[1]
    return run(kernel, outs, grad, qkv_w, x, norm_two, scalars=False, scratch=scratch, flops=flops)


def input_back(part, got, grad_resid, own_x, rows):
    group, width = own_x.shape

    def kernel(coords, part_ref, got_ref, resid_ref, x_ref, rows_ref, out_ref):
        at = pl.ds(pl.multiple_of(coords[3] * group, 16), group)
        normed, rate = normalise(x_ref[...].astype(WIDE))
        grad = part_ref[at, :] + got_ref[...].astype(WIDE)
        out_ref[...] = (resid_ref[at, :] + norm_back(normed, rate, grad, rows_ref[0:1, :])).astype(LOW)

    return run(kernel, [((group, width), LOW)], part, got, grad_resid, own_x, rows)[0]


def adam_update(weight, first, second, grad, rate, decay):
    first_new = BETA_ONE * first + (1.0 - BETA_ONE) * grad
    second_new = BETA_TWO * second + (1.0 - BETA_TWO) * grad * grad
    first_hat = first_new / (1.0 - BETA_ONE**STEP)
    second_hat = second_new / (1.0 - BETA_TWO**STEP)
    weight_new = weight - rate * (first_hat / (jnp.sqrt(second_hat) + ADAM_EPS) + decay * weight)
    return (weight_new, first_new, second_new)


def from_others(low, step):
    return [shift(low, step * k, wrap=False) for k in range(1, lax.axis_size("z"))]


def sum_everywhere(value, direct):
    if not direct:
        return lax.psum(value, ALL)
    value = jnp.broadcast_to(value, (8, LANES))
    value = value + swap(value, "c")
    across = lax.ppermute(value, ("y", "x"), [(i, 3 - i) for i in range(4)])
    value = value + swap(value, "y") + (swap(value, "x") + across)
    near = [shift(value, k) for k in range(1, lax.axis_size("z"))]
    for part in near:
        value = value + part
    return value[0, 0]


def body(
    images,
    cotangent,
    qkv_weight,
    out_weight,
    up_weight,
    down_weight,
    norm_params,
    qkv_first,
    out_first,
    up_first,
    down_first,
    norm_first,
    qkv_second,
    out_second,
    up_second,
    down_second,
    norm_second,
):
    depth, core = lax.axis_size("z"), lax.axis_index("c")
    count, group, width = images.shape
    hidden_units = up_weight.shape[1]
    own_rows = qkv_weight.shape[0]
    own_units = down_weight.shape[0]
    chips = lax.axis_size("y") * lax.axis_size("x")
    block, ff_block = width // (2 * depth), hidden_units // (2 * depth)
    half_qkv, half_ff, half_d = 3 * width // 2, hidden_units // 2, width // 2
    ring = lax.axis_size("y") == 2 and lax.axis_size("x") == 2 and depth % 2 == 0 and own_rows % 32 == 0
    heads = half_d // HEAD_DIM
    tokens = 2 * group

    own_x, own_g = images.reshape(group, width), cotangent.reshape(group, width)
    split_qkv = lambda w: jnp.moveaxis(w.reshape(-1, 3 * depth, 2, block), 2, 0).reshape(2, -1, half_qkv)
    split_up = lambda w: jnp.moveaxis(w.reshape(-1, depth, 2, ff_block), 2, 0).reshape(2, -1, half_ff)

    if ring:
        qkv_mine, qkv_give = cast_qkv(qkv_weight, norm_params, 3 * depth)
        up_mine, up_give, out_part, down_low = cast_rest(after(up_weight, qkv_give), out_weight, down_weight, depth)
        qkv_mate = swap(qkv_give, "c")
        up_mate = swap(up_give, "c")
        x_mate = swap(own_x, "c")
        qkv_column = column_first(join_rows(qkv_mine, qkv_mate))
        down_plane = plane_first(down_low)
        up_part = join_rows(up_mine, up_mate, out_part)
        up_column = column_first(after(up_part, *qkv_column))
        qkv_parts = plane_last(jnp.stack(qkv_column))
        g_mate = swap(after(own_g, *qkv_column), "c")
        up_parts = plane_last(after(jnp.stack(up_column), *qkv_parts[3:]))
        down_parts = column_last(after(down_plane, *up_column))

        def qkv_moves(zz, plane):
            row = lambda h: ((zz * 2 + h) * chips + plane) * own_rows
            moves = [(0, h * own_rows, 0, own_rows, half_qkv, row(h), 0) for h in (0, 1)]
            return moves + [(1, h * own_rows, half_qkv, own_rows, LANES, row(h), 0) for h in (0, 1)]

        def up_moves(zz, plane):
            row = lambda h: ((zz * 2 + h) * chips + plane) * own_rows
            moves = [(0, h * own_rows, 0, own_rows, half_ff, row(h), 0) for h in (0, 1)]
            to = zz * block + plane * own_rows
            return moves + [(1, h * own_rows, half_ff, own_rows, half_d, to, h * half_d) for h in (0, 1)]

        def down_moves(zz, plane):
            return [(0, 0, 0, own_units, width, zz * ff_block + plane * own_units, 0)]

        spots = column_first_spots(depth)
        qkv_w, norm_w = place(qkv_parts, depth, [(width, half_qkv), (width, LANES)], spots, qkv_moves)
        up_w, out_w = place(up_parts, depth, [(width, half_ff), (half_d, width)], spots, up_moves)
        spots = plane_first_spots(depth, own_units)
        (down_w,) = place(down_parts, depth, [(half_ff, width)], spots, down_moves)
    else:
        qkv_low, out_low = qkv_weight.astype(LOW), out_weight.astype(LOW)
        up_low, down_low = up_weight.astype(LOW), down_weight.astype(LOW)
        norm_low = norm_params.astype(LOW)
        x_mate, g_mate = swap(own_x, "c"), swap(own_g, "c")
        whole = lambda w, axis=0: lax.all_gather(w, ALL, axis=axis, tiled=True)
        qkv_w, up_w = mine(split_qkv(whole(qkv_low))), mine(split_up(whole(up_low)))
        rows_half = lambda w, b: mine(jnp.moveaxis(w.reshape(depth, 2, b, width), 1, 0)).reshape(-1, width)
        out_w, down_w = rows_half(whole(out_low), block), rows_half(whole(down_low), ff_block)
        norm_w = jnp.pad(whole(norm_low, 1).T, ((0, 0), (0, LANES - 4)))

    inputs, grad_out = join_rows(own_x, x_mate), join_rows(own_g, g_mate)
    halves = lambda a: a.reshape(2, group, -1)
    rows, normed_one, qk, query, key, value, state = project(inputs, norm_w, qkv_w)
    mixed, mixed_low, denom, state_in = attend(query, key, value, from_others(state, 1))
    out_part = dot(mixed_low, out_w)
    out_got = swap(out_part.astype(LOW), "c")
    resid, normed_two, activated, slope = feed(inputs, out_part, out_got, rows, up_w)
    down_grad = dot_rows(activated, grad_out).astype(LOW)
    grad_hidden, two_part, two_low = feed_back(grad_out, down_w, slope, up_w)
    two_got = swap(two_low, "c")
    grad_resid, grad_resid_low, a_low, b_rows, state_grad, norm_two = attend_turn(
        two_part, two_got, resid, rows, grad_out, out_w, mixed, denom, query
    )
    later = from_others(state_grad, -1)
    up_grad = dot_rows(normed_two, grad_hidden).astype(LOW)
    out_grad = dot_rows(mixed_low, grad_resid_low).astype(LOW)
    grad_projected = attend_back(query, key, value, qk, a_low, b_rows, state_in, later)
    qkv_grad = dot_rows(normed_one, grad_projected).astype(LOW)
    one_part, one_low, norm_cols = project_back(grad_projected, qkv_w, inputs, norm_two)
    input_grad = input_back(one_part, swap(other(halves(one_low)), "c"), grad_resid, own_x, rows)
    down_part = dot(activated, down_w)
    down_got = swap(other(halves(down_part)).astype(LOW), "c").astype(WIDE)
    activations = (mine(halves(resid + down_part)) + down_got).astype(LOW)

    if ring:
        thin, small = own_units // 2, own_rows // 2

        def down_cuts(zz, plane, half):
            return [(0, zz * ff_block + plane * own_units + half * thin, 0, thin, width, 0, 0)]

        def up_cuts(zz, plane, half):
            cuts = [(0, ((zz * 2 + half) * chips + plane) * own_rows, 0, own_rows, half_ff, 0, 0)]
            row = zz * block + plane * own_rows + half * small
            return cuts + [(1, row, p * half_d, small, half_d, p * small, half_ff) for p in (0, 1)]

        def qkv_cuts(zz, plane, half):
            row = ((zz * 2 + half) * chips + plane) * own_rows
            return [(0, row, 0, own_rows, half_qkv, 0, 0), (1, row, 0, own_rows, LANES, 0, half_qkv)]

        down_red, gate = reduce_chips(*unplace([down_grad], depth, (thin, width), down_cuts))
        cuts = unplace([up_grad, out_grad], depth, (own_rows, half_ff + half_d), up_cuts)
        up_red, gate = reduce_chips(*cuts, gate)
        cuts = unplace([qkv_grad, norm_cols], depth, (own_rows, half_qkv + LANES), qkv_cuts)
        qkv_red, gate = reduce_chips(*cuts, gate)
        out_halves = up_red[:, half_ff:].reshape(2, 2, small, half_d)
        out_red = jnp.concatenate([out_halves[:, 0], out_halves[:, 1]], axis=2).reshape(own_rows, width)
        by_rows = lambda a: a.reshape(2, own_rows, -1)
        norm_parts = by_rows(qkv_red[:, half_qkv:])
        norm_red = (mine(norm_parts) + swap(other(norm_parts), "c"))[:, :4].T

        def joined(part, blocks):
            part = by_rows(part)
            got = swap(other(part), "c")
            pair = in_order(mine(part)[None], got[None])
            pair = pair.reshape(2, own_rows, blocks, -1)
            return jnp.moveaxis(pair, 0, 2).reshape(own_rows, -1)

        qkv_red = joined(qkv_red[:, :half_qkv], 3 * depth)
        up_red = joined(up_red[:, :half_ff], depth)
    else:
        scatter = lambda g: lax.psum_scatter(g, ALL, scatter_dimension=0, tiled=True)
        both = lambda a, axis: jnp.stack([jnp.where(core == k, a, 0.0) for k in (0, 1)], axis)
        to_all = lambda a: a.astype(WIDE)
        qkv_red = scatter(both(to_all(qkv_grad).reshape(width, 3 * depth, block), 2).reshape(width, -1))
        up_red = scatter(both(to_all(up_grad).reshape(width, depth, ff_block), 2).reshape(width, -1))
        out_red = scatter(both(to_all(out_grad).reshape(depth, block, width), 1).reshape(width, width))
        down_red = scatter(both(to_all(down_grad).reshape(depth, ff_block, width), 1).reshape(hidden_units, width))
        norm_red = scatter(norm_cols.astype(WIDE))[:, :4].T

    reduced = (qkv_red, out_red, up_red, down_red, norm_red)
    local_squares = sum(jnp.sum(grad * grad) for grad in reduced)
    grad_norm = jnp.sqrt(sum_everywhere(local_squares, ring))
    clip = jnp.minimum(1.0, CLIP_LIMIT / (grad_norm + 1e-06))
    out_fan = max(1, width * 64 // (tokens * depth))
    rates = (3.0 * width**-0.5, 3.0 * out_fan**-0.5, 3.0 * width**-0.5, 3.0 * hidden_units**-0.5, 1.5)
    decays = (WEIGHT_DECAY, WEIGHT_DECAY, WEIGHT_DECAY, WEIGHT_DECAY, 0.0)
    masters = (qkv_weight, out_weight, up_weight, down_weight, norm_params)
    firsts = (qkv_first, out_first, up_first, down_first, norm_first)
    seconds = (qkv_second, out_second, up_second, down_second, norm_second)
    news = [
        adam_update(masters[k], firsts[k], seconds[k], clip * reduced[k], rates[k], decays[k]) for k in range(5)
    ]
    return (
        activations.reshape(count, group, width),
        input_grad.reshape(count, group, width),
        grad_norm,
        *[new[0] for new in news],
        *[new[1] for new in news],
        *[new[2] for new in news],
    )


def solution(mesh):
    depth, planes = mesh.shape["seq"] // 2, mesh.shape["img"]
    across = max(k for k in range(1, planes + 1) if planes % k == 0 and k * k <= planes)
    grid = jax.sharding.Mesh(mesh.devices.reshape(depth, 2, planes // across, across), ALL)
    tokens = P(("y", "x"), ("z", "c"), None)
    matrix, norm = P(ALL, None), P(None, ALL)
    state = (matrix, matrix, matrix, matrix, norm)
    return jax.shard_map(
        body,
        mesh=grid,
        in_specs=(tokens, tokens) + state * 3,
        out_specs=(tokens, tokens, P()) + state * 3,
        check_vma=False,
    )
```

```python
import functools

import jax
import jax.numpy as jnp
from jax import lax
from jax.experimental import pallas as pl
from jax.experimental.pallas import tpu as pltpu
from jax.sharding import PartitionSpec as P

HEAD_DIM = 64
STEP = 10
NORM_EPS = 1e-05
BETA_ONE = 0.9
BETA_TWO = 0.999
ADAM_EPS = 1e-08
WEIGHT_DECAY = 0.1
CLIP_LIMIT = 1.0
LANES = 128

LOW = jnp.bfloat16
WIDE = jnp.float32
ALL = ("z", "c", "y", "x")
SWAP = [(0, 1), (1, 0)]


def swap(value, axis):
    return lax.ppermute(value, axis, SWAP)


def shift(value, step, wrap=True):
    size = lax.axis_size("z")
    pairs = [(i, (i + step) % size) for i in range(size) if wrap or 0 <= i + step < size]
    return lax.ppermute(value, "z", pairs)


def mine(pair_axis_first):
    return jnp.where(lax.axis_index("c") == 0, pair_axis_first[0], pair_axis_first[1])


def other(pair_axis_first):
    return jnp.where(lax.axis_index("c") == 0, pair_axis_first[1], pair_axis_first[0])


def in_order(own, mate, axis=0):
    first = lax.axis_index("c") == 0
    return jnp.concatenate([jnp.where(first, own, mate), jnp.where(first, mate, own)], axis)


def after(value, *before):
    return lax.optimization_barrier((value, *before))[0]


def column_first(shard):
    return [shard] + [shift(shard, k) for k in range(1, lax.axis_size("z"))]


def plane_last(column, between=()):
    half = column.shape[0] // 2
    along_x, along_y = swap(column, "x"), swap(column, "y")
    along_x, along_y = after(along_x, *between), after(along_y, *between)
    far = (swap(along_y[:half], "x"), swap(along_x[half:], "y"))
    return (column, along_x, along_y) + far


def plane_first(shard):
    half = shard.shape[0] // 2
    along_x, along_y = swap(shard, "x"), swap(shard, "y")
    far_low, far_high = swap(along_y[:half], "x"), swap(along_x[half:], "y")
    return jnp.concatenate([shard, along_x, along_y, far_low, far_high])


def column_last(plane):
    parts = [plane]
    for _ in range(1, lax.axis_size("z")):
        parts.append(shift(parts[-1], 1))
    return parts


def column_first_spots(depth):
    half = depth // 2
    spots = [(0, (k,), 0, (k, 0, 0), 0) for k in range(depth)]
    spots += [(1, (k,), 0, (k, 0, 1), 0) for k in range(depth)]
    spots += [(2, (k,), 0, (k, 1, 0), 0) for k in range(depth)]
    spots += [(3, (k,), 0, (k, 1, 1), 0) for k in range(half)]
    return spots + [(4, (k - half,), 0, (k, 1, 1), 0) for k in range(half, depth)]


def plane_first_spots(depth, rows, base):
    return [(base + k, (), p * rows, (k, p // 2, p % 2), 1) for k in range(depth) for p in range(4)]


def reduce_chips(send_x, keep_x, send_y, keep_y, before=(), between=(), last=()):
    depth, rows, cols = send_x.shape[1:]
    got_x, got_y = swap(after(send_x, *before), "x"), swap(after(send_y, *before), "y")
    got_x, got_y = after(got_x, *between), after(got_y, *between)

    def second_hop(kx, gx, ky, gy, to_y, to_x):
        to_y[...] = (kx[1].astype(WIDE) + gx[1].astype(WIDE)).astype(LOW)
        to_x[...] = (ky[1].astype(WIDE) + gy[1].astype(WIDE)).astype(LOW)

    outs = [((depth, rows, cols), LOW)] * 2
    to_y, to_x = run(second_hop, outs, keep_x, got_x, keep_y, got_y, scalars=False, room=24)
    on_y, on_x = swap(to_y, "y"), swap(to_x, "x")
    hop = (on_x, on_y)
    on_y, on_x = after(on_y, *last), after(on_x, *last)

    def third_hop(kx, gx, ky, gy, ony, onx, own, *sends):
        for k in range(depth):
            one = kx[0, k].astype(WIDE) + gx[0, k].astype(WIDE) + ony[k].astype(WIDE)
            two = ky[0, k].astype(WIDE) + gy[0, k].astype(WIDE) + onx[k].astype(WIDE)
            out = sends[k - 1] if k else own
            out[:rows, :] = one.astype(out.dtype)
            out[rows:, :] = two.astype(out.dtype)

    outs = [((2 * rows, cols), WIDE if k == 0 else LOW) for k in range(depth)]
    own, *sends = run(third_hop, outs, keep_x, got_x, keep_y, got_y, on_y, on_x, scalars=False, room=24)
    return [own] + [shift(part, k + 1) for k, part in enumerate(sends)], hop


def sum_of(refs):
    total = refs[0][...]
    for ref in refs[1:]:
        total = total + ref[...].astype(WIDE)
    return total


def spread(value):
    return jnp.broadcast_to(value, (8, LANES))


def total_squares(value):
    return jnp.sum(jnp.sum(value * value, axis=1, keepdims=True), axis=0, keepdims=True)


def finish_down(parts):
    def kernel(*refs):
        total = sum_of(refs[: len(parts)])
        refs[-2][...] = total
        refs[-1][...] = spread(total_squares(total))

    return run(kernel, [(parts[0].shape, WIDE), ((8, LANES), WIDE)], *parts, scalars=False, room=24)


def finish_up(parts, squares, rows, half_ff):
    half_d = parts[0].shape[1] - half_ff
    small = rows // 2

    def kernel(coords, squares_ref, *refs):
        own_ref, mate_ref, out_ref, total_ref, all_ref = refs[len(parts) :]
        total = sum_of(refs[: len(parts)])
        all_ref[...] = total
        core = coords[3]
        own_ref[...] = all_ref[pl.ds(pl.multiple_of(core * rows, 8), rows), :half_ff]
        mate_ref[...] = all_ref[pl.ds(pl.multiple_of((1 - core) * rows, 8), rows), :half_ff]
        for p in range(2):
            for h in range(2):
                block = total[h * rows + p * small : h * rows + (p + 1) * small, half_ff:]
                out_ref[h * small : (h + 1) * small, p * half_d : (p + 1) * half_d] = block
        total_ref[...] = squares_ref[...] + spread(total_squares(total))

    outs = [((rows, half_ff), WIDE)] * 2 + [((rows, 2 * half_d), WIDE), ((8, LANES), WIDE)]
    scratch = [pltpu.VMEM(parts[0].shape, WIDE)]
    return run(kernel, outs, squares, *parts, scratch=scratch, room=24)


def finish_qkv(parts, squares, rows, half_qkv):
    def kernel(coords, squares_ref, *refs):
        own_ref, mate_ref, small_ref, all_ref = refs[len(parts) :]
        total = sum_of(refs[: len(parts)])
        all_ref[...] = total
        core = coords[3]
        own_ref[...] = all_ref[pl.ds(pl.multiple_of(core * rows, 8), rows), :half_qkv]
        mate_ref[...] = all_ref[pl.ds(pl.multiple_of((1 - core) * rows, 8), rows), :half_qkv]
        small_ref[: 2 * rows, :] = total[:, half_qkv:]
        small_ref[2 * rows :, :] = squares_ref[...] + spread(total_squares(total[:, :half_qkv]))

    outs = [((rows, half_qkv), WIDE)] * 2 + [((2 * rows + 8, LANES), WIDE)]
    scratch = [pltpu.VMEM(parts[0].shape, WIDE)]
    return run(kernel, outs, squares, *parts, scratch=scratch, room=24)


def chip_squares(small, got):
    rows = small.shape[0] - 8

    def kernel(small_ref, got_ref, total_ref, norm_ref):
        total = small_ref[...] + got_ref[...]
        norm_ref[...] = total[:rows]
        total_ref[...] = total[rows:] + spread(total_squares(total[:rows]))

    outs = [((8, LANES), WIDE), ((rows, LANES), WIDE)]
    return run(kernel, outs, small, got, scalars=False, room=24)


def sum_chips(value):
    across = lax.ppermute(value, ("y", "x"), [(i, 3 - i) for i in range(4)])
    value = value + swap(value, "y") + (swap(value, "x") + across)
    return [value] + [shift(value, k) for k in range(1, lax.axis_size("z"))]


def interleave(first, own, mate, blocks):
    size = own.shape[1] // blocks
    pieces = []
    for j in range(blocks):
        at = slice(j * size, (j + 1) * size)
        pieces += [jnp.where(first, own[:, at], mate[:, at]), jnp.where(first, mate[:, at], own[:, at])]
    return jnp.concatenate(pieces, axis=1)


def update_all(grads, totals, masters, firsts, seconds, rates, decays, blocks):
    steps = 4
    n, m = len(grads), len(totals)

    def tile(array):
        rows, cols = array.shape
        return pl.BlockSpec((rows // steps, cols), lambda i: (i, 0))

    def whole(array):
        return pl.BlockSpec(array.shape, lambda i: (0, 0))

    def kernel(coords, *refs):
        first = coords[3] == 0
        g, t, old, new = refs[:n], refs[n : n + m], refs[n + m : n + m + 15], refs[n + m + 15 :]
        total = sum_of(t)[0:1, 0:1]
        norm = jnp.sqrt(total)
        clip = jnp.minimum(1.0, CLIP_LIMIT / (norm + 1e-06))
        qkv = interleave(first, g[0][...], g[1][...], blocks[0])
        up = interleave(first, g[3][...], g[4][...], blocks[1])
        for k, grad in enumerate((qkv, g[2][...], up, g[5][...], g[6][...])):
            news = adam_update(old[k][...], old[5 + k][...], old[10 + k][...], clip * grad, rates[k], decays[k])
            for part in range(3):
                new[5 * part + k][...] = news[part]
        new[15][...] = jnp.broadcast_to(norm, (8, LANES))

    state = (*masters, *firsts, *seconds)
    specs = [whole(a) if k % 5 == 4 else tile(a) for k, a in enumerate(state)]
    norm_out = jax.ShapeDtypeStruct((8, LANES), WIDE)
    return pl.pallas_call(
        kernel,
        grid=(steps,),
        out_shape=[jax.ShapeDtypeStruct(a.shape, WIDE) for a in state] + [norm_out],
        in_specs=[pl.BlockSpec(memory_space=pltpu.SMEM)]
        + [tile(a) for a in grads[:-1]]
        + [whole(grads[-1])]
        + [whole(a) for a in totals]
        + specs,
        out_specs=specs + [whole(norm_out)],
        compiler_params=pltpu.CompilerParams(vmem_limit_bytes=32 * 1024 * 1024),
    )(coordinates(), *grads, *totals, *state)


def coordinates():
    return jnp.stack([lax.axis_index(name) for name in ("z", "y", "x", "c")]).astype(jnp.int32)


def chip_of(coords, rel, depth, back):
    dz, dy, dx = rel
    z, y, x = coords[0], coords[1], coords[2]
    zz = lax.rem(z + (depth - dz if back else dz), depth)
    yy = 1 - y if dy else y
    xx = 1 - x if dx else x
    return zz, yy * 2 + xx


def window(row, rows, col, cols):
    rows_at = pl.ds(row if isinstance(row, int) else pl.multiple_of(row, 16), rows)
    return rows_at, pl.ds(col, cols)


VMEM = pl.BlockSpec(memory_space=pltpu.VMEM)
ROOM = pltpu.CompilerParams(vmem_limit_bytes=24 * 1024 * 1024)


def place(parts, depth, outs, spots, moves):
    def kernel(coords, *refs):
        ins, out_refs = refs[: len(parts)], refs[len(parts) :]
        for array, lead, base, rel, piece in spots:
            zz, plane = chip_of(coords, rel, depth, True)
            for o, sr, sc, rows, cols, tr, tc in moves(zz, plane, piece):
                out_refs[o][window(tr, rows, tc, cols)] = ins[array][(*lead, *window(base + sr, rows, sc, cols))]

    return pl.pallas_call(
        kernel,
        out_shape=[jax.ShapeDtypeStruct(s, LOW) for s in outs],
        in_specs=[pl.BlockSpec(memory_space=pltpu.SMEM)] + [VMEM] * len(parts),
        out_specs=[VMEM] * len(outs),
        compiler_params=ROOM,
    )(coordinates(), *parts)


def unplace(grads, depth, rows_cols, moves):
    spots = []
    for dz in range(depth):
        for d in range(2):
            spots += [(0, d, dz, (dz, d, 1), 0), (1, d, dz, (dz, d, 0), 0)]
            spots += [(2, d, dz, (dz, 1, d), 1), (3, d, dz, (dz, 0, d), 1)]

    def kernel(coords, *refs):
        ins, out_refs = refs[: len(grads)], refs[len(grads) :]
        for array, d, dz, rel, half in spots:
            zz, plane = chip_of(coords, rel, depth, False)
            for i, sr, sc, rows, cols, tr, tc in moves(zz, plane, half):
                out_refs[array][(d, dz, *window(tr, rows, tc, cols))] = ins[i][window(sr, rows, sc, cols)]

    return pl.pallas_call(
        kernel,
        out_shape=[jax.ShapeDtypeStruct((2, depth) + rows_cols, LOW)] * 4,
        in_specs=[pl.BlockSpec(memory_space=pltpu.SMEM)] + [VMEM] * len(grads),
        out_specs=[VMEM] * 4,
        compiler_params=ROOM,
    )(coordinates(), *grads)


def cast_qkv(qkv, norm, halves):
    rows, cols = qkv.shape
    wide = cols // 2 + LANES
    block = cols // (2 * halves)

    def kernel(coords, qkv_ref, norm_ref, own_ref, mate_ref, tall):
        first = coords[3] == 0
        for j in range(halves):
            a = qkv_ref[:, 2 * j * block : (2 * j + 1) * block]
            b = qkv_ref[:, (2 * j + 1) * block : (2 * j + 2) * block]
            own_ref[:, j * block : (j + 1) * block] = jnp.where(first, a, b).astype(LOW)
            mate_ref[:, j * block : (j + 1) * block] = jnp.where(first, b, a).astype(LOW)
        tall[...] = jnp.zeros_like(tall)
        tall[0:4, :] = norm_ref[...].astype(LOW).astype(WIDE)
        i = lax.broadcasted_iota(jnp.int32, (rows, rows), 0)
        j = lax.broadcasted_iota(jnp.int32, (rows, rows), 1)
        columns = dot_cols((i == j).astype(LOW), tall[...].astype(LOW)).astype(LOW)
        own_ref[:, cols // 2 :] = columns
        mate_ref[:, cols // 2 :] = columns

    return pl.pallas_call(
        kernel,
        out_shape=[jax.ShapeDtypeStruct((rows, wide), LOW)] * 2,
        in_specs=[pl.BlockSpec(memory_space=pltpu.SMEM), VMEM, VMEM],
        out_specs=[VMEM] * 2,
        scratch_shapes=[pltpu.VMEM((LANES, rows), WIDE)],
        compiler_params=ROOM,
    )(coordinates(), qkv, norm)


def cast_rest(up, out, down, halves):
    rows, cols = up.shape
    block, width, units = cols // (2 * halves), out.shape[1], down.shape[0]

    def kernel(coords, up_ref, out_ref, down_ref, own_ref, mate_ref, part_ref, one_ref, two_ref):
        first = coords[3] == 0
        for j in range(halves):
            a = up_ref[:, 2 * j * block : (2 * j + 1) * block]
            b = up_ref[:, (2 * j + 1) * block : (2 * j + 2) * block]
            own_ref[:, j * block : (j + 1) * block] = jnp.where(first, a, b).astype(LOW)
            mate_ref[:, j * block : (j + 1) * block] = jnp.where(first, b, a).astype(LOW)
        part_ref[:rows, :] = out_ref[:, : width // 2].astype(LOW)
        part_ref[rows:, :] = out_ref[:, width // 2 :].astype(LOW)
        one_ref[...] = down_ref[: units // 2, :].astype(LOW)
        two_ref[...] = down_ref[units // 2 :, :].astype(LOW)

    return pl.pallas_call(
        kernel,
        out_shape=[jax.ShapeDtypeStruct((rows, cols // 2), LOW)] * 2
        + [jax.ShapeDtypeStruct((2 * rows, width // 2), LOW)]
        + [jax.ShapeDtypeStruct((units // 2, width), LOW)] * 2,
        in_specs=[pl.BlockSpec(memory_space=pltpu.SMEM), VMEM, VMEM, VMEM],
        out_specs=[VMEM] * 5,
        compiler_params=ROOM,
    )(coordinates(), up, out, down)


def join_rows(own, mate, side=None):
    rows, cols = own.shape
    wide = cols + (side.shape[1] if side is not None else 0)

    def kernel(coords, own_ref, mate_ref, *refs):
        out_ref = refs[-1]
        core = coords[3]
        out_ref[pl.ds(pl.multiple_of(core * rows, 16), rows), :cols] = own_ref[...]
        out_ref[pl.ds(pl.multiple_of((1 - core) * rows, 16), rows), :cols] = mate_ref[...]
        if side is not None:
            out_ref[:, cols:] = refs[0][...]

    ins = [own, mate] + ([side] if side is not None else [])
    return pl.pallas_call(
        kernel,
        out_shape=jax.ShapeDtypeStruct((2 * rows, wide), LOW),
        in_specs=[pl.BlockSpec(memory_space=pltpu.SMEM)] + [VMEM] * len(ins),
        out_specs=VMEM,
        compiler_params=ROOM,
    )(coordinates(), *ins)


def run(kernel, outs, *ins, scalars=True, scratch=(), flops=10**9, room=40):
    out_shape = [jax.ShapeDtypeStruct(shape, kind) for shape, kind in outs]
    return pl.pallas_call(
        kernel,
        out_shape=out_shape,
        in_specs=([pl.BlockSpec(memory_space=pltpu.SMEM)] if scalars else []) + [VMEM] * len(ins),
        out_specs=[VMEM] * len(outs),
        scratch_shapes=list(scratch),
        compiler_params=pltpu.CompilerParams(vmem_limit_bytes=room * 1024 * 1024),
        cost_estimate=pl.CostEstimate(flops=0, bytes_accessed=0, transcendentals=0),
    )(*([coordinates()] if scalars else []), *ins)


def dot(left, right):
    return jnp.dot(left, right, preferred_element_type=WIDE)


def dot_rows(left, right):
    return lax.dot_general(left, right, (((0,), (0,)), ((), ())), preferred_element_type=WIDE)


def dot_cols(left, right):
    return lax.dot_general(left, right, (((1,), (1,)), ((), ())), preferred_element_type=WIDE)


def eye(rows, cols):
    i = lax.broadcasted_iota(jnp.int32, (rows, cols), 0)
    return (i == lax.broadcasted_iota(jnp.int32, (rows, cols), 1)).astype(LOW)


def normalise(values):
    center = values - jnp.mean(values, axis=-1, keepdims=True)
    rate = lax.rsqrt(jnp.mean(center * center, axis=-1, keepdims=True) + NORM_EPS)
    return center * rate, rate


def norm_back(normed, rate, grad, gain):
    scaled = grad * gain
    shared = jnp.mean(scaled, axis=-1, keepdims=True)
    along = jnp.mean(scaled * normed, axis=-1, keepdims=True)
    return rate * (scaled - shared - normed * along)


def low_lanes(rows):
    return lax.broadcasted_iota(jnp.int32, (rows, LANES), 1) < HEAD_DIM


def by_head(pair):
    wide = pair.astype(WIDE)
    first = low_lanes(pair.shape[0])
    return jnp.where(first, wide, 0.0).astype(LOW), jnp.where(first, 0.0, wide).astype(LOW)


def pack_state(square):
    first = low_lanes(HEAD_DIM)
    return jnp.where(first, square[:HEAD_DIM], square[HEAD_DIM:])


def open_state(packed):
    first = low_lanes(HEAD_DIM)
    return jnp.concatenate([jnp.where(first, packed, 0.0), jnp.where(first, 0.0, packed)])


def feature(values):
    return jnp.where(values > 0.0, values + 1.0, jnp.exp(jnp.minimum(values, 0.0)))


def project(x, norm_w, qkv_w):
    tokens, width = x.shape
    half = qkv_w.shape[1] // 3
    pairs = half // LANES
    step = tokens // 2

    def kernel(x_ref, norm_ref, w_ref, rows_ref, normed_ref, qk_ref, q_ref, k_ref, v_ref, state_ref, sums):
        rows_ref[...] = dot_cols(eye(8, LANES), norm_ref[...])
        gain, bias = rows_ref[0:1, :], rows_ref[1:2, :]
        for i in range(2):
            at = slice(i * step, (i + 1) * step)
            normed = normalise(x_ref[at, :].astype(WIDE))[0]
            normed_ref[at, :] = (normed * gain + bias).astype(LOW)
            low = normed_ref[at, :]
            for j, out in enumerate((q_ref, k_ref)):
                part = dot(low, w_ref[:, j * half : (j + 1) * half])
                qk_ref[at, j * half : (j + 1) * half] = part
                out[at, :] = feature(part).astype(LOW)
            v_ref[at, :] = dot(low, w_ref[:, 2 * half :]).astype(LOW)
        total = dot_rows(jnp.ones((tokens, 8), LOW), k_ref[...])
        sums[...] = jnp.zeros_like(sums)
        for p in range(pairs):
            lanes = slice(p * LANES, (p + 1) * LANES)
            packed = pack_state(dot_rows(k_ref[:, lanes], v_ref[:, lanes]))
            state_ref[p * HEAD_DIM : (p + 1) * HEAD_DIM, :] = packed.astype(LOW)
            sums[p : p + 1, :] = total[0:1, lanes]
        state_ref[pairs * HEAD_DIM :, :] = sums[...].astype(LOW)

    outs = [((8, width), WIDE), ((tokens, width), LOW), ((tokens, 2 * half), WIDE)] + [((tokens, half), LOW)] * 3
    outs += [((pairs * HEAD_DIM + 16, LANES), LOW)]
    scratch = [pltpu.VMEM((16, LANES), WIDE)]
    return run(kernel, outs, x, norm_w, qkv_w, scalars=False, scratch=scratch, flops=2 * x.size * qkv_w.shape[1])


def total_state(refs):
    total = refs[0][...].astype(WIDE)
    for ref in refs[1:]:
        total = total + ref[...].astype(WIDE)
    return total


def causal_mask(step):
    i = lax.broadcasted_iota(jnp.int32, (step, step), 0)
    return i >= lax.broadcasted_iota(jnp.int32, (step, step), 1)


def attend(query, key, value, parts):
    tokens, half = query.shape
    pairs, step = half // LANES, tokens // 2

    def kernel(q_ref, k_ref, v_ref, *refs):
        mixed_ref, low_ref, denom_ref, state_ref = refs[len(parts) :]
        state_ref[...] = total_state(refs[: len(parts)])
        lower = causal_mask(step)
        first = low_lanes(step)
        top = low_lanes(HEAD_DIM)
        diagonal = eye(LANES, LANES).astype(WIDE)
        for p in range(pairs):
            lanes = slice(p * LANES, (p + 1) * LANES)
            packed = state_ref[p * HEAD_DIM : (p + 1) * HEAD_DIM, :]
            sums = state_ref[pairs * HEAD_DIM + p : pairs * HEAD_DIM + p + 1, :]
            column = jnp.sum(diagonal * sums, axis=1, keepdims=True)
            zero = jnp.zeros((HEAD_DIM, LANES), WIDE)
            ext = (
                jnp.concatenate([jnp.where(top, packed, column[:HEAD_DIM]), zero]).astype(LOW),
                jnp.concatenate([zero, jnp.where(top, column[HEAD_DIM:], packed)]).astype(LOW),
            )
            wide = v_ref[:, lanes].astype(WIDE)
            full = low_lanes(tokens)
            value_ext = (jnp.where(full, wide, 1.0).astype(LOW), jnp.where(full, 1.0, wide).astype(LOW))
            queries = by_head(q_ref[:, lanes])
            for i in range(2):
                at = slice(i * step, (i + 1) * step)
                got = []
                for h in range(2):
                    rows = queries[h][at]
                    total = dot(rows, ext[h])
                    for j in range(i + 1):
                        to = slice(j * step, (j + 1) * step)
                        scores = dot_cols(rows, k_ref[to, lanes])
                        if j == i:
                            scores = jnp.where(lower, scores, 0.0)
                        total = total + dot(scores.astype(LOW), value_ext[h][to])
                    got.append(total)
                denom = pltpu.roll(jnp.where(first, got[1], got[0]), HEAD_DIM, 1)
                mixed = jnp.where(first, got[0], got[1]) / denom
                mixed_ref[at, lanes] = mixed
                low_ref[at, lanes] = mixed.astype(LOW)
                denom_ref[at, lanes] = denom

    outs = [((tokens, half), WIDE), ((tokens, half), LOW), ((tokens, half), WIDE), (parts[0].shape, WIDE)]
    return run(kernel, outs, query, key, value, *parts, scalars=False, flops=8 * tokens * tokens * half)


def feed(x, part, got, rows, up_w):
    tokens, width = x.shape
    units, step, cut = up_w.shape[1], tokens // 2, 512

    def kernel(x_ref, part_ref, got_ref, rows_ref, w_ref, resid_ref, normed_ref, act_ref, slope_ref):
        for i in range(2):
            at = slice(i * step, (i + 1) * step)
            resid = x_ref[at, :].astype(WIDE) + part_ref[at, :] + got_ref[at, :].astype(WIDE)
            resid_ref[at, :] = resid
            normed_ref[at, :] = (normalise(resid)[0] * rows_ref[2:3, :] + rows_ref[3:4, :]).astype(LOW)
            for j in range(units // cut):
                to = slice(j * cut, (j + 1) * cut)
                v = dot(normed_ref[at, :], w_ref[:, to])
                root = (2.0 / 3.141592653589793) ** 0.5
                square = v * v
                bend = jnp.tanh(root * v * (1.0 + 0.044715 * square))
                cdf = 0.5 * (1.0 + bend)
                act_ref[at, to] = (v * cdf).astype(LOW)
                slope_ref[at, to] = cdf + 0.5 * v * (1.0 - bend * bend) * (root * (1.0 + 3.0 * 0.044715 * square))

    outs = [((tokens, width), WIDE), ((tokens, width), LOW), ((tokens, units), LOW), ((tokens, units), WIDE)]
    return run(kernel, outs, x, part, got, rows, up_w, scalars=False, flops=2 * x.size * units)


def feed_back(grad_out, down_w, slope, up_w):
    tokens, width = grad_out.shape
    units, step, cut = up_w.shape[1], tokens // 2, 512

    def kernel(g_ref, down_ref, slope_ref, up_ref, hidden_ref, part_ref, low_ref):
        for i in range(2):
            at = slice(i * step, (i + 1) * step)
            for j in range(units // cut):
                to = slice(j * cut, (j + 1) * cut)
                grad = dot_cols(g_ref[at, :], down_ref[to, :]) * slope_ref[at, to]
                hidden_ref[at, to] = grad.astype(LOW)
            part = dot_cols(hidden_ref[at, :], up_ref[...])
            part_ref[at, :] = part
            low_ref[at, :] = part.astype(LOW)

    outs = [((tokens, units), LOW), ((tokens, width), WIDE), ((tokens, width), LOW)]
    return run(kernel, outs, grad_out, down_w, slope, up_w, scalars=False, flops=4 * tokens * width * units)


def attend_turn(part, got, resid, rows, grad_out, out_w, mixed, denom, query):
    tokens, width = resid.shape
    half = mixed.shape[1]
    pairs, step = half // LANES, tokens // 2

    def kernel(
        part_ref, got_ref, resid_ref, rows_ref, g_ref, w_ref, mixed_ref, denom_ref, q_ref,
        grad_ref, low_ref, a_ref, b_ref, state_ref, norm_ref, sums,
    ):
        gain = rows_ref[2:3, :]
        gain_grad, bias_grad = jnp.zeros((1, width), WIDE), jnp.zeros((1, width), WIDE)
        first = low_lanes(step)
        for i in range(2):
            at = slice(i * step, (i + 1) * step)
            normed, rate = normalise(resid_ref[at, :])
            own = part_ref[at, :]
            gain_grad = gain_grad + jnp.sum(own * normed, axis=0, keepdims=True)
            bias_grad = bias_grad + jnp.sum(own, axis=0, keepdims=True)
            grad = g_ref[at, :].astype(WIDE) + norm_back(normed, rate, own + got_ref[at, :].astype(WIDE), gain)
            grad_ref[at, :] = grad
            low_ref[at, :] = grad.astype(LOW)
            turned = dot_cols(low_ref[at, :], w_ref[...]) / denom_ref[at, :]
            a_ref[at, :] = turned.astype(LOW)
            along = turned * mixed_ref[at, :]
            for p in range(pairs):
                lanes = slice(p * LANES, (p + 1) * LANES)
                piece = along[:, lanes]
                low = jnp.sum(jnp.where(first, piece, 0.0), axis=1, keepdims=True)
                high = jnp.sum(jnp.where(first, 0.0, piece), axis=1, keepdims=True)
                b_ref[at, lanes] = -jnp.where(first, low, high)
        norm_ref[0:1, :] = gain_grad
        norm_ref[1:2, :] = bias_grad
        sums[...] = jnp.zeros_like(sums)
        for p in range(pairs):
            lanes = slice(p * LANES, (p + 1) * LANES)
            packed = pack_state(dot_rows(q_ref[:, lanes], a_ref[:, lanes]))
            state_ref[p * HEAD_DIM : (p + 1) * HEAD_DIM, :] = packed.astype(LOW)
            sums[p : p + 1, :] = jnp.sum(q_ref[:, lanes].astype(WIDE) * b_ref[:, lanes], axis=0, keepdims=True)
        state_ref[pairs * HEAD_DIM :, :] = sums[...].astype(LOW)

    outs = [((tokens, width), WIDE), ((tokens, width), LOW), ((tokens, half), LOW), ((tokens, half), WIDE)]
    outs += [((pairs * HEAD_DIM + 16, LANES), LOW), ((2, width), WIDE)]
    ins = (part, got, resid, rows, grad_out, out_w, mixed, denom, query)
    scratch = [pltpu.VMEM((16, LANES), WIDE)]
    return run(kernel, outs, *ins, scalars=False, scratch=scratch, flops=2 * tokens * width * half)


def attend_back(query, key, value, qk, a_low, b_rows, state, parts):
    tokens, half = query.shape
    pairs, step = half // LANES, tokens // 2

    def kernel(q_ref, k_ref, v_ref, qk_ref, a_ref, b_ref, state_ref, *refs):
        out_ref = refs[len(parts)]
        later = total_state(refs[: len(parts)])
        lower = causal_mask(step)
        for p in range(pairs):
            lanes = slice(p * LANES, (p + 1) * LANES)
            rows = slice(p * HEAD_DIM, (p + 1) * HEAD_DIM)
            sums = slice(pairs * HEAD_DIM + p, pairs * HEAD_DIM + p + 1)
            before, after_it = open_state(state_ref[rows, :]).astype(LOW), open_state(later[rows]).astype(LOW)
            queries, keys, pulls = by_head(q_ref[:, lanes]), by_head(k_ref[:, lanes]), by_head(a_ref[:, lanes])
            cuts = [slice(i * step, (i + 1) * step) for i in range(2)]
            grad_q = [dot_cols(a_ref[c, lanes], before) + b_ref[c, lanes] * state_ref[sums, :] for c in cuts]
            grad_k = [dot_cols(v_ref[c, lanes], after_it) + later[sums] for c in cuts]
            grad_v = [dot(k_ref[c, lanes], after_it) for c in cuts]
            for i in range(2):
                for j in range(i + 1):
                    for h in range(2):
                        q, a = queries[h][cuts[i]], pulls[h][cuts[i]]
                        b = b_ref[cuts[i], p * LANES + h * HEAD_DIM : p * LANES + h * HEAD_DIM + 1]
                        scores = dot_cols(q, k_ref[cuts[j], lanes])
                        pull = dot_cols(a, v_ref[cuts[j], lanes]) + b
                        if j == i:
                            scores, pull = jnp.where(lower, scores, 0.0), jnp.where(lower, pull, 0.0)
                        scores, pull = scores.astype(LOW), pull.astype(LOW)
                        grad_q[i] = grad_q[i] + dot(pull, keys[h][cuts[j]])
                        grad_k[j] = grad_k[j] + dot_rows(pull, q)
                        grad_v[j] = grad_v[j] + dot_rows(scores, a)
            for i, c in enumerate(cuts):
                for n, grad in enumerate((grad_q[i], grad_k[i])):
                    at = slice(n * half + p * LANES, n * half + (p + 1) * LANES)
                    raw = qk_ref[c, at]
                    out_ref[c, at] = (grad * jnp.where(raw > 0.0, 1.0, jnp.exp(jnp.minimum(raw, 0.0)))).astype(LOW)
                out_ref[c, 2 * half + p * LANES : 2 * half + (p + 1) * LANES] = grad_v[i].astype(LOW)

    ins = (query, key, value, qk, a_low, b_rows, state, *parts)
    return run(kernel, [((tokens, 3 * half), LOW)], *ins, scalars=False, flops=20 * tokens * tokens * half)[0]


def project_back(grad, qkv_w, x, norm_two):
    tokens, width = x.shape
    step = tokens // 2

    def kernel(grad_ref, w_ref, x_ref, two_ref, part_ref, low_ref, cols_ref, rows):
        gain_grad, bias_grad = jnp.zeros((1, width), WIDE), jnp.zeros((1, width), WIDE)
        for i in range(2):
            at = slice(i * step, (i + 1) * step)
            part = dot_cols(grad_ref[at, :], w_ref[...])
            part_ref[at, :] = part
            low_ref[at, :] = part.astype(LOW)
            gain_grad = gain_grad + jnp.sum(part * normalise(x_ref[at, :].astype(WIDE))[0], axis=0, keepdims=True)
            bias_grad = bias_grad + jnp.sum(part, axis=0, keepdims=True)
        rows[...] = jnp.zeros_like(rows)
        rows[0:1, :], rows[1:2, :], rows[2:4, :] = gain_grad, bias_grad, two_ref[...]
        cols_ref[...] = dot_rows(rows[...].astype(LOW), eye(8, LANES)).astype(LOW)

    outs = [((tokens, width), WIDE), ((tokens, width), LOW), ((width, LANES), LOW)]
    scratch = [pltpu.VMEM((8, width), WIDE)]
    flops = 2 * x.size * grad.shape[1]
    return run(kernel, outs, grad, qkv_w, x, norm_two, scalars=False, scratch=scratch, flops=flops)


def input_back(part, got, grad_resid, own_x, rows):
    group, width = own_x.shape

    def kernel(coords, part_ref, got_ref, resid_ref, x_ref, rows_ref, out_ref):
        at = pl.ds(pl.multiple_of(coords[3] * group, 16), group)
        normed, rate = normalise(x_ref[...].astype(WIDE))
        grad = part_ref[at, :] + got_ref[...].astype(WIDE)
        out_ref[...] = (resid_ref[at, :] + norm_back(normed, rate, grad, rows_ref[0:1, :])).astype(LOW)

    return run(kernel, [((group, width), LOW)], part, got, grad_resid, own_x, rows)[0]


def adam_update(weight, first, second, grad, rate, decay):
    first_new = BETA_ONE * first + (1.0 - BETA_ONE) * grad
    second_new = BETA_TWO * second + (1.0 - BETA_TWO) * grad * grad
    first_hat = first_new / (1.0 - BETA_ONE**STEP)
    second_hat = second_new / (1.0 - BETA_TWO**STEP)
    weight_new = weight - rate * (first_hat / (jnp.sqrt(second_hat) + ADAM_EPS) + decay * weight)
    return (weight_new, first_new, second_new)


def from_others(low, step):
    return [shift(low, step * k, wrap=False) for k in range(1, lax.axis_size("z"))]


def body(
    images,
    cotangent,
    qkv_weight,
    out_weight,
    up_weight,
    down_weight,
    norm_params,
    qkv_first,
    out_first,
    up_first,
    down_first,
    norm_first,
    qkv_second,
    out_second,
    up_second,
    down_second,
    norm_second,
):
    depth, core = lax.axis_size("z"), lax.axis_index("c")
    count, group, width = images.shape
    hidden_units = up_weight.shape[1]
    own_rows = qkv_weight.shape[0]
    own_units = down_weight.shape[0]
    chips = lax.axis_size("y") * lax.axis_size("x")
    block, ff_block = width // (2 * depth), hidden_units // (2 * depth)
    half_qkv, half_ff, half_d = 3 * width // 2, hidden_units // 2, width // 2
    ring = lax.axis_size("y") == 2 and lax.axis_size("x") == 2 and depth % 2 == 0 and own_rows % 32 == 0
    heads = half_d // HEAD_DIM
    tokens = 2 * group

    own_x, own_g = images.reshape(group, width), cotangent.reshape(group, width)
    split_qkv = lambda w: jnp.moveaxis(w.reshape(-1, 3 * depth, 2, block), 2, 0).reshape(2, -1, half_qkv)
    split_up = lambda w: jnp.moveaxis(w.reshape(-1, depth, 2, ff_block), 2, 0).reshape(2, -1, half_ff)

    thin, small = own_units // 2, own_rows // 2
    if ring:
        qkv_mine, qkv_give = cast_qkv(qkv_weight, norm_params, 3 * depth)
        up_mine, up_give, out_part, down_one, down_two = cast_rest(
            after(up_weight, qkv_give), out_weight, down_weight, depth
        )
        qkv_mate, x_mate, up_mate = swap(qkv_give, "c"), swap(own_x, "c"), swap(up_give, "c")
        inputs = join_rows(own_x, x_mate)
        up_part = join_rows(up_mine, up_mate, out_part)
        qkv_part = join_rows(qkv_mine, qkv_mate)
        qkv_part, up_part, inputs = lax.optimization_barrier((qkv_part, up_part, inputs))
        qkv_column = column_first(qkv_part)
        two_plane = plane_first(after(down_two, qkv_part))
        up_column = column_first(after(up_part, two_plane, *qkv_column))
        qkv_parts = plane_last(jnp.stack(qkv_column))
        g_mate = swap(after(own_g, *up_column), "c")
        two_next = shift(after(two_plane, *up_column), 1)

        def qkv_moves(zz, plane, piece):
            row = lambda h: ((zz * 2 + h) * chips + plane) * own_rows
            moves = [(0, h * own_rows, 0, own_rows, half_qkv, row(h), 0) for h in (0, 1)]
            return moves + [(1, h * own_rows, half_qkv, own_rows, LANES, row(h), 0) for h in (0, 1)]

        def up_moves(zz, plane, piece):
            row = lambda h: ((zz * 2 + h) * chips + plane) * own_rows
            moves = [(0, h * own_rows, 0, own_rows, half_ff, row(h), 0) for h in (0, 1)]
            to = zz * block + plane * own_rows
            return moves + [(1, h * own_rows, half_ff, own_rows, half_d, to, h * half_d) for h in (0, 1)]

        def down_moves(zz, plane, piece):
            return [(0, 0, 0, thin, width, zz * ff_block + plane * own_units + piece * thin, 0)]

        spots = column_first_spots(depth)
        qkv_w, norm_w = place(qkv_parts, depth, [(width, half_qkv), (width, LANES)], spots, qkv_moves)
    else:
        qkv_low, out_low = qkv_weight.astype(LOW), out_weight.astype(LOW)
        up_low, down_low = up_weight.astype(LOW), down_weight.astype(LOW)
        norm_low = norm_params.astype(LOW)
        x_mate, g_mate = swap(own_x, "c"), swap(own_g, "c")
        whole = lambda w, axis=0: lax.all_gather(w, ALL, axis=axis, tiled=True)
        qkv_w, up_w = mine(split_qkv(whole(qkv_low))), mine(split_up(whole(up_low)))
        rows_half = lambda w, b: mine(jnp.moveaxis(w.reshape(depth, 2, b, width), 1, 0)).reshape(-1, width)
        out_w, down_w = rows_half(whole(out_low), block), rows_half(whole(down_low), ff_block)
        norm_w = jnp.pad(whole(norm_low, 1).T, ((0, 0), (0, LANES - 4)))

        inputs = join_rows(own_x, x_mate)
    grad_out = join_rows(own_g, g_mate)
    halves = lambda a: a.reshape(2, group, -1)
    rows, normed_one, qk, query, key, value, state = project(inputs, norm_w, qkv_w)
    earlier = from_others(state, 1)
    mixed, mixed_low, denom, state_in = attend(query, key, value, earlier)
    if ring:
        one_column = column_first(after(down_one, two_next, *earlier))
        gate = (mixed_low, two_next, *one_column)
        up_parts = plane_last(after(jnp.stack(up_column), *qkv_parts[3:]), gate)
        two_parts = [two_plane, two_next, shift(after(two_next, *one_column), 1)]
        up_w, out_w = place(up_parts, depth, [(width, half_ff), (half_d, width)], spots, up_moves)
    out_part = dot(mixed_low, out_w)
    out_got = swap(out_part.astype(LOW), "c")
    if ring:
        out_got = after(out_got, *two_parts)
    resid, normed_two, activated, slope = feed(inputs, out_part, out_got, rows, up_w)
    down_grad = dot_rows(activated, grad_out).astype(LOW)
    if ring:
        def down_cuts(zz, plane, half):
            return [(0, zz * ff_block + plane * own_units + half * thin, 0, thin, width, 0, 0)]

        down_cut = unplace([down_grad], depth, (thin, width), down_cuts)
        for _ in range(3, depth):
            two_parts.append(shift(two_parts[-1], 1))
        one_parts = plane_last(after(jnp.stack(one_column), *up_parts[3:]), (activated, *two_parts))
        spots = spots + plane_first_spots(depth, thin, 5)
        down_parts = [after(one_parts[0], down_cut[0]), *one_parts[1:], *two_parts]
        (down_w,) = place(down_parts, depth, [(half_ff, width)], spots, down_moves)

    grad_hidden, two_part, two_low = feed_back(grad_out, down_w, slope, up_w)
    up_grad = dot_rows(normed_two, grad_hidden).astype(LOW)
    two_got = after(swap(two_low, "c"), up_grad)
    grad_resid, grad_resid_low, a_low, b_rows, state_grad, norm_two = attend_turn(
        two_part, two_got, resid, rows, grad_out, out_w, mixed, denom, query
    )
    later = from_others(state_grad, -1)
    out_grad = dot_rows(mixed_low, grad_resid_low).astype(LOW)
    grad_projected = attend_back(query, key, value, qk, a_low, b_rows, state_in, later)
    qkv_grad = dot_rows(normed_one, grad_projected).astype(LOW)
    one_part, one_low, norm_cols = project_back(grad_projected, qkv_w, inputs, norm_two)
    input_grad = input_back(one_part, swap(other(halves(one_low)), "c"), grad_resid, own_x, rows)
    down_part = dot(after(activated, norm_cols), down_w)
    down_give = other(halves(down_part)).astype(LOW)
    down_got = swap(down_give, "c").astype(WIDE)
    activations = (mine(halves(resid + down_part)) + down_got).astype(LOW)

    out_fan = max(1, width * 64 // (tokens * depth))
    rates = (3.0 * width**-0.5, 3.0 * out_fan**-0.5, 3.0 * width**-0.5, 3.0 * hidden_units**-0.5, 1.5)
    decays = (WEIGHT_DECAY, WEIGHT_DECAY, WEIGHT_DECAY, WEIGHT_DECAY, 0.0)
    masters = (qkv_weight, out_weight, up_weight, down_weight, norm_params)
    firsts = (qkv_first, out_first, up_first, down_first, norm_first)
    seconds = (qkv_second, out_second, up_second, down_second, norm_second)
    if ring:

        def up_cuts(zz, plane, half):
            cuts = [(0, ((zz * 2 + half) * chips + plane) * own_rows, 0, own_rows, half_ff, 0, 0)]
            row = zz * block + plane * own_rows + half * small
            return cuts + [(1, row, p * half_d, small, half_d, p * small, half_ff) for p in (0, 1)]

        def qkv_cuts(zz, plane, half):
            row = ((zz * 2 + half) * chips + plane) * own_rows
            return [(0, row, 0, own_rows, half_qkv, 0, 0), (1, row, 0, own_rows, LANES, 0, half_qkv)]

        up_cut = unplace([up_grad, out_grad], depth, (own_rows, half_ff + half_d), up_cuts)
        down_sum, hop = reduce_chips(*down_cut, one_parts[3:], later, (grad_projected,))
        up_sum, hop = reduce_chips(*up_cut, hop, down_sum[1:])
        qkv_cut = unplace([qkv_grad, norm_cols], depth, (own_rows, half_qkv + LANES), qkv_cuts)
        qkv_sum, hop = reduce_chips(*qkv_cut, hop, (*up_sum[1:-1], down_give))
        down_red, squares = finish_down(down_sum)
        up_mine, up_give, out_red, squares = finish_up(up_sum, squares, own_rows, half_ff)
        up_mate = swap(up_give, "c")
        qkv_mine, qkv_give, small_mine = finish_qkv(qkv_sum, squares, own_rows, half_qkv)
        small_mate, qkv_mate = swap(small_mine, "c"), swap(qkv_give, "c")
        squares, norm_sum = chip_squares(small_mine, small_mate)
        norm_red = mine(norm_sum.reshape(2, own_rows, LANES))[:, :4].T
        grads = (qkv_mine, qkv_mate, out_red, up_mine, up_mate, down_red, norm_red)
        *news, grad_norm = update_all(
            grads, sum_chips(squares), masters, firsts, seconds, rates, decays, (3 * depth, depth)
        )
        return (
            activations.reshape(count, group, width),
            input_grad.reshape(count, group, width),
            grad_norm[0, 0],
            *news,
        )
    scatter = lambda g: lax.psum_scatter(g, ALL, scatter_dimension=0, tiled=True)
    both = lambda a, axis: jnp.stack([jnp.where(core == k, a, 0.0) for k in (0, 1)], axis)
    to_all = lambda a: a.astype(WIDE)
    qkv_red = scatter(both(to_all(qkv_grad).reshape(width, 3 * depth, block), 2).reshape(width, -1))
    up_red = scatter(both(to_all(up_grad).reshape(width, depth, ff_block), 2).reshape(width, -1))
    out_red = scatter(both(to_all(out_grad).reshape(depth, block, width), 1).reshape(width, width))
    down_red = scatter(both(to_all(down_grad).reshape(depth, ff_block, width), 1).reshape(hidden_units, width))
    norm_red = scatter(norm_cols.astype(WIDE))[:, :4].T

    reduced = (qkv_red, out_red, up_red, down_red, norm_red)
    local_squares = sum(jnp.sum(grad * grad) for grad in reduced)
    grad_norm = jnp.sqrt(lax.psum(local_squares, ALL))
    clip = jnp.minimum(1.0, CLIP_LIMIT / (grad_norm + 1e-06))
    news = [
        adam_update(masters[k], firsts[k], seconds[k], clip * reduced[k], rates[k], decays[k]) for k in range(5)
    ]
    return (
        activations.reshape(count, group, width),
        input_grad.reshape(count, group, width),
        grad_norm,
        *[new[0] for new in news],
        *[new[1] for new in news],
        *[new[2] for new in news],
    )


def solution(mesh):
    depth, planes = mesh.shape["seq"] // 2, mesh.shape["img"]
    across = max(k for k in range(1, planes + 1) if planes % k == 0 and k * k <= planes)
    grid = jax.sharding.Mesh(mesh.devices.reshape(depth, 2, planes // across, across), ALL)
    tokens = P(("y", "x"), ("z", "c"), None)
    matrix, norm = P(ALL, None), P(None, ALL)
    state = (matrix, matrix, matrix, matrix, norm)
    return jax.shard_map(
        body,
        mesh=grid,
        in_specs=(tokens, tokens) + state * 3,
        out_specs=(tokens, tokens, P()) + state * 3,
        check_vma=False,
    )
```

```python
import functools

import jax
import jax.numpy as jnp
from jax import lax
from jax.experimental import pallas as pl
from jax.experimental.pallas import tpu as pltpu
from jax.sharding import PartitionSpec as P

HEAD_DIM = 64
STEP = 10
NORM_EPS = 1e-05
BETA_ONE = 0.9
BETA_TWO = 0.999
ADAM_EPS = 1e-08
WEIGHT_DECAY = 0.1
CLIP_LIMIT = 1.0
LANES = 128

LOW = jnp.bfloat16
WIDE = jnp.float32
ALL = ("z", "c", "y", "x")
SWAP = [(0, 1), (1, 0)]


def swap(value, axis):
    return lax.ppermute(value, axis, SWAP)


def shift(value, step, wrap=True):
    size = lax.axis_size("z")
    pairs = [(i, (i + step) % size) for i in range(size) if wrap or 0 <= i + step < size]
    return lax.ppermute(value, "z", pairs)


def mine(pair_axis_first):
    return jnp.where(lax.axis_index("c") == 0, pair_axis_first[0], pair_axis_first[1])


def other(pair_axis_first):
    return jnp.where(lax.axis_index("c") == 0, pair_axis_first[1], pair_axis_first[0])


def in_order(own, mate, axis=0):
    first = lax.axis_index("c") == 0
    return jnp.concatenate([jnp.where(first, own, mate), jnp.where(first, mate, own)], axis)


def after(value, *before):
    return lax.optimization_barrier((value, *before))[0]


def column_first(shard):
    return [shard] + [shift(shard, k) for k in range(1, lax.axis_size("z"))]


def plane_last(column, between=()):
    half = column.shape[0] // 2
    along_x, along_y = swap(column, "x"), swap(column, "y")
    along_x, along_y = after(along_x, *between), after(along_y, *between)
    far = (swap(along_y[:half], "x"), swap(along_x[half:], "y"))
    return (column, along_x, along_y) + far


def plane_first(shard):
    half = shard.shape[0] // 2
    along_x, along_y = swap(shard, "x"), swap(shard, "y")
    far_low, far_high = swap(along_y[:half], "x"), swap(along_x[half:], "y")
    return jnp.concatenate([shard, along_x, along_y, far_low, far_high])


def column_last(plane):
    parts = [plane]
    for _ in range(1, lax.axis_size("z")):
        parts.append(shift(parts[-1], 1))
    return parts


def column_first_spots(depth):
    half = depth // 2
    spots = [(0, (k,), 0, (k, 0, 0)) for k in range(depth)]
    spots += [(1, (k,), 0, (k, 0, 1)) for k in range(depth)]
    spots += [(2, (k,), 0, (k, 1, 0)) for k in range(depth)]
    spots += [(3, (k,), 0, (k, 1, 1)) for k in range(half)]
    return spots + [(4, (k - half,), 0, (k, 1, 1)) for k in range(half, depth)]


def plane_first_spots(depth, rows):
    return [(k, (), p * rows, (k, p // 2, p % 2)) for k in range(depth) for p in range(4)]


def first_hop(send_x, keep_x, send_y, keep_y, before=()):
    return keep_x, swap(after(send_x, *before), "x"), keep_y, swap(after(send_y, *before), "y")


def later_hops(keep_x, got_x, keep_y, got_y, between=(), last=()):
    depth, rows, cols = keep_x.shape[1:]
    got_x, got_y = after(got_x, *between), after(got_y, *between)

    def second_hop(kx, gx, ky, gy, to_y, to_x):
        to_y[...] = (kx[1].astype(WIDE) + gx[1].astype(WIDE)).astype(LOW)
        to_x[...] = (ky[1].astype(WIDE) + gy[1].astype(WIDE)).astype(LOW)

    outs = [((depth, rows, cols), LOW)] * 2
    to_y, to_x = run(second_hop, outs, keep_x, got_x, keep_y, got_y, scalars=False, room=24)
    on_y, on_x = swap(to_y, "y"), swap(to_x, "x")
    hop = (on_x, on_y)
    on_y, on_x = after(on_y, *last), after(on_x, *last)

    def third_hop(kx, gx, ky, gy, ony, onx, own, *sends):
        for k in range(depth):
            one = kx[0, k].astype(WIDE) + gx[0, k].astype(WIDE) + ony[k].astype(WIDE)
            two = ky[0, k].astype(WIDE) + gy[0, k].astype(WIDE) + onx[k].astype(WIDE)
            out = sends[k - 1] if k else own
            out[:rows, :] = one.astype(out.dtype)
            out[rows:, :] = two.astype(out.dtype)

    outs = [((2 * rows, cols), WIDE if k == 0 else LOW) for k in range(depth)]
    own, *sends = run(third_hop, outs, keep_x, got_x, keep_y, got_y, on_y, on_x, scalars=False, room=24)
    return [own] + [shift(part, k + 1) for k, part in enumerate(sends)], hop


def sum_of(refs):
    total = refs[0][...]
    for ref in refs[1:]:
        total = total + ref[...].astype(WIDE)
    return total


def spread(value):
    return jnp.broadcast_to(value, (8, LANES))


def total_squares(value):
    return jnp.sum(jnp.sum(value * value, axis=1, keepdims=True), axis=0, keepdims=True)


def finish_down(parts):
    def kernel(*refs):
        total = sum_of(refs[: len(parts)])
        refs[-2][...] = total
        refs[-1][...] = spread(total_squares(total))

    return run(kernel, [(parts[0].shape, WIDE), ((8, LANES), WIDE)], *parts, scalars=False, room=24)


def finish_up(parts, squares, rows, half_ff):
    half_d = parts[0].shape[1] - half_ff
    small = rows // 2

    def kernel(coords, squares_ref, *refs):
        own_ref, mate_ref, out_ref, total_ref, all_ref = refs[len(parts) :]
        total = sum_of(refs[: len(parts)])
        all_ref[...] = total
        core = coords[3]
        own_ref[...] = all_ref[pl.ds(pl.multiple_of(core * rows, 8), rows), :half_ff]
        mate_ref[...] = all_ref[pl.ds(pl.multiple_of((1 - core) * rows, 8), rows), :half_ff]
        for p in range(2):
            for h in range(2):
                block = total[h * rows + p * small : h * rows + (p + 1) * small, half_ff:]
                out_ref[h * small : (h + 1) * small, p * half_d : (p + 1) * half_d] = block
        total_ref[...] = squares_ref[...] + spread(total_squares(total))

    outs = [((rows, half_ff), WIDE)] * 2 + [((rows, 2 * half_d), WIDE), ((8, LANES), WIDE)]
    scratch = [pltpu.VMEM(parts[0].shape, WIDE)]
    return run(kernel, outs, squares, *parts, scratch=scratch, room=24)


def finish_qkv(parts, squares, rows, half_qkv):
    def kernel(coords, squares_ref, *refs):
        own_ref, mate_ref, small_ref, all_ref = refs[len(parts) :]
        total = sum_of(refs[: len(parts)])
        all_ref[...] = total
        core = coords[3]
        own_ref[...] = all_ref[pl.ds(pl.multiple_of(core * rows, 8), rows), :half_qkv]
        mate_ref[...] = all_ref[pl.ds(pl.multiple_of((1 - core) * rows, 8), rows), :half_qkv]
        small_ref[: 2 * rows, :] = total[:, half_qkv:]
        small_ref[2 * rows :, :] = squares_ref[...] + spread(total_squares(total[:, :half_qkv]))

    outs = [((rows, half_qkv), WIDE)] * 2 + [((2 * rows + 8, LANES), WIDE)]
    scratch = [pltpu.VMEM(parts[0].shape, WIDE)]
    return run(kernel, outs, squares, *parts, scratch=scratch, room=24)


def chip_squares(small, got):
    rows = small.shape[0] - 8

    def kernel(small_ref, got_ref, total_ref, norm_ref):
        total = small_ref[...] + got_ref[...]
        norm_ref[...] = total[:rows]
        total_ref[...] = total[rows:] + spread(total_squares(total[:rows]))

    outs = [((8, LANES), WIDE), ((rows, LANES), WIDE)]
    return run(kernel, outs, small, got, scalars=False, room=24)


def sum_chips(value):
    across = lax.ppermute(value, ("y", "x"), [(i, 3 - i) for i in range(4)])
    value = value + swap(value, "y") + (swap(value, "x") + across)
    return [value] + [shift(value, k) for k in range(1, lax.axis_size("z"))]


def interleave(first, own, mate, blocks):
    size = own.shape[1] // blocks
    pieces = []
    for j in range(blocks):
        at = slice(j * size, (j + 1) * size)
        pieces += [jnp.where(first, own[:, at], mate[:, at]), jnp.where(first, mate[:, at], own[:, at])]
    return jnp.concatenate(pieces, axis=1)


def update_all(grads, totals, masters, firsts, seconds, rates, decays, blocks):
    steps = 4
    n, m = len(grads), len(totals)

    def tile(array):
        rows, cols = array.shape
        return pl.BlockSpec((rows // steps, cols), lambda i: (i, 0))

    def whole(array):
        return pl.BlockSpec(array.shape, lambda i: (0, 0))

    def kernel(coords, *refs):
        first = coords[3] == 0
        g, t, old, new = refs[:n], refs[n : n + m], refs[n + m : n + m + 15], refs[n + m + 15 :]
        total = sum_of(t)[0:1, 0:1]
        norm = jnp.sqrt(total)
        clip = jnp.minimum(1.0, CLIP_LIMIT / (norm + 1e-06))
        qkv = interleave(first, g[0][...], g[1][...], blocks[0])
        up = interleave(first, g[3][...], g[4][...], blocks[1])
        for k, grad in enumerate((qkv, g[2][...], up, g[5][...], g[6][...])):
            news = adam_update(old[k][...], old[5 + k][...], old[10 + k][...], clip * grad, rates[k], decays[k])
            for part in range(3):
                new[5 * part + k][...] = news[part]
        new[15][...] = jnp.broadcast_to(norm, (8, LANES))

    state = (*masters, *firsts, *seconds)
    specs = [whole(a) if k % 5 == 4 else tile(a) for k, a in enumerate(state)]
    norm_out = jax.ShapeDtypeStruct((8, LANES), WIDE)
    return pl.pallas_call(
        kernel,
        grid=(steps,),
        out_shape=[jax.ShapeDtypeStruct(a.shape, WIDE) for a in state] + [norm_out],
        in_specs=[pl.BlockSpec(memory_space=pltpu.SMEM)]
        + [tile(a) for a in grads[:-1]]
        + [whole(grads[-1])]
        + [whole(a) for a in totals]
        + specs,
        out_specs=specs + [whole(norm_out)],
        compiler_params=FULL,
    )(coordinates(), *grads, *totals, *state)


def coordinates():
    return jnp.stack([lax.axis_index(name) for name in ("z", "y", "x", "c")]).astype(jnp.int32)


def chip_of(coords, rel, depth, back):
    dz, dy, dx = rel
    z, y, x = coords[0], coords[1], coords[2]
    zz = lax.rem(z + (depth - dz if back else dz), depth)
    yy = 1 - y if dy else y
    xx = 1 - x if dx else x
    return zz, yy * 2 + xx


def window(row, rows, col, cols):
    rows_at = pl.ds(row if isinstance(row, int) else pl.multiple_of(row, 16), rows)
    return rows_at, pl.ds(col, cols)


VMEM = pl.BlockSpec(memory_space=pltpu.VMEM)
ROOM = pltpu.CompilerParams(vmem_limit_bytes=24 * 1024 * 1024)
FULL = pltpu.CompilerParams(vmem_limit_bytes=56 * 1024 * 1024)


def place(parts, depth, outs, spots, moves):
    def kernel(coords, *refs):
        ins, out_refs = refs[: len(parts)], refs[len(parts) :]
        for array, lead, base, rel in spots:
            zz, plane = chip_of(coords, rel, depth, True)
            for o, sr, sc, rows, cols, tr, tc in moves(zz, plane):
                out_refs[o][window(tr, rows, tc, cols)] = ins[array][(*lead, *window(base + sr, rows, sc, cols))]

    return pl.pallas_call(
        kernel,
        out_shape=[jax.ShapeDtypeStruct(s, LOW) for s in outs],
        in_specs=[pl.BlockSpec(memory_space=pltpu.SMEM)] + [VMEM] * len(parts),
        out_specs=[VMEM] * len(outs),
        compiler_params=ROOM,
    )(coordinates(), *parts)


def unplace(grads, depth, rows_cols, moves):
    spots = []
    for dz in range(depth):
        for d in range(2):
            spots += [(0, d, dz, (dz, d, 1), 0), (1, d, dz, (dz, d, 0), 0)]
            spots += [(2, d, dz, (dz, 1, d), 1), (3, d, dz, (dz, 0, d), 1)]

    def kernel(coords, *refs):
        ins, out_refs = refs[: len(grads)], refs[len(grads) :]
        for array, d, dz, rel, half in spots:
            zz, plane = chip_of(coords, rel, depth, False)
            for i, sr, sc, rows, cols, tr, tc in moves(zz, plane, half):
                out_refs[array][(d, dz, *window(tr, rows, tc, cols))] = ins[i][window(sr, rows, sc, cols)]

    return pl.pallas_call(
        kernel,
        out_shape=[jax.ShapeDtypeStruct((2, depth) + rows_cols, LOW)] * 4,
        in_specs=[pl.BlockSpec(memory_space=pltpu.SMEM)] + [VMEM] * len(grads),
        out_specs=[VMEM] * 4,
        compiler_params=ROOM,
    )(coordinates(), *grads)


def cast_qkv(qkv, norm, halves):
    rows, cols = qkv.shape
    wide = cols // 2 + LANES
    block = cols // (2 * halves)

    def kernel(coords, qkv_ref, norm_ref, own_ref, mate_ref, tall):
        first = coords[3] == 0
        for j in range(halves):
            a = qkv_ref[:, 2 * j * block : (2 * j + 1) * block]
            b = qkv_ref[:, (2 * j + 1) * block : (2 * j + 2) * block]
            own_ref[:, j * block : (j + 1) * block] = jnp.where(first, a, b).astype(LOW)
            mate_ref[:, j * block : (j + 1) * block] = jnp.where(first, b, a).astype(LOW)
        tall[...] = jnp.zeros_like(tall)
        tall[0:4, :] = norm_ref[...].astype(LOW).astype(WIDE)
        i = lax.broadcasted_iota(jnp.int32, (rows, rows), 0)
        j = lax.broadcasted_iota(jnp.int32, (rows, rows), 1)
        columns = dot_cols((i == j).astype(LOW), tall[...].astype(LOW)).astype(LOW)
        own_ref[:, cols // 2 :] = columns
        mate_ref[:, cols // 2 :] = columns

    return pl.pallas_call(
        kernel,
        out_shape=[jax.ShapeDtypeStruct((rows, wide), LOW)] * 2,
        in_specs=[pl.BlockSpec(memory_space=pltpu.SMEM), VMEM, VMEM],
        out_specs=[VMEM] * 2,
        scratch_shapes=[pltpu.VMEM((LANES, rows), WIDE)],
        compiler_params=FULL,
    )(coordinates(), qkv, norm)


def cast_rest(up, out, down, halves):
    rows, cols = up.shape
    block, width = cols // (2 * halves), out.shape[1]

    def kernel(coords, up_ref, out_ref, down_ref, own_ref, mate_ref, part_ref, low_ref):
        first = coords[3] == 0
        for j in range(halves):
            a = up_ref[:, 2 * j * block : (2 * j + 1) * block]
            b = up_ref[:, (2 * j + 1) * block : (2 * j + 2) * block]
            own_ref[:, j * block : (j + 1) * block] = jnp.where(first, a, b).astype(LOW)
            mate_ref[:, j * block : (j + 1) * block] = jnp.where(first, b, a).astype(LOW)
        part_ref[:rows, :] = out_ref[:, : width // 2].astype(LOW)
        part_ref[rows:, :] = out_ref[:, width // 2 :].astype(LOW)
        low_ref[...] = down_ref[...].astype(LOW)

    return pl.pallas_call(
        kernel,
        out_shape=[jax.ShapeDtypeStruct((rows, cols // 2), LOW)] * 2
        + [jax.ShapeDtypeStruct((2 * rows, width // 2), LOW), jax.ShapeDtypeStruct(down.shape, LOW)],
        in_specs=[pl.BlockSpec(memory_space=pltpu.SMEM), VMEM, VMEM, VMEM],
        out_specs=[VMEM] * 4,
        compiler_params=FULL,
    )(coordinates(), up, out, down)


def join_rows(own, mate, side=None):
    rows, cols = own.shape
    wide = cols + (side.shape[1] if side is not None else 0)

    def kernel(coords, own_ref, mate_ref, *refs):
        out_ref = refs[-1]
        core = coords[3]
        out_ref[pl.ds(pl.multiple_of(core * rows, 16), rows), :cols] = own_ref[...]
        out_ref[pl.ds(pl.multiple_of((1 - core) * rows, 16), rows), :cols] = mate_ref[...]
        if side is not None:
            out_ref[:, cols:] = refs[0][...]

    ins = [own, mate] + ([side] if side is not None else [])
    return pl.pallas_call(
        kernel,
        out_shape=jax.ShapeDtypeStruct((2 * rows, wide), LOW),
        in_specs=[pl.BlockSpec(memory_space=pltpu.SMEM)] + [VMEM] * len(ins),
        out_specs=VMEM,
        compiler_params=ROOM,
    )(coordinates(), *ins)


def run(kernel, outs, *ins, scalars=True, scratch=(), flops=0, room=24):
    out_shape = [jax.ShapeDtypeStruct(shape, kind) for shape, kind in outs]
    return pl.pallas_call(
        kernel,
        out_shape=out_shape,
        in_specs=([pl.BlockSpec(memory_space=pltpu.SMEM)] if scalars else []) + [VMEM] * len(ins),
        out_specs=[VMEM] * len(outs),
        scratch_shapes=list(scratch),
        compiler_params=pltpu.CompilerParams(vmem_limit_bytes=room * 1024 * 1024),
        cost_estimate=pl.CostEstimate(flops=flops, bytes_accessed=0, transcendentals=0),
    )(*([coordinates()] if scalars else []), *ins)


def dot(left, right):
    return jnp.dot(left, right, preferred_element_type=WIDE)


def dot_rows(left, right):
    return lax.dot_general(left, right, (((0,), (0,)), ((), ())), preferred_element_type=WIDE)


def dot_cols(left, right):
    return lax.dot_general(left, right, (((1,), (1,)), ((), ())), preferred_element_type=WIDE)


def eye(rows, cols):
    i = lax.broadcasted_iota(jnp.int32, (rows, cols), 0)
    return (i == lax.broadcasted_iota(jnp.int32, (rows, cols), 1)).astype(LOW)


def normalise(values):
    center = values - jnp.mean(values, axis=-1, keepdims=True)
    rate = lax.rsqrt(jnp.mean(center * center, axis=-1, keepdims=True) + NORM_EPS)
    return center * rate, rate


def norm_back(normed, rate, grad, gain):
    scaled = grad * gain
    shared = jnp.mean(scaled, axis=-1, keepdims=True)
    along = jnp.mean(scaled * normed, axis=-1, keepdims=True)
    return rate * (scaled - shared - normed * along)


def low_lanes(rows):
    return lax.broadcasted_iota(jnp.int32, (rows, LANES), 1) < HEAD_DIM


def by_head(pair):
    wide = pair.astype(WIDE)
    first = low_lanes(pair.shape[0])
    return jnp.where(first, wide, 0.0).astype(LOW), jnp.where(first, 0.0, wide).astype(LOW)


def pack_state(square):
    first = low_lanes(HEAD_DIM)
    return jnp.where(first, square[:HEAD_DIM], square[HEAD_DIM:])


def open_state(packed):
    first = low_lanes(HEAD_DIM)
    return jnp.concatenate([jnp.where(first, packed, 0.0), jnp.where(first, 0.0, packed)])


def feature(values):
    return jnp.where(values > 0.0, values + 1.0, jnp.exp(jnp.minimum(values, 0.0)))


def project(x, norm_w, qkv_w):
    tokens, width = x.shape
    half = qkv_w.shape[1] // 3
    pairs = half // LANES
    step = tokens // 2

    def kernel(x_ref, norm_ref, w_ref, rows_ref, normed_ref, qk_ref, q_ref, k_ref, v_ref, state_ref, sums):
        rows_ref[...] = dot_cols(eye(8, LANES), norm_ref[...])
        gain, bias = rows_ref[0:1, :], rows_ref[1:2, :]
        for i in range(2):
            at = slice(i * step, (i + 1) * step)
            normed = normalise(x_ref[at, :].astype(WIDE))[0]
            normed_ref[at, :] = (normed * gain + bias).astype(LOW)
            low = normed_ref[at, :]
            for j, out in enumerate((q_ref, k_ref)):
                part = dot(low, w_ref[:, j * half : (j + 1) * half])
                qk_ref[at, j * half : (j + 1) * half] = part
                out[at, :] = feature(part).astype(LOW)
            v_ref[at, :] = dot(low, w_ref[:, 2 * half :]).astype(LOW)
        total = dot_rows(jnp.ones((tokens, 8), LOW), k_ref[...])
        sums[...] = jnp.zeros_like(sums)
        for p in range(pairs):
            lanes = slice(p * LANES, (p + 1) * LANES)
            packed = pack_state(dot_rows(k_ref[:, lanes], v_ref[:, lanes]))
            state_ref[p * HEAD_DIM : (p + 1) * HEAD_DIM, :] = packed.astype(LOW)
            sums[p : p + 1, :] = total[0:1, lanes]
        state_ref[pairs * HEAD_DIM :, :] = sums[...].astype(LOW)

    outs = [((8, width), WIDE), ((tokens, width), LOW), ((tokens, 2 * half), WIDE)] + [((tokens, half), LOW)] * 3
    outs += [((pairs * HEAD_DIM + 16, LANES), LOW)]
    scratch = [pltpu.VMEM((16, LANES), WIDE)]
    return run(kernel, outs, x, norm_w, qkv_w, scalars=False, scratch=scratch)


def total_state(refs):
    total = refs[0][...].astype(WIDE)
    for ref in refs[1:]:
        total = total + ref[...].astype(WIDE)
    return total


def causal_mask(step):
    i = lax.broadcasted_iota(jnp.int32, (step, step), 0)
    return i >= lax.broadcasted_iota(jnp.int32, (step, step), 1)


def attend(query, key, value, parts):
    tokens, half = query.shape
    pairs, step = half // LANES, tokens // 2

    def kernel(q_ref, k_ref, v_ref, *refs):
        mixed_ref, low_ref, denom_ref, state_ref = refs[len(parts) :]
        state_ref[...] = total_state(refs[: len(parts)])
        lower = causal_mask(step)
        first = low_lanes(step)
        top = low_lanes(HEAD_DIM)
        diagonal = eye(LANES, LANES).astype(WIDE)
        for p in range(pairs):
            lanes = slice(p * LANES, (p + 1) * LANES)
            packed = state_ref[p * HEAD_DIM : (p + 1) * HEAD_DIM, :]
            sums = state_ref[pairs * HEAD_DIM + p : pairs * HEAD_DIM + p + 1, :]
            column = jnp.sum(diagonal * sums, axis=1, keepdims=True)
            zero = jnp.zeros((HEAD_DIM, LANES), WIDE)
            ext = (
                jnp.concatenate([jnp.where(top, packed, column[:HEAD_DIM]), zero]).astype(LOW),
                jnp.concatenate([zero, jnp.where(top, column[HEAD_DIM:], packed)]).astype(LOW),
            )
            wide = v_ref[:, lanes].astype(WIDE)
            full = low_lanes(tokens)
            value_ext = (jnp.where(full, wide, 1.0).astype(LOW), jnp.where(full, 1.0, wide).astype(LOW))
            queries = by_head(q_ref[:, lanes])
            for i in range(2):
                at = slice(i * step, (i + 1) * step)
                got = []
                for h in range(2):
                    rows = queries[h][at]
                    total = dot(rows, ext[h])
                    for j in range(i + 1):
                        to = slice(j * step, (j + 1) * step)
                        scores = dot_cols(rows, k_ref[to, lanes])
                        if j == i:
                            scores = jnp.where(lower, scores, 0.0)
                        total = total + dot(scores.astype(LOW), value_ext[h][to])
                    got.append(total)
                denom = pltpu.roll(jnp.where(first, got[1], got[0]), HEAD_DIM, 1)
                mixed = jnp.where(first, got[0], got[1]) / denom
                mixed_ref[at, lanes] = mixed
                low_ref[at, lanes] = mixed.astype(LOW)
                denom_ref[at, lanes] = denom

    outs = [((tokens, half), WIDE), ((tokens, half), LOW), ((tokens, half), WIDE), (parts[0].shape, WIDE)]
    return run(kernel, outs, query, key, value, *parts, scalars=False)


def feed(x, part, got, rows, up_w):
    tokens, width = x.shape
    units, step, cut = up_w.shape[1], tokens // 2, 512

    def kernel(x_ref, part_ref, got_ref, rows_ref, w_ref, resid_ref, normed_ref, act_ref, slope_ref):
        for i in range(2):
            at = slice(i * step, (i + 1) * step)
            resid = x_ref[at, :].astype(WIDE) + part_ref[at, :] + got_ref[at, :].astype(WIDE)
            resid_ref[at, :] = resid
            normed_ref[at, :] = (normalise(resid)[0] * rows_ref[2:3, :] + rows_ref[3:4, :]).astype(LOW)
            for j in range(units // cut):
                to = slice(j * cut, (j + 1) * cut)
                v = dot(normed_ref[at, :], w_ref[:, to])
                root = (2.0 / 3.141592653589793) ** 0.5
                square = v * v
                bend = jnp.tanh(root * v * (1.0 + 0.044715 * square))
                cdf = 0.5 * (1.0 + bend)
                act_ref[at, to] = (v * cdf).astype(LOW)
                slope_ref[at, to] = cdf + 0.5 * v * (1.0 - bend * bend) * (root * (1.0 + 3.0 * 0.044715 * square))

    outs = [((tokens, width), WIDE), ((tokens, width), LOW), ((tokens, units), LOW), ((tokens, units), WIDE)]
    return run(kernel, outs, x, part, got, rows, up_w, scalars=False)


def feed_back(grad_out, down_w, slope, up_w):
    tokens, width = grad_out.shape
    units, step, cut = up_w.shape[1], tokens // 2, 512

    def kernel(g_ref, down_ref, slope_ref, up_ref, hidden_ref, part_ref, low_ref):
        for i in range(2):
            at = slice(i * step, (i + 1) * step)
            for j in range(units // cut):
                to = slice(j * cut, (j + 1) * cut)
                grad = dot_cols(g_ref[at, :], down_ref[to, :]) * slope_ref[at, to]
                hidden_ref[at, to] = grad.astype(LOW)
            part = dot_cols(hidden_ref[at, :], up_ref[...])
            part_ref[at, :] = part
            low_ref[at, :] = part.astype(LOW)

    outs = [((tokens, units), LOW), ((tokens, width), WIDE), ((tokens, width), LOW)]
    return run(kernel, outs, grad_out, down_w, slope, up_w, scalars=False)


def attend_turn(part, got, resid, rows, grad_out, out_w, mixed, denom, query):
    tokens, width = resid.shape
    half = mixed.shape[1]
    pairs, step = half // LANES, tokens // 2

    def kernel(
        part_ref, got_ref, resid_ref, rows_ref, g_ref, w_ref, mixed_ref, denom_ref, q_ref,
        grad_ref, low_ref, a_ref, b_ref, state_ref, norm_ref, sums,
    ):
        gain = rows_ref[2:3, :]
        gain_grad, bias_grad = jnp.zeros((1, width), WIDE), jnp.zeros((1, width), WIDE)
        first = low_lanes(step)
        for i in range(2):
            at = slice(i * step, (i + 1) * step)
            normed, rate = normalise(resid_ref[at, :])
            own = part_ref[at, :]
            gain_grad = gain_grad + jnp.sum(own * normed, axis=0, keepdims=True)
            bias_grad = bias_grad + jnp.sum(own, axis=0, keepdims=True)
            grad = g_ref[at, :].astype(WIDE) + norm_back(normed, rate, own + got_ref[at, :].astype(WIDE), gain)
            grad_ref[at, :] = grad
            low_ref[at, :] = grad.astype(LOW)
            turned = dot_cols(low_ref[at, :], w_ref[...]) / denom_ref[at, :]
            a_ref[at, :] = turned.astype(LOW)
            along = turned * mixed_ref[at, :]
            for p in range(pairs):
                lanes = slice(p * LANES, (p + 1) * LANES)
                piece = along[:, lanes]
                low = jnp.sum(jnp.where(first, piece, 0.0), axis=1, keepdims=True)
                high = jnp.sum(jnp.where(first, 0.0, piece), axis=1, keepdims=True)
                b_ref[at, lanes] = -jnp.where(first, low, high)
        norm_ref[0:1, :] = gain_grad
        norm_ref[1:2, :] = bias_grad
        sums[...] = jnp.zeros_like(sums)
        for p in range(pairs):
            lanes = slice(p * LANES, (p + 1) * LANES)
            packed = pack_state(dot_rows(q_ref[:, lanes], a_ref[:, lanes]))
            state_ref[p * HEAD_DIM : (p + 1) * HEAD_DIM, :] = packed.astype(LOW)
            sums[p : p + 1, :] = jnp.sum(q_ref[:, lanes].astype(WIDE) * b_ref[:, lanes], axis=0, keepdims=True)
        state_ref[pairs * HEAD_DIM :, :] = sums[...].astype(LOW)

    outs = [((tokens, width), WIDE), ((tokens, width), LOW), ((tokens, half), LOW), ((tokens, half), WIDE)]
    outs += [((pairs * HEAD_DIM + 16, LANES), LOW), ((2, width), WIDE)]
    ins = (part, got, resid, rows, grad_out, out_w, mixed, denom, query)
    scratch = [pltpu.VMEM((16, LANES), WIDE)]
    return run(kernel, outs, *ins, scalars=False, scratch=scratch)


def attend_back(query, key, value, qk, a_low, b_rows, state, parts):
    tokens, half = query.shape
    pairs, step = half // LANES, tokens // 2

    def kernel(q_ref, k_ref, v_ref, qk_ref, a_ref, b_ref, state_ref, *refs):
        out_ref = refs[len(parts)]
        later = total_state(refs[: len(parts)])
        lower = causal_mask(step)
        for p in range(pairs):
            lanes = slice(p * LANES, (p + 1) * LANES)
            rows = slice(p * HEAD_DIM, (p + 1) * HEAD_DIM)
            sums = slice(pairs * HEAD_DIM + p, pairs * HEAD_DIM + p + 1)
            before, after_it = open_state(state_ref[rows, :]).astype(LOW), open_state(later[rows]).astype(LOW)
            queries, keys, pulls = by_head(q_ref[:, lanes]), by_head(k_ref[:, lanes]), by_head(a_ref[:, lanes])
            cuts = [slice(i * step, (i + 1) * step) for i in range(2)]
            grad_q = [dot_cols(a_ref[c, lanes], before) + b_ref[c, lanes] * state_ref[sums, :] for c in cuts]
            grad_k = [dot_cols(v_ref[c, lanes], after_it) + later[sums] for c in cuts]
            grad_v = [dot(k_ref[c, lanes], after_it) for c in cuts]
            for i in range(2):
                for j in range(i + 1):
                    for h in range(2):
                        q, a = queries[h][cuts[i]], pulls[h][cuts[i]]
                        b = b_ref[cuts[i], p * LANES + h * HEAD_DIM : p * LANES + h * HEAD_DIM + 1]
                        scores = dot_cols(q, k_ref[cuts[j], lanes])
                        pull = dot_cols(a, v_ref[cuts[j], lanes]) + b
                        if j == i:
                            scores, pull = jnp.where(lower, scores, 0.0), jnp.where(lower, pull, 0.0)
                        scores, pull = scores.astype(LOW), pull.astype(LOW)
                        grad_q[i] = grad_q[i] + dot(pull, keys[h][cuts[j]])
                        grad_k[j] = grad_k[j] + dot_rows(pull, q)
                        grad_v[j] = grad_v[j] + dot_rows(scores, a)
            for i, c in enumerate(cuts):
                for n, grad in enumerate((grad_q[i], grad_k[i])):
                    at = slice(n * half + p * LANES, n * half + (p + 1) * LANES)
                    raw = qk_ref[c, at]
                    out_ref[c, at] = (grad * jnp.where(raw > 0.0, 1.0, jnp.exp(jnp.minimum(raw, 0.0)))).astype(LOW)
                out_ref[c, 2 * half + p * LANES : 2 * half + (p + 1) * LANES] = grad_v[i].astype(LOW)

    ins = (query, key, value, qk, a_low, b_rows, state, *parts)
    return run(kernel, [((tokens, 3 * half), LOW)], *ins, scalars=False)[0]


def project_back(grad, qkv_w, x, norm_two):
    tokens, width = x.shape
    step = tokens // 2

    def kernel(grad_ref, w_ref, x_ref, two_ref, part_ref, low_ref, cols_ref, rows):
        gain_grad, bias_grad = jnp.zeros((1, width), WIDE), jnp.zeros((1, width), WIDE)
        for i in range(2):
            at = slice(i * step, (i + 1) * step)
            part = dot_cols(grad_ref[at, :], w_ref[...])
            part_ref[at, :] = part
            low_ref[at, :] = part.astype(LOW)
            gain_grad = gain_grad + jnp.sum(part * normalise(x_ref[at, :].astype(WIDE))[0], axis=0, keepdims=True)
            bias_grad = bias_grad + jnp.sum(part, axis=0, keepdims=True)
        rows[...] = jnp.zeros_like(rows)
        rows[0:1, :], rows[1:2, :], rows[2:4, :] = gain_grad, bias_grad, two_ref[...]
        cols_ref[...] = dot_rows(rows[...].astype(LOW), eye(8, LANES)).astype(LOW)

    outs = [((tokens, width), WIDE), ((tokens, width), LOW), ((width, LANES), LOW)]
    scratch = [pltpu.VMEM((8, width), WIDE)]
    return run(kernel, outs, grad, qkv_w, x, norm_two, scalars=False, scratch=scratch)


def input_back(part, got, grad_resid, own_x, rows):
    group, width = own_x.shape

    def kernel(coords, part_ref, got_ref, resid_ref, x_ref, rows_ref, out_ref):
        at = pl.ds(pl.multiple_of(coords[3] * group, 16), group)
        normed, rate = normalise(x_ref[...].astype(WIDE))
        grad = part_ref[at, :] + got_ref[...].astype(WIDE)
        out_ref[...] = (resid_ref[at, :] + norm_back(normed, rate, grad, rows_ref[0:1, :])).astype(LOW)

    return run(kernel, [((group, width), LOW)], part, got, grad_resid, own_x, rows)[0]


def adam_update(weight, first, second, grad, rate, decay):
    first_new = BETA_ONE * first + (1.0 - BETA_ONE) * grad
    second_new = BETA_TWO * second + (1.0 - BETA_TWO) * grad * grad
    first_hat = first_new / (1.0 - BETA_ONE**STEP)
    second_hat = second_new / (1.0 - BETA_TWO**STEP)
    weight_new = weight - rate * (first_hat / (jnp.sqrt(second_hat) + ADAM_EPS) + decay * weight)
    return (weight_new, first_new, second_new)


def from_others(low, step):
    return [shift(low, step * k, wrap=False) for k in range(1, lax.axis_size("z"))]


def body(
    images,
    cotangent,
    qkv_weight,
    out_weight,
    up_weight,
    down_weight,
    norm_params,
    qkv_first,
    out_first,
    up_first,
    down_first,
    norm_first,
    qkv_second,
    out_second,
    up_second,
    down_second,
    norm_second,
):
    depth, core = lax.axis_size("z"), lax.axis_index("c")
    count, group, width = images.shape
    hidden_units = up_weight.shape[1]
    own_rows = qkv_weight.shape[0]
    own_units = down_weight.shape[0]
    chips = lax.axis_size("y") * lax.axis_size("x")
    block, ff_block = width // (2 * depth), hidden_units // (2 * depth)
    half_qkv, half_ff, half_d = 3 * width // 2, hidden_units // 2, width // 2
    ring = lax.axis_size("y") == 2 and lax.axis_size("x") == 2 and depth % 2 == 0 and own_rows % 32 == 0
    heads = half_d // HEAD_DIM
    tokens = 2 * group

    own_x, own_g = images.reshape(group, width), cotangent.reshape(group, width)
    split_qkv = lambda w: jnp.moveaxis(w.reshape(-1, 3 * depth, 2, block), 2, 0).reshape(2, -1, half_qkv)
    split_up = lambda w: jnp.moveaxis(w.reshape(-1, depth, 2, ff_block), 2, 0).reshape(2, -1, half_ff)

    thin, small = own_units // 2, own_rows // 2
    if ring:
        qkv_mine, qkv_give = cast_qkv(qkv_weight, norm_params, 3 * depth)
        up_mine, up_give, out_part, down_low = cast_rest(
            after(up_weight, qkv_give), out_weight, down_weight, depth
        )
        qkv_mate, x_mate, up_mate = swap(qkv_give, "c"), swap(own_x, "c"), swap(up_give, "c")
        inputs = join_rows(own_x, x_mate)
        up_part = join_rows(up_mine, up_mate, out_part)
        qkv_part = join_rows(qkv_mine, qkv_mate)
        qkv_part, up_part, inputs = lax.optimization_barrier((qkv_part, up_part, inputs))
        qkv_column = column_first(qkv_part)
        down_plane = plane_first(after(down_low, qkv_part))
        qkv_column = [after(part, down_plane) for part in qkv_column]
        up_column = column_first(after(up_part, *qkv_column))
        qkv_parts = plane_last(jnp.stack(qkv_column))
        g_mate = swap(after(own_g, *up_column), "c")
        down_parts = [down_plane, shift(after(down_plane, *up_column), 1)]

        def qkv_moves(zz, plane):
            row = lambda h: ((zz * 2 + h) * chips + plane) * own_rows
            moves = [(0, h * own_rows, 0, own_rows, half_qkv, row(h), 0) for h in (0, 1)]
            return moves + [(1, h * own_rows, half_qkv, own_rows, LANES, row(h), 0) for h in (0, 1)]

        def up_moves(zz, plane):
            row = lambda h: ((zz * 2 + h) * chips + plane) * own_rows
            moves = [(0, h * own_rows, 0, own_rows, half_ff, row(h), 0) for h in (0, 1)]
            to = zz * block + plane * own_rows
            return moves + [(1, h * own_rows, half_ff, own_rows, half_d, to, h * half_d) for h in (0, 1)]

        def down_moves(zz, plane):
            return [(0, 0, 0, own_units, width, zz * ff_block + plane * own_units, 0)]

        spots = column_first_spots(depth)
        qkv_w, norm_w = place(qkv_parts, depth, [(width, half_qkv), (width, LANES)], spots, qkv_moves)
    else:
        qkv_low, out_low = qkv_weight.astype(LOW), out_weight.astype(LOW)
        up_low, down_low = up_weight.astype(LOW), down_weight.astype(LOW)
        norm_low = norm_params.astype(LOW)
        x_mate, g_mate = swap(own_x, "c"), swap(own_g, "c")
        whole = lambda w, axis=0: lax.all_gather(w, ALL, axis=axis, tiled=True)
        qkv_w, up_w = mine(split_qkv(whole(qkv_low))), mine(split_up(whole(up_low)))
        rows_half = lambda w, b: mine(jnp.moveaxis(w.reshape(depth, 2, b, width), 1, 0)).reshape(-1, width)
        out_w, down_w = rows_half(whole(out_low), block), rows_half(whole(down_low), ff_block)
        norm_w = jnp.pad(whole(norm_low, 1).T, ((0, 0), (0, LANES - 4)))

        inputs = join_rows(own_x, x_mate)
    grad_out = join_rows(own_g, g_mate)
    halves = lambda a: a.reshape(2, group, -1)
    rows, normed_one, qk, query, key, value, state = project(inputs, norm_w, qkv_w)
    earlier = from_others(state, 1)
    mixed, mixed_low, denom, state_in = attend(query, key, value, earlier)
    if ring:
        up_parts = plane_last(after(jnp.stack(up_column), *qkv_parts[3:]), (mixed_low, down_parts[-1]))
        for _ in range(2, depth):
            down_parts.append(shift(down_parts[-1], 1))
        up_w, out_w = place(up_parts, depth, [(width, half_ff), (half_d, width)], spots, up_moves)
    out_part = dot(mixed_low, out_w)
    out_got = swap(out_part.astype(LOW), "c")
    resid, normed_two, activated, slope = feed(inputs, out_part, out_got, rows, up_w)
    down_grad = dot_rows(activated, grad_out).astype(LOW)
    if ring:
        def down_cuts(zz, plane, half):
            return [(0, zz * ff_block + plane * own_units + half * thin, 0, thin, width, 0, 0)]

        down_cut = unplace([down_grad], depth, (thin, width), down_cuts)
        down_hop = first_hop(*down_cut)
        spots = plane_first_spots(depth, own_units)
        down_parts[0] = after(down_parts[0], down_cut[0])
        (down_w,) = place(down_parts, depth, [(half_ff, width)], spots, down_moves)

    grad_hidden, two_part, two_low = feed_back(grad_out, down_w, slope, up_w)
    up_grad = dot_rows(normed_two, grad_hidden).astype(LOW)
    two_got = after(swap(after(two_low, *down_hop[1::2]) if ring else two_low, "c"), up_grad)
    grad_resid, grad_resid_low, a_low, b_rows, state_grad, norm_two = attend_turn(
        two_part, two_got, resid, rows, grad_out, out_w, mixed, denom, query
    )
    later = from_others(state_grad, -1)
    out_grad = dot_rows(mixed_low, grad_resid_low).astype(LOW)
    grad_projected = attend_back(query, key, value, qk, a_low, b_rows, state_in, later)
    qkv_grad = dot_rows(normed_one, grad_projected).astype(LOW)
    one_part, one_low, norm_cols = project_back(grad_projected, qkv_w, inputs, norm_two)
    input_grad = input_back(one_part, swap(other(halves(one_low)), "c"), grad_resid, own_x, rows)

    def finish_activations(*before):
        down_part = dot(after(activated, *before), down_w)
        down_give = other(halves(down_part)).astype(LOW)
        down_got = swap(down_give, "c").astype(WIDE)
        return (mine(halves(resid + down_part)) + down_got).astype(LOW), down_give

    out_fan = max(1, width * 64 // (tokens * depth))
    rates = (3.0 * width**-0.5, 3.0 * out_fan**-0.5, 3.0 * width**-0.5, 3.0 * hidden_units**-0.5, 1.5)
    decays = (WEIGHT_DECAY, WEIGHT_DECAY, WEIGHT_DECAY, WEIGHT_DECAY, 0.0)
    masters = (qkv_weight, out_weight, up_weight, down_weight, norm_params)
    firsts = (qkv_first, out_first, up_first, down_first, norm_first)
    seconds = (qkv_second, out_second, up_second, down_second, norm_second)
    if ring:

        def up_cuts(zz, plane, half):
            cuts = [(0, ((zz * 2 + half) * chips + plane) * own_rows, 0, own_rows, half_ff, 0, 0)]
            row = zz * block + plane * own_rows + half * small
            return cuts + [(1, row, p * half_d, small, half_d, p * small, half_ff) for p in (0, 1)]

        def qkv_cuts(zz, plane, half):
            row = ((zz * 2 + half) * chips + plane) * own_rows
            return [(0, row, 0, own_rows, half_qkv, 0, 0), (1, row, 0, own_rows, LANES, 0, half_qkv)]

        up_cut = unplace([up_grad, out_grad], depth, (own_rows, half_ff + half_d), up_cuts)
        down_sum, hop = later_hops(*down_hop, (), (grad_projected,))
        up_sum, hop = later_hops(*first_hop(*up_cut, (*hop, *later)), down_sum[1:])
        qkv_cut = unplace([qkv_grad, norm_cols], depth, (own_rows, half_qkv + LANES), qkv_cuts)
        activations, down_give = finish_activations(up_sum[0])
        qkv_sum, hop = later_hops(*first_hop(*qkv_cut, hop), (*up_sum[1:-1], down_give))
        down_red, squares = finish_down(down_sum)
        up_mine, up_give, out_red, squares = finish_up(up_sum, squares, own_rows, half_ff)
        up_mate = swap(up_give, "c")
        qkv_sum[0] = after(qkv_sum[0], input_grad, activations, up_mate)
        qkv_mine, qkv_give, small_mine = finish_qkv(qkv_sum, squares, own_rows, half_qkv)
        small_mate, qkv_mate = swap(small_mine, "c"), swap(qkv_give, "c")
        squares, norm_sum = chip_squares(small_mine, small_mate)
        norm_red = mine(norm_sum.reshape(2, own_rows, LANES))[:, :4].T
        grads = (qkv_mine, qkv_mate, out_red, up_mine, up_mate, down_red, norm_red)
        *news, grad_norm = update_all(
            grads, sum_chips(squares), masters, firsts, seconds, rates, decays, (3 * depth, depth)
        )
        return (
            activations.reshape(count, group, width),
            input_grad.reshape(count, group, width),
            grad_norm[0, 0],
            *news,
        )
    activations = finish_activations()[0]
    scatter = lambda g: lax.psum_scatter(g, ALL, scatter_dimension=0, tiled=True)
    both = lambda a, axis: jnp.stack([jnp.where(core == k, a, 0.0) for k in (0, 1)], axis)
    to_all = lambda a: a.astype(WIDE)
    qkv_red = scatter(both(to_all(qkv_grad).reshape(width, 3 * depth, block), 2).reshape(width, -1))
    up_red = scatter(both(to_all(up_grad).reshape(width, depth, ff_block), 2).reshape(width, -1))
    out_red = scatter(both(to_all(out_grad).reshape(depth, block, width), 1).reshape(width, width))
    down_red = scatter(both(to_all(down_grad).reshape(depth, ff_block, width), 1).reshape(hidden_units, width))
    norm_red = scatter(norm_cols.astype(WIDE))[:, :4].T

    reduced = (qkv_red, out_red, up_red, down_red, norm_red)
    local_squares = sum(jnp.sum(grad * grad) for grad in reduced)
    grad_norm = jnp.sqrt(lax.psum(local_squares, ALL))
    clip = jnp.minimum(1.0, CLIP_LIMIT / (grad_norm + 1e-06))
    news = [
        adam_update(masters[k], firsts[k], seconds[k], clip * reduced[k], rates[k], decays[k]) for k in range(5)
    ]
    return (
        activations.reshape(count, group, width),
        input_grad.reshape(count, group, width),
        grad_norm,
        *[new[0] for new in news],
        *[new[1] for new in news],
        *[new[2] for new in news],
    )


def solution(mesh):
    depth, planes = mesh.shape["seq"] // 2, mesh.shape["img"]
    across = max(k for k in range(1, planes + 1) if planes % k == 0 and k * k <= planes)
    grid = jax.sharding.Mesh(mesh.devices.reshape(depth, 2, planes // across, across), ALL)
    tokens = P(("y", "x"), ("z", "c"), None)
    matrix, norm = P(ALL, None), P(None, ALL)
    state = (matrix, matrix, matrix, matrix, norm)
    return jax.shard_map(
        body,
        mesh=grid,
        in_specs=(tokens, tokens) + state * 3,
        out_specs=(tokens, tokens, P()) + state * 3,
        check_vma=False,
    )
```

```python
import functools

import jax
import jax.numpy as jnp
from jax import lax
from jax.experimental import pallas as pl
from jax.experimental.pallas import tpu as pltpu
from jax.sharding import PartitionSpec as P

HEAD_DIM = 64
STEP = 10
NORM_EPS = 1e-05
BETA_ONE = 0.9
BETA_TWO = 0.999
ADAM_EPS = 1e-08
WEIGHT_DECAY = 0.1
CLIP_LIMIT = 1.0
LANES = 128

LOW = jnp.bfloat16
WIDE = jnp.float32
ALL = ("z", "c", "y", "x")
SWAP = [(0, 1), (1, 0)]


def swap(value, axis):
    return lax.ppermute(value, axis, SWAP)


def shift(value, step, wrap=True):
    size = lax.axis_size("z")
    pairs = [(i, (i + step) % size) for i in range(size) if wrap or 0 <= i + step < size]
    return lax.ppermute(value, "z", pairs)


def mine(pair_axis_first):
    return jnp.where(lax.axis_index("c") == 0, pair_axis_first[0], pair_axis_first[1])


def other(pair_axis_first):
    return jnp.where(lax.axis_index("c") == 0, pair_axis_first[1], pair_axis_first[0])


def in_order(own, mate, axis=0):
    first = lax.axis_index("c") == 0
    return jnp.concatenate([jnp.where(first, own, mate), jnp.where(first, mate, own)], axis)


def after(value, *before):
    return lax.optimization_barrier((*before, value))[-1]


def column_first(shard):
    return [shard] + [shift(shard, k) for k in range(1, lax.axis_size("z"))]


def plane_last(column, between=()):
    half = column.shape[0] // 2
    along_x, along_y = swap(column, "x"), swap(column, "y")
    along_x, along_y = after(along_x, *between), after(along_y, *between)
    far = (swap(along_y[:half], "x"), swap(along_x[half:], "y"))
    return (column, along_x, along_y) + far


def plane_first(shard):
    half = shard.shape[0] // 2
    along_x, along_y = swap(shard, "x"), swap(shard, "y")
    far_low, far_high = swap(along_y[:half], "x"), swap(along_x[half:], "y")
    return jnp.concatenate([shard, along_x, along_y, far_low, far_high])


def column_last(plane):
    parts = [plane]
    for _ in range(1, lax.axis_size("z")):
        parts.append(shift(parts[-1], 1))
    return parts


def column_first_spots(depth):
    half = depth // 2
    spots = [(0, (k,), 0, (k, 0, 0)) for k in range(depth)]
    spots += [(1, (k,), 0, (k, 0, 1)) for k in range(depth)]
    spots += [(2, (k,), 0, (k, 1, 0)) for k in range(depth)]
    spots += [(3, (k,), 0, (k, 1, 1)) for k in range(half)]
    return spots + [(4, (k - half,), 0, (k, 1, 1)) for k in range(half, depth)]


def plane_first_spots(depth, rows):
    return [(k, (), p * rows, (k, p // 2, p % 2)) for k in range(depth) for p in range(4)]


def first_hop(send_x, keep_x, send_y, keep_y, before=()):
    return keep_x, swap(after(send_x, *before), "x"), keep_y, swap(after(send_y, *before), "y")


def later_hops(keep_x, got_x, keep_y, got_y, between=(), last=()):
    depth, rows, cols = keep_x.shape[1:]

    def second_hop(kx, gx, ky, gy, to_y, to_x):
        to_y[...] = (kx[1].astype(WIDE) + gx[1].astype(WIDE)).astype(LOW)
        to_x[...] = (ky[1].astype(WIDE) + gy[1].astype(WIDE)).astype(LOW)

    outs = [((depth, rows, cols), LOW)] * 2
    to_y, to_x = run(second_hop, outs, keep_x, got_x, keep_y, got_y, scalars=False, deps=between)
    on_y, on_x = swap(to_y, "y"), swap(to_x, "x")
    hop = (on_x, on_y)

    def third_hop(kx, gx, ky, gy, ony, onx, own, *sends):
        for k in range(depth):
            one = kx[0, k].astype(WIDE) + gx[0, k].astype(WIDE) + ony[k].astype(WIDE)
            two = ky[0, k].astype(WIDE) + gy[0, k].astype(WIDE) + onx[k].astype(WIDE)
            out = sends[k - 1] if k else own
            out[:rows, :] = one.astype(out.dtype)
            out[rows:, :] = two.astype(out.dtype)

    outs = [((2 * rows, cols), WIDE if k == 0 else LOW) for k in range(depth)]
    own, *sends = run(third_hop, outs, keep_x, got_x, keep_y, got_y, on_y, on_x, scalars=False, deps=last)
    return [own] + [shift(part, k + 1) for k, part in enumerate(sends)], hop


def sum_of(refs):
    total = refs[0][...]
    for ref in refs[1:]:
        total = total + ref[...].astype(WIDE)
    return total


def spread(value):
    return jnp.broadcast_to(value, (8, LANES))


def total_squares(value):
    return jnp.sum(jnp.sum(value * value, axis=1, keepdims=True), axis=0, keepdims=True)


def finish_down(parts):
    def kernel(*refs):
        total = sum_of(refs[: len(parts)])
        refs[-2][...] = total
        refs[-1][...] = spread(total_squares(total))

    return run(kernel, [(parts[0].shape, WIDE), ((8, LANES), WIDE)], *parts, scalars=False)


def finish_up(parts, squares, rows, half_ff):
    half_d = parts[0].shape[1] - half_ff
    small = rows // 2

    def kernel(coords, squares_ref, *refs):
        own_ref, mate_ref, out_ref, total_ref, all_ref = refs[len(parts) :]
        total = sum_of(refs[: len(parts)])
        all_ref[...] = total
        core = coords[3]
        own_ref[...] = all_ref[pl.ds(pl.multiple_of(core * rows, 8), rows), :half_ff]
        mate_ref[...] = all_ref[pl.ds(pl.multiple_of((1 - core) * rows, 8), rows), :half_ff]
        for p in range(2):
            for h in range(2):
                block = total[h * rows + p * small : h * rows + (p + 1) * small, half_ff:]
                out_ref[h * small : (h + 1) * small, p * half_d : (p + 1) * half_d] = block
        total_ref[...] = squares_ref[...] + spread(total_squares(total))

    outs = [((rows, half_ff), WIDE)] * 2 + [((rows, 2 * half_d), WIDE), ((8, LANES), WIDE)]
    scratch = [pltpu.VMEM(parts[0].shape, WIDE)]
    return run(kernel, outs, squares, *parts, scratch=scratch)


def finish_qkv(parts, squares, rows, half_qkv, deps=()):
    def kernel(coords, squares_ref, *refs):
        own_ref, mate_ref, small_ref, all_ref = refs[len(parts) :]
        total = sum_of(refs[: len(parts)])
        all_ref[...] = total
        core = coords[3]
        own_ref[...] = all_ref[pl.ds(pl.multiple_of(core * rows, 8), rows), :half_qkv]
        mate_ref[...] = all_ref[pl.ds(pl.multiple_of((1 - core) * rows, 8), rows), :half_qkv]
        small_ref[: 2 * rows, :] = total[:, half_qkv:]
        small_ref[2 * rows :, :] = squares_ref[...] + spread(total_squares(total[:, :half_qkv]))

    outs = [((rows, half_qkv), WIDE)] * 2 + [((2 * rows + 8, LANES), WIDE)]
    scratch = [pltpu.VMEM(parts[0].shape, WIDE)]
    return run(kernel, outs, squares, *parts, scratch=scratch, deps=deps)


def chip_squares(small, got):
    rows = small.shape[0] - 8

    def kernel(small_ref, got_ref, total_ref, norm_ref):
        total = small_ref[...] + got_ref[...]
        norm_ref[...] = total[:rows]
        total_ref[...] = total[rows:] + spread(total_squares(total[:rows]))

    outs = [((8, LANES), WIDE), ((rows, LANES), WIDE)]
    return run(kernel, outs, small, got, scalars=False)


def sum_chips(value):
    across = lax.ppermute(value, ("y", "x"), [(i, 3 - i) for i in range(4)])
    value = value + swap(value, "y") + (swap(value, "x") + across)
    size, near = lax.axis_size("z"), 1
    while near < size // 2:
        value = value + lax.ppermute(value, "z", [(i, i ^ near) for i in range(size)])
        near *= 2
    return [value, lax.ppermute(value, "z", [(i, i ^ near) for i in range(size)])]


def interleave(first, own, mate, blocks):
    size = own.shape[1] // blocks
    pieces = []
    for j in range(blocks):
        at = slice(j * size, (j + 1) * size)
        pieces += [jnp.where(first, own[:, at], mate[:, at]), jnp.where(first, mate[:, at], own[:, at])]
    return jnp.concatenate(pieces, axis=1)


def update_all(grads, totals, masters, firsts, seconds, rates, decays, blocks):
    steps = 4
    n, m = len(grads), len(totals)

    def tile(array):
        rows, cols = array.shape
        return pl.BlockSpec((rows // steps, cols), lambda i: (i, 0))

    def whole(array):
        return pl.BlockSpec(array.shape, lambda i: (0, 0))

    def kernel(coords, *refs):
        first = coords[3] == 0
        g, t, old, new = refs[:n], refs[n : n + m], refs[n + m : n + m + 15], refs[n + m + 15 :]
        total = sum_of(t)[0:1, 0:1]
        norm = jnp.sqrt(total)
        clip = jnp.minimum(1.0, CLIP_LIMIT / (norm + 1e-06))
        qkv = interleave(first, g[0][...], g[1][...], blocks[0])
        up = interleave(first, g[3][...], g[4][...], blocks[1])
        for k, grad in enumerate((qkv, g[2][...], up, g[5][...], g[6][...])):
            news = adam_update(old[k][...], old[5 + k][...], old[10 + k][...], clip * grad, rates[k], decays[k])
            for part in range(3):
                new[5 * part + k][...] = news[part]
        new[15][...] = norm

    state = (*masters, *firsts, *seconds)
    specs = [whole(a) if k % 5 == 4 else tile(a) for k, a in enumerate(state)]
    norm_out = jax.ShapeDtypeStruct((1, 1), WIDE)
    return pl.pallas_call(
        kernel,
        grid=(steps,),
        out_shape=[jax.ShapeDtypeStruct(a.shape, WIDE) for a in state] + [norm_out],
        in_specs=[pl.BlockSpec(memory_space=pltpu.SMEM)]
        + [tile(a) for a in grads[:-1]]
        + [whole(grads[-1])]
        + [whole(a) for a in totals]
        + specs,
        out_specs=specs + [whole(norm_out)],
        compiler_params=FULL,
    )(coordinates(), *grads, *totals, *state)


def coordinates():
    return jnp.stack([lax.axis_index(name) for name in ("z", "y", "x", "c")]).astype(jnp.int32)


def chip_of(coords, rel, depth, back):
    dz, dy, dx = rel
    z, y, x = coords[0], coords[1], coords[2]
    zz = lax.rem(z + (depth - dz if back else dz), depth)
    yy = 1 - y if dy else y
    xx = 1 - x if dx else x
    return zz, yy * 2 + xx


def window(row, rows, col, cols):
    rows_at = pl.ds(row if isinstance(row, int) else pl.multiple_of(row, 16), rows)
    return rows_at, pl.ds(col, cols)


VMEM = pl.BlockSpec(memory_space=pltpu.VMEM)
ROOM_MB = 16
ROOM = pltpu.CompilerParams(vmem_limit_bytes=ROOM_MB * 1024 * 1024)
FULL = pltpu.CompilerParams(vmem_limit_bytes=56 * 1024 * 1024)


def place(parts, depth, outs, spots, moves, deps=()):
    def kernel(coords, *refs):
        ins, out_refs = refs[: len(parts)], refs[len(parts) + len(deps) :]
        for array, lead, base, rel in spots:
            zz, plane = chip_of(coords, rel, depth, True)
            for o, sr, sc, rows, cols, tr, tc in moves(zz, plane):
                out_refs[o][window(tr, rows, tc, cols)] = ins[array][(*lead, *window(base + sr, rows, sc, cols))]

    return pl.pallas_call(
        kernel,
        out_shape=[jax.ShapeDtypeStruct(s, LOW) for s in outs],
        in_specs=[pl.BlockSpec(memory_space=pltpu.SMEM)]
        + [VMEM] * len(parts)
        + [pl.BlockSpec(memory_space=pl.ANY)] * len(deps),
        out_specs=[VMEM] * len(outs),
        compiler_params=ROOM,
    )(coordinates(), *parts, *deps)


def unplace(grads, depth, rows_cols, moves):
    spots = []
    for dz in range(depth):
        for d in range(2):
            spots += [(0, d, dz, (dz, d, 1), 0), (1, d, dz, (dz, d, 0), 0)]
            spots += [(2, d, dz, (dz, 1, d), 1), (3, d, dz, (dz, 0, d), 1)]

    def kernel(coords, *refs):
        ins, out_refs = refs[: len(grads)], refs[len(grads) :]
        for array, d, dz, rel, half in spots:
            zz, plane = chip_of(coords, rel, depth, False)
            for i, sr, sc, rows, cols, tr, tc in moves(zz, plane, half):
                out_refs[array][(d, dz, *window(tr, rows, tc, cols))] = ins[i][window(sr, rows, sc, cols)]

    return pl.pallas_call(
        kernel,
        out_shape=[jax.ShapeDtypeStruct((2, depth) + rows_cols, LOW)] * 4,
        in_specs=[pl.BlockSpec(memory_space=pltpu.SMEM)] + [VMEM] * len(grads),
        out_specs=[VMEM] * 4,
        compiler_params=ROOM,
    )(coordinates(), *grads)


def cast_qkv(qkv, norm, halves):
    rows, cols = qkv.shape
    wide = cols // 2 + LANES
    block = cols // (2 * halves)

    def kernel(coords, qkv_ref, norm_ref, own_ref, mate_ref, tall):
        first = coords[3] == 0
        for j in range(halves):
            a = qkv_ref[:, 2 * j * block : (2 * j + 1) * block]
            b = qkv_ref[:, (2 * j + 1) * block : (2 * j + 2) * block]
            own_ref[:, j * block : (j + 1) * block] = jnp.where(first, a, b).astype(LOW)
            mate_ref[:, j * block : (j + 1) * block] = jnp.where(first, b, a).astype(LOW)
        tall[...] = jnp.zeros_like(tall)
        tall[0:4, :] = norm_ref[...].astype(LOW).astype(WIDE)
        i = lax.broadcasted_iota(jnp.int32, (rows, rows), 0)
        j = lax.broadcasted_iota(jnp.int32, (rows, rows), 1)
        columns = dot_cols((i == j).astype(LOW), tall[...].astype(LOW)).astype(LOW)
        own_ref[:, cols // 2 :] = columns
        mate_ref[:, cols // 2 :] = columns

    return pl.pallas_call(
        kernel,
        out_shape=[jax.ShapeDtypeStruct((rows, wide), LOW)] * 2,
        in_specs=[pl.BlockSpec(memory_space=pltpu.SMEM), VMEM, VMEM],
        out_specs=[VMEM] * 2,
        scratch_shapes=[pltpu.VMEM((LANES, rows), WIDE)],
        compiler_params=ROOM,
    )(coordinates(), qkv, norm)


def cast_rest(up, out, down, halves):
    rows, cols = up.shape
    block, width = cols // (2 * halves), out.shape[1]

    def kernel(coords, up_ref, out_ref, down_ref, own_ref, mate_ref, part_ref, low_ref):
        first = coords[3] == 0
        for j in range(halves):
            a = up_ref[:, 2 * j * block : (2 * j + 1) * block]
            b = up_ref[:, (2 * j + 1) * block : (2 * j + 2) * block]
            own_ref[:, j * block : (j + 1) * block] = jnp.where(first, a, b).astype(LOW)
            mate_ref[:, j * block : (j + 1) * block] = jnp.where(first, b, a).astype(LOW)
        part_ref[:rows, :] = out_ref[:, : width // 2].astype(LOW)
        part_ref[rows:, :] = out_ref[:, width // 2 :].astype(LOW)
        low_ref[...] = down_ref[...].astype(LOW)

    return pl.pallas_call(
        kernel,
        out_shape=[jax.ShapeDtypeStruct((rows, cols // 2), LOW)] * 2
        + [jax.ShapeDtypeStruct((2 * rows, width // 2), LOW), jax.ShapeDtypeStruct(down.shape, LOW)],
        in_specs=[pl.BlockSpec(memory_space=pltpu.SMEM), VMEM, VMEM, VMEM],
        out_specs=[VMEM] * 4,
        compiler_params=ROOM,
    )(coordinates(), up, out, down)


def join_rows(own, mate, side=None):
    rows, cols = own.shape
    wide = cols + (side.shape[1] if side is not None else 0)

    def kernel(coords, own_ref, mate_ref, *refs):
        out_ref = refs[-1]
        core = coords[3]
        out_ref[pl.ds(pl.multiple_of(core * rows, 16), rows), :cols] = own_ref[...]
        out_ref[pl.ds(pl.multiple_of((1 - core) * rows, 16), rows), :cols] = mate_ref[...]
        if side is not None:
            out_ref[:, cols:] = refs[0][...]

    ins = [own, mate] + ([side] if side is not None else [])
    return pl.pallas_call(
        kernel,
        out_shape=jax.ShapeDtypeStruct((2 * rows, wide), LOW),
        in_specs=[pl.BlockSpec(memory_space=pltpu.SMEM)] + [VMEM] * len(ins),
        out_specs=VMEM,
        compiler_params=ROOM,
    )(coordinates(), *ins)


def run(kernel, outs, *ins, scalars=True, scratch=(), flops=0, room=ROOM_MB, deps=()):
    first = len(ins) + scalars

    def body_of(*refs):
        return kernel(*refs[:first], *refs[first + len(deps) :])

    out_shape = [jax.ShapeDtypeStruct(shape, kind) for shape, kind in outs]
    return pl.pallas_call(
        body_of,
        out_shape=out_shape,
        in_specs=([pl.BlockSpec(memory_space=pltpu.SMEM)] if scalars else [])
        + [VMEM] * len(ins)
        + [pl.BlockSpec(memory_space=pl.ANY)] * len(deps),
        out_specs=[VMEM] * len(outs),
        scratch_shapes=list(scratch),
        compiler_params=pltpu.CompilerParams(vmem_limit_bytes=room * 1024 * 1024),
        cost_estimate=pl.CostEstimate(flops=flops, bytes_accessed=0, transcendentals=0),
    )(*([coordinates()] if scalars else []), *ins, *deps)


def dot(left, right):
    return jnp.dot(left, right, preferred_element_type=WIDE)


def dot_rows(left, right):
    return lax.dot_general(left, right, (((0,), (0,)), ((), ())), preferred_element_type=WIDE)


def dot_cols(left, right):
    return lax.dot_general(left, right, (((1,), (1,)), ((), ())), preferred_element_type=WIDE)


def eye(rows, cols):
    i = lax.broadcasted_iota(jnp.int32, (rows, cols), 0)
    return (i == lax.broadcasted_iota(jnp.int32, (rows, cols), 1)).astype(LOW)


def normalise(values):
    center = values - jnp.mean(values, axis=-1, keepdims=True)
    rate = lax.rsqrt(jnp.mean(center * center, axis=-1, keepdims=True) + NORM_EPS)
    return center * rate, rate


def norm_back(normed, rate, grad, gain):
    scaled = grad * gain
    shared = jnp.mean(scaled, axis=-1, keepdims=True)
    along = jnp.mean(scaled * normed, axis=-1, keepdims=True)
    return rate * (scaled - shared - normed * along)


def low_lanes(rows):
    return lax.broadcasted_iota(jnp.int32, (rows, LANES), 1) < HEAD_DIM


def by_head(pair):
    wide = pair.astype(WIDE)
    first = low_lanes(pair.shape[0])
    return jnp.where(first, wide, 0.0).astype(LOW), jnp.where(first, 0.0, wide).astype(LOW)


def pack_state(square):
    first = low_lanes(HEAD_DIM)
    return jnp.where(first, square[:HEAD_DIM], square[HEAD_DIM:])


def open_state(packed):
    first = low_lanes(HEAD_DIM)
    return jnp.concatenate([jnp.where(first, packed, 0.0), jnp.where(first, 0.0, packed)])


def feature(values):
    return jnp.where(values > 0.0, values + 1.0, jnp.exp(jnp.minimum(values, 0.0)))


def project(x, norm_w, qkv_w):
    tokens, width = x.shape
    half = qkv_w.shape[1] // 3
    pairs = half // LANES
    step = tokens // 2

    def kernel(x_ref, norm_ref, w_ref, rows_ref, normed_ref, qk_ref, q_ref, k_ref, v_ref, state_ref, sums):
        rows_ref[...] = dot_cols(eye(8, LANES), norm_ref[...])
        gain, bias = rows_ref[0:1, :], rows_ref[1:2, :]
        @pl.loop(0, 2)
        def _(i):
            at = at_block(i, step)
            normed = normalise(x_ref[at, :].astype(WIDE))[0]
            normed_ref[at, :] = (normed * gain + bias).astype(LOW)
            low = normed_ref[at, :]
            for j, out in enumerate((q_ref, k_ref)):
                part = dot(low, w_ref[:, j * half : (j + 1) * half])
                qk_ref[at, j * half : (j + 1) * half] = part
                out[at, :] = feature(part).astype(LOW)
            v_ref[at, :] = dot(low, w_ref[:, 2 * half :]).astype(LOW)
        total = dot_rows(jnp.ones((tokens, 8), LOW), k_ref[...])
        sums[...] = jnp.zeros_like(sums)
        for p in range(pairs):
            lanes = slice(p * LANES, (p + 1) * LANES)
            packed = pack_state(dot_rows(k_ref[:, lanes], v_ref[:, lanes]))
            state_ref[p * HEAD_DIM : (p + 1) * HEAD_DIM, :] = packed.astype(LOW)
            sums[p : p + 1, :] = total[0:1, lanes]
        state_ref[pairs * HEAD_DIM :, :] = sums[...].astype(LOW)

    outs = [((8, width), WIDE), ((tokens, width), LOW), ((tokens, 2 * half), WIDE)] + [((tokens, half), LOW)] * 3
    outs += [((pairs * HEAD_DIM + 16, LANES), LOW)]
    scratch = [pltpu.VMEM((16, LANES), WIDE)]
    return run(kernel, outs, x, norm_w, qkv_w, scalars=False, scratch=scratch)


def at_block(index, size):
    return pl.ds(pl.multiple_of(index * size, size), size)


def total_state(refs):
    total = refs[0][...].astype(WIDE)
    for ref in refs[1:]:
        total = total + ref[...].astype(WIDE)
    return total


def causal_mask(step):
    i = lax.broadcasted_iota(jnp.int32, (step, step), 0)
    return i >= lax.broadcasted_iota(jnp.int32, (step, step), 1)


def attend(query, key, value, parts, deps=()):
    tokens, half = query.shape
    pairs, step = half // LANES, tokens // 2

    def kernel(q_ref, k_ref, v_ref, *refs):
        mixed_ref, low_ref, denom_ref, state_ref, token_ref = refs[len(parts) :]
        token_ref[...] = jnp.zeros_like(token_ref)
        state_ref[...] = total_state(refs[: len(parts)])
        lower = causal_mask(step)
        first = low_lanes(step)
        top = low_lanes(HEAD_DIM)
        diagonal = eye(LANES, LANES).astype(WIDE)
        @pl.loop(0, pairs)
        def _(p):
            lanes = at_block(p, LANES)
            packed = state_ref[at_block(p, HEAD_DIM), :]
            sums = state_ref[pl.ds(pairs * HEAD_DIM + p, 1), :]
            column = jnp.sum(diagonal * sums, axis=1, keepdims=True)
            zero = jnp.zeros((HEAD_DIM, LANES), WIDE)
            ext = (
                jnp.concatenate([jnp.where(top, packed, column[:HEAD_DIM]), zero]).astype(LOW),
                jnp.concatenate([zero, jnp.where(top, column[HEAD_DIM:], packed)]).astype(LOW),
            )
            wide = v_ref[:, lanes].astype(WIDE)
            full = low_lanes(tokens)
            value_ext = (jnp.where(full, wide, 1.0).astype(LOW), jnp.where(full, 1.0, wide).astype(LOW))
            queries = by_head(q_ref[:, lanes])
            for i in range(2):
                at = slice(i * step, (i + 1) * step)
                got = []
                for h in range(2):
                    rows = queries[h][at]
                    total = dot(rows, ext[h])
                    for j in range(i + 1):
                        to = slice(j * step, (j + 1) * step)
                        scores = dot_cols(rows, k_ref[to, lanes])
                        if j == i:
                            scores = jnp.where(lower, scores, 0.0)
                        total = total + dot(scores.astype(LOW), value_ext[h][to])
                    got.append(total)
                denom = pltpu.roll(jnp.where(first, got[1], got[0]), HEAD_DIM, 1)
                mixed = jnp.where(first, got[0], got[1]) / denom
                mixed_ref[at, lanes] = mixed
                low_ref[at, lanes] = mixed.astype(LOW)
                denom_ref[at, lanes] = denom

    outs = [((tokens, half), WIDE), ((tokens, half), LOW), ((tokens, half), WIDE), (parts[0].shape, WIDE)]
    outs += [((8, LANES), WIDE)]
    return run(kernel, outs, query, key, value, *parts, scalars=False, deps=deps)


def out_project(mixed, out_w):
    def kernel(mixed_ref, w_ref, part_ref, low_ref):
        part = dot(mixed_ref[...], w_ref[...])
        part_ref[...] = part
        low_ref[...] = part.astype(LOW)

    shape = (mixed.shape[0], out_w.shape[1])
    return run(kernel, [(shape, WIDE), (shape, LOW)], mixed, out_w, scalars=False)


def feed(x, part, got, rows, up_w):
    tokens, width = x.shape
    units, step, cut = up_w.shape[1], tokens // 2, 512

    def kernel(x_ref, part_ref, got_ref, rows_ref, w_ref, resid_ref, normed_ref, act_ref, slope_ref):
        @pl.loop(0, 2)
        def _(i):
            at = at_block(i, step)
            resid = x_ref[at, :].astype(WIDE) + part_ref[at, :] + got_ref[at, :].astype(WIDE)
            resid_ref[at, :] = resid
            normed_ref[at, :] = (normalise(resid)[0] * rows_ref[2:3, :] + rows_ref[3:4, :]).astype(LOW)

        @pl.loop(0, units // cut)
        def _(j):
            to = at_block(j, cut)
            v = dot(normed_ref[...], w_ref[:, to])
            root = (2.0 / 3.141592653589793) ** 0.5
            square = v * v
            bend = jnp.tanh(root * v * (1.0 + 0.044715 * square))
            cdf = 0.5 * (1.0 + bend)
            act_ref[:, to] = (v * cdf).astype(LOW)
            slope_ref[:, to] = cdf + 0.5 * v * (1.0 - bend * bend) * (root * (1.0 + 3.0 * 0.044715 * square))

    outs = [((tokens, width), WIDE), ((tokens, width), LOW), ((tokens, units), LOW), ((tokens, units), WIDE)]
    return run(kernel, outs, x, part, got, rows, up_w, scalars=False)


def feed_back(grad_out, down_w, slope, up_w):
    tokens, width = grad_out.shape
    units, cut = up_w.shape[1], 512

    def kernel(g_ref, down_ref, slope_ref, up_ref, hidden_ref, part_ref, low_ref):
        @pl.loop(0, units // cut)
        def _(j):
            to = at_block(j, cut)
            hidden_ref[:, to] = (dot_cols(g_ref[...], down_ref[to, :]) * slope_ref[:, to]).astype(LOW)

        @pl.loop(0, width // cut)
        def _(j):
            to = at_block(j, cut)
            part = dot_cols(hidden_ref[...], up_ref[to, :])
            part_ref[:, to] = part
            low_ref[:, to] = part.astype(LOW)

    outs = [((tokens, units), LOW), ((tokens, width), WIDE), ((tokens, width), LOW)]
    return run(kernel, outs, grad_out, down_w, slope, up_w, scalars=False)


def down_project(activated, down_w, resid, deps):
    tokens, width = resid.shape
    group, cut = tokens // 2, width // 2

    def kernel(coords, act_ref, w_ref, resid_ref, own_ref, give_ref):
        own = pl.ds(pl.multiple_of(coords[3] * group, 16), group)
        mate = pl.ds(pl.multiple_of((1 - coords[3]) * group, 16), group)

        @pl.loop(0, 2)
        def _(j):
            to = at_block(j, cut)
            own_ref[:, to] = resid_ref[own, to] + dot(act_ref[own, :], w_ref[:, to])
            give_ref[:, to] = dot(act_ref[mate, :], w_ref[:, to]).astype(LOW)

    outs = [((group, width), WIDE), ((group, width), LOW)]
    return run(kernel, outs, activated, down_w, resid, deps=deps)


def weight_grad(rows, grad, deps=()):
    tokens, width = rows.shape
    units, cut = grad.shape[1], 512

    def kernel(rows_ref, grad_ref, out_ref):
        @pl.loop(0, units // cut)
        def _(j):
            to = at_block(j, cut)
            out_ref[:, to] = dot_rows(rows_ref[...], grad_ref[:, to]).astype(LOW)

    return run(kernel, [((width, units), LOW)], rows, grad, scalars=False, deps=deps)[0]


def attend_turn(part, got, resid, rows, grad_out, out_w, mixed, denom, query):
    tokens, width = resid.shape
    half = mixed.shape[1]
    pairs, step = half // LANES, tokens // 2

    def kernel(
        part_ref, got_ref, resid_ref, rows_ref, g_ref, w_ref, mixed_ref, denom_ref, q_ref,
        grad_ref, low_ref, a_ref, b_ref, state_ref, norm_ref, sums,
    ):
        gain = rows_ref[2:3, :]
        first = low_lanes(step)
        norm_ref[...] = jnp.zeros_like(norm_ref)

        @pl.loop(0, 2)
        def _(i):
            at = at_block(i, step)
            normed, rate = normalise(resid_ref[at, :])
            own = part_ref[at, :]
            norm_ref[0:1, :] += jnp.sum(own * normed, axis=0, keepdims=True)
            norm_ref[1:2, :] += jnp.sum(own, axis=0, keepdims=True)
            grad = g_ref[at, :].astype(WIDE) + norm_back(normed, rate, own + got_ref[at, :].astype(WIDE), gain)
            grad_ref[at, :] = grad
            low_ref[at, :] = grad.astype(LOW)
            turned = dot_cols(low_ref[at, :], w_ref[...]) / denom_ref[at, :]
            a_ref[at, :] = turned.astype(LOW)
            along = turned * mixed_ref[at, :]
            for p in range(pairs):
                lanes = slice(p * LANES, (p + 1) * LANES)
                piece = along[:, lanes]
                low = jnp.sum(jnp.where(first, piece, 0.0), axis=1, keepdims=True)
                high = jnp.sum(jnp.where(first, 0.0, piece), axis=1, keepdims=True)
                b_ref[at, lanes] = -jnp.where(first, low, high)
        sums[...] = jnp.zeros_like(sums)
        for p in range(pairs):
            lanes = slice(p * LANES, (p + 1) * LANES)
            packed = pack_state(dot_rows(q_ref[:, lanes], a_ref[:, lanes]))
            state_ref[p * HEAD_DIM : (p + 1) * HEAD_DIM, :] = packed.astype(LOW)
            sums[p : p + 1, :] = jnp.sum(q_ref[:, lanes].astype(WIDE) * b_ref[:, lanes], axis=0, keepdims=True)
        state_ref[pairs * HEAD_DIM :, :] = sums[...].astype(LOW)

    outs = [((tokens, width), WIDE), ((tokens, width), LOW), ((tokens, half), LOW), ((tokens, half), WIDE)]
    outs += [((pairs * HEAD_DIM + 16, LANES), LOW), ((2, width), WIDE)]
    ins = (part, got, resid, rows, grad_out, out_w, mixed, denom, query)
    scratch = [pltpu.VMEM((16, LANES), WIDE)]
    return run(kernel, outs, *ins, scalars=False, scratch=scratch)


def attend_back(query, key, value, qk, a_low, b_rows, state, parts, deps=()):
    tokens, half = query.shape
    pairs, step = half // LANES, tokens // 2

    def kernel(q_ref, k_ref, v_ref, qk_ref, a_ref, b_ref, state_ref, *refs):
        out_ref, later = refs[len(parts) :]
        later[...] = total_state(refs[: len(parts)])
        lower = causal_mask(step)
        @pl.loop(0, pairs)
        def _(p):
            lanes, rows = at_block(p, LANES), at_block(p, HEAD_DIM)
            sums = pl.ds(pairs * HEAD_DIM + p, 1)
            before, after_it = open_state(state_ref[rows, :]).astype(LOW), open_state(later[rows, :]).astype(LOW)
            queries, keys, pulls = by_head(q_ref[:, lanes]), by_head(k_ref[:, lanes]), by_head(a_ref[:, lanes])
            cuts = [slice(i * step, (i + 1) * step) for i in range(2)]
            grad_q = [dot_cols(a_ref[c, lanes], before) + b_ref[c, lanes] * state_ref[sums, :] for c in cuts]
            grad_k = [dot_cols(v_ref[c, lanes], after_it) + later[sums, :] for c in cuts]
            shifts = b_ref[:, lanes]
            grad_v = [dot(k_ref[c, lanes], after_it) for c in cuts]
            for i in range(2):
                for j in range(i + 1):
                    for h in range(2):
                        q, a = queries[h][cuts[i]], pulls[h][cuts[i]]
                        b = shifts[cuts[i], h * HEAD_DIM : h * HEAD_DIM + 1]
                        scores = dot_cols(q, k_ref[cuts[j], lanes])
                        pull = dot_cols(a, v_ref[cuts[j], lanes]) + b
                        if j == i:
                            scores, pull = jnp.where(lower, scores, 0.0), jnp.where(lower, pull, 0.0)
                        scores, pull = scores.astype(LOW), pull.astype(LOW)
                        grad_q[i] = grad_q[i] + dot(pull, keys[h][cuts[j]])
                        grad_k[j] = grad_k[j] + dot_rows(pull, q)
                        grad_v[j] = grad_v[j] + dot_rows(scores, a)
            for i, c in enumerate(cuts):
                for n, grad in enumerate((grad_q[i], grad_k[i])):
                    at = at_block(n * pairs + p, LANES)
                    raw = qk_ref[c, at]
                    out_ref[c, at] = (grad * jnp.where(raw > 0.0, 1.0, jnp.exp(jnp.minimum(raw, 0.0)))).astype(LOW)
                out_ref[c, at_block(2 * pairs + p, LANES)] = grad_v[i].astype(LOW)

    ins = (query, key, value, qk, a_low, b_rows, state, *parts)
    scratch = [pltpu.VMEM(parts[0].shape, WIDE)]
    return run(kernel, [((tokens, 3 * half), LOW)], *ins, scalars=False, scratch=scratch, deps=deps)[0]


def project_back(grad, qkv_w, x, norm_two):
    tokens, width = x.shape
    step = tokens // 2

    def kernel(grad_ref, w_ref, x_ref, two_ref, part_ref, low_ref, cols_ref, rows):
        rows[...] = jnp.zeros_like(rows)

        @pl.loop(0, 2)
        def _(i):
            at = at_block(i, step)
            part = dot_cols(grad_ref[at, :], w_ref[...])
            part_ref[at, :] = part
            low_ref[at, :] = part.astype(LOW)
            rows[0:1, :] += jnp.sum(part * normalise(x_ref[at, :].astype(WIDE))[0], axis=0, keepdims=True)
            rows[1:2, :] += jnp.sum(part, axis=0, keepdims=True)

        rows[2:4, :] = two_ref[...]
        cols_ref[...] = dot_rows(rows[...].astype(LOW), eye(8, LANES)).astype(LOW)

    outs = [((tokens, width), WIDE), ((tokens, width), LOW), ((width, LANES), LOW)]
    scratch = [pltpu.VMEM((8, width), WIDE)]
    return run(kernel, outs, grad, qkv_w, x, norm_two, scalars=False, scratch=scratch)


def input_back(part, got, grad_resid, own_x, rows):
    group, width = own_x.shape

    def kernel(coords, part_ref, got_ref, resid_ref, x_ref, rows_ref, out_ref):
        at = pl.ds(pl.multiple_of(coords[3] * group, 16), group)
        normed, rate = normalise(x_ref[...].astype(WIDE))
        grad = part_ref[at, :] + got_ref[...].astype(WIDE)
        out_ref[...] = (resid_ref[at, :] + norm_back(normed, rate, grad, rows_ref[0:1, :])).astype(LOW)

    return run(kernel, [((group, width), LOW)], part, got, grad_resid, own_x, rows)[0]


def adam_update(weight, first, second, grad, rate, decay):
    first_new = BETA_ONE * first + (1.0 - BETA_ONE) * grad
    second_new = BETA_TWO * second + (1.0 - BETA_TWO) * grad * grad
    first_hat = first_new / (1.0 - BETA_ONE**STEP)
    second_hat = second_new / (1.0 - BETA_TWO**STEP)
    weight_new = weight - rate * (first_hat / (jnp.sqrt(second_hat) + ADAM_EPS) + decay * weight)
    return (weight_new, first_new, second_new)


def from_others(low, step):
    if lax.axis_size("z") == 4:
        near = shift(low, step, wrap=False)
        pair = (low.astype(WIDE) + near.astype(WIDE)).astype(LOW)
        return [near, shift(pair, 2 * step, wrap=False)]
    return [shift(low, step * k, wrap=False) for k in range(1, lax.axis_size("z"))]


def body(
    images,
    cotangent,
    qkv_weight,
    out_weight,
    up_weight,
    down_weight,
    norm_params,
    qkv_first,
    out_first,
    up_first,
    down_first,
    norm_first,
    qkv_second,
    out_second,
    up_second,
    down_second,
    norm_second,
):
    depth, core = lax.axis_size("z"), lax.axis_index("c")
    count, group, width = images.shape
    hidden_units = up_weight.shape[1]
    own_rows = qkv_weight.shape[0]
    own_units = down_weight.shape[0]
    chips = lax.axis_size("y") * lax.axis_size("x")
    block, ff_block = width // (2 * depth), hidden_units // (2 * depth)
    half_qkv, half_ff, half_d = 3 * width // 2, hidden_units // 2, width // 2
    ring = lax.axis_size("y") == 2 and lax.axis_size("x") == 2 and depth == 4 and own_rows % 32 == 0
    heads = half_d // HEAD_DIM
    tokens = 2 * group

    own_x, own_g = images.reshape(group, width), cotangent.reshape(group, width)
    split_qkv = lambda w: jnp.moveaxis(w.reshape(-1, 3 * depth, 2, block), 2, 0).reshape(2, -1, half_qkv)
    split_up = lambda w: jnp.moveaxis(w.reshape(-1, depth, 2, ff_block), 2, 0).reshape(2, -1, half_ff)

    thin, small = own_units // 2, own_rows // 2
    if ring:
        qkv_mine, qkv_give = cast_qkv(qkv_weight, norm_params, 3 * depth)
        qkv_part = join_rows(qkv_mine, swap(qkv_give, "c"))
        up_mine, up_give, out_part, down_low = cast_rest(
            after(up_weight, qkv_part), out_weight, down_weight, depth
        )
        inputs = join_rows(own_x, swap(own_x, "c"))
        up_part = join_rows(up_mine, swap(up_give, "c"), out_part)
        qkv_column = column_first(qkv_part)
        down_plane = plane_first(after(down_low, qkv_part))
        qkv_column = [after(part, down_plane, up_part, inputs) for part in qkv_column]
        up_column = column_first(after(up_part, *qkv_column))
        qkv_parts = plane_last(jnp.stack(qkv_column))
        g_mate = swap(after(own_g, *up_column), "c")
        down_parts = [down_plane, shift(after(down_plane, *up_column), 1)]

        def qkv_moves(zz, plane):
            row = lambda h: ((zz * 2 + h) * chips + plane) * own_rows
            moves = [(0, h * own_rows, 0, own_rows, half_qkv, row(h), 0) for h in (0, 1)]
            return moves + [(1, h * own_rows, half_qkv, own_rows, LANES, row(h), 0) for h in (0, 1)]

        def up_moves(zz, plane):
            row = lambda h: ((zz * 2 + h) * chips + plane) * own_rows
            moves = [(0, h * own_rows, 0, own_rows, half_ff, row(h), 0) for h in (0, 1)]
            to = zz * block + plane * own_rows
            return moves + [(1, h * own_rows, half_ff, own_rows, half_d, to, h * half_d) for h in (0, 1)]

        def down_moves(zz, plane):
            return [(0, 0, 0, own_units, width, zz * ff_block + plane * own_units, 0)]

        spots = column_first_spots(depth)
        qkv_w, norm_w = place(qkv_parts, depth, [(width, half_qkv), (width, LANES)], spots, qkv_moves)
    else:
        qkv_low, out_low = qkv_weight.astype(LOW), out_weight.astype(LOW)
        up_low, down_low = up_weight.astype(LOW), down_weight.astype(LOW)
        norm_low = norm_params.astype(LOW)
        x_mate, g_mate = swap(own_x, "c"), swap(own_g, "c")
        whole = lambda w, axis=0: lax.all_gather(w, ALL, axis=axis, tiled=True)
        qkv_w, up_w = mine(split_qkv(whole(qkv_low))), mine(split_up(whole(up_low)))
        rows_half = lambda w, b: mine(jnp.moveaxis(w.reshape(depth, 2, b, width), 1, 0)).reshape(-1, width)
        out_w, down_w = rows_half(whole(out_low), block), rows_half(whole(down_low), ff_block)
        norm_w = jnp.pad(whole(norm_low, 1).T, ((0, 0), (0, LANES - 4)))

        inputs = join_rows(own_x, x_mate)
    grad_out = join_rows(own_g, g_mate)
    halves = lambda a: a.reshape(2, group, -1)
    rows, normed_one, qk, query, key, value, state = project(inputs, norm_w, qkv_w)
    earlier = from_others(state, 1)
    mixed, mixed_low, denom, state_in, attended = attend(query, key, value, earlier, (grad_out,))
    if ring:
        up_parts = plane_last(after(jnp.stack(up_column), *qkv_parts[3:]), tuple(earlier))
        down_parts.append(shift(after(down_parts[-1], *earlier), 1))
        for _ in range(3, depth):
            down_parts.append(shift(down_parts[-1], 1))
        up_w, out_w = place(
            up_parts, depth, [(width, half_ff), (half_d, width)], spots, up_moves, down_parts[2:3]
        )
    out_part, out_low = out_project(mixed_low, out_w)
    out_got = swap(out_low, "c")
    resid, normed_two, activated, slope = feed(inputs, out_part, out_got, rows, up_w)
    down_grad = dot_rows(activated, grad_out).astype(LOW)
    if ring:
        def down_cuts(zz, plane, half):
            return [(0, zz * ff_block + plane * own_units + half * thin, 0, thin, width, 0, 0)]

        down_cut = unplace([down_grad], depth, (thin, width), down_cuts)
        down_hop = first_hop(*down_cut)
        spots = plane_first_spots(depth, own_units)
        (down_w,) = place(down_parts, depth, [(half_ff, width)], spots, down_moves, (down_cut[0],))

    grad_hidden, two_part, two_low = feed_back(grad_out, down_w, slope, up_w)
    down_own, down_give = down_project(activated, down_w, resid, (two_low,))
    down_got = swap(down_give, "c")
    activations = (down_own + down_got.astype(WIDE)).astype(LOW)
    up_grad = weight_grad(normed_two, grad_hidden, down_hop[1::2] if ring else ())
    two_got = after(swap(two_low, "c"), up_grad)
    grad_resid, grad_resid_low, a_low, b_rows, state_grad, norm_two = attend_turn(
        two_part, two_got, resid, rows, grad_out, out_w, mixed, denom, query
    )
    later = from_others(state_grad, -1)
    out_grad = dot_rows(mixed_low, grad_resid_low).astype(LOW)
    deps = ()
    if ring:

        def up_cuts(zz, plane, half):
            cuts = [(0, ((zz * 2 + half) * chips + plane) * own_rows, 0, own_rows, half_ff, 0, 0)]
            row = zz * block + plane * own_rows + half * small
            return cuts + [(1, row, p * half_d, small, half_d, p * small, half_ff) for p in (0, 1)]

        up_cut = unplace([up_grad, out_grad], depth, (own_rows, half_ff + half_d), up_cuts)
        deps = (up_cut[0],)
    grad_projected = attend_back(query, key, value, qk, a_low, b_rows, state_in, later, deps)
    qkv_grad = dot_rows(normed_one, grad_projected).astype(LOW)
    one_part, one_low, norm_cols = project_back(grad_projected, qkv_w, inputs, norm_two)
    input_grad = input_back(one_part, swap(other(halves(one_low)), "c"), grad_resid, own_x, rows)

    out_fan = max(1, width * 64 // (tokens * depth))
    rates = (3.0 * width**-0.5, 3.0 * out_fan**-0.5, 3.0 * width**-0.5, 3.0 * hidden_units**-0.5, 1.5)
    decays = (WEIGHT_DECAY, WEIGHT_DECAY, WEIGHT_DECAY, WEIGHT_DECAY, 0.0)
    masters = (qkv_weight, out_weight, up_weight, down_weight, norm_params)
    firsts = (qkv_first, out_first, up_first, down_first, norm_first)
    seconds = (qkv_second, out_second, up_second, down_second, norm_second)
    if ring:

        def qkv_cuts(zz, plane, half):
            row = ((zz * 2 + half) * chips + plane) * own_rows
            return [(0, row, 0, own_rows, half_qkv, 0, 0), (1, row, 0, own_rows, LANES, 0, half_qkv)]

        down_sum, hop = later_hops(*down_hop)
        up_sum, hop = later_hops(*first_hop(*up_cut, (*hop, *later)), (*down_sum[1:], grad_projected))
        qkv_cut = unplace([qkv_grad, norm_cols], depth, (own_rows, half_qkv + LANES), qkv_cuts)
        qkv_sum, hop = later_hops(*first_hop(*qkv_cut, hop), (), up_sum[1:])
        down_red, squares = finish_down(down_sum)
        up_mine, up_give, out_red, squares = finish_up(up_sum, squares, own_rows, half_ff)
        up_mate = swap(up_give, "c")
        deps = (input_grad, activations, up_mate)
        qkv_mine, qkv_give, small_mine = finish_qkv(qkv_sum, squares, own_rows, half_qkv, deps)
        small_mate, qkv_mate = swap(small_mine, "c"), swap(qkv_give, "c")
        squares, norm_sum = chip_squares(small_mine, small_mate)
        norm_red = mine(norm_sum.reshape(2, own_rows, LANES))[:, :4].T
        grads = (qkv_mine, qkv_mate, out_red, up_mine, up_mate, down_red, norm_red)
        *news, grad_norm = update_all(
            grads, sum_chips(squares), masters, firsts, seconds, rates, decays, (3 * depth, depth)
        )
        return (
            activations.reshape(count, group, width),
            input_grad.reshape(count, group, width),
            grad_norm.reshape(()),
            *news,
        )
    scatter = lambda g: lax.psum_scatter(g, ALL, scatter_dimension=0, tiled=True)
    both = lambda a, axis: jnp.stack([jnp.where(core == k, a, 0.0) for k in (0, 1)], axis)
    to_all = lambda a: a.astype(WIDE)
    qkv_red = scatter(both(to_all(qkv_grad).reshape(width, 3 * depth, block), 2).reshape(width, -1))
    up_red = scatter(both(to_all(up_grad).reshape(width, depth, ff_block), 2).reshape(width, -1))
    out_red = scatter(both(to_all(out_grad).reshape(depth, block, width), 1).reshape(width, width))
    down_red = scatter(both(to_all(down_grad).reshape(depth, ff_block, width), 1).reshape(hidden_units, width))
    norm_red = scatter(norm_cols.astype(WIDE))[:, :4].T

    reduced = (qkv_red, out_red, up_red, down_red, norm_red)
    local_squares = sum(jnp.sum(grad * grad) for grad in reduced)
    grad_norm = jnp.sqrt(lax.psum(local_squares, ALL))
    clip = jnp.minimum(1.0, CLIP_LIMIT / (grad_norm + 1e-06))
    news = [
        adam_update(masters[k], firsts[k], seconds[k], clip * reduced[k], rates[k], decays[k]) for k in range(5)
    ]
    return (
        activations.reshape(count, group, width),
        input_grad.reshape(count, group, width),
        grad_norm,
        *[new[0] for new in news],
        *[new[1] for new in news],
        *[new[2] for new in news],
    )


def solution(mesh):
    depth, planes = mesh.shape["seq"] // 2, mesh.shape["img"]
    across = max(k for k in range(1, planes + 1) if planes % k == 0 and k * k <= planes)
    grid = jax.sharding.Mesh(mesh.devices.reshape(depth, 2, planes // across, across), ALL)
    tokens = P(("y", "x"), ("z", "c"), None)
    matrix, norm = P(ALL, None), P(None, ALL)
    state = (matrix, matrix, matrix, matrix, norm)
    return jax.shard_map(
        body,
        mesh=grid,
        in_specs=(tokens, tokens) + state * 3,
        out_specs=(tokens, tokens, P()) + state * 3,
        check_vma=False,
    )
```

```python
import functools

import jax
import jax.numpy as jnp
from jax import lax
from jax.experimental import pallas as pl
from jax.experimental.pallas import tpu as pltpu
from jax.sharding import PartitionSpec as P

HEAD_DIM = 64
STEP = 10
NORM_EPS = 1e-05
BETA_ONE = 0.9
BETA_TWO = 0.999
ADAM_EPS = 1e-08
WEIGHT_DECAY = 0.1
CLIP_LIMIT = 1.0
LANES = 128

LOW = jnp.bfloat16
WIDE = jnp.float32
ALL = ("z", "c", "y", "x")
SWAP = [(0, 1), (1, 0)]


def swap(value, axis):
    return lax.ppermute(value, axis, SWAP)


def shift(value, step, wrap=True):
    size = lax.axis_size("z")
    pairs = [(i, (i + step) % size) for i in range(size) if wrap or 0 <= i + step < size]
    return lax.ppermute(value, "z", pairs)


def mine(pair_axis_first):
    return jnp.where(lax.axis_index("c") == 0, pair_axis_first[0], pair_axis_first[1])


def other(pair_axis_first):
    return jnp.where(lax.axis_index("c") == 0, pair_axis_first[1], pair_axis_first[0])


def in_order(own, mate, axis=0):
    first = lax.axis_index("c") == 0
    return jnp.concatenate([jnp.where(first, own, mate), jnp.where(first, mate, own)], axis)


def after(value, *before):
    return lax.optimization_barrier((*before, value))[-1]


def column_first(shard):
    return [shard] + [shift(shard, k) for k in range(1, lax.axis_size("z"))]


def plane_last(column, between=()):
    half = column.shape[0] // 2
    along_x, along_y = swap(column, "x"), swap(column, "y")
    along_x, along_y = after(along_x, *between), after(along_y, *between)
    far = (swap(along_y[:half], "x"), swap(along_x[half:], "y"))
    return (column, along_x, along_y) + far


def plane_first(shard):
    far = lax.ppermute(shard, ("y", "x"), [(i, 3 - i) for i in range(4)])
    return jnp.concatenate([shard, swap(shard, "x"), swap(shard, "y"), far])


def column_last(plane):
    parts = [plane]
    for _ in range(1, lax.axis_size("z")):
        parts.append(shift(parts[-1], 1))
    return parts


def column_first_spots(depth):
    half = depth // 2
    spots = [(0, (k,), 0, (k, 0, 0), 0) for k in range(depth)]
    spots += [(1, (k,), 0, (k, 0, 1), 0) for k in range(depth)]
    spots += [(2, (k,), 0, (k, 1, 0), 0) for k in range(depth)]
    spots += [(3, (k,), 0, (k, 1, 1), 0) for k in range(half)]
    return spots + [(4, (k - half,), 0, (k, 1, 1), 0) for k in range(half, depth)]


def plane_first_spots(depth, rows, base):
    return [(base + k, (), p * rows, (k, p // 2, p % 2), 1) for k in range(depth) for p in range(4)]


def first_hop(send_x, keep_x, send_y, keep_y, before=()):
    return keep_x, swap(after(send_x, *before), "x"), keep_y, swap(after(send_y, *before), "y")


def second_hop_of(keep_x, got_x, keep_y, got_y, deps=()):
    depth, rows, cols = keep_x.shape[1:]

    def second_hop(kx, gx, ky, gy, to_y, to_x):
        to_y[...] = (kx[1].astype(WIDE) + gx[1].astype(WIDE)).astype(LOW)
        to_x[...] = (ky[1].astype(WIDE) + gy[1].astype(WIDE)).astype(LOW)

    outs = [((depth, rows, cols), LOW)] * 2
    return run(second_hop, outs, keep_x, got_x, keep_y, got_y, scalars=False, deps=deps)


def third_hop_of(keep_x, got_x, keep_y, got_y, on_y, on_x, deps=()):
    depth, rows, cols = keep_x.shape[1:]

    def third_hop(kx, gx, ky, gy, ony, onx, own, *sends):
        for k in range(depth):
            one = kx[0, k].astype(WIDE) + gx[0, k].astype(WIDE) + ony[k].astype(WIDE)
            two = ky[0, k].astype(WIDE) + gy[0, k].astype(WIDE) + onx[k].astype(WIDE)
            out = sends[k - 1] if k else own
            out[:rows, :] = one.astype(out.dtype)
            out[rows:, :] = two.astype(out.dtype)

    outs = [((2 * rows, cols), WIDE if k == 0 else LOW) for k in range(depth)]
    own, *sends = run(third_hop, outs, keep_x, got_x, keep_y, got_y, on_y, on_x, scalars=False, deps=deps)
    return [own] + [shift(part, k + 1) for k, part in enumerate(sends)]


def sum_of(refs):
    total = refs[0][...]
    for ref in refs[1:]:
        total = total + ref[...].astype(WIDE)
    return total


def spread(value):
    return jnp.broadcast_to(value, (8, LANES))


def total_squares(value):
    return jnp.sum(jnp.sum(value * value, axis=1, keepdims=True), axis=0, keepdims=True)


def finish_down(parts):
    def kernel(*refs):
        total = sum_of(refs[: len(parts)])
        refs[-2][...] = total
        refs[-1][...] = spread(total_squares(total))

    return run(kernel, [(parts[0].shape, WIDE), ((8, LANES), WIDE)], *parts, scalars=False)


def finish_up(parts, squares, rows, half_ff):
    half_d = parts[0].shape[1] - half_ff
    small = rows // 2

    def kernel(coords, squares_ref, *refs):
        own_ref, mate_ref, out_ref, total_ref, all_ref = refs[len(parts) :]
        total = sum_of(refs[: len(parts)])
        all_ref[...] = total
        core = coords[3]
        own_ref[...] = all_ref[pl.ds(pl.multiple_of(core * rows, 8), rows), :half_ff]
        mate_ref[...] = all_ref[pl.ds(pl.multiple_of((1 - core) * rows, 8), rows), :half_ff]
        for p in range(2):
            for h in range(2):
                block = total[h * rows + p * small : h * rows + (p + 1) * small, half_ff:]
                out_ref[h * small : (h + 1) * small, p * half_d : (p + 1) * half_d] = block
        total_ref[...] = squares_ref[...] + spread(total_squares(total))

    outs = [((rows, half_ff), WIDE)] * 2 + [((rows, 2 * half_d), WIDE), ((8, LANES), WIDE)]
    scratch = [pltpu.VMEM(parts[0].shape, WIDE)]
    return run(kernel, outs, squares, *parts, scratch=scratch)


def finish_qkv(parts, squares, rows, half_qkv, deps=()):
    def kernel(coords, squares_ref, *refs):
        own_ref, mate_ref, small_ref, all_ref = refs[len(parts) :]
        total = sum_of(refs[: len(parts)])
        all_ref[...] = total
        core = coords[3]
        own_ref[...] = all_ref[pl.ds(pl.multiple_of(core * rows, 8), rows), :half_qkv]
        mate_ref[...] = all_ref[pl.ds(pl.multiple_of((1 - core) * rows, 8), rows), :half_qkv]
        small_ref[: 2 * rows, :] = total[:, half_qkv:]
        small_ref[2 * rows :, :] = squares_ref[...] + spread(total_squares(total[:, :half_qkv]))

    outs = [((rows, half_qkv), WIDE)] * 2 + [((2 * rows + 8, LANES), WIDE)]
    scratch = [pltpu.VMEM(parts[0].shape, WIDE)]
    return run(kernel, outs, squares, *parts, scratch=scratch, deps=deps)


def chip_squares(small, got):
    rows = small.shape[0] - 8

    def kernel(small_ref, got_ref, total_ref, norm_ref):
        total = small_ref[...] + got_ref[...]
        norm_ref[...] = total[:rows]
        total_ref[...] = total[rows:] + spread(total_squares(total[:rows]))

    outs = [((8, LANES), WIDE), ((rows, LANES), WIDE)]
    return run(kernel, outs, small, got, scalars=False)


def sum_chips(value):
    across = lax.ppermute(value, ("y", "x"), [(i, 3 - i) for i in range(4)])
    value = value + swap(value, "y") + (swap(value, "x") + across)
    size, near = lax.axis_size("z"), 1
    while near < size // 2:
        value = value + lax.ppermute(value, "z", [(i, i ^ near) for i in range(size)])
        near *= 2
    return [value, lax.ppermute(value, "z", [(i, i ^ near) for i in range(size)])]


def interleave(first, own, mate, blocks):
    size = own.shape[1] // blocks
    pieces = []
    for j in range(blocks):
        at = slice(j * size, (j + 1) * size)
        pieces += [jnp.where(first, own[:, at], mate[:, at]), jnp.where(first, mate[:, at], own[:, at])]
    return jnp.concatenate(pieces, axis=1)


def update_all(grads, totals, masters, firsts, seconds, rates, decays, blocks):
    steps = 4
    n, m = len(grads), len(totals)

    def tile(array):
        rows, cols = array.shape
        return pl.BlockSpec((rows // steps, cols), lambda i: (i, 0))

    def whole(array):
        return pl.BlockSpec(array.shape, lambda i: (0, 0))

    def kernel(coords, *refs):
        first = coords[3] == 0
        g, t, old, new = refs[:n], refs[n : n + m], refs[n + m : n + m + 15], refs[n + m + 15 :]
        total = sum_of(t)[0:1, 0:1]
        norm = jnp.sqrt(total)
        clip = jnp.minimum(1.0, CLIP_LIMIT / (norm + 1e-06))
        qkv = interleave(first, g[0][...], g[1][...], blocks[0])
        up = interleave(first, g[3][...], g[4][...], blocks[1])
        for k, grad in enumerate((qkv, g[2][...], up, g[5][...], g[6][...])):
            news = adam_update(old[k][...], old[5 + k][...], old[10 + k][...], clip * grad, rates[k], decays[k])
            for part in range(3):
                new[5 * part + k][...] = news[part]
        new[15][...] = norm

    state = (*masters, *firsts, *seconds)
    specs = [whole(a) if k % 5 == 4 else tile(a) for k, a in enumerate(state)]
    norm_out = jax.ShapeDtypeStruct((1, 1), WIDE)
    return pl.pallas_call(
        kernel,
        grid=(steps,),
        out_shape=[jax.ShapeDtypeStruct(a.shape, WIDE) for a in state] + [norm_out],
        in_specs=[pl.BlockSpec(memory_space=pltpu.SMEM)]
        + [tile(a) for a in grads[:-1]]
        + [whole(grads[-1])]
        + [whole(a) for a in totals]
        + specs,
        out_specs=specs + [whole(norm_out)],
        compiler_params=FULL,
    )(coordinates(), *grads, *totals, *state)


def coordinates():
    return jnp.stack([lax.axis_index(name) for name in ("z", "y", "x", "c")]).astype(jnp.int32)


def chip_of(coords, rel, depth, back):
    dz, dy, dx = rel
    z, y, x = coords[0], coords[1], coords[2]
    zz = lax.rem(z + (depth - dz if back else dz), depth)
    yy = 1 - y if dy else y
    xx = 1 - x if dx else x
    return zz, yy * 2 + xx


def window(row, rows, col, cols):
    rows_at = pl.ds(row if isinstance(row, int) else pl.multiple_of(row, 16), rows)
    return rows_at, pl.ds(col, cols)


VMEM = pl.BlockSpec(memory_space=pltpu.VMEM)
ROOM_MB = 16
ROOM = pltpu.CompilerParams(vmem_limit_bytes=ROOM_MB * 1024 * 1024)
FULL = pltpu.CompilerParams(vmem_limit_bytes=56 * 1024 * 1024)


def place(parts, depth, outs, spots, moves, deps=()):
    def kernel(coords, *refs):
        ins, out_refs = refs[: len(parts)], refs[len(parts) + len(deps) :]
        for array, lead, base, rel, piece in spots:
            zz, plane = chip_of(coords, rel, depth, True)
            for o, sr, sc, rows, cols, tr, tc in moves(zz, plane, piece):
                out_refs[o][window(tr, rows, tc, cols)] = ins[array][(*lead, *window(base + sr, rows, sc, cols))]

    return pl.pallas_call(
        kernel,
        out_shape=[jax.ShapeDtypeStruct(s, LOW) for s in outs],
        in_specs=[pl.BlockSpec(memory_space=pltpu.SMEM)]
        + [VMEM] * len(parts)
        + [pl.BlockSpec(memory_space=pl.ANY)] * len(deps),
        out_specs=[VMEM] * len(outs),
        compiler_params=ROOM,
    )(coordinates(), *parts, *deps)


def unplace(grads, depth, rows_cols, moves):
    spots = []
    for dz in range(depth):
        for d in range(2):
            spots += [(0, d, dz, (dz, d, 1), 0), (1, d, dz, (dz, d, 0), 0)]
            spots += [(2, d, dz, (dz, 1, d), 1), (3, d, dz, (dz, 0, d), 1)]

    def kernel(coords, *refs):
        ins, out_refs = refs[: len(grads)], refs[len(grads) :]
        for array, d, dz, rel, half in spots:
            zz, plane = chip_of(coords, rel, depth, False)
            for i, sr, sc, rows, cols, tr, tc in moves(zz, plane, half):
                out_refs[array][(d, dz, *window(tr, rows, tc, cols))] = ins[i][window(sr, rows, sc, cols)]

    return pl.pallas_call(
        kernel,
        out_shape=[jax.ShapeDtypeStruct((2, depth) + rows_cols, LOW)] * 4,
        in_specs=[pl.BlockSpec(memory_space=pltpu.SMEM)] + [VMEM] * len(grads),
        out_specs=[VMEM] * 4,
        compiler_params=ROOM,
    )(coordinates(), *grads)


def cast_qkv(qkv, norm, halves):
    rows, cols = qkv.shape
    wide = cols // 2 + LANES
    block = cols // (2 * halves)

    def kernel(coords, qkv_ref, norm_ref, own_ref, mate_ref, tall):
        first = coords[3] == 0
        for j in range(halves):
            a = qkv_ref[:, 2 * j * block : (2 * j + 1) * block]
            b = qkv_ref[:, (2 * j + 1) * block : (2 * j + 2) * block]
            own_ref[:, j * block : (j + 1) * block] = jnp.where(first, a, b).astype(LOW)
            mate_ref[:, j * block : (j + 1) * block] = jnp.where(first, b, a).astype(LOW)
        tall[...] = jnp.zeros_like(tall)
        tall[0:4, :] = norm_ref[...].astype(LOW).astype(WIDE)
        i = lax.broadcasted_iota(jnp.int32, (rows, rows), 0)
        j = lax.broadcasted_iota(jnp.int32, (rows, rows), 1)
        columns = dot_cols((i == j).astype(LOW), tall[...].astype(LOW)).astype(LOW)
        own_ref[:, cols // 2 :] = columns
        mate_ref[:, cols // 2 :] = columns

    return pl.pallas_call(
        kernel,
        out_shape=[jax.ShapeDtypeStruct((rows, wide), LOW)] * 2,
        in_specs=[pl.BlockSpec(memory_space=pltpu.SMEM), VMEM, VMEM],
        out_specs=[VMEM] * 2,
        scratch_shapes=[pltpu.VMEM((LANES, rows), WIDE)],
        compiler_params=ROOM,
    )(coordinates(), qkv, norm)


def cast_down(down):
    half = down.shape[0] // 2

    def kernel(down_ref, one_ref, two_ref):
        one_ref[...] = down_ref[:half, :].astype(LOW)
        two_ref[...] = down_ref[half:, :].astype(LOW)

    return pl.pallas_call(
        kernel,
        out_shape=[jax.ShapeDtypeStruct((half, down.shape[1]), LOW)] * 2,
        in_specs=[VMEM],
        out_specs=[VMEM] * 2,
        compiler_params=ROOM,
    )(down)


def cast_rest(up, out, halves):
    rows, cols = up.shape
    block, width = cols // (2 * halves), out.shape[1]

    def kernel(coords, up_ref, out_ref, own_ref, mate_ref, part_ref):
        first = coords[3] == 0
        for j in range(halves):
            a = up_ref[:, 2 * j * block : (2 * j + 1) * block]
            b = up_ref[:, (2 * j + 1) * block : (2 * j + 2) * block]
            own_ref[:, j * block : (j + 1) * block] = jnp.where(first, a, b).astype(LOW)
            mate_ref[:, j * block : (j + 1) * block] = jnp.where(first, b, a).astype(LOW)
        part_ref[:rows, :] = out_ref[:, : width // 2].astype(LOW)
        part_ref[rows:, :] = out_ref[:, width // 2 :].astype(LOW)

    return pl.pallas_call(
        kernel,
        out_shape=[jax.ShapeDtypeStruct((rows, cols // 2), LOW)] * 2
        + [jax.ShapeDtypeStruct((2 * rows, width // 2), LOW)],
        in_specs=[pl.BlockSpec(memory_space=pltpu.SMEM), VMEM, VMEM],
        out_specs=[VMEM] * 3,
        compiler_params=ROOM,
    )(coordinates(), up, out)


def join_rows(own, mate, side=None):
    rows, cols = own.shape
    wide = cols + (side.shape[1] if side is not None else 0)

    def kernel(coords, own_ref, mate_ref, *refs):
        out_ref = refs[-1]
        core = coords[3]
        out_ref[pl.ds(pl.multiple_of(core * rows, 16), rows), :cols] = own_ref[...]
        out_ref[pl.ds(pl.multiple_of((1 - core) * rows, 16), rows), :cols] = mate_ref[...]
        if side is not None:
            out_ref[:, cols:] = refs[0][...]

    ins = [own, mate] + ([side] if side is not None else [])
    return pl.pallas_call(
        kernel,
        out_shape=jax.ShapeDtypeStruct((2 * rows, wide), LOW),
        in_specs=[pl.BlockSpec(memory_space=pltpu.SMEM)] + [VMEM] * len(ins),
        out_specs=VMEM,
        compiler_params=ROOM,
    )(coordinates(), *ins)


def run(kernel, outs, *ins, scalars=True, scratch=(), flops=0, room=ROOM_MB, deps=()):
    first = len(ins) + scalars

    def body_of(*refs):
        return kernel(*refs[:first], *refs[first + len(deps) :])

    out_shape = [jax.ShapeDtypeStruct(shape, kind) for shape, kind in outs]
    return pl.pallas_call(
        body_of,
        out_shape=out_shape,
        in_specs=([pl.BlockSpec(memory_space=pltpu.SMEM)] if scalars else [])
        + [VMEM] * len(ins)
        + [pl.BlockSpec(memory_space=pl.ANY)] * len(deps),
        out_specs=[VMEM] * len(outs),
        scratch_shapes=list(scratch),
        compiler_params=pltpu.CompilerParams(vmem_limit_bytes=room * 1024 * 1024),
        cost_estimate=pl.CostEstimate(flops=flops, bytes_accessed=0, transcendentals=0),
    )(*([coordinates()] if scalars else []), *ins, *deps)


def dot(left, right):
    return jnp.dot(left, right, preferred_element_type=WIDE)


def dot_rows(left, right):
    return lax.dot_general(left, right, (((0,), (0,)), ((), ())), preferred_element_type=WIDE)


def dot_cols(left, right):
    return lax.dot_general(left, right, (((1,), (1,)), ((), ())), preferred_element_type=WIDE)


def eye(rows, cols):
    i = lax.broadcasted_iota(jnp.int32, (rows, cols), 0)
    return (i == lax.broadcasted_iota(jnp.int32, (rows, cols), 1)).astype(LOW)


def normalise(values):
    center = values - jnp.mean(values, axis=-1, keepdims=True)
    rate = lax.rsqrt(jnp.mean(center * center, axis=-1, keepdims=True) + NORM_EPS)
    return center * rate, rate


def norm_back(normed, rate, grad, gain):
    scaled = grad * gain
    shared = jnp.mean(scaled, axis=-1, keepdims=True)
    along = jnp.mean(scaled * normed, axis=-1, keepdims=True)
    return rate * (scaled - shared - normed * along)


def low_lanes(rows):
    return lax.broadcasted_iota(jnp.int32, (rows, LANES), 1) < HEAD_DIM


def by_head(pair):
    wide = pair.astype(WIDE)
    first = low_lanes(pair.shape[0])
    return jnp.where(first, wide, 0.0).astype(LOW), jnp.where(first, 0.0, wide).astype(LOW)


def pack_state(square):
    first = low_lanes(HEAD_DIM)
    return jnp.where(first, square[:HEAD_DIM], square[HEAD_DIM:])


def open_state(packed):
    first = low_lanes(HEAD_DIM)
    return jnp.concatenate([jnp.where(first, packed, 0.0), jnp.where(first, 0.0, packed)])


def feature(values):
    return jnp.where(values > 0.0, values + 1.0, jnp.exp(jnp.minimum(values, 0.0)))


def project(x, norm_w, qkv_w):
    tokens, width = x.shape
    half = qkv_w.shape[1] // 3
    pairs = half // LANES
    step = tokens // 2

    def kernel(x_ref, norm_ref, w_ref, rows_ref, normed_ref, qk_ref, q_ref, k_ref, v_ref, state_ref, sums):
        rows_ref[...] = dot_cols(eye(8, LANES), norm_ref[...])
        gain, bias = rows_ref[0:1, :], rows_ref[1:2, :]
        @pl.loop(0, 2)
        def _(i):
            at = at_block(i, step)
            normed = normalise(x_ref[at, :].astype(WIDE))[0]
            normed_ref[at, :] = (normed * gain + bias).astype(LOW)
            low = normed_ref[at, :]
            for j, out in enumerate((q_ref, k_ref)):
                part = dot(low, w_ref[:, j * half : (j + 1) * half])
                qk_ref[at, j * half : (j + 1) * half] = part
                out[at, :] = feature(part).astype(LOW)
            v_ref[at, :] = dot(low, w_ref[:, 2 * half :]).astype(LOW)
        total = dot_rows(jnp.ones((tokens, 8), LOW), k_ref[...])
        sums[...] = jnp.zeros_like(sums)
        for p in range(pairs):
            lanes = slice(p * LANES, (p + 1) * LANES)
            packed = pack_state(dot_rows(k_ref[:, lanes], v_ref[:, lanes]))
            state_ref[p * HEAD_DIM : (p + 1) * HEAD_DIM, :] = packed.astype(LOW)
            sums[p : p + 1, :] = total[0:1, lanes]
        state_ref[pairs * HEAD_DIM :, :] = sums[...].astype(LOW)

    outs = [((8, width), WIDE), ((tokens, width), LOW), ((tokens, 2 * half), WIDE)] + [((tokens, half), LOW)] * 3
    outs += [((pairs * HEAD_DIM + 16, LANES), LOW)]
    scratch = [pltpu.VMEM((16, LANES), WIDE)]
    return run(kernel, outs, x, norm_w, qkv_w, scalars=False, scratch=scratch)


def at_block(index, size):
    return pl.ds(pl.multiple_of(index * size, size), size)


def total_state(refs):
    total = refs[0][...].astype(WIDE)
    for ref in refs[1:]:
        total = total + ref[...].astype(WIDE)
    return total


def causal_mask(step):
    i = lax.broadcasted_iota(jnp.int32, (step, step), 0)
    return i >= lax.broadcasted_iota(jnp.int32, (step, step), 1)


def attend(query, key, value, parts, deps=()):
    tokens, half = query.shape
    pairs, step = half // LANES, tokens // 2

    def kernel(q_ref, k_ref, v_ref, *refs):
        mixed_ref, low_ref, denom_ref, state_ref, token_ref = refs[len(parts) :]
        token_ref[...] = jnp.zeros_like(token_ref)
        state_ref[...] = total_state(refs[: len(parts)])
        lower = causal_mask(step)
        first = low_lanes(step)
        top = low_lanes(HEAD_DIM)
        diagonal = eye(LANES, LANES).astype(WIDE)
        @pl.loop(0, pairs)
        def _(p):
            lanes = at_block(p, LANES)
            packed = state_ref[at_block(p, HEAD_DIM), :]
            sums = state_ref[pl.ds(pairs * HEAD_DIM + p, 1), :]
            column = jnp.sum(diagonal * sums, axis=1, keepdims=True)
            zero = jnp.zeros((HEAD_DIM, LANES), WIDE)
            ext = (
                jnp.concatenate([jnp.where(top, packed, column[:HEAD_DIM]), zero]).astype(LOW),
                jnp.concatenate([zero, jnp.where(top, column[HEAD_DIM:], packed)]).astype(LOW),
            )
            wide = v_ref[:, lanes].astype(WIDE)
            full = low_lanes(tokens)
            value_ext = (jnp.where(full, wide, 1.0).astype(LOW), jnp.where(full, 1.0, wide).astype(LOW))
            queries = by_head(q_ref[:, lanes])
            for i in range(2):
                at = slice(i * step, (i + 1) * step)
                got = []
                for h in range(2):
                    rows = queries[h][at]
                    total = dot(rows, ext[h])
                    for j in range(i + 1):
                        to = slice(j * step, (j + 1) * step)
                        scores = dot_cols(rows, k_ref[to, lanes])
                        if j == i:
                            scores = jnp.where(lower, scores, 0.0)
                        total = total + dot(scores.astype(LOW), value_ext[h][to])
                    got.append(total)
                denom = pltpu.roll(jnp.where(first, got[1], got[0]), HEAD_DIM, 1)
                mixed = jnp.where(first, got[0], got[1]) / denom
                mixed_ref[at, lanes] = mixed
                low_ref[at, lanes] = mixed.astype(LOW)
                denom_ref[at, lanes] = denom

    outs = [((tokens, half), WIDE), ((tokens, half), LOW), ((tokens, half), WIDE), (parts[0].shape, WIDE)]
    outs += [((8, LANES), WIDE)]
    return run(kernel, outs, query, key, value, *parts, scalars=False, deps=deps)


def out_project(mixed, out_w):
    def kernel(mixed_ref, w_ref, part_ref, low_ref):
        part = dot(mixed_ref[...], w_ref[...])
        part_ref[...] = part
        low_ref[...] = part.astype(LOW)

    shape = (mixed.shape[0], out_w.shape[1])
    return run(kernel, [(shape, WIDE), (shape, LOW)], mixed, out_w, scalars=False)


def feed(x, part, got, rows, up_w):
    tokens, width = x.shape
    units, step, cut = up_w.shape[1], tokens // 2, 512

    def kernel(x_ref, part_ref, got_ref, rows_ref, w_ref, resid_ref, normed_ref, act_ref, slope_ref):
        @pl.loop(0, 2)
        def _(i):
            at = at_block(i, step)
            resid = x_ref[at, :].astype(WIDE) + part_ref[at, :] + got_ref[at, :].astype(WIDE)
            resid_ref[at, :] = resid
            normed_ref[at, :] = (normalise(resid)[0] * rows_ref[2:3, :] + rows_ref[3:4, :]).astype(LOW)

        @pl.loop(0, units // cut)
        def _(j):
            to = at_block(j, cut)
            v = dot(normed_ref[...], w_ref[:, to])
            root = (2.0 / 3.141592653589793) ** 0.5
            square = v * v
            bend = jnp.tanh(root * v * (1.0 + 0.044715 * square))
            cdf = 0.5 * (1.0 + bend)
            act_ref[:, to] = (v * cdf).astype(LOW)
            slope_ref[:, to] = cdf + 0.5 * v * (1.0 - bend * bend) * (root * (1.0 + 3.0 * 0.044715 * square))

    outs = [((tokens, width), WIDE), ((tokens, width), LOW), ((tokens, units), LOW), ((tokens, units), WIDE)]
    return run(kernel, outs, x, part, got, rows, up_w, scalars=False)


def feed_back(grad_out, down_w, slope, up_w):
    tokens, width = grad_out.shape
    units, cut = up_w.shape[1], 512

    def kernel(g_ref, down_ref, slope_ref, up_ref, hidden_ref, part_ref, low_ref):
        @pl.loop(0, units // cut)
        def _(j):
            to = at_block(j, cut)
            hidden_ref[:, to] = (dot_cols(g_ref[...], down_ref[to, :]) * slope_ref[:, to]).astype(LOW)

        @pl.loop(0, width // cut)
        def _(j):
            to = at_block(j, cut)
            part = dot_cols(hidden_ref[...], up_ref[to, :])
            part_ref[:, to] = part
            low_ref[:, to] = part.astype(LOW)

    outs = [((tokens, units), LOW), ((tokens, width), WIDE), ((tokens, width), LOW)]
    return run(kernel, outs, grad_out, down_w, slope, up_w, scalars=False)


def down_project(activated, down_w, resid, deps):
    tokens, width = resid.shape
    group, cut = tokens // 2, width // 2

    def kernel(coords, act_ref, w_ref, resid_ref, own_ref, give_ref):
        own = pl.ds(pl.multiple_of(coords[3] * group, 16), group)
        mate = pl.ds(pl.multiple_of((1 - coords[3]) * group, 16), group)

        @pl.loop(0, 2)
        def _(j):
            to = at_block(j, cut)
            own_ref[:, to] = resid_ref[own, to] + dot(act_ref[own, :], w_ref[:, to])
            give_ref[:, to] = dot(act_ref[mate, :], w_ref[:, to]).astype(LOW)

    outs = [((group, width), WIDE), ((group, width), LOW)]
    return run(kernel, outs, activated, down_w, resid, deps=deps)


def weight_grad(rows, grad, deps=()):
    tokens, width = rows.shape
    units, cut = grad.shape[1], 512

    def kernel(rows_ref, grad_ref, out_ref):
        @pl.loop(0, units // cut)
        def _(j):
            to = at_block(j, cut)
            out_ref[:, to] = dot_rows(rows_ref[...], grad_ref[:, to]).astype(LOW)

    return run(kernel, [((width, units), LOW)], rows, grad, scalars=False, deps=deps)[0]


def attend_turn(part, got, resid, rows, grad_out, out_w, mixed, denom, query, deps):
    tokens, width = resid.shape
    half = mixed.shape[1]
    pairs, step = half // LANES, tokens // 2

    def kernel(
        part_ref, got_ref, resid_ref, rows_ref, g_ref, w_ref, mixed_ref, denom_ref, q_ref,
        grad_ref, low_ref, a_ref, b_ref, state_ref, norm_ref, sums,
    ):
        gain = rows_ref[2:3, :]
        first = low_lanes(step)
        norm_ref[...] = jnp.zeros_like(norm_ref)

        @pl.loop(0, 2)
        def _(i):
            at = at_block(i, step)
            normed, rate = normalise(resid_ref[at, :])
            own = part_ref[at, :]
            norm_ref[0:1, :] += jnp.sum(own * normed, axis=0, keepdims=True)
            norm_ref[1:2, :] += jnp.sum(own, axis=0, keepdims=True)
            grad = g_ref[at, :].astype(WIDE) + norm_back(normed, rate, own + got_ref[at, :].astype(WIDE), gain)
            grad_ref[at, :] = grad
            low_ref[at, :] = grad.astype(LOW)
            turned = dot_cols(low_ref[at, :], w_ref[...]) / denom_ref[at, :]
            a_ref[at, :] = turned.astype(LOW)
            along = turned * mixed_ref[at, :]
            for p in range(pairs):
                lanes = slice(p * LANES, (p + 1) * LANES)
                piece = along[:, lanes]
                low = jnp.sum(jnp.where(first, piece, 0.0), axis=1, keepdims=True)
                high = jnp.sum(jnp.where(first, 0.0, piece), axis=1, keepdims=True)
                b_ref[at, lanes] = -jnp.where(first, low, high)
        sums[...] = jnp.zeros_like(sums)
        for p in range(pairs):
            lanes = slice(p * LANES, (p + 1) * LANES)
            packed = pack_state(dot_rows(q_ref[:, lanes], a_ref[:, lanes]))
            state_ref[p * HEAD_DIM : (p + 1) * HEAD_DIM, :] = packed.astype(LOW)
            sums[p : p + 1, :] = jnp.sum(q_ref[:, lanes].astype(WIDE) * b_ref[:, lanes], axis=0, keepdims=True)
        state_ref[pairs * HEAD_DIM :, :] = sums[...].astype(LOW)

    outs = [((tokens, width), WIDE), ((tokens, width), LOW), ((tokens, half), LOW), ((tokens, half), WIDE)]
    outs += [((pairs * HEAD_DIM + 16, LANES), LOW), ((2, width), WIDE)]
    ins = (part, got, resid, rows, grad_out, out_w, mixed, denom, query)
    scratch = [pltpu.VMEM((16, LANES), WIDE)]
    return run(kernel, outs, *ins, scalars=False, scratch=scratch, deps=deps)


def attend_back(query, key, value, qk, a_low, b_rows, state, parts, deps=()):
    tokens, half = query.shape
    pairs, step = half // LANES, tokens // 2

    def kernel(q_ref, k_ref, v_ref, qk_ref, a_ref, b_ref, state_ref, *refs):
        out_ref, later = refs[len(parts) :]
        later[...] = total_state(refs[: len(parts)])
        lower = causal_mask(step)
        @pl.loop(0, pairs)
        def _(p):
            lanes, rows = at_block(p, LANES), at_block(p, HEAD_DIM)
            sums = pl.ds(pairs * HEAD_DIM + p, 1)
            before, after_it = open_state(state_ref[rows, :]).astype(LOW), open_state(later[rows, :]).astype(LOW)
            queries, keys, pulls = by_head(q_ref[:, lanes]), by_head(k_ref[:, lanes]), by_head(a_ref[:, lanes])
            cuts = [slice(i * step, (i + 1) * step) for i in range(2)]
            grad_q = [dot_cols(a_ref[c, lanes], before) + b_ref[c, lanes] * state_ref[sums, :] for c in cuts]
            grad_k = [dot_cols(v_ref[c, lanes], after_it) + later[sums, :] for c in cuts]
            shifts = b_ref[:, lanes]
            grad_v = [dot(k_ref[c, lanes], after_it) for c in cuts]
            for i in range(2):
                for j in range(i + 1):
                    for h in range(2):
                        q, a = queries[h][cuts[i]], pulls[h][cuts[i]]
                        b = shifts[cuts[i], h * HEAD_DIM : h * HEAD_DIM + 1]
                        scores = dot_cols(q, k_ref[cuts[j], lanes])
                        pull = dot_cols(a, v_ref[cuts[j], lanes]) + b
                        if j == i:
                            scores, pull = jnp.where(lower, scores, 0.0), jnp.where(lower, pull, 0.0)
                        scores, pull = scores.astype(LOW), pull.astype(LOW)
                        grad_q[i] = grad_q[i] + dot(pull, keys[h][cuts[j]])
                        grad_k[j] = grad_k[j] + dot_rows(pull, q)
                        grad_v[j] = grad_v[j] + dot_rows(scores, a)
            for i, c in enumerate(cuts):
                for n, grad in enumerate((grad_q[i], grad_k[i])):
                    at = at_block(n * pairs + p, LANES)
                    raw = qk_ref[c, at]
                    out_ref[c, at] = (grad * jnp.where(raw > 0.0, 1.0, jnp.exp(jnp.minimum(raw, 0.0)))).astype(LOW)
                out_ref[c, at_block(2 * pairs + p, LANES)] = grad_v[i].astype(LOW)

    ins = (query, key, value, qk, a_low, b_rows, state, *parts)
    scratch = [pltpu.VMEM(parts[0].shape, WIDE)]
    return run(kernel, [((tokens, 3 * half), LOW)], *ins, scalars=False, scratch=scratch, deps=deps)[0]


def project_back(grad, qkv_w, x, norm_two):
    tokens, width = x.shape
    step = tokens // 2

    def kernel(grad_ref, w_ref, x_ref, two_ref, part_ref, low_ref, cols_ref, rows):
        rows[...] = jnp.zeros_like(rows)

        @pl.loop(0, 2)
        def _(i):
            at = at_block(i, step)
            part = dot_cols(grad_ref[at, :], w_ref[...])
            part_ref[at, :] = part
            low_ref[at, :] = part.astype(LOW)
            rows[0:1, :] += jnp.sum(part * normalise(x_ref[at, :].astype(WIDE))[0], axis=0, keepdims=True)
            rows[1:2, :] += jnp.sum(part, axis=0, keepdims=True)

        rows[2:4, :] = two_ref[...]
        cols_ref[...] = dot_rows(rows[...].astype(LOW), eye(8, LANES)).astype(LOW)

    outs = [((tokens, width), WIDE), ((tokens, width), LOW), ((width, LANES), LOW)]
    scratch = [pltpu.VMEM((8, width), WIDE)]
    return run(kernel, outs, grad, qkv_w, x, norm_two, scalars=False, scratch=scratch)


def input_back(part, got, grad_resid, own_x, rows):
    group, width = own_x.shape

    def kernel(coords, part_ref, got_ref, resid_ref, x_ref, rows_ref, out_ref):
        at = pl.ds(pl.multiple_of(coords[3] * group, 16), group)
        normed, rate = normalise(x_ref[...].astype(WIDE))
        grad = part_ref[at, :] + got_ref[...].astype(WIDE)
        out_ref[...] = (resid_ref[at, :] + norm_back(normed, rate, grad, rows_ref[0:1, :])).astype(LOW)

    return run(kernel, [((group, width), LOW)], part, got, grad_resid, own_x, rows)[0]


def adam_update(weight, first, second, grad, rate, decay):
    first_new = BETA_ONE * first + (1.0 - BETA_ONE) * grad
    second_new = BETA_TWO * second + (1.0 - BETA_TWO) * grad * grad
    first_hat = first_new / (1.0 - BETA_ONE**STEP)
    second_hat = second_new / (1.0 - BETA_TWO**STEP)
    weight_new = weight - rate * (first_hat / (jnp.sqrt(second_hat) + ADAM_EPS) + decay * weight)
    return (weight_new, first_new, second_new)


def from_others(low, step):
    if lax.axis_size("z") == 4:
        near = shift(low, step, wrap=False)
        pair = (low.astype(WIDE) + near.astype(WIDE)).astype(LOW)
        return [near, shift(pair, 2 * step, wrap=False)]
    return [shift(low, step * k, wrap=False) for k in range(1, lax.axis_size("z"))]


def body(
    images,
    cotangent,
    qkv_weight,
    out_weight,
    up_weight,
    down_weight,
    norm_params,
    qkv_first,
    out_first,
    up_first,
    down_first,
    norm_first,
    qkv_second,
    out_second,
    up_second,
    down_second,
    norm_second,
):
    depth, core = lax.axis_size("z"), lax.axis_index("c")
    count, group, width = images.shape
    hidden_units = up_weight.shape[1]
    own_rows = qkv_weight.shape[0]
    own_units = down_weight.shape[0]
    chips = lax.axis_size("y") * lax.axis_size("x")
    block, ff_block = width // (2 * depth), hidden_units // (2 * depth)
    half_qkv, half_ff, half_d = 3 * width // 2, hidden_units // 2, width // 2
    ring = lax.axis_size("y") == 2 and lax.axis_size("x") == 2 and depth == 4 and own_rows % 32 == 0
    heads = half_d // HEAD_DIM
    tokens = 2 * group

    own_x, own_g = images.reshape(group, width), cotangent.reshape(group, width)
    split_qkv = lambda w: jnp.moveaxis(w.reshape(-1, 3 * depth, 2, block), 2, 0).reshape(2, -1, half_qkv)
    split_up = lambda w: jnp.moveaxis(w.reshape(-1, depth, 2, ff_block), 2, 0).reshape(2, -1, half_ff)

    thin, small = own_units // 2, own_rows // 2
    if ring:
        qkv_mine, qkv_give = cast_qkv(qkv_weight, norm_params, 3 * depth)
        qkv_part = join_rows(qkv_mine, swap(qkv_give, "c"))
        down_one, down_two = cast_down(down_weight)
        up_mine, up_give, out_part = cast_rest(after(up_weight, qkv_part), out_weight, depth)
        inputs = join_rows(own_x, swap(own_x, "c"))
        up_part = join_rows(up_mine, swap(up_give, "c"), out_part)
        qkv_column = column_first(qkv_part)
        two_plane = plane_first(after(down_two, qkv_part))
        qkv_column = [after(part, two_plane, up_part, inputs) for part in qkv_column]
        up_column = column_first(after(up_part, *qkv_column))
        qkv_parts = plane_last(jnp.stack(qkv_column))
        g_mate = swap(after(own_g, *up_column), "c")
        two_parts = [two_plane, shift(after(two_plane, *up_column), 1)]
        one_column = column_first(after(down_one, two_parts[1]))

        def qkv_moves(zz, plane, piece):
            row = lambda h: ((zz * 2 + h) * chips + plane) * own_rows
            moves = [(0, h * own_rows, 0, own_rows, half_qkv, row(h), 0) for h in (0, 1)]
            return moves + [(1, h * own_rows, half_qkv, own_rows, LANES, row(h), 0) for h in (0, 1)]

        def up_moves(zz, plane, piece):
            row = lambda h: ((zz * 2 + h) * chips + plane) * own_rows
            moves = [(0, h * own_rows, 0, own_rows, half_ff, row(h), 0) for h in (0, 1)]
            to = zz * block + plane * own_rows
            return moves + [(1, h * own_rows, half_ff, own_rows, half_d, to, h * half_d) for h in (0, 1)]

        def down_moves(zz, plane, piece):
            return [(0, 0, 0, thin, width, zz * ff_block + plane * own_units + piece * thin, 0)]

        spots = column_first_spots(depth)
        qkv_w, norm_w = place(qkv_parts, depth, [(width, half_qkv), (width, LANES)], spots, qkv_moves)
    else:
        qkv_low, out_low = qkv_weight.astype(LOW), out_weight.astype(LOW)
        up_low, down_low = up_weight.astype(LOW), down_weight.astype(LOW)
        norm_low = norm_params.astype(LOW)
        x_mate, g_mate = swap(own_x, "c"), swap(own_g, "c")
        whole = lambda w, axis=0: lax.all_gather(w, ALL, axis=axis, tiled=True)
        qkv_w, up_w = mine(split_qkv(whole(qkv_low))), mine(split_up(whole(up_low)))
        rows_half = lambda w, b: mine(jnp.moveaxis(w.reshape(depth, 2, b, width), 1, 0)).reshape(-1, width)
        out_w, down_w = rows_half(whole(out_low), block), rows_half(whole(down_low), ff_block)
        norm_w = jnp.pad(whole(norm_low, 1).T, ((0, 0), (0, LANES - 4)))

        inputs = join_rows(own_x, x_mate)
    grad_out = join_rows(own_g, g_mate)
    halves = lambda a: a.reshape(2, group, -1)
    rows, normed_one, qk, query, key, value, state = project(inputs, norm_w, qkv_w)
    earlier = from_others(state, 1)
    mixed, mixed_low, denom, state_in, attended = attend(query, key, value, earlier, (grad_out,))
    if ring:
        gate = (*earlier, *one_column[1:])
        up_parts = plane_last(after(jnp.stack(up_column), *qkv_parts[3:]), gate)
        two_parts.append(shift(after(two_parts[-1], *gate), 1))
        for _ in range(3, depth):
            two_parts.append(shift(two_parts[-1], 1))
        up_w, out_w = place(
            up_parts, depth, [(width, half_ff), (half_d, width)], spots, up_moves, two_parts[2:3]
        )
    out_part, out_low = out_project(mixed_low, out_w)
    out_got = swap(out_low, "c")
    resid, normed_two, activated, slope = feed(inputs, out_part, out_got, rows, up_w)
    down_grad = dot_rows(activated, grad_out).astype(LOW)
    if ring:
        def down_cuts(zz, plane, half):
            return [(0, zz * ff_block + plane * own_units + half * thin, 0, thin, width, 0, 0)]

        down_cut = unplace([down_grad], depth, (thin, width), down_cuts)
        down_hop = first_hop(*down_cut)
        one_parts = plane_last(after(jnp.stack(one_column), *up_parts[3:]), (down_cut[0][0, 0, :16, :LANES],))
        spots = spots + plane_first_spots(depth, thin, 5)
        down_parts = [*one_parts, *two_parts]
        (down_w,) = place(down_parts, depth, [(half_ff, width)], spots, down_moves, (down_cut[0],))

    grad_hidden, two_part, two_low = feed_back(grad_out, down_w, slope, up_w)
    down_own, down_give = down_project(activated, down_w, resid, (two_low,))
    down_got = swap(down_give, "c")
    activations = (down_own + down_got.astype(WIDE)).astype(LOW)
    up_grad = weight_grad(normed_two, grad_hidden)
    two_got = swap(two_low, "c")
    deps = (up_grad,)
    if ring:
        down_turn = second_hop_of(*down_hop)
        deps = (up_grad, down_turn[0])
    grad_resid, grad_resid_low, a_low, b_rows, state_grad, norm_two = attend_turn(
        two_part, two_got, resid, rows, grad_out, out_w, mixed, denom, query, deps
    )
    later = from_others(state_grad, -1)
    out_grad = dot_rows(mixed_low, grad_resid_low).astype(LOW)
    deps = ()
    if ring:

        def up_cuts(zz, plane, half):
            cuts = [(0, ((zz * 2 + half) * chips + plane) * own_rows, 0, own_rows, half_ff, 0, 0)]
            row = zz * block + plane * own_rows + half * small
            return cuts + [(1, row, p * half_d, small, half_d, p * small, half_ff) for p in (0, 1)]

        up_cut = unplace([up_grad, out_grad], depth, (own_rows, half_ff + half_d), up_cuts)
        deps = (up_cut[0],)
    grad_projected = attend_back(query, key, value, qk, a_low, b_rows, state_in, later, deps)
    qkv_grad = dot_rows(normed_one, grad_projected).astype(LOW)
    one_part, one_low, norm_cols = project_back(grad_projected, qkv_w, inputs, norm_two)
    input_grad = input_back(one_part, swap(other(halves(one_low)), "c"), grad_resid, own_x, rows)

    out_fan = max(1, width * 64 // (tokens * depth))
    rates = (3.0 * width**-0.5, 3.0 * out_fan**-0.5, 3.0 * width**-0.5, 3.0 * hidden_units**-0.5, 1.5)
    decays = (WEIGHT_DECAY, WEIGHT_DECAY, WEIGHT_DECAY, WEIGHT_DECAY, 0.0)
    masters = (qkv_weight, out_weight, up_weight, down_weight, norm_params)
    firsts = (qkv_first, out_first, up_first, down_first, norm_first)
    seconds = (qkv_second, out_second, up_second, down_second, norm_second)
    if ring:

        def qkv_cuts(zz, plane, half):
            row = ((zz * 2 + half) * chips + plane) * own_rows
            return [(0, row, 0, own_rows, half_qkv, 0, 0), (1, row, 0, own_rows, LANES, 0, half_qkv)]

        hop = swap(down_turn[0], "y"), swap(down_turn[1], "x")
        down_sum = third_hop_of(*down_hop, *hop)
        up_hop = first_hop(*up_cut, (*hop, *later))
        turn = second_hop_of(*up_hop, (*down_sum[1:], grad_projected))
        hop = swap(turn[0], "y"), swap(turn[1], "x")
        up_sum = third_hop_of(*up_hop, *hop)
        qkv_cut = unplace([qkv_grad, norm_cols], depth, (own_rows, half_qkv + LANES), qkv_cuts)
        qkv_hop = first_hop(*qkv_cut, hop)
        turn = second_hop_of(*qkv_hop)
        hop = swap(turn[0], "y"), swap(turn[1], "x")
        qkv_sum = third_hop_of(*qkv_hop, *hop, up_sum[1:])
        down_red, squares = finish_down(down_sum)
        up_mine, up_give, out_red, squares = finish_up(up_sum, squares, own_rows, half_ff)
        up_mate = swap(up_give, "c")
        deps = (input_grad, activations, up_mate)
        qkv_mine, qkv_give, small_mine = finish_qkv(qkv_sum, squares, own_rows, half_qkv, deps)
        small_mate, qkv_mate = swap(small_mine, "c"), swap(qkv_give, "c")
        squares, norm_sum = chip_squares(small_mine, small_mate)
        norm_red = mine(norm_sum.reshape(2, own_rows, LANES))[:, :4].T
        grads = (qkv_mine, qkv_mate, out_red, up_mine, up_mate, down_red, norm_red)
        *news, grad_norm = update_all(
            grads, sum_chips(squares), masters, firsts, seconds, rates, decays, (3 * depth, depth)
        )
        return (
            activations.reshape(count, group, width),
            input_grad.reshape(count, group, width),
            grad_norm.reshape(()),
            *news,
        )
    scatter = lambda g: lax.psum_scatter(g, ALL, scatter_dimension=0, tiled=True)
    both = lambda a, axis: jnp.stack([jnp.where(core == k, a, 0.0) for k in (0, 1)], axis)
    to_all = lambda a: a.astype(WIDE)
    qkv_red = scatter(both(to_all(qkv_grad).reshape(width, 3 * depth, block), 2).reshape(width, -1))
    up_red = scatter(both(to_all(up_grad).reshape(width, depth, ff_block), 2).reshape(width, -1))
    out_red = scatter(both(to_all(out_grad).reshape(depth, block, width), 1).reshape(width, width))
    down_red = scatter(both(to_all(down_grad).reshape(depth, ff_block, width), 1).reshape(hidden_units, width))
    norm_red = scatter(norm_cols.astype(WIDE))[:, :4].T

    reduced = (qkv_red, out_red, up_red, down_red, norm_red)
    local_squares = sum(jnp.sum(grad * grad) for grad in reduced)
    grad_norm = jnp.sqrt(lax.psum(local_squares, ALL))
    clip = jnp.minimum(1.0, CLIP_LIMIT / (grad_norm + 1e-06))
    news = [
        adam_update(masters[k], firsts[k], seconds[k], clip * reduced[k], rates[k], decays[k]) for k in range(5)
    ]
    return (
        activations.reshape(count, group, width),
        input_grad.reshape(count, group, width),
        grad_norm,
        *[new[0] for new in news],
        *[new[1] for new in news],
        *[new[2] for new in news],
    )


def solution(mesh):
    depth, planes = mesh.shape["seq"] // 2, mesh.shape["img"]
    across = max(k for k in range(1, planes + 1) if planes % k == 0 and k * k <= planes)
    grid = jax.sharding.Mesh(mesh.devices.reshape(depth, 2, planes // across, across), ALL)
    tokens = P(("y", "x"), ("z", "c"), None)
    matrix, norm = P(ALL, None), P(None, ALL)
    state = (matrix, matrix, matrix, matrix, norm)
    return jax.shard_map(
        body,
        mesh=grid,
        in_specs=(tokens, tokens) + state * 3,
        out_specs=(tokens, tokens, P()) + state * 3,
        check_vma=False,
    )
```

```python
import functools

import jax
import jax.numpy as jnp
from jax import lax
from jax.experimental import pallas as pl
from jax.experimental.pallas import tpu as pltpu
from jax.sharding import PartitionSpec as P

HEAD_DIM = 64
STEP = 10
NORM_EPS = 1e-05
BETA_ONE = 0.9
BETA_TWO = 0.999
ADAM_EPS = 1e-08
WEIGHT_DECAY = 0.1
CLIP_LIMIT = 1.0
LANES = 128

LOW = jnp.bfloat16
WIDE = jnp.float32
ALL = ("z", "c", "y", "x")
SWAP = [(0, 1), (1, 0)]


def swap(value, axis):
    return lax.ppermute(value, axis, SWAP)


def shift(value, step, wrap=True):
    size = lax.axis_size("z")
    pairs = [(i, (i + step) % size) for i in range(size) if wrap or 0 <= i + step < size]
    return lax.ppermute(value, "z", pairs)


def mine(pair_axis_first):
    return jnp.where(lax.axis_index("c") == 0, pair_axis_first[0], pair_axis_first[1])


def other(pair_axis_first):
    return jnp.where(lax.axis_index("c") == 0, pair_axis_first[1], pair_axis_first[0])


def in_order(own, mate, axis=0):
    first = lax.axis_index("c") == 0
    return jnp.concatenate([jnp.where(first, own, mate), jnp.where(first, mate, own)], axis)


def after(value, *before):
    return lax.optimization_barrier((*before, value))[-1]


def column_first(shard):
    return [shard] + [shift(shard, k) for k in range(1, lax.axis_size("z"))]


def plane_last(column, between=()):
    half = column.shape[0] // 2
    along_x, along_y = swap(column, "x"), swap(column, "y")
    along_x, along_y = after(along_x, *between), after(along_y, *between)
    far = (swap(along_y[:half], "x"), swap(along_x[half:], "y"))
    return (column, along_x, along_y) + far


def plane_first(shard):
    far = lax.ppermute(shard, ("y", "x"), [(i, 3 - i) for i in range(4)])
    return jnp.concatenate([shard, swap(shard, "x"), swap(shard, "y"), far])


def column_last(plane):
    parts = [plane]
    for _ in range(1, lax.axis_size("z")):
        parts.append(shift(parts[-1], 1))
    return parts


def column_first_spots(depth):
    half = depth // 2
    spots = [(0, (k,), 0, (k, 0, 0), 0) for k in range(depth)]
    spots += [(1, (k,), 0, (k, 0, 1), 0) for k in range(depth)]
    spots += [(2, (k,), 0, (k, 1, 0), 0) for k in range(depth)]
    spots += [(3, (k,), 0, (k, 1, 1), 0) for k in range(half)]
    return spots + [(4, (k - half,), 0, (k, 1, 1), 0) for k in range(half, depth)]


def plane_first_spots(depth, rows, base):
    return [(base + k, (), p * rows, (k, p // 2, p % 2), 1) for k in range(depth) for p in range(4)]


def first_hop(send_x, keep_x, send_y, keep_y, before=()):
    return keep_x, swap(after(send_x, *before), "x"), keep_y, swap(after(send_y, *before), "y")


def second_hop_of(keep_x, got_x, keep_y, got_y, deps=()):
    depth, rows, cols = keep_x.shape[1:]

    def second_hop(kx, gx, ky, gy, to_y, to_x):
        to_y[...] = (kx[1].astype(WIDE) + gx[1].astype(WIDE)).astype(LOW)
        to_x[...] = (ky[1].astype(WIDE) + gy[1].astype(WIDE)).astype(LOW)

    outs = [((depth, rows, cols), LOW)] * 2
    return run(second_hop, outs, keep_x, got_x, keep_y, got_y, scalars=False, deps=deps)


def third_hop_of(keep_x, got_x, keep_y, got_y, on_y, on_x, deps=()):
    depth, rows, cols = keep_x.shape[1:]

    def third_hop(kx, gx, ky, gy, ony, onx, own, *sends):
        for k in range(depth):
            one = kx[0, k].astype(WIDE) + gx[0, k].astype(WIDE) + ony[k].astype(WIDE)
            two = ky[0, k].astype(WIDE) + gy[0, k].astype(WIDE) + onx[k].astype(WIDE)
            out = sends[k - 1] if k else own
            out[:rows, :] = one.astype(out.dtype)
            out[rows:, :] = two.astype(out.dtype)

    outs = [((2 * rows, cols), WIDE if k == 0 else LOW) for k in range(depth)]
    own, *sends = run(third_hop, outs, keep_x, got_x, keep_y, got_y, on_y, on_x, scalars=False, deps=deps)
    return [own] + [shift(part, k + 1) for k, part in enumerate(sends)]


def sum_of(refs):
    total = refs[0][...]
    for ref in refs[1:]:
        total = total + ref[...].astype(WIDE)
    return total


def spread(value):
    return jnp.broadcast_to(value, (8, LANES))


def total_squares(value):
    return jnp.sum(jnp.sum(value * value, axis=1, keepdims=True), axis=0, keepdims=True)


def finish_down(parts):
    def kernel(*refs):
        total = sum_of(refs[: len(parts)])
        refs[-2][...] = total
        refs[-1][...] = spread(total_squares(total))

    return run(kernel, [(parts[0].shape, WIDE), ((8, LANES), WIDE)], *parts, scalars=False)


def finish_up(parts, squares, rows, half_ff):
    half_d = parts[0].shape[1] - half_ff
    small = rows // 2

    def kernel(coords, squares_ref, *refs):
        own_ref, mate_ref, out_ref, total_ref, all_ref = refs[len(parts) :]
        total = sum_of(refs[: len(parts)])
        all_ref[...] = total
        core = coords[3]
        own_ref[...] = all_ref[pl.ds(pl.multiple_of(core * rows, 8), rows), :half_ff]
        mate_ref[...] = all_ref[pl.ds(pl.multiple_of((1 - core) * rows, 8), rows), :half_ff]
        for p in range(2):
            for h in range(2):
                block = total[h * rows + p * small : h * rows + (p + 1) * small, half_ff:]
                out_ref[h * small : (h + 1) * small, p * half_d : (p + 1) * half_d] = block
        total_ref[...] = squares_ref[...] + spread(total_squares(total))

    outs = [((rows, half_ff), WIDE)] * 2 + [((rows, 2 * half_d), WIDE), ((8, LANES), WIDE)]
    scratch = [pltpu.VMEM(parts[0].shape, WIDE)]
    return run(kernel, outs, squares, *parts, scratch=scratch)


def finish_qkv(parts, squares, rows, half_qkv, deps=()):
    def kernel(coords, squares_ref, *refs):
        own_ref, mate_ref, small_ref, all_ref = refs[len(parts) :]
        total = sum_of(refs[: len(parts)])
        all_ref[...] = total
        core = coords[3]
        own_ref[...] = all_ref[pl.ds(pl.multiple_of(core * rows, 8), rows), :half_qkv]
        mate_ref[...] = all_ref[pl.ds(pl.multiple_of((1 - core) * rows, 8), rows), :half_qkv]
        small_ref[: 2 * rows, :] = total[:, half_qkv:]
        small_ref[2 * rows :, :] = squares_ref[...] + spread(total_squares(total[:, :half_qkv]))

    outs = [((rows, half_qkv), WIDE)] * 2 + [((2 * rows + 8, LANES), WIDE)]
    scratch = [pltpu.VMEM(parts[0].shape, WIDE)]
    return run(kernel, outs, squares, *parts, scratch=scratch, deps=deps)


def chip_squares(small, got):
    rows = small.shape[0] - 8

    def kernel(small_ref, got_ref, total_ref, norm_ref):
        total = small_ref[...] + got_ref[...]
        norm_ref[...] = total[:rows]
        total_ref[...] = total[rows:] + spread(total_squares(total[:rows]))

    outs = [((8, LANES), WIDE), ((rows, LANES), WIDE)]
    return run(kernel, outs, small, got, scalars=False)


def sum_chips(value):
    across = lax.ppermute(value, ("y", "x"), [(i, 3 - i) for i in range(4)])
    value = value + swap(value, "y") + (swap(value, "x") + across)
    size, near = lax.axis_size("z"), 1
    while near < size // 2:
        value = value + lax.ppermute(value, "z", [(i, i ^ near) for i in range(size)])
        near *= 2
    return [value, lax.ppermute(value, "z", [(i, i ^ near) for i in range(size)])]


def interleave(first, own, mate, blocks):
    size = own.shape[1] // blocks
    pieces = []
    for j in range(blocks):
        at = slice(j * size, (j + 1) * size)
        pieces += [jnp.where(first, own[:, at], mate[:, at]), jnp.where(first, mate[:, at], own[:, at])]
    return jnp.concatenate(pieces, axis=1)


def update_all(grads, totals, masters, firsts, seconds, rates, decays, blocks):
    steps = 2
    n, m = len(grads), len(totals)

    def tile(array):
        rows, cols = array.shape
        return pl.BlockSpec((rows // steps, cols), lambda i: (i, 0))

    def whole(array):
        return pl.BlockSpec(array.shape, lambda i: (0, 0))

    def kernel(coords, *refs):
        first = coords[3] == 0
        g, t, old, new = refs[:n], refs[n : n + m], refs[n + m : n + m + 15], refs[n + m + 15 :]
        total = sum_of(t)[0:1, 0:1]
        norm = jnp.sqrt(total)
        clip = jnp.minimum(1.0, CLIP_LIMIT / (norm + 1e-06))
        qkv = interleave(first, g[0][...], g[1][...], blocks[0])
        up = interleave(first, g[3][...], g[4][...], blocks[1])
        for k, grad in enumerate((qkv, g[2][...], up, g[5][...], g[6][...])):
            news = adam_update(old[k][...], old[5 + k][...], old[10 + k][...], clip * grad, rates[k], decays[k])
            for part in range(3):
                new[5 * part + k][...] = news[part]
        new[15][...] = norm

    state = (*masters, *firsts, *seconds)
    specs = [whole(a) if k % 5 == 4 else tile(a) for k, a in enumerate(state)]
    norm_out = jax.ShapeDtypeStruct((1, 1), WIDE)
    return pl.pallas_call(
        kernel,
        grid=(steps,),
        out_shape=[jax.ShapeDtypeStruct(a.shape, WIDE) for a in state] + [norm_out],
        in_specs=[pl.BlockSpec(memory_space=pltpu.SMEM)]
        + [tile(a) for a in grads[:-1]]
        + [whole(grads[-1])]
        + [whole(a) for a in totals]
        + specs,
        out_specs=specs + [whole(norm_out)],
        compiler_params=FULL,
    )(coordinates(), *grads, *totals, *state)


def coordinates():
    return jnp.stack([lax.axis_index(name) for name in ("z", "y", "x", "c")]).astype(jnp.int32)


def chip_of(coords, rel, depth, back):
    dz, dy, dx = rel
    z, y, x = coords[0], coords[1], coords[2]
    zz = lax.rem(z + (depth - dz if back else dz), depth)
    yy = 1 - y if dy else y
    xx = 1 - x if dx else x
    return zz, yy * 2 + xx


def window(row, rows, col, cols):
    rows_at = pl.ds(row if isinstance(row, int) else pl.multiple_of(row, 16), rows)
    return rows_at, pl.ds(col, cols)


VMEM = pl.BlockSpec(memory_space=pltpu.VMEM)
ROOM_MB = 16
ROOM = pltpu.CompilerParams(vmem_limit_bytes=ROOM_MB * 1024 * 1024)
FULL = pltpu.CompilerParams(vmem_limit_bytes=56 * 1024 * 1024)


def place(parts, depth, outs, spots, moves, deps=()):
    def kernel(coords, *refs):
        ins, out_refs = refs[: len(parts)], refs[len(parts) + len(deps) :]
        for array, lead, base, rel, piece in spots:
            zz, plane = chip_of(coords, rel, depth, True)
            for o, sr, sc, rows, cols, tr, tc in moves(zz, plane, piece):
                out_refs[o][window(tr, rows, tc, cols)] = ins[array][(*lead, *window(base + sr, rows, sc, cols))]

    return pl.pallas_call(
        kernel,
        out_shape=[jax.ShapeDtypeStruct(s, LOW) for s in outs],
        in_specs=[pl.BlockSpec(memory_space=pltpu.SMEM)]
        + [VMEM] * len(parts)
        + [pl.BlockSpec(memory_space=pl.ANY)] * len(deps),
        out_specs=[VMEM] * len(outs),
        compiler_params=ROOM,
    )(coordinates(), *parts, *deps)


def unplace(grads, depth, rows_cols, moves):
    spots = []
    for dz in range(depth):
        for d in range(2):
            spots += [(0, d, dz, (dz, d, 1), 0), (1, d, dz, (dz, d, 0), 0)]
            spots += [(2, d, dz, (dz, 1, d), 1), (3, d, dz, (dz, 0, d), 1)]

    def kernel(coords, *refs):
        ins, out_refs = refs[: len(grads)], refs[len(grads) :]
        for array, d, dz, rel, half in spots:
            zz, plane = chip_of(coords, rel, depth, False)
            for i, sr, sc, rows, cols, tr, tc in moves(zz, plane, half):
                out_refs[array][(d, dz, *window(tr, rows, tc, cols))] = ins[i][window(sr, rows, sc, cols)]

    return pl.pallas_call(
        kernel,
        out_shape=[jax.ShapeDtypeStruct((2, depth) + rows_cols, LOW)] * 4,
        in_specs=[pl.BlockSpec(memory_space=pltpu.SMEM)] + [VMEM] * len(grads),
        out_specs=[VMEM] * 4,
        compiler_params=ROOM,
    )(coordinates(), *grads)


def cast_qkv(qkv, norm, halves):
    rows, cols = qkv.shape
    wide = cols // 2 + LANES
    block = cols // (2 * halves)

    def kernel(coords, qkv_ref, norm_ref, own_ref, mate_ref, tall):
        first = coords[3] == 0
        for j in range(halves):
            a = qkv_ref[:, 2 * j * block : (2 * j + 1) * block]
            b = qkv_ref[:, (2 * j + 1) * block : (2 * j + 2) * block]
            own_ref[:, j * block : (j + 1) * block] = jnp.where(first, a, b).astype(LOW)
            mate_ref[:, j * block : (j + 1) * block] = jnp.where(first, b, a).astype(LOW)
        tall[...] = jnp.zeros_like(tall)
        tall[0:4, :] = norm_ref[...].astype(LOW).astype(WIDE)
        i = lax.broadcasted_iota(jnp.int32, (rows, rows), 0)
        j = lax.broadcasted_iota(jnp.int32, (rows, rows), 1)
        columns = dot_cols((i == j).astype(LOW), tall[...].astype(LOW)).astype(LOW)
        own_ref[:, cols // 2 :] = columns
        mate_ref[:, cols // 2 :] = columns

    return pl.pallas_call(
        kernel,
        out_shape=[jax.ShapeDtypeStruct((rows, wide), LOW)] * 2,
        in_specs=[pl.BlockSpec(memory_space=pltpu.SMEM), VMEM, VMEM],
        out_specs=[VMEM] * 2,
        scratch_shapes=[pltpu.VMEM((LANES, rows), WIDE)],
        compiler_params=ROOM,
    )(coordinates(), qkv, norm)


def cast_down(down):
    half = down.shape[0] // 2

    def kernel(down_ref, one_ref, two_ref):
        one_ref[...] = down_ref[:half, :].astype(LOW)
        two_ref[...] = down_ref[half:, :].astype(LOW)

    return pl.pallas_call(
        kernel,
        out_shape=[jax.ShapeDtypeStruct((half, down.shape[1]), LOW)] * 2,
        in_specs=[VMEM],
        out_specs=[VMEM] * 2,
        compiler_params=ROOM,
    )(down)


def cast_rest(up, out, halves):
    rows, cols = up.shape
    block, width = cols // (2 * halves), out.shape[1]

    def kernel(coords, up_ref, out_ref, own_ref, mate_ref, part_ref):
        first = coords[3] == 0
        for j in range(halves):
            a = up_ref[:, 2 * j * block : (2 * j + 1) * block]
            b = up_ref[:, (2 * j + 1) * block : (2 * j + 2) * block]
            own_ref[:, j * block : (j + 1) * block] = jnp.where(first, a, b).astype(LOW)
            mate_ref[:, j * block : (j + 1) * block] = jnp.where(first, b, a).astype(LOW)
        part_ref[:rows, :] = out_ref[:, : width // 2].astype(LOW)
        part_ref[rows:, :] = out_ref[:, width // 2 :].astype(LOW)

    return pl.pallas_call(
        kernel,
        out_shape=[jax.ShapeDtypeStruct((rows, cols // 2), LOW)] * 2
        + [jax.ShapeDtypeStruct((2 * rows, width // 2), LOW)],
        in_specs=[pl.BlockSpec(memory_space=pltpu.SMEM), VMEM, VMEM],
        out_specs=[VMEM] * 3,
        compiler_params=ROOM,
    )(coordinates(), up, out)


def join_rows(own, mate, side=None):
    rows, cols = own.shape
    wide = cols + (side.shape[1] if side is not None else 0)

    def kernel(coords, own_ref, mate_ref, *refs):
        out_ref = refs[-1]
        core = coords[3]
        out_ref[pl.ds(pl.multiple_of(core * rows, 16), rows), :cols] = own_ref[...]
        out_ref[pl.ds(pl.multiple_of((1 - core) * rows, 16), rows), :cols] = mate_ref[...]
        if side is not None:
            out_ref[:, cols:] = refs[0][...]

    ins = [own, mate] + ([side] if side is not None else [])
    return pl.pallas_call(
        kernel,
        out_shape=jax.ShapeDtypeStruct((2 * rows, wide), LOW),
        in_specs=[pl.BlockSpec(memory_space=pltpu.SMEM)] + [VMEM] * len(ins),
        out_specs=VMEM,
        compiler_params=ROOM,
    )(coordinates(), *ins)


def run(kernel, outs, *ins, scalars=True, scratch=(), flops=0, room=ROOM_MB, deps=()):
    first = len(ins) + scalars

    def body_of(*refs):
        return kernel(*refs[:first], *refs[first + len(deps) :])

    out_shape = [jax.ShapeDtypeStruct(shape, kind) for shape, kind in outs]
    return pl.pallas_call(
        body_of,
        out_shape=out_shape,
        in_specs=([pl.BlockSpec(memory_space=pltpu.SMEM)] if scalars else [])
        + [VMEM] * len(ins)
        + [pl.BlockSpec(memory_space=pl.ANY)] * len(deps),
        out_specs=[VMEM] * len(outs),
        scratch_shapes=list(scratch),
        compiler_params=pltpu.CompilerParams(vmem_limit_bytes=room * 1024 * 1024),
        cost_estimate=pl.CostEstimate(flops=flops, bytes_accessed=0, transcendentals=0),
    )(*([coordinates()] if scalars else []), *ins, *deps)


def dot(left, right):
    return jnp.dot(left, right, preferred_element_type=WIDE)


def dot_rows(left, right):
    return lax.dot_general(left, right, (((0,), (0,)), ((), ())), preferred_element_type=WIDE)


def dot_cols(left, right):
    return lax.dot_general(left, right, (((1,), (1,)), ((), ())), preferred_element_type=WIDE)


def eye(rows, cols):
    i = lax.broadcasted_iota(jnp.int32, (rows, cols), 0)
    return (i == lax.broadcasted_iota(jnp.int32, (rows, cols), 1)).astype(LOW)


def normalise(values):
    center = values - jnp.mean(values, axis=-1, keepdims=True)
    rate = lax.rsqrt(jnp.mean(center * center, axis=-1, keepdims=True) + NORM_EPS)
    return center * rate, rate


def norm_back(normed, rate, grad, gain):
    scaled = grad * gain
    shared = jnp.mean(scaled, axis=-1, keepdims=True)
    along = jnp.mean(scaled * normed, axis=-1, keepdims=True)
    return rate * (scaled - shared - normed * along)


def low_lanes(rows):
    return lax.broadcasted_iota(jnp.int32, (rows, LANES), 1) < HEAD_DIM


def by_head(pair):
    wide = pair.astype(WIDE)
    first = low_lanes(pair.shape[0])
    return jnp.where(first, wide, 0.0).astype(LOW), jnp.where(first, 0.0, wide).astype(LOW)


def pack_state(square):
    first = low_lanes(HEAD_DIM)
    return jnp.where(first, square[:HEAD_DIM], square[HEAD_DIM:])


def open_state(packed):
    first = low_lanes(HEAD_DIM)
    return jnp.concatenate([jnp.where(first, packed, 0.0), jnp.where(first, 0.0, packed)])


def feature(values):
    return jnp.where(values > 0.0, values + 1.0, jnp.exp(jnp.minimum(values, 0.0)))


def project(x, norm_w, qkv_w):
    tokens, width = x.shape
    half = qkv_w.shape[1] // 3
    pairs = half // LANES
    step = tokens // 2

    def kernel(x_ref, norm_ref, w_ref, rows_ref, normed_ref, qk_ref, q_ref, k_ref, v_ref, state_ref, sums):
        rows_ref[...] = dot_cols(eye(8, LANES), norm_ref[...])
        gain, bias = rows_ref[0:1, :], rows_ref[1:2, :]
        @pl.loop(0, 2)
        def _(i):
            at = at_block(i, step)
            normed = normalise(x_ref[at, :].astype(WIDE))[0]
            normed_ref[at, :] = (normed * gain + bias).astype(LOW)
            low = normed_ref[at, :]
            for j, out in enumerate((q_ref, k_ref)):
                part = dot(low, w_ref[:, j * half : (j + 1) * half])
                qk_ref[at, j * half : (j + 1) * half] = part
                out[at, :] = feature(part).astype(LOW)
            v_ref[at, :] = dot(low, w_ref[:, 2 * half :]).astype(LOW)
        total = dot_rows(jnp.ones((tokens, 8), LOW), k_ref[...])
        sums[...] = jnp.zeros_like(sums)
        for p in range(pairs):
            lanes = slice(p * LANES, (p + 1) * LANES)
            packed = pack_state(dot_rows(k_ref[:, lanes], v_ref[:, lanes]))
            state_ref[p * HEAD_DIM : (p + 1) * HEAD_DIM, :] = packed.astype(LOW)
            sums[p : p + 1, :] = total[0:1, lanes]
        state_ref[pairs * HEAD_DIM :, :] = sums[...].astype(LOW)

    outs = [((8, width), WIDE), ((tokens, width), LOW), ((tokens, 2 * half), WIDE)] + [((tokens, half), LOW)] * 3
    outs += [((pairs * HEAD_DIM + 16, LANES), LOW)]
    scratch = [pltpu.VMEM((16, LANES), WIDE)]
    return run(kernel, outs, x, norm_w, qkv_w, scalars=False, scratch=scratch)


def at_block(index, size):
    return pl.ds(pl.multiple_of(index * size, size), size)


def total_state(refs):
    total = refs[0][...].astype(WIDE)
    for ref in refs[1:]:
        total = total + ref[...].astype(WIDE)
    return total


def causal_mask(step):
    i = lax.broadcasted_iota(jnp.int32, (step, step), 0)
    return i >= lax.broadcasted_iota(jnp.int32, (step, step), 1)


def attend(query, key, value, parts, deps=()):
    tokens, half = query.shape
    pairs, step = half // LANES, tokens // 2

    def kernel(q_ref, k_ref, v_ref, *refs):
        mixed_ref, low_ref, denom_ref, state_ref, token_ref = refs[len(parts) :]
        token_ref[...] = jnp.zeros_like(token_ref)
        state_ref[...] = total_state(refs[: len(parts)])
        lower = causal_mask(step)
        first = low_lanes(step)
        top = low_lanes(HEAD_DIM)
        diagonal = eye(LANES, LANES).astype(WIDE)
        @pl.loop(0, pairs)
        def _(p):
            lanes = at_block(p, LANES)
            packed = state_ref[at_block(p, HEAD_DIM), :]
            sums = state_ref[pl.ds(pairs * HEAD_DIM + p, 1), :]
            column = jnp.sum(diagonal * sums, axis=1, keepdims=True)
            zero = jnp.zeros((HEAD_DIM, LANES), WIDE)
            ext = (
                jnp.concatenate([jnp.where(top, packed, column[:HEAD_DIM]), zero]).astype(LOW),
                jnp.concatenate([zero, jnp.where(top, column[HEAD_DIM:], packed)]).astype(LOW),
            )
            wide = v_ref[:, lanes].astype(WIDE)
            full = low_lanes(tokens)
            value_ext = (jnp.where(full, wide, 1.0).astype(LOW), jnp.where(full, 1.0, wide).astype(LOW))
            queries = by_head(q_ref[:, lanes])
            for i in range(2):
                at = slice(i * step, (i + 1) * step)
                got = []
                for h in range(2):
                    rows = queries[h][at]
                    total = dot(rows, ext[h])
                    for j in range(i + 1):
                        to = slice(j * step, (j + 1) * step)
                        scores = dot_cols(rows, k_ref[to, lanes])
                        if j == i:
                            scores = jnp.where(lower, scores, 0.0)
                        total = total + dot(scores.astype(LOW), value_ext[h][to])
                    got.append(total)
                denom = pltpu.roll(jnp.where(first, got[1], got[0]), HEAD_DIM, 1)
                mixed = jnp.where(first, got[0], got[1]) / denom
                mixed_ref[at, lanes] = mixed
                low_ref[at, lanes] = mixed.astype(LOW)
                denom_ref[at, lanes] = denom

    outs = [((tokens, half), WIDE), ((tokens, half), LOW), ((tokens, half), WIDE), (parts[0].shape, WIDE)]
    outs += [((8, LANES), WIDE)]
    return run(kernel, outs, query, key, value, *parts, scalars=False, deps=deps)


def out_project(mixed, out_w):
    def kernel(mixed_ref, w_ref, part_ref, low_ref):
        part = dot(mixed_ref[...], w_ref[...])
        part_ref[...] = part
        low_ref[...] = part.astype(LOW)

    shape = (mixed.shape[0], out_w.shape[1])
    return run(kernel, [(shape, WIDE), (shape, LOW)], mixed, out_w, scalars=False)


def feed(x, part, got, rows, up_w):
    tokens, width = x.shape
    units, step, cut = up_w.shape[1], tokens // 2, 512

    def kernel(x_ref, part_ref, got_ref, rows_ref, w_ref, resid_ref, normed_ref, act_ref, slope_ref):
        @pl.loop(0, 2)
        def _(i):
            at = at_block(i, step)
            resid = x_ref[at, :].astype(WIDE) + part_ref[at, :] + got_ref[at, :].astype(WIDE)
            resid_ref[at, :] = resid
            normed_ref[at, :] = (normalise(resid)[0] * rows_ref[2:3, :] + rows_ref[3:4, :]).astype(LOW)

        @pl.loop(0, units // cut)
        def _(j):
            to = at_block(j, cut)
            v = dot(normed_ref[...], w_ref[:, to])
            root = (2.0 / 3.141592653589793) ** 0.5
            square = v * v
            bend = jnp.tanh(root * v * (1.0 + 0.044715 * square))
            cdf = 0.5 * (1.0 + bend)
            act_ref[:, to] = (v * cdf).astype(LOW)
            slope_ref[:, to] = cdf + 0.5 * v * (1.0 - bend * bend) * (root * (1.0 + 3.0 * 0.044715 * square))

    outs = [((tokens, width), WIDE), ((tokens, width), LOW), ((tokens, units), LOW), ((tokens, units), WIDE)]
    return run(kernel, outs, x, part, got, rows, up_w, scalars=False)


def feed_back(grad_out, down_w, slope, up_w):
    tokens, width = grad_out.shape
    units, cut = up_w.shape[1], 512

    def kernel(g_ref, down_ref, slope_ref, up_ref, hidden_ref, part_ref, low_ref):
        @pl.loop(0, units // cut)
        def _(j):
            to = at_block(j, cut)
            hidden_ref[:, to] = (dot_cols(g_ref[...], down_ref[to, :]) * slope_ref[:, to]).astype(LOW)

        @pl.loop(0, width // cut)
        def _(j):
            to = at_block(j, cut)
            part = dot_cols(hidden_ref[...], up_ref[to, :])
            part_ref[:, to] = part
            low_ref[:, to] = part.astype(LOW)

    outs = [((tokens, units), LOW), ((tokens, width), WIDE), ((tokens, width), LOW)]
    return run(kernel, outs, grad_out, down_w, slope, up_w, scalars=False)


def down_project(activated, down_w, resid, deps):
    tokens, width = resid.shape
    group, cut = tokens // 2, width // 2

    def kernel(coords, act_ref, w_ref, resid_ref, own_ref, give_ref):
        own = pl.ds(pl.multiple_of(coords[3] * group, 16), group)
        mate = pl.ds(pl.multiple_of((1 - coords[3]) * group, 16), group)

        @pl.loop(0, 2)
        def _(j):
            to = at_block(j, cut)
            own_ref[:, to] = resid_ref[own, to] + dot(act_ref[own, :], w_ref[:, to])
            give_ref[:, to] = dot(act_ref[mate, :], w_ref[:, to]).astype(LOW)

    outs = [((group, width), WIDE), ((group, width), LOW)]
    return run(kernel, outs, activated, down_w, resid, deps=deps)


def weight_grad(rows, grad, deps=()):
    tokens, width = rows.shape
    units, cut = grad.shape[1], 512

    def kernel(rows_ref, grad_ref, out_ref):
        @pl.loop(0, units // cut)
        def _(j):
            to = at_block(j, cut)
            out_ref[:, to] = dot_rows(rows_ref[...], grad_ref[:, to]).astype(LOW)

    return run(kernel, [((width, units), LOW)], rows, grad, scalars=False, deps=deps)[0]


def attend_turn(part, got, resid, rows, grad_out, out_w, mixed, denom, query, deps):
    tokens, width = resid.shape
    half = mixed.shape[1]
    pairs, step = half // LANES, tokens // 2

    def kernel(
        part_ref, got_ref, resid_ref, rows_ref, g_ref, w_ref, mixed_ref, denom_ref, q_ref,
        grad_ref, low_ref, a_ref, b_ref, state_ref, norm_ref, sums,
    ):
        gain = rows_ref[2:3, :]
        first = low_lanes(step)
        norm_ref[...] = jnp.zeros_like(norm_ref)

        @pl.loop(0, 2)
        def _(i):
            at = at_block(i, step)
            normed, rate = normalise(resid_ref[at, :])
            own = part_ref[at, :]
            norm_ref[0:1, :] += jnp.sum(own * normed, axis=0, keepdims=True)
            norm_ref[1:2, :] += jnp.sum(own, axis=0, keepdims=True)
            grad = g_ref[at, :].astype(WIDE) + norm_back(normed, rate, own + got_ref[at, :].astype(WIDE), gain)
            grad_ref[at, :] = grad
            low_ref[at, :] = grad.astype(LOW)
            turned = dot_cols(low_ref[at, :], w_ref[...]) / denom_ref[at, :]
            a_ref[at, :] = turned.astype(LOW)
            along = turned * mixed_ref[at, :]
            for p in range(pairs):
                lanes = slice(p * LANES, (p + 1) * LANES)
                piece = along[:, lanes]
                low = jnp.sum(jnp.where(first, piece, 0.0), axis=1, keepdims=True)
                high = jnp.sum(jnp.where(first, 0.0, piece), axis=1, keepdims=True)
                b_ref[at, lanes] = -jnp.where(first, low, high)
        sums[...] = jnp.zeros_like(sums)
        for p in range(pairs):
            lanes = slice(p * LANES, (p + 1) * LANES)
            packed = pack_state(dot_rows(q_ref[:, lanes], a_ref[:, lanes]))
            state_ref[p * HEAD_DIM : (p + 1) * HEAD_DIM, :] = packed.astype(LOW)
            sums[p : p + 1, :] = jnp.sum(q_ref[:, lanes].astype(WIDE) * b_ref[:, lanes], axis=0, keepdims=True)
        state_ref[pairs * HEAD_DIM :, :] = sums[...].astype(LOW)

    outs = [((tokens, width), WIDE), ((tokens, width), LOW), ((tokens, half), LOW), ((tokens, half), WIDE)]
    outs += [((pairs * HEAD_DIM + 16, LANES), LOW), ((2, width), WIDE)]
    ins = (part, got, resid, rows, grad_out, out_w, mixed, denom, query)
    scratch = [pltpu.VMEM((16, LANES), WIDE)]
    return run(kernel, outs, *ins, scalars=False, scratch=scratch, deps=deps)


def attend_back(query, key, value, qk, a_low, b_rows, state, parts, deps=()):
    tokens, half = query.shape
    pairs, step = half // LANES, tokens // 2

    def kernel(q_ref, k_ref, v_ref, qk_ref, a_ref, b_ref, state_ref, *refs):
        out_ref, later = refs[len(parts) :]
        later[...] = total_state(refs[: len(parts)])
        lower = causal_mask(step)
        @pl.loop(0, pairs)
        def _(p):
            lanes, rows = at_block(p, LANES), at_block(p, HEAD_DIM)
            sums = pl.ds(pairs * HEAD_DIM + p, 1)
            before, after_it = open_state(state_ref[rows, :]).astype(LOW), open_state(later[rows, :]).astype(LOW)
            queries, keys, pulls = by_head(q_ref[:, lanes]), by_head(k_ref[:, lanes]), by_head(a_ref[:, lanes])
            cuts = [slice(i * step, (i + 1) * step) for i in range(2)]
            grad_q = [dot_cols(a_ref[c, lanes], before) + b_ref[c, lanes] * state_ref[sums, :] for c in cuts]
            grad_k = [dot_cols(v_ref[c, lanes], after_it) + later[sums, :] for c in cuts]
            shifts = b_ref[:, lanes]
            grad_v = [dot(k_ref[c, lanes], after_it) for c in cuts]
            for i in range(2):
                for j in range(i + 1):
                    for h in range(2):
                        q, a = queries[h][cuts[i]], pulls[h][cuts[i]]
                        b = shifts[cuts[i], h * HEAD_DIM : h * HEAD_DIM + 1]
                        scores = dot_cols(q, k_ref[cuts[j], lanes])
                        pull = dot_cols(a, v_ref[cuts[j], lanes]) + b
                        if j == i:
                            scores, pull = jnp.where(lower, scores, 0.0), jnp.where(lower, pull, 0.0)
                        scores, pull = scores.astype(LOW), pull.astype(LOW)
                        grad_q[i] = grad_q[i] + dot(pull, keys[h][cuts[j]])
                        grad_k[j] = grad_k[j] + dot_rows(pull, q)
                        grad_v[j] = grad_v[j] + dot_rows(scores, a)
            for i, c in enumerate(cuts):
                for n, grad in enumerate((grad_q[i], grad_k[i])):
                    at = at_block(n * pairs + p, LANES)
                    raw = qk_ref[c, at]
                    out_ref[c, at] = (grad * jnp.where(raw > 0.0, 1.0, jnp.exp(jnp.minimum(raw, 0.0)))).astype(LOW)
                out_ref[c, at_block(2 * pairs + p, LANES)] = grad_v[i].astype(LOW)

    ins = (query, key, value, qk, a_low, b_rows, state, *parts)
    scratch = [pltpu.VMEM(parts[0].shape, WIDE)]
    return run(kernel, [((tokens, 3 * half), LOW)], *ins, scalars=False, scratch=scratch, deps=deps)[0]


def project_back(grad, qkv_w, x, norm_two):
    tokens, width = x.shape
    step = tokens // 2

    def kernel(grad_ref, w_ref, x_ref, two_ref, part_ref, low_ref, cols_ref, rows):
        rows[...] = jnp.zeros_like(rows)

        @pl.loop(0, 2)
        def _(i):
            at = at_block(i, step)
            part = dot_cols(grad_ref[at, :], w_ref[...])
            part_ref[at, :] = part
            low_ref[at, :] = part.astype(LOW)
            rows[0:1, :] += jnp.sum(part * normalise(x_ref[at, :].astype(WIDE))[0], axis=0, keepdims=True)
            rows[1:2, :] += jnp.sum(part, axis=0, keepdims=True)

        rows[2:4, :] = two_ref[...]
        cols_ref[...] = dot_rows(rows[...].astype(LOW), eye(8, LANES)).astype(LOW)

    outs = [((tokens, width), WIDE), ((tokens, width), LOW), ((width, LANES), LOW)]
    scratch = [pltpu.VMEM((8, width), WIDE)]
    return run(kernel, outs, grad, qkv_w, x, norm_two, scalars=False, scratch=scratch)


def input_back(part, got, grad_resid, own_x, rows):
    group, width = own_x.shape

    def kernel(coords, part_ref, got_ref, resid_ref, x_ref, rows_ref, out_ref):
        at = pl.ds(pl.multiple_of(coords[3] * group, 16), group)
        normed, rate = normalise(x_ref[...].astype(WIDE))
        grad = part_ref[at, :] + got_ref[...].astype(WIDE)
        out_ref[...] = (resid_ref[at, :] + norm_back(normed, rate, grad, rows_ref[0:1, :])).astype(LOW)

    return run(kernel, [((group, width), LOW)], part, got, grad_resid, own_x, rows)[0]


def adam_update(weight, first, second, grad, rate, decay):
    first_new = BETA_ONE * first + (1.0 - BETA_ONE) * grad
    second_new = BETA_TWO * second + (1.0 - BETA_TWO) * grad * grad
    first_hat = first_new / (1.0 - BETA_ONE**STEP)
    second_hat = second_new / (1.0 - BETA_TWO**STEP)
    weight_new = weight - rate * (first_hat / (jnp.sqrt(second_hat) + ADAM_EPS) + decay * weight)
    return (weight_new, first_new, second_new)


def from_others(low, step):
    if lax.axis_size("z") == 4 and step == 1:
        near = shift(low, step, wrap=False)
        pair = (low.astype(WIDE) + near.astype(WIDE)).astype(LOW)
        return [near, shift(pair, 2 * step, wrap=False)]
    return [shift(low, step * k, wrap=False) for k in range(1, lax.axis_size("z"))]


def body(
    images,
    cotangent,
    qkv_weight,
    out_weight,
    up_weight,
    down_weight,
    norm_params,
    qkv_first,
    out_first,
    up_first,
    down_first,
    norm_first,
    qkv_second,
    out_second,
    up_second,
    down_second,
    norm_second,
):
    depth, core = lax.axis_size("z"), lax.axis_index("c")
    count, group, width = images.shape
    hidden_units = up_weight.shape[1]
    own_rows = qkv_weight.shape[0]
    own_units = down_weight.shape[0]
    chips = lax.axis_size("y") * lax.axis_size("x")
    block, ff_block = width // (2 * depth), hidden_units // (2 * depth)
    half_qkv, half_ff, half_d = 3 * width // 2, hidden_units // 2, width // 2
    ring = lax.axis_size("y") == 2 and lax.axis_size("x") == 2 and depth == 4 and own_rows % 32 == 0
    heads = half_d // HEAD_DIM
    tokens = 2 * group

    own_x, own_g = images.reshape(group, width), cotangent.reshape(group, width)
    split_qkv = lambda w: jnp.moveaxis(w.reshape(-1, 3 * depth, 2, block), 2, 0).reshape(2, -1, half_qkv)
    split_up = lambda w: jnp.moveaxis(w.reshape(-1, depth, 2, ff_block), 2, 0).reshape(2, -1, half_ff)

    thin, small = own_units // 2, own_rows // 2
    if ring:
        qkv_mine, qkv_give = cast_qkv(qkv_weight, norm_params, 3 * depth)
        qkv_part = join_rows(qkv_mine, swap(qkv_give, "c"))
        down_one, down_two = cast_down(down_weight)
        up_mine, up_give, out_part = cast_rest(after(up_weight, qkv_part), out_weight, depth)
        inputs = join_rows(own_x, swap(own_x, "c"))
        up_part = join_rows(up_mine, swap(up_give, "c"), out_part)
        qkv_column = column_first(qkv_part)
        two_plane = plane_first(after(down_two, qkv_part))
        qkv_column = [after(part, two_plane, up_part, inputs) for part in qkv_column]
        up_column = column_first(after(up_part, *qkv_column))
        qkv_parts = plane_last(jnp.stack(qkv_column))
        g_mate = swap(after(own_g, *up_column), "c")
        two_parts = [two_plane, shift(after(two_plane, *up_column), 1)]
        one_column = column_first(after(down_one, two_parts[1]))

        def qkv_moves(zz, plane, piece):
            row = lambda h: ((zz * 2 + h) * chips + plane) * own_rows
            moves = [(0, h * own_rows, 0, own_rows, half_qkv, row(h), 0) for h in (0, 1)]
            return moves + [(1, h * own_rows, half_qkv, own_rows, LANES, row(h), 0) for h in (0, 1)]

        def up_moves(zz, plane, piece):
            row = lambda h: ((zz * 2 + h) * chips + plane) * own_rows
            moves = [(0, h * own_rows, 0, own_rows, half_ff, row(h), 0) for h in (0, 1)]
            to = zz * block + plane * own_rows
            return moves + [(1, h * own_rows, half_ff, own_rows, half_d, to, h * half_d) for h in (0, 1)]

        def down_moves(zz, plane, piece):
            return [(0, 0, 0, thin, width, zz * ff_block + plane * own_units + piece * thin, 0)]

        spots = column_first_spots(depth)
        qkv_w, norm_w = place(qkv_parts, depth, [(width, half_qkv), (width, LANES)], spots, qkv_moves)
    else:
        qkv_low, out_low = qkv_weight.astype(LOW), out_weight.astype(LOW)
        up_low, down_low = up_weight.astype(LOW), down_weight.astype(LOW)
        norm_low = norm_params.astype(LOW)
        x_mate, g_mate = swap(own_x, "c"), swap(own_g, "c")
        whole = lambda w, axis=0: lax.all_gather(w, ALL, axis=axis, tiled=True)
        qkv_w, up_w = mine(split_qkv(whole(qkv_low))), mine(split_up(whole(up_low)))
        rows_half = lambda w, b: mine(jnp.moveaxis(w.reshape(depth, 2, b, width), 1, 0)).reshape(-1, width)
        out_w, down_w = rows_half(whole(out_low), block), rows_half(whole(down_low), ff_block)
        norm_w = jnp.pad(whole(norm_low, 1).T, ((0, 0), (0, LANES - 4)))

        inputs = join_rows(own_x, x_mate)
    grad_out = join_rows(own_g, g_mate)
    halves = lambda a: a.reshape(2, group, -1)
    rows, normed_one, qk, query, key, value, state = project(inputs, norm_w, qkv_w)
    earlier = from_others(state, 1)
    mixed, mixed_low, denom, state_in, attended = attend(query, key, value, earlier, (grad_out,))
    if ring:
        gate = (*earlier, *one_column[1:])
        up_parts = plane_last(after(jnp.stack(up_column), *qkv_parts[3:]), gate)
        two_parts.append(shift(after(two_parts[-1], *gate), 1))
        for _ in range(3, depth):
            two_parts.append(shift(two_parts[-1], 1))
        up_w, out_w = place(
            up_parts, depth, [(width, half_ff), (half_d, width)], spots, up_moves, two_parts[2:3]
        )
    out_part, out_low = out_project(mixed_low, out_w)
    out_got = swap(out_low, "c")
    resid, normed_two, activated, slope = feed(inputs, out_part, out_got, rows, up_w)
    down_grad = dot_rows(activated, grad_out).astype(LOW)
    if ring:
        def down_cuts(zz, plane, half):
            return [(0, zz * ff_block + plane * own_units + half * thin, 0, thin, width, 0, 0)]

        down_cut = unplace([down_grad], depth, (thin, width), down_cuts)
        down_hop = first_hop(*down_cut)
        one_parts = plane_last(after(jnp.stack(one_column), *up_parts[3:]), (down_cut[0][0, 0, :16, :LANES],))
        spots = spots + plane_first_spots(depth, thin, 5)
        down_parts = [*one_parts, *two_parts]
        (down_w,) = place(down_parts, depth, [(half_ff, width)], spots, down_moves, (down_cut[0],))

    grad_hidden, two_part, two_low = feed_back(grad_out, down_w, slope, up_w)
    down_own, down_give = down_project(activated, down_w, resid, (two_low,))
    down_got = swap(down_give, "c")
    activations = (down_own + down_got.astype(WIDE)).astype(LOW)
    up_grad = weight_grad(normed_two, grad_hidden)
    two_got = swap(two_low, "c")
    deps = (up_grad,)
    if ring:
        down_turn = second_hop_of(*down_hop, (up_grad,))
        deps = (up_grad, down_turn[0])
    grad_resid, grad_resid_low, a_low, b_rows, state_grad, norm_two = attend_turn(
        two_part, two_got, resid, rows, grad_out, out_w, mixed, denom, query, deps
    )
    later = from_others(state_grad, -1)
    out_grad = dot_rows(mixed_low, grad_resid_low).astype(LOW)
    deps = ()
    if ring:

        def up_cuts(zz, plane, half):
            cuts = [(0, ((zz * 2 + half) * chips + plane) * own_rows, 0, own_rows, half_ff, 0, 0)]
            row = zz * block + plane * own_rows + half * small
            return cuts + [(1, row, p * half_d, small, half_d, p * small, half_ff) for p in (0, 1)]

        up_cut = unplace([up_grad, out_grad], depth, (own_rows, half_ff + half_d), up_cuts)
        deps = (up_cut[0],)
    grad_projected = attend_back(query, key, value, qk, a_low, b_rows, state_in, later, deps)
    qkv_grad = dot_rows(normed_one, grad_projected).astype(LOW)
    one_part, one_low, norm_cols = project_back(grad_projected, qkv_w, inputs, norm_two)
    input_grad = input_back(one_part, swap(other(halves(one_low)), "c"), grad_resid, own_x, rows)

    out_fan = max(1, width * 64 // (tokens * depth))
    rates = (3.0 * width**-0.5, 3.0 * out_fan**-0.5, 3.0 * width**-0.5, 3.0 * hidden_units**-0.5, 1.5)
    decays = (WEIGHT_DECAY, WEIGHT_DECAY, WEIGHT_DECAY, WEIGHT_DECAY, 0.0)
    masters = (qkv_weight, out_weight, up_weight, down_weight, norm_params)
    firsts = (qkv_first, out_first, up_first, down_first, norm_first)
    seconds = (qkv_second, out_second, up_second, down_second, norm_second)
    if ring:

        def qkv_cuts(zz, plane, half):
            row = ((zz * 2 + half) * chips + plane) * own_rows
            return [(0, row, 0, own_rows, half_qkv, 0, 0), (1, row, 0, own_rows, LANES, 0, half_qkv)]

        hop = swap(down_turn[0], "y"), swap(down_turn[1], "x")
        down_sum = third_hop_of(*down_hop, *hop)
        up_hop = first_hop(*up_cut, (*hop, *later))
        turn = second_hop_of(*up_hop, (*down_sum[1:], grad_projected))
        hop = swap(turn[0], "y"), swap(turn[1], "x")
        up_sum = third_hop_of(*up_hop, *hop)
        qkv_cut = unplace([qkv_grad, norm_cols], depth, (own_rows, half_qkv + LANES), qkv_cuts)
        qkv_hop = first_hop(*qkv_cut, hop)
        turn = second_hop_of(*qkv_hop)
        hop = swap(turn[0], "y"), swap(turn[1], "x")
        qkv_sum = third_hop_of(*qkv_hop, *hop, up_sum[1:])
        down_red, squares = finish_down(down_sum)
        up_mine, up_give, out_red, squares = finish_up(up_sum, squares, own_rows, half_ff)
        up_mate = swap(up_give, "c")
        deps = (input_grad, activations, up_mate)
        qkv_mine, qkv_give, small_mine = finish_qkv(qkv_sum, squares, own_rows, half_qkv, deps)
        small_mate, qkv_mate = swap(small_mine, "c"), swap(qkv_give, "c")
        squares, norm_sum = chip_squares(small_mine, small_mate)
        norm_red = mine(norm_sum.reshape(2, own_rows, LANES))[:, :4].T
        grads = (qkv_mine, qkv_mate, out_red, up_mine, up_mate, down_red, norm_red)
        *news, grad_norm = update_all(
            grads, sum_chips(squares), masters, firsts, seconds, rates, decays, (3 * depth, depth)
        )
        return (
            activations.reshape(count, group, width),
            input_grad.reshape(count, group, width),
            grad_norm.reshape(()),
            *news,
        )
    scatter = lambda g: lax.psum_scatter(g, ALL, scatter_dimension=0, tiled=True)
    both = lambda a, axis: jnp.stack([jnp.where(core == k, a, 0.0) for k in (0, 1)], axis)
    to_all = lambda a: a.astype(WIDE)
    qkv_red = scatter(both(to_all(qkv_grad).reshape(width, 3 * depth, block), 2).reshape(width, -1))
    up_red = scatter(both(to_all(up_grad).reshape(width, depth, ff_block), 2).reshape(width, -1))
    out_red = scatter(both(to_all(out_grad).reshape(depth, block, width), 1).reshape(width, width))
    down_red = scatter(both(to_all(down_grad).reshape(depth, ff_block, width), 1).reshape(hidden_units, width))
    norm_red = scatter(norm_cols.astype(WIDE))[:, :4].T

    reduced = (qkv_red, out_red, up_red, down_red, norm_red)
    local_squares = sum(jnp.sum(grad * grad) for grad in reduced)
    grad_norm = jnp.sqrt(lax.psum(local_squares, ALL))
    clip = jnp.minimum(1.0, CLIP_LIMIT / (grad_norm + 1e-06))
    news = [
        adam_update(masters[k], firsts[k], seconds[k], clip * reduced[k], rates[k], decays[k]) for k in range(5)
    ]
    return (
        activations.reshape(count, group, width),
        input_grad.reshape(count, group, width),
        grad_norm,
        *[new[0] for new in news],
        *[new[1] for new in news],
        *[new[2] for new in news],
    )


def solution(mesh):
    depth, planes = mesh.shape["seq"] // 2, mesh.shape["img"]
    across = max(k for k in range(1, planes + 1) if planes % k == 0 and k * k <= planes)
    grid = jax.sharding.Mesh(mesh.devices.reshape(depth, 2, planes // across, across), ALL)
    tokens = P(("y", "x"), ("z", "c"), None)
    matrix, norm = P(ALL, None), P(None, ALL)
    state = (matrix, matrix, matrix, matrix, norm)
    return jax.shard_map(
        body,
        mesh=grid,
        in_specs=(tokens, tokens) + state * 3,
        out_specs=(tokens, tokens, P()) + state * 3,
        check_vma=False,
    )
```

```python
import functools

import jax
import jax.numpy as jnp
from jax import lax
from jax.experimental import pallas as pl
from jax.experimental.pallas import tpu as pltpu
from jax.sharding import PartitionSpec as P

HEAD_DIM = 64
STEP = 10
NORM_EPS = 1e-05
BETA_ONE = 0.9
BETA_TWO = 0.999
ADAM_EPS = 1e-08
WEIGHT_DECAY = 0.1
CLIP_LIMIT = 1.0
LANES = 128

LOW = jnp.bfloat16
WIDE = jnp.float32
ALL = ("z", "c", "y", "x")
SWAP = [(0, 1), (1, 0)]


def swap(value, axis):
    return lax.ppermute(value, axis, SWAP)


def shift(value, step, wrap=True):
    size = lax.axis_size("z")
    pairs = [(i, (i + step) % size) for i in range(size) if wrap or 0 <= i + step < size]
    return lax.ppermute(value, "z", pairs)


def mine(pair_axis_first):
    return jnp.where(lax.axis_index("c") == 0, pair_axis_first[0], pair_axis_first[1])


def other(pair_axis_first):
    return jnp.where(lax.axis_index("c") == 0, pair_axis_first[1], pair_axis_first[0])


def in_order(own, mate, axis=0):
    first = lax.axis_index("c") == 0
    return jnp.concatenate([jnp.where(first, own, mate), jnp.where(first, mate, own)], axis)


def after(value, *before):
    return lax.optimization_barrier((*before, value))[-1]


def column_first(shard):
    return [shard] + [shift(shard, k) for k in range(1, lax.axis_size("z"))]


def plane_last(column, between=()):
    half = column.shape[0] // 2
    along_x, along_y = swap(column, "x"), swap(column, "y")
    along_x, along_y = after(along_x, *between), after(along_y, *between)
    far = (swap(along_y[:half], "x"), swap(along_x[half:], "y"))
    return (column, along_x, along_y) + far


def plane_first(shard):
    far = lax.ppermute(shard, ("y", "x"), [(i, 3 - i) for i in range(4)])
    return jnp.concatenate([shard, swap(shard, "x"), swap(shard, "y"), far])


def column_last(plane):
    parts = [plane]
    for _ in range(1, lax.axis_size("z")):
        parts.append(shift(parts[-1], 1))
    return parts


def column_first_spots(depth):
    half = depth // 2
    spots = [(0, (k,), 0, (k, 0, 0), 0) for k in range(depth)]
    spots += [(1, (k,), 0, (k, 0, 1), 0) for k in range(depth)]
    spots += [(2, (k,), 0, (k, 1, 0), 0) for k in range(depth)]
    spots += [(3, (k,), 0, (k, 1, 1), 0) for k in range(half)]
    return spots + [(4, (k - half,), 0, (k, 1, 1), 0) for k in range(half, depth)]


def plane_first_spots(depth, rows, base):
    return [(base + k, (), p * rows, (k, p // 2, p % 2), 1) for k in range(depth) for p in range(4)]


def first_hop(send_x, keep_x, send_y, keep_y, before=()):
    return keep_x, swap(after(send_x, *before), "x"), keep_y, swap(after(send_y, *before), "y")


def second_hop_of(keep_x, got_x, keep_y, got_y, deps=()):
    depth, rows, cols = keep_x.shape[1:]

    def second_hop(kx, gx, ky, gy, to_y, to_x):
        to_y[...] = (kx[1].astype(WIDE) + gx[1].astype(WIDE)).astype(LOW)
        to_x[...] = (ky[1].astype(WIDE) + gy[1].astype(WIDE)).astype(LOW)

    outs = [((depth, rows, cols), LOW)] * 2
    return run(second_hop, outs, keep_x, got_x, keep_y, got_y, scalars=False, deps=deps)


def third_hop_of(keep_x, got_x, keep_y, got_y, on_y, on_x, deps=()):
    depth, rows, cols = keep_x.shape[1:]

    def third_hop(kx, gx, ky, gy, ony, onx, own, *sends):
        for k in range(depth):
            one = kx[0, k].astype(WIDE) + gx[0, k].astype(WIDE) + ony[k].astype(WIDE)
            two = ky[0, k].astype(WIDE) + gy[0, k].astype(WIDE) + onx[k].astype(WIDE)
            out = sends[k - 1] if k else own
            out[:rows, :] = one.astype(out.dtype)
            out[rows:, :] = two.astype(out.dtype)

    outs = [((2 * rows, cols), WIDE if k == 0 else LOW) for k in range(depth)]
    own, *sends = run(third_hop, outs, keep_x, got_x, keep_y, got_y, on_y, on_x, scalars=False, deps=deps)
    return [own] + [shift(part, k + 1) for k, part in enumerate(sends)]


def sum_of(refs):
    total = refs[0][...]
    for ref in refs[1:]:
        total = total + ref[...].astype(WIDE)
    return total


def spread(value):
    return jnp.broadcast_to(value, (8, LANES))


def total_squares(value):
    return jnp.sum(jnp.sum(value * value, axis=1, keepdims=True), axis=0, keepdims=True)


def finish_down(parts, deps=()):
    def kernel(*refs):
        total = sum_of(refs[: len(parts)])
        refs[-2][...] = total
        refs[-1][...] = spread(total_squares(total))

    return run(kernel, [(parts[0].shape, WIDE), ((8, LANES), WIDE)], *parts, scalars=False, deps=deps)


def finish_up(parts, squares, rows, half_ff):
    half_d = parts[0].shape[1] - half_ff
    small = rows // 2

    def kernel(coords, squares_ref, *refs):
        own_ref, mate_ref, out_ref, total_ref, all_ref = refs[len(parts) :]
        total = sum_of(refs[: len(parts)])
        all_ref[...] = total
        core = coords[3]
        own_ref[...] = all_ref[pl.ds(pl.multiple_of(core * rows, 8), rows), :half_ff]
        mate_ref[...] = all_ref[pl.ds(pl.multiple_of((1 - core) * rows, 8), rows), :half_ff]
        for p in range(2):
            for h in range(2):
                block = total[h * rows + p * small : h * rows + (p + 1) * small, half_ff:]
                out_ref[h * small : (h + 1) * small, p * half_d : (p + 1) * half_d] = block
        total_ref[...] = squares_ref[...] + spread(total_squares(total))

    outs = [((rows, half_ff), WIDE)] * 2 + [((rows, 2 * half_d), WIDE), ((8, LANES), WIDE)]
    scratch = [pltpu.VMEM(parts[0].shape, WIDE)]
    return run(kernel, outs, squares, *parts, scratch=scratch)


def finish_qkv(parts, squares, rows, half_qkv, deps=()):
    def kernel(coords, squares_ref, *refs):
        own_ref, mate_ref, small_ref, all_ref = refs[len(parts) :]
        total = sum_of(refs[: len(parts)])
        all_ref[...] = total
        core = coords[3]
        own_ref[...] = all_ref[pl.ds(pl.multiple_of(core * rows, 8), rows), :half_qkv]
        mate_ref[...] = all_ref[pl.ds(pl.multiple_of((1 - core) * rows, 8), rows), :half_qkv]
        small_ref[: 2 * rows, :] = total[:, half_qkv:]
        small_ref[2 * rows :, :] = squares_ref[...] + spread(total_squares(total[:, :half_qkv]))

    outs = [((rows, half_qkv), WIDE)] * 2 + [((2 * rows + 8, LANES), WIDE)]
    scratch = [pltpu.VMEM(parts[0].shape, WIDE)]
    return run(kernel, outs, squares, *parts, scratch=scratch, deps=deps)


def chip_squares(small, got):
    rows = small.shape[0] - 8

    def kernel(small_ref, got_ref, total_ref, norm_ref):
        total = small_ref[...] + got_ref[...]
        norm_ref[...] = total[:rows]
        total_ref[...] = total[rows:] + spread(total_squares(total[:rows]))

    outs = [((8, LANES), WIDE), ((rows, LANES), WIDE)]
    return run(kernel, outs, small, got, scalars=False)


def sum_chips(value):
    across = lax.ppermute(value, ("y", "x"), [(i, 3 - i) for i in range(4)])
    value = value + swap(value, "y") + (swap(value, "x") + across)
    size, near = lax.axis_size("z"), 1
    while near < size // 2:
        value = value + lax.ppermute(value, "z", [(i, i ^ near) for i in range(size)])
        near *= 2
    return [value, lax.ppermute(value, "z", [(i, i ^ near) for i in range(size)])]


def interleave(first, own, mate, blocks):
    size = own.shape[1] // blocks
    pieces = []
    for j in range(blocks):
        at = slice(j * size, (j + 1) * size)
        pieces += [jnp.where(first, own[:, at], mate[:, at]), jnp.where(first, mate[:, at], own[:, at])]
    return jnp.concatenate(pieces, axis=1)


def update_all(grads, totals, masters, firsts, seconds, rates, decays, blocks):
    steps = 2
    n, m = len(grads), len(totals)

    def tile(array):
        rows, cols = array.shape
        return pl.BlockSpec((rows // steps, cols), lambda i: (i, 0))

    def whole(array):
        return pl.BlockSpec(array.shape, lambda i: (0, 0))

    def kernel(coords, *refs):
        first = coords[3] == 0
        g, t, old, new = refs[:n], refs[n : n + m], refs[n + m : n + m + 15], refs[n + m + 15 :]
        total = sum_of(t)[0:1, 0:1]
        norm = jnp.sqrt(total)
        clip = jnp.minimum(1.0, CLIP_LIMIT / (norm + 1e-06))
        qkv = interleave(first, g[0][...], g[1][...], blocks[0])
        up = interleave(first, g[3][...], g[4][...], blocks[1])
        for k, grad in enumerate((qkv, g[2][...], up, g[5][...], g[6][...])):
            news = adam_update(old[k][...], old[5 + k][...], old[10 + k][...], clip * grad, rates[k], decays[k])
            for part in range(3):
                new[5 * part + k][...] = news[part]
        new[15][...] = norm

    state = (*masters, *firsts, *seconds)
    specs = [whole(a) if k % 5 == 4 else tile(a) for k, a in enumerate(state)]
    norm_out = jax.ShapeDtypeStruct((1, 1), WIDE)
    return pl.pallas_call(
        kernel,
        grid=(steps,),
        out_shape=[jax.ShapeDtypeStruct(a.shape, WIDE) for a in state] + [norm_out],
        in_specs=[pl.BlockSpec(memory_space=pltpu.SMEM)]
        + [tile(a) for a in grads[:-1]]
        + [whole(grads[-1])]
        + [whole(a) for a in totals]
        + specs,
        out_specs=specs + [whole(norm_out)],
        compiler_params=FULL,
    )(coordinates(), *grads, *totals, *state)


def coordinates():
    return jnp.stack([lax.axis_index(name) for name in ("z", "y", "x", "c")]).astype(jnp.int32)


def chip_of(coords, rel, depth, back):
    dz, dy, dx = rel
    z, y, x = coords[0], coords[1], coords[2]
    zz = lax.rem(z + (depth - dz if back else dz), depth)
    yy = 1 - y if dy else y
    xx = 1 - x if dx else x
    return zz, yy * 2 + xx


def window(row, rows, col, cols):
    rows_at = pl.ds(row if isinstance(row, int) else pl.multiple_of(row, 16), rows)
    return rows_at, pl.ds(col, cols)


VMEM = pl.BlockSpec(memory_space=pltpu.VMEM)
ROOM_MB = 16
ROOM = pltpu.CompilerParams(vmem_limit_bytes=ROOM_MB * 1024 * 1024)
FULL = pltpu.CompilerParams(vmem_limit_bytes=56 * 1024 * 1024)


def place(parts, depth, outs, spots, moves, deps=()):
    def kernel(coords, *refs):
        ins, out_refs = refs[: len(parts)], refs[len(parts) + len(deps) :]
        for array, lead, base, rel, piece in spots:
            zz, plane = chip_of(coords, rel, depth, True)
            for o, sr, sc, rows, cols, tr, tc in moves(zz, plane, piece):
                out_refs[o][window(tr, rows, tc, cols)] = ins[array][(*lead, *window(base + sr, rows, sc, cols))]

    return pl.pallas_call(
        kernel,
        out_shape=[jax.ShapeDtypeStruct(s, LOW) for s in outs],
        in_specs=[pl.BlockSpec(memory_space=pltpu.SMEM)]
        + [VMEM] * len(parts)
        + [pl.BlockSpec(memory_space=pl.ANY)] * len(deps),
        out_specs=[VMEM] * len(outs),
        compiler_params=ROOM,
    )(coordinates(), *parts, *deps)


def unplace(grads, depth, rows_cols, moves):
    spots = []
    for dz in range(depth):
        for d in range(2):
            spots += [(0, d, dz, (dz, d, 1), 0), (1, d, dz, (dz, d, 0), 0)]
            spots += [(2, d, dz, (dz, 1, d), 1), (3, d, dz, (dz, 0, d), 1)]

    def kernel(coords, *refs):
        ins, out_refs = refs[: len(grads)], refs[len(grads) :]
        for array, d, dz, rel, half in spots:
            zz, plane = chip_of(coords, rel, depth, False)
            for i, sr, sc, rows, cols, tr, tc in moves(zz, plane, half):
                out_refs[array][(d, dz, *window(tr, rows, tc, cols))] = ins[i][window(sr, rows, sc, cols)]

    return pl.pallas_call(
        kernel,
        out_shape=[jax.ShapeDtypeStruct((2, depth) + rows_cols, LOW)] * 4,
        in_specs=[pl.BlockSpec(memory_space=pltpu.SMEM)] + [VMEM] * len(grads),
        out_specs=[VMEM] * 4,
        compiler_params=ROOM,
    )(coordinates(), *grads)


def cast_qkv(qkv, norm, halves):
    rows, cols = qkv.shape
    wide = cols // 2 + LANES
    block = cols // (2 * halves)

    def kernel(coords, qkv_ref, norm_ref, own_ref, mate_ref, tall):
        first = coords[3] == 0
        for j in range(halves):
            a = qkv_ref[:, 2 * j * block : (2 * j + 1) * block]
            b = qkv_ref[:, (2 * j + 1) * block : (2 * j + 2) * block]
            own_ref[:, j * block : (j + 1) * block] = jnp.where(first, a, b).astype(LOW)
            mate_ref[:, j * block : (j + 1) * block] = jnp.where(first, b, a).astype(LOW)
        tall[...] = jnp.zeros_like(tall)
        tall[0:4, :] = norm_ref[...].astype(LOW).astype(WIDE)
        i = lax.broadcasted_iota(jnp.int32, (rows, rows), 0)
        j = lax.broadcasted_iota(jnp.int32, (rows, rows), 1)
        columns = dot_cols((i == j).astype(LOW), tall[...].astype(LOW)).astype(LOW)
        own_ref[:, cols // 2 :] = columns
        mate_ref[:, cols // 2 :] = columns

    return pl.pallas_call(
        kernel,
        out_shape=[jax.ShapeDtypeStruct((rows, wide), LOW)] * 2,
        in_specs=[pl.BlockSpec(memory_space=pltpu.SMEM), VMEM, VMEM],
        out_specs=[VMEM] * 2,
        scratch_shapes=[pltpu.VMEM((LANES, rows), WIDE)],
        compiler_params=ROOM,
    )(coordinates(), qkv, norm)


def cast_down(down, last):
    rows, cols = down.shape

    def kernel(down_ref, one_ref, two_ref):
        one_ref[...] = down_ref[:last, :].astype(LOW)
        two_ref[...] = down_ref[last:, :].astype(LOW)

    return pl.pallas_call(
        kernel,
        out_shape=[jax.ShapeDtypeStruct((last, cols), LOW), jax.ShapeDtypeStruct((rows - last, cols), LOW)],
        in_specs=[VMEM],
        out_specs=[VMEM] * 2,
        compiler_params=ROOM,
    )(down)


def cast_rest(up, out, halves):
    rows, cols = up.shape
    block, width = cols // (2 * halves), out.shape[1]

    def kernel(coords, up_ref, out_ref, own_ref, mate_ref, part_ref):
        first = coords[3] == 0
        for j in range(halves):
            a = up_ref[:, 2 * j * block : (2 * j + 1) * block]
            b = up_ref[:, (2 * j + 1) * block : (2 * j + 2) * block]
            own_ref[:, j * block : (j + 1) * block] = jnp.where(first, a, b).astype(LOW)
            mate_ref[:, j * block : (j + 1) * block] = jnp.where(first, b, a).astype(LOW)
        part_ref[:rows, :] = out_ref[:, : width // 2].astype(LOW)
        part_ref[rows:, :] = out_ref[:, width // 2 :].astype(LOW)

    return pl.pallas_call(
        kernel,
        out_shape=[jax.ShapeDtypeStruct((rows, cols // 2), LOW)] * 2
        + [jax.ShapeDtypeStruct((2 * rows, width // 2), LOW)],
        in_specs=[pl.BlockSpec(memory_space=pltpu.SMEM), VMEM, VMEM],
        out_specs=[VMEM] * 3,
        compiler_params=ROOM,
    )(coordinates(), up, out)


def join_rows(own, mate, side=None):
    rows, cols = own.shape
    wide = cols + (side.shape[1] if side is not None else 0)

    def kernel(coords, own_ref, mate_ref, *refs):
        out_ref = refs[-1]
        core = coords[3]
        out_ref[pl.ds(pl.multiple_of(core * rows, 16), rows), :cols] = own_ref[...]
        out_ref[pl.ds(pl.multiple_of((1 - core) * rows, 16), rows), :cols] = mate_ref[...]
        if side is not None:
            out_ref[:, cols:] = refs[0][...]

    ins = [own, mate] + ([side] if side is not None else [])
    return pl.pallas_call(
        kernel,
        out_shape=jax.ShapeDtypeStruct((2 * rows, wide), LOW),
        in_specs=[pl.BlockSpec(memory_space=pltpu.SMEM)] + [VMEM] * len(ins),
        out_specs=VMEM,
        compiler_params=ROOM,
    )(coordinates(), *ins)


def run(kernel, outs, *ins, scalars=True, scratch=(), flops=0, room=ROOM_MB, deps=()):
    first = len(ins) + scalars

    def body_of(*refs):
        return kernel(*refs[:first], *refs[first + len(deps) :])

    out_shape = [jax.ShapeDtypeStruct(shape, kind) for shape, kind in outs]
    return pl.pallas_call(
        body_of,
        out_shape=out_shape,
        in_specs=([pl.BlockSpec(memory_space=pltpu.SMEM)] if scalars else [])
        + [VMEM] * len(ins)
        + [pl.BlockSpec(memory_space=pl.ANY)] * len(deps),
        out_specs=[VMEM] * len(outs),
        scratch_shapes=list(scratch),
        compiler_params=pltpu.CompilerParams(vmem_limit_bytes=room * 1024 * 1024),
        cost_estimate=pl.CostEstimate(flops=flops, bytes_accessed=0, transcendentals=0),
    )(*([coordinates()] if scalars else []), *ins, *deps)


def dot(left, right):
    return jnp.dot(left, right, preferred_element_type=WIDE)


def dot_rows(left, right):
    return lax.dot_general(left, right, (((0,), (0,)), ((), ())), preferred_element_type=WIDE)


def dot_cols(left, right):
    return lax.dot_general(left, right, (((1,), (1,)), ((), ())), preferred_element_type=WIDE)


def eye(rows, cols):
    i = lax.broadcasted_iota(jnp.int32, (rows, cols), 0)
    return (i == lax.broadcasted_iota(jnp.int32, (rows, cols), 1)).astype(LOW)


def normalise(values):
    center = values - jnp.mean(values, axis=-1, keepdims=True)
    rate = lax.rsqrt(jnp.mean(center * center, axis=-1, keepdims=True) + NORM_EPS)
    return center * rate, rate


def norm_back(normed, rate, grad, gain):
    scaled = grad * gain
    shared = jnp.mean(scaled, axis=-1, keepdims=True)
    along = jnp.mean(scaled * normed, axis=-1, keepdims=True)
    return rate * (scaled - shared - normed * along)


def low_lanes(rows):
    return lax.broadcasted_iota(jnp.int32, (rows, LANES), 1) < HEAD_DIM


def by_head(pair):
    wide = pair.astype(WIDE)
    first = low_lanes(pair.shape[0])
    return jnp.where(first, wide, 0.0).astype(LOW), jnp.where(first, 0.0, wide).astype(LOW)


def pack_state(square):
    first = low_lanes(HEAD_DIM)
    return jnp.where(first, square[:HEAD_DIM], square[HEAD_DIM:])


def open_state(packed):
    first = low_lanes(HEAD_DIM)
    return jnp.concatenate([jnp.where(first, packed, 0.0), jnp.where(first, 0.0, packed)])


def feature(values):
    return jnp.where(values > 0.0, values + 1.0, jnp.exp(jnp.minimum(values, 0.0)))


def project(x, norm_w, qkv_w):
    tokens, width = x.shape
    half = qkv_w.shape[1] // 3
    pairs = half // LANES
    step = tokens // 2

    def kernel(x_ref, norm_ref, w_ref, rows_ref, normed_ref, qk_ref, q_ref, k_ref, v_ref, state_ref, sums):
        rows_ref[...] = dot_cols(eye(8, LANES), norm_ref[...])
        gain, bias = rows_ref[0:1, :], rows_ref[1:2, :]
        @pl.loop(0, 2)
        def _(i):
            at = at_block(i, step)
            normed = normalise(x_ref[at, :].astype(WIDE))[0]
            normed_ref[at, :] = (normed * gain + bias).astype(LOW)
            low = normed_ref[at, :]
            for j, out in enumerate((q_ref, k_ref)):
                part = dot(low, w_ref[:, j * half : (j + 1) * half])
                qk_ref[at, j * half : (j + 1) * half] = part
                out[at, :] = feature(part).astype(LOW)
            v_ref[at, :] = dot(low, w_ref[:, 2 * half :]).astype(LOW)
        total = dot_rows(jnp.ones((tokens, 8), LOW), k_ref[...])
        sums[...] = jnp.zeros_like(sums)
        for p in range(pairs):
            lanes = slice(p * LANES, (p + 1) * LANES)
            packed = pack_state(dot_rows(k_ref[:, lanes], v_ref[:, lanes]))
            state_ref[p * HEAD_DIM : (p + 1) * HEAD_DIM, :] = packed.astype(LOW)
            sums[p : p + 1, :] = total[0:1, lanes]
        state_ref[pairs * HEAD_DIM :, :] = sums[...].astype(LOW)

    outs = [((8, width), WIDE), ((tokens, width), LOW), ((tokens, 2 * half), WIDE)] + [((tokens, half), LOW)] * 3
    outs += [((pairs * HEAD_DIM + 16, LANES), LOW)]
    scratch = [pltpu.VMEM((16, LANES), WIDE)]
    return run(kernel, outs, x, norm_w, qkv_w, scalars=False, scratch=scratch)


def at_block(index, size):
    return pl.ds(pl.multiple_of(index * size, size), size)


def total_state(refs):
    total = refs[0][...].astype(WIDE)
    for ref in refs[1:]:
        total = total + ref[...].astype(WIDE)
    return total


def causal_mask(step):
    i = lax.broadcasted_iota(jnp.int32, (step, step), 0)
    return i >= lax.broadcasted_iota(jnp.int32, (step, step), 1)


def attend(query, key, value, parts, deps=()):
    tokens, half = query.shape
    pairs, step = half // LANES, tokens // 2

    def kernel(q_ref, k_ref, v_ref, *refs):
        mixed_ref, low_ref, denom_ref, state_ref, token_ref = refs[len(parts) :]
        token_ref[...] = jnp.zeros_like(token_ref)
        state_ref[...] = total_state(refs[: len(parts)])
        lower = causal_mask(step)
        first = low_lanes(step)
        top = low_lanes(HEAD_DIM)
        diagonal = eye(LANES, LANES).astype(WIDE)
        @pl.loop(0, pairs)
        def _(p):
            lanes = at_block(p, LANES)
            packed = state_ref[at_block(p, HEAD_DIM), :]
            sums = state_ref[pl.ds(pairs * HEAD_DIM + p, 1), :]
            column = jnp.sum(diagonal * sums, axis=1, keepdims=True)
            zero = jnp.zeros((HEAD_DIM, LANES), WIDE)
            ext = (
                jnp.concatenate([jnp.where(top, packed, column[:HEAD_DIM]), zero]).astype(LOW),
                jnp.concatenate([zero, jnp.where(top, column[HEAD_DIM:], packed)]).astype(LOW),
            )
            wide = v_ref[:, lanes].astype(WIDE)
            full = low_lanes(tokens)
            value_ext = (jnp.where(full, wide, 1.0).astype(LOW), jnp.where(full, 1.0, wide).astype(LOW))
            queries = by_head(q_ref[:, lanes])
            for i in range(2):
                at = slice(i * step, (i + 1) * step)
                got = []
                for h in range(2):
                    rows = queries[h][at]
                    total = dot(rows, ext[h])
                    for j in range(i + 1):
                        to = slice(j * step, (j + 1) * step)
                        scores = dot_cols(rows, k_ref[to, lanes])
                        if j == i:
                            scores = jnp.where(lower, scores, 0.0)
                        total = total + dot(scores.astype(LOW), value_ext[h][to])
                    got.append(total)
                denom = pltpu.roll(jnp.where(first, got[1], got[0]), HEAD_DIM, 1)
                mixed = jnp.where(first, got[0], got[1]) / denom
                mixed_ref[at, lanes] = mixed
                low_ref[at, lanes] = mixed.astype(LOW)
                denom_ref[at, lanes] = denom

    outs = [((tokens, half), WIDE), ((tokens, half), LOW), ((tokens, half), WIDE), (parts[0].shape, WIDE)]
    outs += [((8, LANES), WIDE)]
    return run(kernel, outs, query, key, value, *parts, scalars=False, deps=deps)


def out_project(mixed, out_w):
    def kernel(mixed_ref, w_ref, part_ref, low_ref):
        part = dot(mixed_ref[...], w_ref[...])
        part_ref[...] = part
        low_ref[...] = part.astype(LOW)

    shape = (mixed.shape[0], out_w.shape[1])
    return run(kernel, [(shape, WIDE), (shape, LOW)], mixed, out_w, scalars=False)


def feed(x, part, got, rows, up_w):
    tokens, width = x.shape
    units, step, cut = up_w.shape[1], tokens // 2, 512

    def kernel(x_ref, part_ref, got_ref, rows_ref, w_ref, resid_ref, normed_ref, act_ref, slope_ref):
        @pl.loop(0, 2)
        def _(i):
            at = at_block(i, step)
            resid = x_ref[at, :].astype(WIDE) + part_ref[at, :] + got_ref[at, :].astype(WIDE)
            resid_ref[at, :] = resid
            normed_ref[at, :] = (normalise(resid)[0] * rows_ref[2:3, :] + rows_ref[3:4, :]).astype(LOW)

        @pl.loop(0, units // cut)
        def _(j):
            to = at_block(j, cut)
            v = dot(normed_ref[...], w_ref[:, to])
            root = (2.0 / 3.141592653589793) ** 0.5
            square = v * v
            bend = jnp.tanh(root * v * (1.0 + 0.044715 * square))
            cdf = 0.5 * (1.0 + bend)
            act_ref[:, to] = (v * cdf).astype(LOW)
            slope_ref[:, to] = cdf + 0.5 * v * (1.0 - bend * bend) * (root * (1.0 + 3.0 * 0.044715 * square))

    outs = [((tokens, width), WIDE), ((tokens, width), LOW), ((tokens, units), LOW), ((tokens, units), WIDE)]
    return run(kernel, outs, x, part, got, rows, up_w, scalars=False)


def feed_back(grad_out, down_w, slope, up_w):
    tokens, width = grad_out.shape
    units, cut = up_w.shape[1], 512

    def kernel(g_ref, down_ref, slope_ref, up_ref, hidden_ref, part_ref, low_ref):
        @pl.loop(0, units // cut)
        def _(j):
            to = at_block(j, cut)
            hidden_ref[:, to] = (dot_cols(g_ref[...], down_ref[to, :]) * slope_ref[:, to]).astype(LOW)

        @pl.loop(0, width // cut)
        def _(j):
            to = at_block(j, cut)
            part = dot_cols(hidden_ref[...], up_ref[to, :])
            part_ref[:, to] = part
            low_ref[:, to] = part.astype(LOW)

    outs = [((tokens, units), LOW), ((tokens, width), WIDE), ((tokens, width), LOW)]
    return run(kernel, outs, grad_out, down_w, slope, up_w, scalars=False)


def down_project(activated, down_w, resid, deps):
    tokens, width = resid.shape
    group, cut = tokens // 2, width // 2

    def kernel(coords, act_ref, w_ref, resid_ref, own_ref, give_ref):
        own = pl.ds(pl.multiple_of(coords[3] * group, 16), group)
        mate = pl.ds(pl.multiple_of((1 - coords[3]) * group, 16), group)

        @pl.loop(0, 2)
        def _(j):
            to = at_block(j, cut)
            own_ref[:, to] = resid_ref[own, to] + dot(act_ref[own, :], w_ref[:, to])
            give_ref[:, to] = dot(act_ref[mate, :], w_ref[:, to]).astype(LOW)

    outs = [((group, width), WIDE), ((group, width), LOW)]
    return run(kernel, outs, activated, down_w, resid, deps=deps)


def weight_grad(rows, grad, deps=()):
    tokens, width = rows.shape
    units, cut = grad.shape[1], 512

    def kernel(rows_ref, grad_ref, out_ref):
        @pl.loop(0, units // cut)
        def _(j):
            to = at_block(j, cut)
            out_ref[:, to] = dot_rows(rows_ref[...], grad_ref[:, to]).astype(LOW)

    return run(kernel, [((width, units), LOW)], rows, grad, scalars=False, deps=deps)[0]


def attend_turn(part, got, resid, rows, grad_out, out_w, mixed, denom, query, deps):
    tokens, width = resid.shape
    half = mixed.shape[1]
    pairs, step = half // LANES, tokens // 2

    def kernel(
        part_ref, got_ref, resid_ref, rows_ref, g_ref, w_ref, mixed_ref, denom_ref, q_ref,
        grad_ref, low_ref, a_ref, b_ref, state_ref, norm_ref, sums,
    ):
        gain = rows_ref[2:3, :]
        first = low_lanes(step)
        norm_ref[...] = jnp.zeros_like(norm_ref)

        @pl.loop(0, 2)
        def _(i):
            at = at_block(i, step)
            normed, rate = normalise(resid_ref[at, :])
            own = part_ref[at, :]
            norm_ref[0:1, :] += jnp.sum(own * normed, axis=0, keepdims=True)
            norm_ref[1:2, :] += jnp.sum(own, axis=0, keepdims=True)
            grad = g_ref[at, :].astype(WIDE) + norm_back(normed, rate, own + got_ref[at, :].astype(WIDE), gain)
            grad_ref[at, :] = grad
            low_ref[at, :] = grad.astype(LOW)
            turned = dot_cols(low_ref[at, :], w_ref[...]) / denom_ref[at, :]
            a_ref[at, :] = turned.astype(LOW)
            along = turned * mixed_ref[at, :]
            for p in range(pairs):
                lanes = slice(p * LANES, (p + 1) * LANES)
                piece = along[:, lanes]
                low = jnp.sum(jnp.where(first, piece, 0.0), axis=1, keepdims=True)
                high = jnp.sum(jnp.where(first, 0.0, piece), axis=1, keepdims=True)
                b_ref[at, lanes] = -jnp.where(first, low, high)
        sums[...] = jnp.zeros_like(sums)
        for p in range(pairs):
            lanes = slice(p * LANES, (p + 1) * LANES)
            packed = pack_state(dot_rows(q_ref[:, lanes], a_ref[:, lanes]))
            state_ref[p * HEAD_DIM : (p + 1) * HEAD_DIM, :] = packed.astype(LOW)
            sums[p : p + 1, :] = jnp.sum(q_ref[:, lanes].astype(WIDE) * b_ref[:, lanes], axis=0, keepdims=True)
        state_ref[pairs * HEAD_DIM :, :] = sums[...].astype(LOW)

    outs = [((tokens, width), WIDE), ((tokens, width), LOW), ((tokens, half), LOW), ((tokens, half), WIDE)]
    outs += [((pairs * HEAD_DIM + 16, LANES), LOW), ((2, width), WIDE)]
    ins = (part, got, resid, rows, grad_out, out_w, mixed, denom, query)
    scratch = [pltpu.VMEM((16, LANES), WIDE)]
    return run(kernel, outs, *ins, scalars=False, scratch=scratch, deps=deps)


def attend_back(query, key, value, qk, a_low, b_rows, state, parts, deps=()):
    tokens, half = query.shape
    pairs, step = half // LANES, tokens // 2

    def kernel(q_ref, k_ref, v_ref, qk_ref, a_ref, b_ref, state_ref, *refs):
        out_ref, later = refs[len(parts) :]
        later[...] = total_state(refs[: len(parts)])
        lower = causal_mask(step)
        @pl.loop(0, pairs)
        def _(p):
            lanes, rows = at_block(p, LANES), at_block(p, HEAD_DIM)
            sums = pl.ds(pairs * HEAD_DIM + p, 1)
            before, after_it = open_state(state_ref[rows, :]).astype(LOW), open_state(later[rows, :]).astype(LOW)
            queries, keys, pulls = by_head(q_ref[:, lanes]), by_head(k_ref[:, lanes]), by_head(a_ref[:, lanes])
            cuts = [slice(i * step, (i + 1) * step) for i in range(2)]
            grad_q = [dot_cols(a_ref[c, lanes], before) + b_ref[c, lanes] * state_ref[sums, :] for c in cuts]
            grad_k = [dot_cols(v_ref[c, lanes], after_it) + later[sums, :] for c in cuts]
            shifts = b_ref[:, lanes]
            grad_v = [dot(k_ref[c, lanes], after_it) for c in cuts]
            for i in range(2):
                for j in range(i + 1):
                    for h in range(2):
                        q, a = queries[h][cuts[i]], pulls[h][cuts[i]]
                        b = shifts[cuts[i], h * HEAD_DIM : h * HEAD_DIM + 1]
                        scores = dot_cols(q, k_ref[cuts[j], lanes])
                        pull = dot_cols(a, v_ref[cuts[j], lanes]) + b
                        if j == i:
                            scores, pull = jnp.where(lower, scores, 0.0), jnp.where(lower, pull, 0.0)
                        scores, pull = scores.astype(LOW), pull.astype(LOW)
                        grad_q[i] = grad_q[i] + dot(pull, keys[h][cuts[j]])
                        grad_k[j] = grad_k[j] + dot_rows(pull, q)
                        grad_v[j] = grad_v[j] + dot_rows(scores, a)
            for i, c in enumerate(cuts):
                for n, grad in enumerate((grad_q[i], grad_k[i])):
                    at = at_block(n * pairs + p, LANES)
                    raw = qk_ref[c, at]
                    out_ref[c, at] = (grad * jnp.where(raw > 0.0, 1.0, jnp.exp(jnp.minimum(raw, 0.0)))).astype(LOW)
                out_ref[c, at_block(2 * pairs + p, LANES)] = grad_v[i].astype(LOW)

    ins = (query, key, value, qk, a_low, b_rows, state, *parts)
    scratch = [pltpu.VMEM(parts[0].shape, WIDE)]
    return run(kernel, [((tokens, 3 * half), LOW)], *ins, scalars=False, scratch=scratch, deps=deps)[0]


def project_back(grad, qkv_w, x, norm_two):
    tokens, width = x.shape
    step = tokens // 2

    def kernel(grad_ref, w_ref, x_ref, two_ref, part_ref, low_ref, cols_ref, rows):
        rows[...] = jnp.zeros_like(rows)

        @pl.loop(0, 2)
        def _(i):
            at = at_block(i, step)
            part = dot_cols(grad_ref[at, :], w_ref[...])
            part_ref[at, :] = part
            low_ref[at, :] = part.astype(LOW)
            rows[0:1, :] += jnp.sum(part * normalise(x_ref[at, :].astype(WIDE))[0], axis=0, keepdims=True)
            rows[1:2, :] += jnp.sum(part, axis=0, keepdims=True)

        rows[2:4, :] = two_ref[...]
        cols_ref[...] = dot_rows(rows[...].astype(LOW), eye(8, LANES)).astype(LOW)

    outs = [((tokens, width), WIDE), ((tokens, width), LOW), ((width, LANES), LOW)]
    scratch = [pltpu.VMEM((8, width), WIDE)]
    return run(kernel, outs, grad, qkv_w, x, norm_two, scalars=False, scratch=scratch)


def input_back(part, got, grad_resid, own_x, rows):
    group, width = own_x.shape

    def kernel(coords, part_ref, got_ref, resid_ref, x_ref, rows_ref, out_ref):
        at = pl.ds(pl.multiple_of(coords[3] * group, 16), group)
        normed, rate = normalise(x_ref[...].astype(WIDE))
        grad = part_ref[at, :] + got_ref[...].astype(WIDE)
        out_ref[...] = (resid_ref[at, :] + norm_back(normed, rate, grad, rows_ref[0:1, :])).astype(LOW)

    return run(kernel, [((group, width), LOW)], part, got, grad_resid, own_x, rows)[0]


def adam_update(weight, first, second, grad, rate, decay):
    first_new = BETA_ONE * first + (1.0 - BETA_ONE) * grad
    second_new = BETA_TWO * second + (1.0 - BETA_TWO) * grad * grad
    first_hat = first_new / (1.0 - BETA_ONE**STEP)
    second_hat = second_new / (1.0 - BETA_TWO**STEP)
    weight_new = weight - rate * (first_hat / (jnp.sqrt(second_hat) + ADAM_EPS) + decay * weight)
    return (weight_new, first_new, second_new)


def from_others(low, step):
    if lax.axis_size("z") == 4 and step == 1:
        near = shift(low, step, wrap=False)
        pair = (low.astype(WIDE) + near.astype(WIDE)).astype(LOW)
        return [near, shift(pair, 2 * step, wrap=False)]
    return [shift(low, step * k, wrap=False) for k in range(1, lax.axis_size("z"))]


def body(
    images,
    cotangent,
    qkv_weight,
    out_weight,
    up_weight,
    down_weight,
    norm_params,
    qkv_first,
    out_first,
    up_first,
    down_first,
    norm_first,
    qkv_second,
    out_second,
    up_second,
    down_second,
    norm_second,
):
    depth, core = lax.axis_size("z"), lax.axis_index("c")
    count, group, width = images.shape
    hidden_units = up_weight.shape[1]
    own_rows = qkv_weight.shape[0]
    own_units = down_weight.shape[0]
    chips = lax.axis_size("y") * lax.axis_size("x")
    block, ff_block = width // (2 * depth), hidden_units // (2 * depth)
    half_qkv, half_ff, half_d = 3 * width // 2, hidden_units // 2, width // 2
    ring = lax.axis_size("y") == 2 and lax.axis_size("x") == 2 and depth == 4 and own_rows % 32 == 0
    heads = half_d // HEAD_DIM
    tokens = 2 * group

    own_x, own_g = images.reshape(group, width), cotangent.reshape(group, width)
    split_qkv = lambda w: jnp.moveaxis(w.reshape(-1, 3 * depth, 2, block), 2, 0).reshape(2, -1, half_qkv)
    split_up = lambda w: jnp.moveaxis(w.reshape(-1, depth, 2, ff_block), 2, 0).reshape(2, -1, half_ff)

    thin, small, last = own_units // 2, own_rows // 2, 3 * own_units // 8
    if ring:
        qkv_mine, qkv_give = cast_qkv(qkv_weight, norm_params, 3 * depth)
        qkv_part = join_rows(qkv_mine, swap(qkv_give, "c"))
        down_one, down_two = cast_down(down_weight, last)
        up_mine, up_give, out_part = cast_rest(after(up_weight, qkv_part), out_weight, depth)
        inputs = join_rows(own_x, swap(own_x, "c"))
        up_part = join_rows(up_mine, swap(up_give, "c"), out_part)
        qkv_column = column_first(qkv_part)
        two_plane = plane_first(after(down_two, qkv_part))
        qkv_column = [after(part, two_plane, up_part, inputs) for part in qkv_column]
        up_column = column_first(after(up_part, *qkv_column))
        qkv_parts = plane_last(jnp.stack(qkv_column))
        g_mate = swap(after(own_g, *up_column), "c")
        two_parts = [two_plane, shift(after(two_plane, *up_column), 1)]
        one_column = column_first(after(down_one, two_parts[1]))

        def qkv_moves(zz, plane, piece):
            row = lambda h: ((zz * 2 + h) * chips + plane) * own_rows
            moves = [(0, h * own_rows, 0, own_rows, half_qkv, row(h), 0) for h in (0, 1)]
            return moves + [(1, h * own_rows, half_qkv, own_rows, LANES, row(h), 0) for h in (0, 1)]

        def up_moves(zz, plane, piece):
            row = lambda h: ((zz * 2 + h) * chips + plane) * own_rows
            moves = [(0, h * own_rows, 0, own_rows, half_ff, row(h), 0) for h in (0, 1)]
            to = zz * block + plane * own_rows
            return moves + [(1, h * own_rows, half_ff, own_rows, half_d, to, h * half_d) for h in (0, 1)]

        def down_moves(zz, plane, piece):
            rows = own_units - last if piece else last
            return [(0, 0, 0, rows, width, zz * ff_block + plane * own_units + piece * last, 0)]

        spots = column_first_spots(depth)
        qkv_w, norm_w = place(qkv_parts, depth, [(width, half_qkv), (width, LANES)], spots, qkv_moves)
    else:
        qkv_low, out_low = qkv_weight.astype(LOW), out_weight.astype(LOW)
        up_low, down_low = up_weight.astype(LOW), down_weight.astype(LOW)
        norm_low = norm_params.astype(LOW)
        x_mate, g_mate = swap(own_x, "c"), swap(own_g, "c")
        whole = lambda w, axis=0: lax.all_gather(w, ALL, axis=axis, tiled=True)
        qkv_w, up_w = mine(split_qkv(whole(qkv_low))), mine(split_up(whole(up_low)))
        rows_half = lambda w, b: mine(jnp.moveaxis(w.reshape(depth, 2, b, width), 1, 0)).reshape(-1, width)
        out_w, down_w = rows_half(whole(out_low), block), rows_half(whole(down_low), ff_block)
        norm_w = jnp.pad(whole(norm_low, 1).T, ((0, 0), (0, LANES - 4)))

        inputs = join_rows(own_x, x_mate)
    grad_out = join_rows(own_g, g_mate)
    halves = lambda a: a.reshape(2, group, -1)
    rows, normed_one, qk, query, key, value, state = project(inputs, norm_w, qkv_w)
    earlier = from_others(state, 1)
    mixed, mixed_low, denom, state_in, attended = attend(query, key, value, earlier, (grad_out,))
    if ring:
        gate = (*earlier, *one_column[1:])
        up_parts = plane_last(after(jnp.stack(up_column), *qkv_parts[3:]), gate)
        two_parts.append(shift(after(two_parts[-1], *gate), 1))
        for _ in range(3, depth):
            two_parts.append(shift(two_parts[-1], 1))
        up_w, out_w = place(
            up_parts, depth, [(width, half_ff), (half_d, width)], spots, up_moves, two_parts[2:3]
        )
    out_part, out_low = out_project(mixed_low, out_w)
    out_got = swap(out_low, "c")
    resid, normed_two, activated, slope = feed(inputs, out_part, out_got, rows, up_w)
    down_grad = dot_rows(activated, grad_out).astype(LOW)
    if ring:
        def down_cuts(zz, plane, half):
            return [(0, zz * ff_block + plane * own_units + half * thin, 0, thin, width, 0, 0)]

        down_cut = unplace([down_grad], depth, (thin, width), down_cuts)
        one_parts = plane_last(after(jnp.stack(one_column), *up_parts[3:]), (down_cut[0][0, 0, :16, :LANES],))
        down_hop = first_hop(*down_cut, one_parts[3:])
        spots = spots + plane_first_spots(depth, own_units - last, 5)
        down_parts = [*one_parts, *two_parts]
        (down_w,) = place(down_parts, depth, [(half_ff, width)], spots, down_moves, (down_cut[0],))

    grad_hidden, two_part, two_low = feed_back(grad_out, down_w, slope, up_w)
    down_own, down_give = down_project(activated, down_w, resid, (two_low,))
    down_got = swap(down_give, "c")
    activations = (down_own + down_got.astype(WIDE)).astype(LOW)
    up_grad = weight_grad(normed_two, grad_hidden)
    two_got = swap(two_low, "c")
    deps = (up_grad,)
    if ring:
        down_turn = second_hop_of(*down_hop, (up_grad,))
        deps = (up_grad, down_turn[0])
    grad_resid, grad_resid_low, a_low, b_rows, state_grad, norm_two = attend_turn(
        two_part, two_got, resid, rows, grad_out, out_w, mixed, denom, query, deps
    )
    later = from_others(state_grad, -1)
    out_grad = dot_rows(mixed_low, grad_resid_low).astype(LOW)
    deps = ()
    if ring:

        def up_cuts(zz, plane, half):
            cuts = [(0, ((zz * 2 + half) * chips + plane) * own_rows, 0, own_rows, half_ff, 0, 0)]
            row = zz * block + plane * own_rows + half * small
            return cuts + [(1, row, p * half_d, small, half_d, p * small, half_ff) for p in (0, 1)]

        up_cut = unplace([up_grad, out_grad], depth, (own_rows, half_ff + half_d), up_cuts)
        deps = (up_cut[0],)
    grad_projected = attend_back(query, key, value, qk, a_low, b_rows, state_in, later, deps)
    qkv_grad = dot_rows(normed_one, grad_projected).astype(LOW)
    one_part, one_low, norm_cols = project_back(grad_projected, qkv_w, inputs, norm_two)
    input_grad = input_back(one_part, swap(other(halves(one_low)), "c"), grad_resid, own_x, rows)

    out_fan = max(1, width * 64 // (tokens * depth))
    rates = (3.0 * width**-0.5, 3.0 * out_fan**-0.5, 3.0 * width**-0.5, 3.0 * hidden_units**-0.5, 1.5)
    decays = (WEIGHT_DECAY, WEIGHT_DECAY, WEIGHT_DECAY, WEIGHT_DECAY, 0.0)
    masters = (qkv_weight, out_weight, up_weight, down_weight, norm_params)
    firsts = (qkv_first, out_first, up_first, down_first, norm_first)
    seconds = (qkv_second, out_second, up_second, down_second, norm_second)
    if ring:

        def qkv_cuts(zz, plane, half):
            row = ((zz * 2 + half) * chips + plane) * own_rows
            return [(0, row, 0, own_rows, half_qkv, 0, 0), (1, row, 0, own_rows, LANES, 0, half_qkv)]

        hop = swap(down_turn[0], "y"), swap(down_turn[1], "x")
        down_sum = third_hop_of(*down_hop, *hop)
        up_hop = first_hop(*up_cut, (*hop, *later))
        turn = second_hop_of(*up_hop, (*down_sum[1:], grad_projected))
        hop = swap(turn[0], "y"), swap(turn[1], "x")
        up_sum = third_hop_of(*up_hop, *hop)
        qkv_cut = unplace([qkv_grad, norm_cols], depth, (own_rows, half_qkv + LANES), qkv_cuts)
        qkv_hop = first_hop(*qkv_cut, hop)
        turn = second_hop_of(*qkv_hop)
        hop = swap(turn[0], "y"), swap(turn[1], "x")
        qkv_sum = third_hop_of(*qkv_hop, *hop, up_sum[1:])
        down_red, squares = finish_down(down_sum, qkv_sum[:1])
        up_mine, up_give, out_red, squares = finish_up(up_sum, squares, own_rows, half_ff)
        up_mate = swap(up_give, "c")
        deps = (input_grad, activations, up_mate)
        qkv_mine, qkv_give, small_mine = finish_qkv(qkv_sum, squares, own_rows, half_qkv, deps)
        small_mate, qkv_mate = swap(small_mine, "c"), swap(qkv_give, "c")
        squares, norm_sum = chip_squares(small_mine, small_mate)
        norm_red = mine(norm_sum.reshape(2, own_rows, LANES))[:, :4].T
        grads = (qkv_mine, qkv_mate, out_red, up_mine, up_mate, down_red, norm_red)
        *news, grad_norm = update_all(
            grads, sum_chips(squares), masters, firsts, seconds, rates, decays, (3 * depth, depth)
        )
        return (
            activations.reshape(count, group, width),
            input_grad.reshape(count, group, width),
            grad_norm.reshape(()),
            *news,
        )
    scatter = lambda g: lax.psum_scatter(g, ALL, scatter_dimension=0, tiled=True)
    both = lambda a, axis: jnp.stack([jnp.where(core == k, a, 0.0) for k in (0, 1)], axis)
    to_all = lambda a: a.astype(WIDE)
    qkv_red = scatter(both(to_all(qkv_grad).reshape(width, 3 * depth, block), 2).reshape(width, -1))
    up_red = scatter(both(to_all(up_grad).reshape(width, depth, ff_block), 2).reshape(width, -1))
    out_red = scatter(both(to_all(out_grad).reshape(depth, block, width), 1).reshape(width, width))
    down_red = scatter(both(to_all(down_grad).reshape(depth, ff_block, width), 1).reshape(hidden_units, width))
    norm_red = scatter(norm_cols.astype(WIDE))[:, :4].T

    reduced = (qkv_red, out_red, up_red, down_red, norm_red)
    local_squares = sum(jnp.sum(grad * grad) for grad in reduced)
    grad_norm = jnp.sqrt(lax.psum(local_squares, ALL))
    clip = jnp.minimum(1.0, CLIP_LIMIT / (grad_norm + 1e-06))
    news = [
        adam_update(masters[k], firsts[k], seconds[k], clip * reduced[k], rates[k], decays[k]) for k in range(5)
    ]
    return (
        activations.reshape(count, group, width),
        input_grad.reshape(count, group, width),
        grad_norm,
        *[new[0] for new in news],
        *[new[1] for new in news],
        *[new[2] for new in news],
    )


def solution(mesh):
    depth, planes = mesh.shape["seq"] // 2, mesh.shape["img"]
    across = max(k for k in range(1, planes + 1) if planes % k == 0 and k * k <= planes)
    grid = jax.sharding.Mesh(mesh.devices.reshape(depth, 2, planes // across, across), ALL)
    tokens = P(("y", "x"), ("z", "c"), None)
    matrix, norm = P(ALL, None), P(None, ALL)
    state = (matrix, matrix, matrix, matrix, norm)
    return jax.shard_map(
        body,
        mesh=grid,
        in_specs=(tokens, tokens) + state * 3,
        out_specs=(tokens, tokens, P()) + state * 3,
        check_vma=False,
    )
```

```python
import functools

import jax
import jax.numpy as jnp
from jax import lax
from jax.experimental import pallas as pl
from jax.experimental.pallas import tpu as pltpu
from jax.sharding import PartitionSpec as P

HEAD_DIM = 64
STEP = 10
NORM_EPS = 1e-05
BETA_ONE = 0.9
BETA_TWO = 0.999
ADAM_EPS = 1e-08
WEIGHT_DECAY = 0.1
CLIP_LIMIT = 1.0
LANES = 128

LOW = jnp.bfloat16
WIDE = jnp.float32
ALL = ("z", "c", "y", "x")
SWAP = [(0, 1), (1, 0)]


def swap(value, axis):
    return lax.ppermute(value, axis, SWAP)


def shift(value, step, wrap=True):
    size = lax.axis_size("z")
    pairs = [(i, (i + step) % size) for i in range(size) if wrap or 0 <= i + step < size]
    return lax.ppermute(value, "z", pairs)


def mine(pair_axis_first):
    return jnp.where(lax.axis_index("c") == 0, pair_axis_first[0], pair_axis_first[1])


def other(pair_axis_first):
    return jnp.where(lax.axis_index("c") == 0, pair_axis_first[1], pair_axis_first[0])


def in_order(own, mate, axis=0):
    first = lax.axis_index("c") == 0
    return jnp.concatenate([jnp.where(first, own, mate), jnp.where(first, mate, own)], axis)


def after(value, *before):
    return lax.optimization_barrier((*before, value))[-1]


def column_first(shard):
    return [shard] + [shift(shard, k) for k in range(1, lax.axis_size("z"))]


def plane_last(column, between=()):
    half = column.shape[0] // 2
    along_x, along_y = swap(column, "x"), swap(column, "y")
    along_x, along_y = after(along_x, *between), after(along_y, *between)
    far = (swap(along_y[:half], "x"), swap(along_x[half:], "y"))
    return (column, along_x, along_y) + far


def plane_first(shard):
    far = lax.ppermute(shard, ("y", "x"), [(i, 3 - i) for i in range(4)])
    return jnp.concatenate([shard, swap(shard, "x"), swap(shard, "y"), far])


def column_last(plane):
    parts = [plane]
    for _ in range(1, lax.axis_size("z")):
        parts.append(shift(parts[-1], 1))
    return parts


def column_first_spots(depth):
    half = depth // 2
    spots = [(0, (k,), 0, (k, 0, 0), 0) for k in range(depth)]
    spots += [(1, (k,), 0, (k, 0, 1), 0) for k in range(depth)]
    spots += [(2, (k,), 0, (k, 1, 0), 0) for k in range(depth)]
    spots += [(3, (k,), 0, (k, 1, 1), 0) for k in range(half)]
    return spots + [(4, (k - half,), 0, (k, 1, 1), 0) for k in range(half, depth)]


def plane_first_spots(depth, rows, base):
    return [(base + k, (), p * rows, (k, p // 2, p % 2), 1) for k in range(depth) for p in range(4)]


def first_hop(send_x, keep_x, send_y, keep_y, before=()):
    return keep_x, swap(after(send_x, *before), "x"), keep_y, swap(after(send_y, *before), "y")


def second_hop_of(keep_x, got_x, keep_y, got_y, deps=()):
    depth, rows, cols = keep_x.shape[1:]

    def second_hop(kx, gx, ky, gy, to_y, to_x):
        to_y[...] = (kx[1].astype(WIDE) + gx[1].astype(WIDE)).astype(LOW)
        to_x[...] = (ky[1].astype(WIDE) + gy[1].astype(WIDE)).astype(LOW)

    outs = [((depth, rows, cols), LOW)] * 2
    return run(second_hop, outs, keep_x, got_x, keep_y, got_y, scalars=False, deps=deps)


def third_hop_of(keep_x, got_x, keep_y, got_y, on_y, on_x, deps=()):
    depth, rows, cols = keep_x.shape[1:]

    def third_hop(kx, gx, ky, gy, ony, onx, own, *sends):
        for k in range(depth):
            one = kx[0, k].astype(WIDE) + gx[0, k].astype(WIDE) + ony[k].astype(WIDE)
            two = ky[0, k].astype(WIDE) + gy[0, k].astype(WIDE) + onx[k].astype(WIDE)
            out = sends[k - 1] if k else own
            out[:rows, :] = one.astype(out.dtype)
            out[rows:, :] = two.astype(out.dtype)

    outs = [((2 * rows, cols), WIDE if k == 0 else LOW) for k in range(depth)]
    own, *sends = run(third_hop, outs, keep_x, got_x, keep_y, got_y, on_y, on_x, scalars=False, deps=deps)
    return [own] + [shift(part, k + 1) for k, part in enumerate(sends)]


def sum_of(refs):
    total = refs[0][...]
    for ref in refs[1:]:
        total = total + ref[...].astype(WIDE)
    return total


def spread(value):
    return jnp.broadcast_to(value, (8, LANES))


def total_squares(value):
    return jnp.sum(jnp.sum(value * value, axis=1, keepdims=True), axis=0, keepdims=True)


def finish_down(parts, deps=()):
    def kernel(*refs):
        total = sum_of(refs[: len(parts)])
        refs[-2][...] = total
        refs[-1][...] = spread(total_squares(total))

    return run(kernel, [(parts[0].shape, WIDE), ((8, LANES), WIDE)], *parts, scalars=False, deps=deps)


def finish_up(parts, squares, rows, half_ff):
    half_d = parts[0].shape[1] - half_ff
    small = rows // 2

    def kernel(coords, squares_ref, *refs):
        own_ref, mate_ref, out_ref, total_ref, all_ref = refs[len(parts) :]
        total = sum_of(refs[: len(parts)])
        all_ref[...] = total
        core = coords[3]
        own_ref[...] = all_ref[pl.ds(pl.multiple_of(core * rows, 8), rows), :half_ff]
        mate_ref[...] = all_ref[pl.ds(pl.multiple_of((1 - core) * rows, 8), rows), :half_ff]
        for p in range(2):
            for h in range(2):
                block = total[h * rows + p * small : h * rows + (p + 1) * small, half_ff:]
                out_ref[h * small : (h + 1) * small, p * half_d : (p + 1) * half_d] = block
        total_ref[...] = squares_ref[...] + spread(total_squares(total))

    outs = [((rows, half_ff), WIDE)] * 2 + [((rows, 2 * half_d), WIDE), ((8, LANES), WIDE)]
    scratch = [pltpu.VMEM(parts[0].shape, WIDE)]
    return run(kernel, outs, squares, *parts, scratch=scratch)


def finish_qkv(parts, squares, rows, half_qkv, deps=()):
    def kernel(coords, squares_ref, *refs):
        own_ref, mate_ref, small_ref, all_ref = refs[len(parts) :]
        total = sum_of(refs[: len(parts)])
        all_ref[...] = total
        core = coords[3]
        own_ref[...] = all_ref[pl.ds(pl.multiple_of(core * rows, 8), rows), :half_qkv]
        mate_ref[...] = all_ref[pl.ds(pl.multiple_of((1 - core) * rows, 8), rows), :half_qkv]
        small_ref[: 2 * rows, :] = total[:, half_qkv:]
        small_ref[2 * rows :, :] = squares_ref[...] + spread(total_squares(total[:, :half_qkv]))

    outs = [((rows, half_qkv), WIDE)] * 2 + [((2 * rows + 8, LANES), WIDE)]
    scratch = [pltpu.VMEM(parts[0].shape, WIDE)]
    return run(kernel, outs, squares, *parts, scratch=scratch, deps=deps)


def chip_squares(small, got):
    rows = small.shape[0] - 8

    def kernel(small_ref, got_ref, total_ref, norm_ref):
        total = small_ref[...] + got_ref[...]
        norm_ref[...] = total[:rows]
        total_ref[...] = total[rows:] + spread(total_squares(total[:rows]))

    outs = [((8, LANES), WIDE), ((rows, LANES), WIDE)]
    return run(kernel, outs, small, got, scalars=False)


def sum_chips(value):
    across = lax.ppermute(value, ("y", "x"), [(i, 3 - i) for i in range(4)])
    value = value + swap(value, "y") + (swap(value, "x") + across)
    size, near = lax.axis_size("z"), 1
    while near < size // 2:
        value = value + lax.ppermute(value, "z", [(i, i ^ near) for i in range(size)])
        near *= 2
    return [value, lax.ppermute(value, "z", [(i, i ^ near) for i in range(size)])]


def interleave(first, own, mate, blocks):
    size = own.shape[1] // blocks
    pieces = []
    for j in range(blocks):
        at = slice(j * size, (j + 1) * size)
        pieces += [jnp.where(first, own[:, at], mate[:, at]), jnp.where(first, mate[:, at], own[:, at])]
    return jnp.concatenate(pieces, axis=1)


def update_all(grads, totals, masters, firsts, seconds, rates, decays, blocks):
    steps = 2
    n, m = len(grads), len(totals)

    def tile(array):
        rows, cols = array.shape
        return pl.BlockSpec((rows // steps, cols), lambda i: (i, 0))

    def whole(array):
        return pl.BlockSpec(array.shape, lambda i: (0, 0))

    def kernel(coords, *refs):
        first = coords[3] == 0
        g, t, old, new = refs[:n], refs[n : n + m], refs[n + m : n + m + 15], refs[n + m + 15 :]
        total = sum_of(t)[0:1, 0:1]
        norm = jnp.sqrt(total)
        clip = jnp.minimum(1.0, CLIP_LIMIT / (norm + 1e-06))
        qkv = interleave(first, g[0][...], g[1][...], blocks[0])
        up = interleave(first, g[3][...], g[4][...], blocks[1])
        for k, grad in enumerate((qkv, g[2][...], up, g[5][...], g[6][...])):
            news = adam_update(old[k][...], old[5 + k][...], old[10 + k][...], clip * grad, rates[k], decays[k])
            for part in range(3):
                new[5 * part + k][...] = news[part]
        new[15][...] = norm

    state = (*masters, *firsts, *seconds)
    specs = [whole(a) if k % 5 == 4 else tile(a) for k, a in enumerate(state)]
    norm_out = jax.ShapeDtypeStruct((1, 1), WIDE)
    return pl.pallas_call(
        kernel,
        grid=(steps,),
        out_shape=[jax.ShapeDtypeStruct(a.shape, WIDE) for a in state] + [norm_out],
        in_specs=[pl.BlockSpec(memory_space=pltpu.SMEM)]
        + [tile(a) for a in grads[:-1]]
        + [whole(grads[-1])]
        + [whole(a) for a in totals]
        + specs,
        out_specs=specs + [whole(norm_out)],
        compiler_params=FULL,
    )(coordinates(), *grads, *totals, *state)


def coordinates():
    return jnp.stack([lax.axis_index(name) for name in ("z", "y", "x", "c")]).astype(jnp.int32)


def chip_of(coords, rel, depth, back):
    dz, dy, dx = rel
    z, y, x = coords[0], coords[1], coords[2]
    zz = lax.rem(z + (depth - dz if back else dz), depth)
    yy = 1 - y if dy else y
    xx = 1 - x if dx else x
    return zz, yy * 2 + xx


def window(row, rows, col, cols):
    rows_at = pl.ds(row if isinstance(row, int) else pl.multiple_of(row, 16), rows)
    return rows_at, pl.ds(col, cols)


VMEM = pl.BlockSpec(memory_space=pltpu.VMEM)
ROOM_MB = 16
ROOM = pltpu.CompilerParams(vmem_limit_bytes=ROOM_MB * 1024 * 1024)
FULL = pltpu.CompilerParams(vmem_limit_bytes=56 * 1024 * 1024)


def place(parts, depth, outs, spots, moves, deps=()):
    def kernel(coords, *refs):
        ins, out_refs = refs[: len(parts)], refs[len(parts) + len(deps) :]
        for array, lead, base, rel, piece in spots:
            zz, plane = chip_of(coords, rel, depth, True)
            for o, sr, sc, rows, cols, tr, tc in moves(zz, plane, piece):
                out_refs[o][window(tr, rows, tc, cols)] = ins[array][(*lead, *window(base + sr, rows, sc, cols))]

    return pl.pallas_call(
        kernel,
        out_shape=[jax.ShapeDtypeStruct(s, LOW) for s in outs],
        in_specs=[pl.BlockSpec(memory_space=pltpu.SMEM)]
        + [VMEM] * len(parts)
        + [pl.BlockSpec(memory_space=pl.ANY)] * len(deps),
        out_specs=[VMEM] * len(outs),
        compiler_params=ROOM,
    )(coordinates(), *parts, *deps)


def unplace(grads, depth, rows_cols, moves):
    spots = []
    for dz in range(depth):
        for d in range(2):
            spots += [(0, d, dz, (dz, d, 1), 0), (1, d, dz, (dz, d, 0), 0)]
            spots += [(2, d, dz, (dz, 1, d), 1), (3, d, dz, (dz, 0, d), 1)]

    def kernel(coords, *refs):
        ins, out_refs = refs[: len(grads)], refs[len(grads) :]
        for array, d, dz, rel, half in spots:
            zz, plane = chip_of(coords, rel, depth, False)
            for i, sr, sc, rows, cols, tr, tc in moves(zz, plane, half):
                out_refs[array][(d, dz, *window(tr, rows, tc, cols))] = ins[i][window(sr, rows, sc, cols)]

    return pl.pallas_call(
        kernel,
        out_shape=[jax.ShapeDtypeStruct((2, depth) + rows_cols, LOW)] * 4,
        in_specs=[pl.BlockSpec(memory_space=pltpu.SMEM)] + [VMEM] * len(grads),
        out_specs=[VMEM] * 4,
        compiler_params=ROOM,
    )(coordinates(), *grads)


def cast_qkv(qkv, norm, halves):
    rows, cols = qkv.shape
    wide = cols // 2 + LANES
    block = cols // (2 * halves)

    def kernel(coords, qkv_ref, norm_ref, own_ref, mate_ref, tall):
        first = coords[3] == 0
        for j in range(halves):
            a = qkv_ref[:, 2 * j * block : (2 * j + 1) * block]
            b = qkv_ref[:, (2 * j + 1) * block : (2 * j + 2) * block]
            own_ref[:, j * block : (j + 1) * block] = jnp.where(first, a, b).astype(LOW)
            mate_ref[:, j * block : (j + 1) * block] = jnp.where(first, b, a).astype(LOW)
        tall[...] = jnp.zeros_like(tall)
        tall[0:4, :] = norm_ref[...].astype(LOW).astype(WIDE)
        i = lax.broadcasted_iota(jnp.int32, (rows, rows), 0)
        j = lax.broadcasted_iota(jnp.int32, (rows, rows), 1)
        columns = dot_cols((i == j).astype(LOW), tall[...].astype(LOW)).astype(LOW)
        own_ref[:, cols // 2 :] = columns
        mate_ref[:, cols // 2 :] = columns

    return pl.pallas_call(
        kernel,
        out_shape=[jax.ShapeDtypeStruct((rows, wide), LOW)] * 2,
        in_specs=[pl.BlockSpec(memory_space=pltpu.SMEM), VMEM, VMEM],
        out_specs=[VMEM] * 2,
        scratch_shapes=[pltpu.VMEM((LANES, rows), WIDE)],
        compiler_params=ROOM,
    )(coordinates(), qkv, norm)


def cast_down(down, last):
    rows, cols = down.shape

    def kernel(down_ref, one_ref, two_ref):
        one_ref[...] = down_ref[:last, :].astype(LOW)
        two_ref[...] = down_ref[last:, :].astype(LOW)

    return pl.pallas_call(
        kernel,
        out_shape=[jax.ShapeDtypeStruct((last, cols), LOW), jax.ShapeDtypeStruct((rows - last, cols), LOW)],
        in_specs=[VMEM],
        out_specs=[VMEM] * 2,
        compiler_params=ROOM,
    )(down)


def cast_rest(up, out, halves):
    rows, cols = up.shape
    block, width = cols // (2 * halves), out.shape[1]

    def kernel(coords, up_ref, out_ref, own_ref, mate_ref, part_ref):
        first = coords[3] == 0
        for j in range(halves):
            a = up_ref[:, 2 * j * block : (2 * j + 1) * block]
            b = up_ref[:, (2 * j + 1) * block : (2 * j + 2) * block]
            own_ref[:, j * block : (j + 1) * block] = jnp.where(first, a, b).astype(LOW)
            mate_ref[:, j * block : (j + 1) * block] = jnp.where(first, b, a).astype(LOW)
        part_ref[:rows, :] = out_ref[:, : width // 2].astype(LOW)
        part_ref[rows:, :] = out_ref[:, width // 2 :].astype(LOW)

    return pl.pallas_call(
        kernel,
        out_shape=[jax.ShapeDtypeStruct((rows, cols // 2), LOW)] * 2
        + [jax.ShapeDtypeStruct((2 * rows, width // 2), LOW)],
        in_specs=[pl.BlockSpec(memory_space=pltpu.SMEM), VMEM, VMEM],
        out_specs=[VMEM] * 3,
        compiler_params=ROOM,
    )(coordinates(), up, out)


def join_rows(own, mate, side=None):
    rows, cols = own.shape
    wide = cols + (side.shape[1] if side is not None else 0)

    def kernel(coords, own_ref, mate_ref, *refs):
        out_ref = refs[-1]
        core = coords[3]
        out_ref[pl.ds(pl.multiple_of(core * rows, 16), rows), :cols] = own_ref[...]
        out_ref[pl.ds(pl.multiple_of((1 - core) * rows, 16), rows), :cols] = mate_ref[...]
        if side is not None:
            out_ref[:, cols:] = refs[0][...]

    ins = [own, mate] + ([side] if side is not None else [])
    return pl.pallas_call(
        kernel,
        out_shape=jax.ShapeDtypeStruct((2 * rows, wide), LOW),
        in_specs=[pl.BlockSpec(memory_space=pltpu.SMEM)] + [VMEM] * len(ins),
        out_specs=VMEM,
        compiler_params=ROOM,
    )(coordinates(), *ins)


def run(kernel, outs, *ins, scalars=True, scratch=(), flops=0, room=ROOM_MB, deps=()):
    first = len(ins) + scalars

    def body_of(*refs):
        return kernel(*refs[:first], *refs[first + len(deps) :])

    out_shape = [jax.ShapeDtypeStruct(shape, kind) for shape, kind in outs]
    return pl.pallas_call(
        body_of,
        out_shape=out_shape,
        in_specs=([pl.BlockSpec(memory_space=pltpu.SMEM)] if scalars else [])
        + [VMEM] * len(ins)
        + [pl.BlockSpec(memory_space=pl.ANY)] * len(deps),
        out_specs=[VMEM] * len(outs),
        scratch_shapes=list(scratch),
        compiler_params=pltpu.CompilerParams(vmem_limit_bytes=room * 1024 * 1024),
        cost_estimate=pl.CostEstimate(flops=flops, bytes_accessed=0, transcendentals=0),
    )(*([coordinates()] if scalars else []), *ins, *deps)


def dot(left, right):
    return jnp.dot(left, right, preferred_element_type=WIDE)


def dot_rows(left, right):
    return lax.dot_general(left, right, (((0,), (0,)), ((), ())), preferred_element_type=WIDE)


def dot_cols(left, right):
    return lax.dot_general(left, right, (((1,), (1,)), ((), ())), preferred_element_type=WIDE)


def eye(rows, cols):
    i = lax.broadcasted_iota(jnp.int32, (rows, cols), 0)
    return (i == lax.broadcasted_iota(jnp.int32, (rows, cols), 1)).astype(LOW)


def normalise(values):
    center = values - jnp.mean(values, axis=-1, keepdims=True)
    rate = lax.rsqrt(jnp.mean(center * center, axis=-1, keepdims=True) + NORM_EPS)
    return center * rate, rate


def norm_back(normed, rate, grad, gain):
    scaled = grad * gain
    shared = jnp.mean(scaled, axis=-1, keepdims=True)
    along = jnp.mean(scaled * normed, axis=-1, keepdims=True)
    return rate * (scaled - shared - normed * along)


def low_lanes(rows):
    return lax.broadcasted_iota(jnp.int32, (rows, LANES), 1) < HEAD_DIM


def by_head(pair):
    wide = pair.astype(WIDE)
    first = low_lanes(pair.shape[0])
    return jnp.where(first, wide, 0.0).astype(LOW), jnp.where(first, 0.0, wide).astype(LOW)


def pack_state(square):
    first = low_lanes(HEAD_DIM)
    return jnp.where(first, square[:HEAD_DIM], square[HEAD_DIM:])


def open_state(packed):
    first = low_lanes(HEAD_DIM)
    return jnp.concatenate([jnp.where(first, packed, 0.0), jnp.where(first, 0.0, packed)])


def feature(values):
    return jnp.where(values > 0.0, values + 1.0, jnp.exp(jnp.minimum(values, 0.0)))


def project(x, norm_w, qkv_w):
    tokens, width = x.shape
    half = qkv_w.shape[1] // 3
    pairs = half // LANES
    step = tokens // 2

    def kernel(x_ref, norm_ref, w_ref, rows_ref, normed_ref, qk_ref, q_ref, k_ref, v_ref, state_ref, sums):
        rows_ref[...] = dot_cols(eye(8, LANES), norm_ref[...])
        gain, bias = rows_ref[0:1, :], rows_ref[1:2, :]
        @pl.loop(0, 2)
        def _(i):
            at = at_block(i, step)
            normed = normalise(x_ref[at, :].astype(WIDE))[0]
            normed_ref[at, :] = (normed * gain + bias).astype(LOW)
            low = normed_ref[at, :]
            for j, out in enumerate((q_ref, k_ref)):
                part = dot(low, w_ref[:, j * half : (j + 1) * half])
                qk_ref[at, j * half : (j + 1) * half] = part
                out[at, :] = feature(part).astype(LOW)
            v_ref[at, :] = dot(low, w_ref[:, 2 * half :]).astype(LOW)
        total = dot_rows(jnp.ones((tokens, 8), LOW), k_ref[...])
        sums[...] = jnp.zeros_like(sums)
        for p in range(pairs):
            lanes = slice(p * LANES, (p + 1) * LANES)
            packed = pack_state(dot_rows(k_ref[:, lanes], v_ref[:, lanes]))
            state_ref[p * HEAD_DIM : (p + 1) * HEAD_DIM, :] = packed.astype(LOW)
            sums[p : p + 1, :] = total[0:1, lanes]
        state_ref[pairs * HEAD_DIM :, :] = sums[...].astype(LOW)

    outs = [((8, width), WIDE), ((tokens, width), LOW), ((tokens, 2 * half), WIDE)] + [((tokens, half), LOW)] * 3
    outs += [((pairs * HEAD_DIM + 16, LANES), LOW)]
    scratch = [pltpu.VMEM((16, LANES), WIDE)]
    return run(kernel, outs, x, norm_w, qkv_w, scalars=False, scratch=scratch)


def at_block(index, size):
    return pl.ds(pl.multiple_of(index * size, size), size)


def total_state(refs):
    total = refs[0][...].astype(WIDE)
    for ref in refs[1:]:
        total = total + ref[...].astype(WIDE)
    return total


def causal_mask(step):
    i = lax.broadcasted_iota(jnp.int32, (step, step), 0)
    return i >= lax.broadcasted_iota(jnp.int32, (step, step), 1)


def attend(query, key, value, parts, deps=()):
    tokens, half = query.shape
    pairs, step = half // LANES, tokens // 2

    def kernel(q_ref, k_ref, v_ref, *refs):
        mixed_ref, low_ref, denom_ref, state_ref, token_ref = refs[len(parts) :]
        token_ref[...] = jnp.zeros_like(token_ref)
        state_ref[...] = total_state(refs[: len(parts)])
        lower = causal_mask(step)
        first = low_lanes(step)
        top = low_lanes(HEAD_DIM)
        diagonal = eye(LANES, LANES).astype(WIDE)
        @pl.loop(0, pairs)
        def _(p):
            lanes = at_block(p, LANES)
            packed = state_ref[at_block(p, HEAD_DIM), :]
            sums = state_ref[pl.ds(pairs * HEAD_DIM + p, 1), :]
            column = jnp.sum(diagonal * sums, axis=1, keepdims=True)
            zero = jnp.zeros((HEAD_DIM, LANES), WIDE)
            ext = (
                jnp.concatenate([jnp.where(top, packed, column[:HEAD_DIM]), zero]).astype(LOW),
                jnp.concatenate([zero, jnp.where(top, column[HEAD_DIM:], packed)]).astype(LOW),
            )
            wide = v_ref[:, lanes].astype(WIDE)
            full = low_lanes(tokens)
            value_ext = (jnp.where(full, wide, 1.0).astype(LOW), jnp.where(full, 1.0, wide).astype(LOW))
            queries = by_head(q_ref[:, lanes])
            for i in range(2):
                at = slice(i * step, (i + 1) * step)
                got = []
                for h in range(2):
                    rows = queries[h][at]
                    total = dot(rows, ext[h])
                    for j in range(i + 1):
                        to = slice(j * step, (j + 1) * step)
                        scores = dot_cols(rows, k_ref[to, lanes])
                        if j == i:
                            scores = jnp.where(lower, scores, 0.0)
                        total = total + dot(scores.astype(LOW), value_ext[h][to])
                    got.append(total)
                denom = pltpu.roll(jnp.where(first, got[1], got[0]), HEAD_DIM, 1)
                mixed = jnp.where(first, got[0], got[1]) / denom
                mixed_ref[at, lanes] = mixed
                low_ref[at, lanes] = mixed.astype(LOW)
                denom_ref[at, lanes] = denom

    outs = [((tokens, half), WIDE), ((tokens, half), LOW), ((tokens, half), WIDE), (parts[0].shape, WIDE)]
    outs += [((8, LANES), WIDE)]
    return run(kernel, outs, query, key, value, *parts, scalars=False, deps=deps)


def out_project(mixed, out_w):
    def kernel(mixed_ref, w_ref, part_ref, low_ref):
        part = dot(mixed_ref[...], w_ref[...])
        part_ref[...] = part
        low_ref[...] = part.astype(LOW)

    shape = (mixed.shape[0], out_w.shape[1])
    return run(kernel, [(shape, WIDE), (shape, LOW)], mixed, out_w, scalars=False)


def feed(x, part, got, rows, up_w):
    tokens, width = x.shape
    units, step, cut = up_w.shape[1], tokens // 2, 512

    def kernel(x_ref, part_ref, got_ref, rows_ref, w_ref, resid_ref, normed_ref, act_ref, slope_ref):
        @pl.loop(0, 2)
        def _(i):
            at = at_block(i, step)
            resid = x_ref[at, :].astype(WIDE) + part_ref[at, :] + got_ref[at, :].astype(WIDE)
            resid_ref[at, :] = resid
            normed_ref[at, :] = (normalise(resid)[0] * rows_ref[2:3, :] + rows_ref[3:4, :]).astype(LOW)

        @pl.loop(0, units // cut)
        def _(j):
            to = at_block(j, cut)
            v = dot(normed_ref[...], w_ref[:, to])
            root = (2.0 / 3.141592653589793) ** 0.5
            square = v * v
            bend = jnp.tanh(root * v * (1.0 + 0.044715 * square))
            cdf = 0.5 * (1.0 + bend)
            act_ref[:, to] = (v * cdf).astype(LOW)
            slope_ref[:, to] = cdf + 0.5 * v * (1.0 - bend * bend) * (root * (1.0 + 3.0 * 0.044715 * square))

    outs = [((tokens, width), WIDE), ((tokens, width), LOW), ((tokens, units), LOW), ((tokens, units), WIDE)]
    return run(kernel, outs, x, part, got, rows, up_w, scalars=False)


def feed_back(grad_out, down_w, slope, up_w):
    tokens, width = grad_out.shape
    units, cut = up_w.shape[1], 512

    def kernel(g_ref, down_ref, slope_ref, up_ref, hidden_ref, part_ref, low_ref):
        @pl.loop(0, units // cut)
        def _(j):
            to = at_block(j, cut)
            hidden_ref[:, to] = (dot_cols(g_ref[...], down_ref[to, :]) * slope_ref[:, to]).astype(LOW)

        @pl.loop(0, width // cut)
        def _(j):
            to = at_block(j, cut)
            part = dot_cols(hidden_ref[...], up_ref[to, :])
            part_ref[:, to] = part
            low_ref[:, to] = part.astype(LOW)

    outs = [((tokens, units), LOW), ((tokens, width), WIDE), ((tokens, width), LOW)]
    return run(kernel, outs, grad_out, down_w, slope, up_w, scalars=False)


def down_project(activated, down_w, resid, deps):
    tokens, width = resid.shape
    group, cut = tokens // 2, width // 2

    def kernel(coords, act_ref, w_ref, resid_ref, own_ref, give_ref):
        own = pl.ds(pl.multiple_of(coords[3] * group, 16), group)
        mate = pl.ds(pl.multiple_of((1 - coords[3]) * group, 16), group)

        @pl.loop(0, 2)
        def _(j):
            to = at_block(j, cut)
            own_ref[:, to] = resid_ref[own, to] + dot(act_ref[own, :], w_ref[:, to])
            give_ref[:, to] = dot(act_ref[mate, :], w_ref[:, to]).astype(LOW)

    outs = [((group, width), WIDE), ((group, width), LOW)]
    return run(kernel, outs, activated, down_w, resid, deps=deps)


def weight_grad(rows, grad, deps=()):
    tokens, width = rows.shape
    units, cut = grad.shape[1], 512

    def kernel(rows_ref, grad_ref, out_ref):
        @pl.loop(0, units // cut)
        def _(j):
            to = at_block(j, cut)
            out_ref[:, to] = dot_rows(rows_ref[...], grad_ref[:, to]).astype(LOW)

    return run(kernel, [((width, units), LOW)], rows, grad, scalars=False, deps=deps)[0]


def attend_turn(part, got, resid, rows, grad_out, out_w, mixed, denom, query, deps):
    tokens, width = resid.shape
    half = mixed.shape[1]
    pairs, step = half // LANES, tokens // 2

    def kernel(
        part_ref, got_ref, resid_ref, rows_ref, g_ref, w_ref, mixed_ref, denom_ref, q_ref,
        grad_ref, low_ref, a_ref, b_ref, state_ref, norm_ref, sums,
    ):
        gain = rows_ref[2:3, :]
        first = low_lanes(step)
        norm_ref[...] = jnp.zeros_like(norm_ref)

        @pl.loop(0, 2)
        def _(i):
            at = at_block(i, step)
            normed, rate = normalise(resid_ref[at, :])
            own = part_ref[at, :]
            norm_ref[0:1, :] += jnp.sum(own * normed, axis=0, keepdims=True)
            norm_ref[1:2, :] += jnp.sum(own, axis=0, keepdims=True)
            grad = g_ref[at, :].astype(WIDE) + norm_back(normed, rate, own + got_ref[at, :].astype(WIDE), gain)
            grad_ref[at, :] = grad
            low_ref[at, :] = grad.astype(LOW)
            turned = dot_cols(low_ref[at, :], w_ref[...]) / denom_ref[at, :]
            a_ref[at, :] = turned.astype(LOW)
            along = turned * mixed_ref[at, :]
            for p in range(pairs):
                lanes = slice(p * LANES, (p + 1) * LANES)
                piece = along[:, lanes]
                low = jnp.sum(jnp.where(first, piece, 0.0), axis=1, keepdims=True)
                high = jnp.sum(jnp.where(first, 0.0, piece), axis=1, keepdims=True)
                b_ref[at, lanes] = -jnp.where(first, low, high)
        sums[...] = jnp.zeros_like(sums)
        for p in range(pairs):
            lanes = slice(p * LANES, (p + 1) * LANES)
            packed = pack_state(dot_rows(q_ref[:, lanes], a_ref[:, lanes]))
            state_ref[p * HEAD_DIM : (p + 1) * HEAD_DIM, :] = packed.astype(LOW)
            sums[p : p + 1, :] = jnp.sum(q_ref[:, lanes].astype(WIDE) * b_ref[:, lanes], axis=0, keepdims=True)
        state_ref[pairs * HEAD_DIM :, :] = sums[...].astype(LOW)

    outs = [((tokens, width), WIDE), ((tokens, width), LOW), ((tokens, half), LOW), ((tokens, half), WIDE)]
    outs += [((pairs * HEAD_DIM + 16, LANES), LOW), ((2, width), WIDE)]
    ins = (part, got, resid, rows, grad_out, out_w, mixed, denom, query)
    scratch = [pltpu.VMEM((16, LANES), WIDE)]
    return run(kernel, outs, *ins, scalars=False, scratch=scratch, deps=deps)


def attend_back(query, key, value, qk, a_low, b_rows, state, parts, deps=()):
    tokens, half = query.shape
    pairs, step = half // LANES, tokens // 2

    def kernel(q_ref, k_ref, v_ref, qk_ref, a_ref, b_ref, state_ref, *refs):
        out_ref, later = refs[len(parts) :]
        later[...] = total_state(refs[: len(parts)])
        lower = causal_mask(step)
        @pl.loop(0, pairs)
        def _(p):
            lanes, rows = at_block(p, LANES), at_block(p, HEAD_DIM)
            sums = pl.ds(pairs * HEAD_DIM + p, 1)
            before, after_it = open_state(state_ref[rows, :]).astype(LOW), open_state(later[rows, :]).astype(LOW)
            queries, keys, pulls = by_head(q_ref[:, lanes]), by_head(k_ref[:, lanes]), by_head(a_ref[:, lanes])
            cuts = [slice(i * step, (i + 1) * step) for i in range(2)]
            grad_q = [dot_cols(a_ref[c, lanes], before) + b_ref[c, lanes] * state_ref[sums, :] for c in cuts]
            grad_k = [dot_cols(v_ref[c, lanes], after_it) + later[sums, :] for c in cuts]
            shifts = b_ref[:, lanes]
            grad_v = [dot(k_ref[c, lanes], after_it) for c in cuts]
            for i in range(2):
                for j in range(i + 1):
                    for h in range(2):
                        q, a = queries[h][cuts[i]], pulls[h][cuts[i]]
                        b = shifts[cuts[i], h * HEAD_DIM : h * HEAD_DIM + 1]
                        scores = dot_cols(q, k_ref[cuts[j], lanes])
                        pull = dot_cols(a, v_ref[cuts[j], lanes]) + b
                        if j == i:
                            scores, pull = jnp.where(lower, scores, 0.0), jnp.where(lower, pull, 0.0)
                        scores, pull = scores.astype(LOW), pull.astype(LOW)
                        grad_q[i] = grad_q[i] + dot(pull, keys[h][cuts[j]])
                        grad_k[j] = grad_k[j] + dot_rows(pull, q)
                        grad_v[j] = grad_v[j] + dot_rows(scores, a)
            for i, c in enumerate(cuts):
                for n, grad in enumerate((grad_q[i], grad_k[i])):
                    at = at_block(n * pairs + p, LANES)
                    raw = qk_ref[c, at]
                    out_ref[c, at] = (grad * jnp.where(raw > 0.0, 1.0, jnp.exp(jnp.minimum(raw, 0.0)))).astype(LOW)
                out_ref[c, at_block(2 * pairs + p, LANES)] = grad_v[i].astype(LOW)

    ins = (query, key, value, qk, a_low, b_rows, state, *parts)
    scratch = [pltpu.VMEM(parts[0].shape, WIDE)]
    return run(kernel, [((tokens, 3 * half), LOW)], *ins, scalars=False, scratch=scratch, deps=deps)[0]


def project_back(grad, qkv_w, x, norm_two):
    tokens, width = x.shape
    step = tokens // 2

    def kernel(grad_ref, w_ref, x_ref, two_ref, part_ref, low_ref, cols_ref, rows):
        rows[...] = jnp.zeros_like(rows)

        @pl.loop(0, 2)
        def _(i):
            at = at_block(i, step)
            part = dot_cols(grad_ref[at, :], w_ref[...])
            part_ref[at, :] = part
            low_ref[at, :] = part.astype(LOW)
            rows[0:1, :] += jnp.sum(part * normalise(x_ref[at, :].astype(WIDE))[0], axis=0, keepdims=True)
            rows[1:2, :] += jnp.sum(part, axis=0, keepdims=True)

        rows[2:4, :] = two_ref[...]
        cols_ref[...] = dot_rows(rows[...].astype(LOW), eye(8, LANES)).astype(LOW)

    outs = [((tokens, width), WIDE), ((tokens, width), LOW), ((width, LANES), LOW)]
    scratch = [pltpu.VMEM((8, width), WIDE)]
    return run(kernel, outs, grad, qkv_w, x, norm_two, scalars=False, scratch=scratch)


def input_back(part, got, grad_resid, own_x, rows):
    group, width = own_x.shape

    def kernel(coords, part_ref, got_ref, resid_ref, x_ref, rows_ref, out_ref):
        at = pl.ds(pl.multiple_of(coords[3] * group, 16), group)
        normed, rate = normalise(x_ref[...].astype(WIDE))
        grad = part_ref[at, :] + got_ref[...].astype(WIDE)
        out_ref[...] = (resid_ref[at, :] + norm_back(normed, rate, grad, rows_ref[0:1, :])).astype(LOW)

    return run(kernel, [((group, width), LOW)], part, got, grad_resid, own_x, rows)[0]


def adam_update(weight, first, second, grad, rate, decay):
    first_new = BETA_ONE * first + (1.0 - BETA_ONE) * grad
    second_new = BETA_TWO * second + (1.0 - BETA_TWO) * grad * grad
    first_hat = first_new / (1.0 - BETA_ONE**STEP)
    second_hat = second_new / (1.0 - BETA_TWO**STEP)
    weight_new = weight - rate * (first_hat / (jnp.sqrt(second_hat) + ADAM_EPS) + decay * weight)
    return (weight_new, first_new, second_new)


def from_others(low, step):
    if lax.axis_size("z") == 4 and step == 1:
        near = shift(low, step, wrap=False)
        pair = (low.astype(WIDE) + near.astype(WIDE)).astype(LOW)
        return [near, shift(pair, 2 * step, wrap=False)]
    return [shift(low, step * k, wrap=False) for k in range(1, lax.axis_size("z"))]


def body(
    images,
    cotangent,
    qkv_weight,
    out_weight,
    up_weight,
    down_weight,
    norm_params,
    qkv_first,
    out_first,
    up_first,
    down_first,
    norm_first,
    qkv_second,
    out_second,
    up_second,
    down_second,
    norm_second,
):
    depth, core = lax.axis_size("z"), lax.axis_index("c")
    count, group, width = images.shape
    hidden_units = up_weight.shape[1]
    own_rows = qkv_weight.shape[0]
    own_units = down_weight.shape[0]
    chips = lax.axis_size("y") * lax.axis_size("x")
    block, ff_block = width // (2 * depth), hidden_units // (2 * depth)
    half_qkv, half_ff, half_d = 3 * width // 2, hidden_units // 2, width // 2
    ring = lax.axis_size("y") == 2 and lax.axis_size("x") == 2 and depth == 4 and own_rows % 32 == 0
    heads = half_d // HEAD_DIM
    tokens = 2 * group

    own_x, own_g = images.reshape(group, width), cotangent.reshape(group, width)
    split_qkv = lambda w: jnp.moveaxis(w.reshape(-1, 3 * depth, 2, block), 2, 0).reshape(2, -1, half_qkv)
    split_up = lambda w: jnp.moveaxis(w.reshape(-1, depth, 2, ff_block), 2, 0).reshape(2, -1, half_ff)

    thin, small, last = own_units // 2, own_rows // 2, 3 * own_units // 8
    if ring:
        qkv_mine, qkv_give = cast_qkv(qkv_weight, norm_params, 3 * depth)
        qkv_part = join_rows(qkv_mine, swap(qkv_give, "c"))
        down_one, down_two = cast_down(down_weight, last)
        two_plane = plane_first(after(down_two, qkv_part))
        up_mine, up_give, out_part = cast_rest(after(up_weight, two_plane), out_weight, depth)
        inputs = join_rows(own_x, swap(own_x, "c"))
        up_part = join_rows(up_mine, swap(up_give, "c"), out_part)
        qkv_column = column_first(qkv_part)
        qkv_column = [after(part, two_plane, up_part, inputs) for part in qkv_column]
        up_column = column_first(after(up_part, *qkv_column))
        qkv_parts = plane_last(jnp.stack(qkv_column))
        g_mate = swap(after(own_g, *up_column), "c")
        two_parts = [two_plane, shift(after(two_plane, *up_column), 1)]
        one_column = column_first(after(down_one, two_parts[1]))

        def qkv_moves(zz, plane, piece):
            row = lambda h: ((zz * 2 + h) * chips + plane) * own_rows
            moves = [(0, h * own_rows, 0, own_rows, half_qkv, row(h), 0) for h in (0, 1)]
            return moves + [(1, h * own_rows, half_qkv, own_rows, LANES, row(h), 0) for h in (0, 1)]

        def up_moves(zz, plane, piece):
            row = lambda h: ((zz * 2 + h) * chips + plane) * own_rows
            moves = [(0, h * own_rows, 0, own_rows, half_ff, row(h), 0) for h in (0, 1)]
            to = zz * block + plane * own_rows
            return moves + [(1, h * own_rows, half_ff, own_rows, half_d, to, h * half_d) for h in (0, 1)]

        def down_moves(zz, plane, piece):
            rows = own_units - last if piece else last
            return [(0, 0, 0, rows, width, zz * ff_block + plane * own_units + piece * last, 0)]

        spots = column_first_spots(depth)
        qkv_w, norm_w = place(qkv_parts, depth, [(width, half_qkv), (width, LANES)], spots, qkv_moves)
    else:
        qkv_low, out_low = qkv_weight.astype(LOW), out_weight.astype(LOW)
        up_low, down_low = up_weight.astype(LOW), down_weight.astype(LOW)
        norm_low = norm_params.astype(LOW)
        x_mate, g_mate = swap(own_x, "c"), swap(own_g, "c")
        whole = lambda w, axis=0: lax.all_gather(w, ALL, axis=axis, tiled=True)
        qkv_w, up_w = mine(split_qkv(whole(qkv_low))), mine(split_up(whole(up_low)))
        rows_half = lambda w, b: mine(jnp.moveaxis(w.reshape(depth, 2, b, width), 1, 0)).reshape(-1, width)
        out_w, down_w = rows_half(whole(out_low), block), rows_half(whole(down_low), ff_block)
        norm_w = jnp.pad(whole(norm_low, 1).T, ((0, 0), (0, LANES - 4)))

        inputs = join_rows(own_x, x_mate)
    grad_out = join_rows(own_g, g_mate)
    halves = lambda a: a.reshape(2, group, -1)
    rows, normed_one, qk, query, key, value, state = project(inputs, norm_w, qkv_w)
    earlier = from_others(state, 1)
    mixed, mixed_low, denom, state_in, attended = attend(query, key, value, earlier, (grad_out,))
    if ring:
        gate = (*earlier, *one_column[1:])
        up_parts = plane_last(after(jnp.stack(up_column), *qkv_parts[3:]), gate)
        two_parts.append(shift(after(two_parts[-1], *gate), 1))
        for _ in range(3, depth):
            two_parts.append(shift(two_parts[-1], 1))
        up_w, out_w = place(
            up_parts, depth, [(width, half_ff), (half_d, width)], spots, up_moves, two_parts[2:3]
        )
    out_part, out_low = out_project(mixed_low, out_w)
    out_got = swap(out_low, "c")
    resid, normed_two, activated, slope = feed(inputs, out_part, out_got, rows, up_w)
    down_grad = dot_rows(activated, grad_out).astype(LOW)
    if ring:
        def down_cuts(zz, plane, half):
            return [(0, zz * ff_block + plane * own_units + half * thin, 0, thin, width, 0, 0)]

        down_cut = unplace([down_grad], depth, (thin, width), down_cuts)
        one_parts = plane_last(after(jnp.stack(one_column), *up_parts[3:]), (down_cut[0][0, 0, :16, :LANES],))
        down_hop = first_hop(*down_cut, one_parts[3:])
        spots = spots + plane_first_spots(depth, own_units - last, 5)
        down_parts = [*one_parts, *two_parts]
        (down_w,) = place(down_parts, depth, [(half_ff, width)], spots, down_moves, (down_cut[0],))

    grad_hidden, two_part, two_low = feed_back(grad_out, down_w, slope, up_w)
    down_own, down_give = down_project(activated, down_w, resid, (two_low,))
    down_got = swap(down_give, "c")
    activations = (down_own + down_got.astype(WIDE)).astype(LOW)
    up_grad = weight_grad(normed_two, grad_hidden)
    two_got = swap(two_low, "c")
    deps = (up_grad,)
    if ring:
        down_turn = second_hop_of(*down_hop, (up_grad,))
        deps = (up_grad, down_turn[0])
    grad_resid, grad_resid_low, a_low, b_rows, state_grad, norm_two = attend_turn(
        two_part, two_got, resid, rows, grad_out, out_w, mixed, denom, query, deps
    )
    later = from_others(state_grad, -1)
    out_grad = dot_rows(mixed_low, grad_resid_low).astype(LOW)
    deps = ()
    if ring:

        def up_cuts(zz, plane, half):
            cuts = [(0, ((zz * 2 + half) * chips + plane) * own_rows, 0, own_rows, half_ff, 0, 0)]
            row = zz * block + plane * own_rows + half * small
            return cuts + [(1, row, p * half_d, small, half_d, p * small, half_ff) for p in (0, 1)]

        up_cut = unplace([up_grad, out_grad], depth, (own_rows, half_ff + half_d), up_cuts)
        deps = (up_cut[0],)
    grad_projected = attend_back(query, key, value, qk, a_low, b_rows, state_in, later, deps)
    qkv_grad = dot_rows(normed_one, grad_projected).astype(LOW)
    one_part, one_low, norm_cols = project_back(grad_projected, qkv_w, inputs, norm_two)
    input_grad = input_back(one_part, swap(other(halves(one_low)), "c"), grad_resid, own_x, rows)

    out_fan = max(1, width * 64 // (tokens * depth))
    rates = (3.0 * width**-0.5, 3.0 * out_fan**-0.5, 3.0 * width**-0.5, 3.0 * hidden_units**-0.5, 1.5)
    decays = (WEIGHT_DECAY, WEIGHT_DECAY, WEIGHT_DECAY, WEIGHT_DECAY, 0.0)
    masters = (qkv_weight, out_weight, up_weight, down_weight, norm_params)
    firsts = (qkv_first, out_first, up_first, down_first, norm_first)
    seconds = (qkv_second, out_second, up_second, down_second, norm_second)
    if ring:

        def qkv_cuts(zz, plane, half):
            row = ((zz * 2 + half) * chips + plane) * own_rows
            return [(0, row, 0, own_rows, half_qkv, 0, 0), (1, row, 0, own_rows, LANES, 0, half_qkv)]

        hop = swap(down_turn[0], "y"), swap(down_turn[1], "x")
        down_sum = third_hop_of(*down_hop, *hop)
        up_hop = first_hop(*up_cut, (*hop, *later))
        turn = second_hop_of(*up_hop, (*down_sum[1:], grad_projected))
        hop = swap(turn[0], "y"), swap(turn[1], "x")
        up_sum = third_hop_of(*up_hop, *hop)
        qkv_cut = unplace([qkv_grad, norm_cols], depth, (own_rows, half_qkv + LANES), qkv_cuts)
        qkv_hop = first_hop(*qkv_cut, hop)
        turn = second_hop_of(*qkv_hop)
        hop = swap(turn[0], "y"), swap(turn[1], "x")
        qkv_sum = third_hop_of(*qkv_hop, *hop, up_sum[1:])
        down_red, squares = finish_down(down_sum, qkv_sum[:1])
        up_mine, up_give, out_red, squares = finish_up(up_sum, squares, own_rows, half_ff)
        up_mate = swap(up_give, "c")
        deps = (input_grad, activations, up_mate)
        qkv_mine, qkv_give, small_mine = finish_qkv(qkv_sum, squares, own_rows, half_qkv, deps)
        small_mate, qkv_mate = swap(small_mine, "c"), swap(qkv_give, "c")
        squares, norm_sum = chip_squares(small_mine, small_mate)
        norm_red = mine(norm_sum.reshape(2, own_rows, LANES))[:, :4].T
        grads = (qkv_mine, qkv_mate, out_red, up_mine, up_mate, down_red, norm_red)
        *news, grad_norm = update_all(
            grads, sum_chips(squares), masters, firsts, seconds, rates, decays, (3 * depth, depth)
        )
        return (
            activations.reshape(count, group, width),
            input_grad.reshape(count, group, width),
            grad_norm.reshape(()),
            *news,
        )
    scatter = lambda g: lax.psum_scatter(g, ALL, scatter_dimension=0, tiled=True)
    both = lambda a, axis: jnp.stack([jnp.where(core == k, a, 0.0) for k in (0, 1)], axis)
    to_all = lambda a: a.astype(WIDE)
    qkv_red = scatter(both(to_all(qkv_grad).reshape(width, 3 * depth, block), 2).reshape(width, -1))
    up_red = scatter(both(to_all(up_grad).reshape(width, depth, ff_block), 2).reshape(width, -1))
    out_red = scatter(both(to_all(out_grad).reshape(depth, block, width), 1).reshape(width, width))
    down_red = scatter(both(to_all(down_grad).reshape(depth, ff_block, width), 1).reshape(hidden_units, width))
    norm_red = scatter(norm_cols.astype(WIDE))[:, :4].T

    reduced = (qkv_red, out_red, up_red, down_red, norm_red)
    local_squares = sum(jnp.sum(grad * grad) for grad in reduced)
    grad_norm = jnp.sqrt(lax.psum(local_squares, ALL))
    clip = jnp.minimum(1.0, CLIP_LIMIT / (grad_norm + 1e-06))
    news = [
        adam_update(masters[k], firsts[k], seconds[k], clip * reduced[k], rates[k], decays[k]) for k in range(5)
    ]
    return (
        activations.reshape(count, group, width),
        input_grad.reshape(count, group, width),
        grad_norm,
        *[new[0] for new in news],
        *[new[1] for new in news],
        *[new[2] for new in news],
    )


def solution(mesh):
    depth, planes = mesh.shape["seq"] // 2, mesh.shape["img"]
    across = max(k for k in range(1, planes + 1) if planes % k == 0 and k * k <= planes)
    grid = jax.sharding.Mesh(mesh.devices.reshape(depth, 2, planes // across, across), ALL)
    tokens = P(("y", "x"), ("z", "c"), None)
    matrix, norm = P(ALL, None), P(None, ALL)
    state = (matrix, matrix, matrix, matrix, norm)
    return jax.shard_map(
        body,
        mesh=grid,
        in_specs=(tokens, tokens) + state * 3,
        out_specs=(tokens, tokens, P()) + state * 3,
        check_vma=False,
    )
```

```python
import functools

import jax
import jax.numpy as jnp
from jax import lax
from jax.experimental import pallas as pl
from jax.experimental.pallas import tpu as pltpu
from jax.sharding import PartitionSpec as P

HEAD_DIM = 64
STEP = 10
NORM_EPS = 1e-05
BETA_ONE = 0.9
BETA_TWO = 0.999
ADAM_EPS = 1e-08
WEIGHT_DECAY = 0.1
CLIP_LIMIT = 1.0
LANES = 128

LOW = jnp.bfloat16
WIDE = jnp.float32
ALL = ("z", "c", "y", "x")
SWAP = [(0, 1), (1, 0)]


def swap(value, axis):
    return lax.ppermute(value, axis, SWAP)


def shift(value, step, wrap=True):
    size = lax.axis_size("z")
    pairs = [(i, (i + step) % size) for i in range(size) if wrap or 0 <= i + step < size]
    return lax.ppermute(value, "z", pairs)


def mine(pair_axis_first):
    return jnp.where(lax.axis_index("c") == 0, pair_axis_first[0], pair_axis_first[1])


def other(pair_axis_first):
    return jnp.where(lax.axis_index("c") == 0, pair_axis_first[1], pair_axis_first[0])


def in_order(own, mate, axis=0):
    first = lax.axis_index("c") == 0
    return jnp.concatenate([jnp.where(first, own, mate), jnp.where(first, mate, own)], axis)


def after(value, *before):
    return lax.optimization_barrier((*before, value))[-1]


def column_first(shard):
    return [shard] + [shift(shard, k) for k in range(1, lax.axis_size("z"))]


def plane_last(column, between=()):
    half = column.shape[0] // 2
    along_x, along_y = swap(column, "x"), swap(column, "y")
    along_x, along_y = after(along_x, *between), after(along_y, *between)
    far = (swap(along_y[:half], "x"), swap(along_x[half:], "y"))
    return (column, along_x, along_y) + far


def plane_first(shard, along_x, along_y, *before):
    far = lax.ppermute(after(shard, *before), ("y", "x"), [(i, 3 - i) for i in range(4)])
    return jnp.concatenate([shard, along_x, along_y, far])


def column_last(plane):
    parts = [plane]
    for _ in range(1, lax.axis_size("z")):
        parts.append(shift(parts[-1], 1))
    return parts


def column_first_spots(depth):
    half = depth // 2
    spots = [(0, (k,), 0, (k, 0, 0), 0) for k in range(depth)]
    spots += [(1, (k,), 0, (k, 0, 1), 0) for k in range(depth)]
    spots += [(2, (k,), 0, (k, 1, 0), 0) for k in range(depth)]
    spots += [(3, (k,), 0, (k, 1, 1), 0) for k in range(half)]
    return spots + [(4, (k - half,), 0, (k, 1, 1), 0) for k in range(half, depth)]


def plane_first_spots(depth, rows, base):
    return [(base + k, (), p * rows, (k, p // 2, p % 2), 1) for k in range(depth) for p in range(4)]


def first_hop(send_x, keep_x, send_y, keep_y, before=()):
    return keep_x, swap(after(send_x, *before), "x"), keep_y, swap(after(send_y, *before), "y")


def second_hop_of(keep_x, got_x, keep_y, got_y, deps=()):
    depth, rows, cols = keep_x.shape[1:]

    def second_hop(kx, gx, ky, gy, to_y, to_x):
        to_y[...] = (kx[1].astype(WIDE) + gx[1].astype(WIDE)).astype(LOW)
        to_x[...] = (ky[1].astype(WIDE) + gy[1].astype(WIDE)).astype(LOW)

    outs = [((depth, rows, cols), LOW)] * 2
    return run(second_hop, outs, keep_x, got_x, keep_y, got_y, scalars=False, deps=deps)


def third_hop_of(keep_x, got_x, keep_y, got_y, on_y, on_x, deps=()):
    depth, rows, cols = keep_x.shape[1:]

    def third_hop(kx, gx, ky, gy, ony, onx, own, *sends):
        for k in range(depth):
            one = kx[0, k].astype(WIDE) + gx[0, k].astype(WIDE) + ony[k].astype(WIDE)
            two = ky[0, k].astype(WIDE) + gy[0, k].astype(WIDE) + onx[k].astype(WIDE)
            out = sends[k - 1] if k else own
            out[:rows, :] = one.astype(out.dtype)
            out[rows:, :] = two.astype(out.dtype)

    outs = [((2 * rows, cols), WIDE if k == 0 else LOW) for k in range(depth)]
    own, *sends = run(third_hop, outs, keep_x, got_x, keep_y, got_y, on_y, on_x, scalars=False, deps=deps)
    return [own] + [shift(part, k + 1) for k, part in enumerate(sends)]


def sum_of(refs):
    total = refs[0][...]
    for ref in refs[1:]:
        total = total + ref[...].astype(WIDE)
    return total


def spread(value):
    return jnp.broadcast_to(value, (8, LANES))


def total_squares(value):
    return jnp.sum(jnp.sum(value * value, axis=1, keepdims=True), axis=0, keepdims=True)


def finish_down(parts, deps=()):
    def kernel(*refs):
        total = sum_of(refs[: len(parts)])
        refs[-2][...] = total
        refs[-1][...] = spread(total_squares(total))

    return run(kernel, [(parts[0].shape, WIDE), ((8, LANES), WIDE)], *parts, scalars=False, deps=deps)


def finish_up(parts, squares, rows, half_ff):
    half_d = parts[0].shape[1] - half_ff
    small = rows // 2

    def kernel(coords, squares_ref, *refs):
        own_ref, mate_ref, out_ref, total_ref, all_ref = refs[len(parts) :]
        total = sum_of(refs[: len(parts)])
        all_ref[...] = total
        core = coords[3]
        own_ref[...] = all_ref[pl.ds(pl.multiple_of(core * rows, 8), rows), :half_ff]
        mate_ref[...] = all_ref[pl.ds(pl.multiple_of((1 - core) * rows, 8), rows), :half_ff]
        for p in range(2):
            for h in range(2):
                block = total[h * rows + p * small : h * rows + (p + 1) * small, half_ff:]
                out_ref[h * small : (h + 1) * small, p * half_d : (p + 1) * half_d] = block
        total_ref[...] = squares_ref[...] + spread(total_squares(total))

    outs = [((rows, half_ff), WIDE)] * 2 + [((rows, 2 * half_d), WIDE), ((8, LANES), WIDE)]
    scratch = [pltpu.VMEM(parts[0].shape, WIDE)]
    return run(kernel, outs, squares, *parts, scratch=scratch)


def finish_qkv(parts, squares, rows, half_qkv, deps=()):
    def kernel(coords, squares_ref, *refs):
        own_ref, mate_ref, small_ref, all_ref = refs[len(parts) :]
        total = sum_of(refs[: len(parts)])
        all_ref[...] = total
        core = coords[3]
        own_ref[...] = all_ref[pl.ds(pl.multiple_of(core * rows, 8), rows), :half_qkv]
        mate_ref[...] = all_ref[pl.ds(pl.multiple_of((1 - core) * rows, 8), rows), :half_qkv]
        small_ref[: 2 * rows, :] = total[:, half_qkv:]
        small_ref[2 * rows :, :] = squares_ref[...] + spread(total_squares(total[:, :half_qkv]))

    outs = [((rows, half_qkv), WIDE)] * 2 + [((2 * rows + 8, LANES), WIDE)]
    scratch = [pltpu.VMEM(parts[0].shape, WIDE)]
    return run(kernel, outs, squares, *parts, scratch=scratch, deps=deps)


def chip_squares(small, got):
    rows = small.shape[0] - 8

    def kernel(small_ref, got_ref, total_ref, norm_ref):
        total = small_ref[...] + got_ref[...]
        norm_ref[...] = total[:rows]
        total_ref[...] = total[rows:] + spread(total_squares(total[:rows]))

    outs = [((8, LANES), WIDE), ((rows, LANES), WIDE)]
    return run(kernel, outs, small, got, scalars=False)


def sum_chips(value):
    across = lax.ppermute(value, ("y", "x"), [(i, 3 - i) for i in range(4)])
    value = value + swap(value, "y") + (swap(value, "x") + across)
    size, near = lax.axis_size("z"), 1
    while near < size // 2:
        value = value + lax.ppermute(value, "z", [(i, i ^ near) for i in range(size)])
        near *= 2
    return [value, lax.ppermute(value, "z", [(i, i ^ near) for i in range(size)])]


def interleave(first, own, mate, blocks):
    size = own.shape[1] // blocks
    pieces = []
    for j in range(blocks):
        at = slice(j * size, (j + 1) * size)
        pieces += [jnp.where(first, own[:, at], mate[:, at]), jnp.where(first, mate[:, at], own[:, at])]
    return jnp.concatenate(pieces, axis=1)


def update_all(grads, totals, masters, firsts, seconds, rates, decays, blocks):
    steps = 2
    n, m = len(grads), len(totals)

    def tile(array):
        rows, cols = array.shape
        return pl.BlockSpec((rows // steps, cols), lambda i: (i, 0))

    def whole(array):
        return pl.BlockSpec(array.shape, lambda i: (0, 0))

    def kernel(coords, *refs):
        first = coords[3] == 0
        g, t, old, new = refs[:n], refs[n : n + m], refs[n + m : n + m + 15], refs[n + m + 15 :]
        total = sum_of(t)[0:1, 0:1]
        norm = jnp.sqrt(total)
        clip = jnp.minimum(1.0, CLIP_LIMIT / (norm + 1e-06))
        qkv = interleave(first, g[0][...], g[1][...], blocks[0])
        up = interleave(first, g[3][...], g[4][...], blocks[1])
        for k, grad in enumerate((qkv, g[2][...], up, g[5][...], g[6][...])):
            news = adam_update(old[k][...], old[5 + k][...], old[10 + k][...], clip * grad, rates[k], decays[k])
            for part in range(3):
                new[5 * part + k][...] = news[part]
        new[15][...] = norm

    state = (*masters, *firsts, *seconds)
    specs = [whole(a) if k % 5 == 4 else tile(a) for k, a in enumerate(state)]
    norm_out = jax.ShapeDtypeStruct((1, 1), WIDE)
    return pl.pallas_call(
        kernel,
        grid=(steps,),
        out_shape=[jax.ShapeDtypeStruct(a.shape, WIDE) for a in state] + [norm_out],
        in_specs=[pl.BlockSpec(memory_space=pltpu.SMEM)]
        + [tile(a) for a in grads[:-1]]
        + [whole(grads[-1])]
        + [whole(a) for a in totals]
        + specs,
        out_specs=specs + [whole(norm_out)],
        compiler_params=FULL,
    )(coordinates(), *grads, *totals, *state)


def coordinates():
    return jnp.stack([lax.axis_index(name) for name in ("z", "y", "x", "c")]).astype(jnp.int32)


def chip_of(coords, rel, depth, back):
    dz, dy, dx = rel
    z, y, x = coords[0], coords[1], coords[2]
    zz = lax.rem(z + (depth - dz if back else dz), depth)
    yy = 1 - y if dy else y
    xx = 1 - x if dx else x
    return zz, yy * 2 + xx


def window(row, rows, col, cols):
    rows_at = pl.ds(row if isinstance(row, int) else pl.multiple_of(row, 16), rows)
    return rows_at, pl.ds(col, cols)


VMEM = pl.BlockSpec(memory_space=pltpu.VMEM)
ROOM_MB = 16
ROOM = pltpu.CompilerParams(vmem_limit_bytes=ROOM_MB * 1024 * 1024)
FULL = pltpu.CompilerParams(vmem_limit_bytes=56 * 1024 * 1024)


def place(parts, depth, outs, spots, moves, deps=()):
    def kernel(coords, *refs):
        ins, out_refs = refs[: len(parts)], refs[len(parts) + len(deps) :]
        for array, lead, base, rel, piece in spots:
            zz, plane = chip_of(coords, rel, depth, True)
            for o, sr, sc, rows, cols, tr, tc in moves(zz, plane, piece):
                out_refs[o][window(tr, rows, tc, cols)] = ins[array][(*lead, *window(base + sr, rows, sc, cols))]

    return pl.pallas_call(
        kernel,
        out_shape=[jax.ShapeDtypeStruct(s, LOW) for s in outs],
        in_specs=[pl.BlockSpec(memory_space=pltpu.SMEM)]
        + [VMEM] * len(parts)
        + [pl.BlockSpec(memory_space=pl.ANY)] * len(deps),
        out_specs=[VMEM] * len(outs),
        compiler_params=ROOM,
    )(coordinates(), *parts, *deps)


def unplace(grads, depth, rows_cols, moves):
    spots = []
    for dz in range(depth):
        for d in range(2):
            spots += [(0, d, dz, (dz, d, 1), 0), (1, d, dz, (dz, d, 0), 0)]
            spots += [(2, d, dz, (dz, 1, d), 1), (3, d, dz, (dz, 0, d), 1)]

    def kernel(coords, *refs):
        ins, out_refs = refs[: len(grads)], refs[len(grads) :]
        for array, d, dz, rel, half in spots:
            zz, plane = chip_of(coords, rel, depth, False)
            for i, sr, sc, rows, cols, tr, tc in moves(zz, plane, half):
                out_refs[array][(d, dz, *window(tr, rows, tc, cols))] = ins[i][window(sr, rows, sc, cols)]

    return pl.pallas_call(
        kernel,
        out_shape=[jax.ShapeDtypeStruct((2, depth) + rows_cols, LOW)] * 4,
        in_specs=[pl.BlockSpec(memory_space=pltpu.SMEM)] + [VMEM] * len(grads),
        out_specs=[VMEM] * 4,
        compiler_params=ROOM,
    )(coordinates(), *grads)


def cast_qkv(qkv, norm, halves):
    rows, cols = qkv.shape
    wide = cols // 2 + LANES
    block = cols // (2 * halves)

    def kernel(coords, qkv_ref, norm_ref, own_ref, mate_ref, tall):
        first = coords[3] == 0
        for j in range(halves):
            a = qkv_ref[:, 2 * j * block : (2 * j + 1) * block]
            b = qkv_ref[:, (2 * j + 1) * block : (2 * j + 2) * block]
            own_ref[:, j * block : (j + 1) * block] = jnp.where(first, a, b).astype(LOW)
            mate_ref[:, j * block : (j + 1) * block] = jnp.where(first, b, a).astype(LOW)
        tall[...] = jnp.zeros_like(tall)
        tall[0:4, :] = norm_ref[...].astype(LOW).astype(WIDE)
        i = lax.broadcasted_iota(jnp.int32, (rows, rows), 0)
        j = lax.broadcasted_iota(jnp.int32, (rows, rows), 1)
        columns = dot_cols((i == j).astype(LOW), tall[...].astype(LOW)).astype(LOW)
        own_ref[:, cols // 2 :] = columns
        mate_ref[:, cols // 2 :] = columns

    return pl.pallas_call(
        kernel,
        out_shape=[jax.ShapeDtypeStruct((rows, wide), LOW)] * 2,
        in_specs=[pl.BlockSpec(memory_space=pltpu.SMEM), VMEM, VMEM],
        out_specs=[VMEM] * 2,
        scratch_shapes=[pltpu.VMEM((LANES, rows), WIDE)],
        compiler_params=ROOM,
    )(coordinates(), qkv, norm)


def cast_down(down, last):
    rows, cols = down.shape

    def kernel(down_ref, one_ref, two_ref):
        one_ref[...] = down_ref[:last, :].astype(LOW)
        two_ref[...] = down_ref[last:, :].astype(LOW)

    return pl.pallas_call(
        kernel,
        out_shape=[jax.ShapeDtypeStruct((last, cols), LOW), jax.ShapeDtypeStruct((rows - last, cols), LOW)],
        in_specs=[VMEM],
        out_specs=[VMEM] * 2,
        compiler_params=ROOM,
    )(down)


def cast_rest(up, out, halves):
    rows, cols = up.shape
    block, width = cols // (2 * halves), out.shape[1]

    def kernel(coords, up_ref, out_ref, own_ref, mate_ref, part_ref):
        first = coords[3] == 0
        for j in range(halves):
            a = up_ref[:, 2 * j * block : (2 * j + 1) * block]
            b = up_ref[:, (2 * j + 1) * block : (2 * j + 2) * block]
            own_ref[:, j * block : (j + 1) * block] = jnp.where(first, a, b).astype(LOW)
            mate_ref[:, j * block : (j + 1) * block] = jnp.where(first, b, a).astype(LOW)
        part_ref[:rows, :] = out_ref[:, : width // 2].astype(LOW)
        part_ref[rows:, :] = out_ref[:, width // 2 :].astype(LOW)

    return pl.pallas_call(
        kernel,
        out_shape=[jax.ShapeDtypeStruct((rows, cols // 2), LOW)] * 2
        + [jax.ShapeDtypeStruct((2 * rows, width // 2), LOW)],
        in_specs=[pl.BlockSpec(memory_space=pltpu.SMEM), VMEM, VMEM],
        out_specs=[VMEM] * 3,
        compiler_params=ROOM,
    )(coordinates(), up, out)


def join_rows(own, mate, side=None):
    rows, cols = own.shape
    wide = cols + (side.shape[1] if side is not None else 0)

    def kernel(coords, own_ref, mate_ref, *refs):
        out_ref = refs[-1]
        core = coords[3]
        out_ref[pl.ds(pl.multiple_of(core * rows, 16), rows), :cols] = own_ref[...]
        out_ref[pl.ds(pl.multiple_of((1 - core) * rows, 16), rows), :cols] = mate_ref[...]
        if side is not None:
            out_ref[:, cols:] = refs[0][...]

    ins = [own, mate] + ([side] if side is not None else [])
    return pl.pallas_call(
        kernel,
        out_shape=jax.ShapeDtypeStruct((2 * rows, wide), LOW),
        in_specs=[pl.BlockSpec(memory_space=pltpu.SMEM)] + [VMEM] * len(ins),
        out_specs=VMEM,
        compiler_params=ROOM,
    )(coordinates(), *ins)


def run(kernel, outs, *ins, scalars=True, scratch=(), flops=0, room=ROOM_MB, deps=()):
    first = len(ins) + scalars

    def body_of(*refs):
        return kernel(*refs[:first], *refs[first + len(deps) :])

    out_shape = [jax.ShapeDtypeStruct(shape, kind) for shape, kind in outs]
    return pl.pallas_call(
        body_of,
        out_shape=out_shape,
        in_specs=([pl.BlockSpec(memory_space=pltpu.SMEM)] if scalars else [])
        + [VMEM] * len(ins)
        + [pl.BlockSpec(memory_space=pl.ANY)] * len(deps),
        out_specs=[VMEM] * len(outs),
        scratch_shapes=list(scratch),
        compiler_params=pltpu.CompilerParams(vmem_limit_bytes=room * 1024 * 1024),
        cost_estimate=pl.CostEstimate(flops=flops, bytes_accessed=0, transcendentals=0),
    )(*([coordinates()] if scalars else []), *ins, *deps)


def dot(left, right):
    return jnp.dot(left, right, preferred_element_type=WIDE)


def dot_rows(left, right):
    return lax.dot_general(left, right, (((0,), (0,)), ((), ())), preferred_element_type=WIDE)


def dot_cols(left, right):
    return lax.dot_general(left, right, (((1,), (1,)), ((), ())), preferred_element_type=WIDE)


def eye(rows, cols):
    i = lax.broadcasted_iota(jnp.int32, (rows, cols), 0)
    return (i == lax.broadcasted_iota(jnp.int32, (rows, cols), 1)).astype(LOW)


def normalise(values):
    center = values - jnp.mean(values, axis=-1, keepdims=True)
    rate = lax.rsqrt(jnp.mean(center * center, axis=-1, keepdims=True) + NORM_EPS)
    return center * rate, rate


def norm_back(normed, rate, grad, gain):
    scaled = grad * gain
    shared = jnp.mean(scaled, axis=-1, keepdims=True)
    along = jnp.mean(scaled * normed, axis=-1, keepdims=True)
    return rate * (scaled - shared - normed * along)


def low_lanes(rows):
    return lax.broadcasted_iota(jnp.int32, (rows, LANES), 1) < HEAD_DIM


def by_head(pair):
    wide = pair.astype(WIDE)
    first = low_lanes(pair.shape[0])
    return jnp.where(first, wide, 0.0).astype(LOW), jnp.where(first, 0.0, wide).astype(LOW)


def pack_state(square):
    first = low_lanes(HEAD_DIM)
    return jnp.where(first, square[:HEAD_DIM], square[HEAD_DIM:])


def open_state(packed):
    first = low_lanes(HEAD_DIM)
    return jnp.concatenate([jnp.where(first, packed, 0.0), jnp.where(first, 0.0, packed)])


def feature(values):
    return jnp.where(values > 0.0, values + 1.0, jnp.exp(jnp.minimum(values, 0.0)))


def project(x, norm_w, qkv_w):
    tokens, width = x.shape
    half = qkv_w.shape[1] // 3
    pairs = half // LANES
    step = tokens // 2

    def kernel(x_ref, norm_ref, w_ref, rows_ref, normed_ref, qk_ref, q_ref, k_ref, v_ref, state_ref, sums):
        rows_ref[...] = dot_cols(eye(8, LANES), norm_ref[...])
        gain, bias = rows_ref[0:1, :], rows_ref[1:2, :]
        @pl.loop(0, 2)
        def _(i):
            at = at_block(i, step)
            normed = normalise(x_ref[at, :].astype(WIDE))[0]
            normed_ref[at, :] = (normed * gain + bias).astype(LOW)
            low = normed_ref[at, :]
            for j, out in enumerate((q_ref, k_ref)):
                part = dot(low, w_ref[:, j * half : (j + 1) * half])
                qk_ref[at, j * half : (j + 1) * half] = part
                out[at, :] = feature(part).astype(LOW)
            v_ref[at, :] = dot(low, w_ref[:, 2 * half :]).astype(LOW)
        total = dot_rows(jnp.ones((tokens, 8), LOW), k_ref[...])
        sums[...] = jnp.zeros_like(sums)
        for p in range(pairs):
            lanes = slice(p * LANES, (p + 1) * LANES)
            packed = pack_state(dot_rows(k_ref[:, lanes], v_ref[:, lanes]))
            state_ref[p * HEAD_DIM : (p + 1) * HEAD_DIM, :] = packed.astype(LOW)
            sums[p : p + 1, :] = total[0:1, lanes]
        state_ref[pairs * HEAD_DIM :, :] = sums[...].astype(LOW)

    outs = [((8, width), WIDE), ((tokens, width), LOW), ((tokens, 2 * half), WIDE)] + [((tokens, half), LOW)] * 3
    outs += [((pairs * HEAD_DIM + 16, LANES), LOW)]
    scratch = [pltpu.VMEM((16, LANES), WIDE)]
    return run(kernel, outs, x, norm_w, qkv_w, scalars=False, scratch=scratch)


def at_block(index, size):
    return pl.ds(pl.multiple_of(index * size, size), size)


def total_state(refs):
    total = refs[0][...].astype(WIDE)
    for ref in refs[1:]:
        total = total + ref[...].astype(WIDE)
    return total


def causal_mask(step):
    i = lax.broadcasted_iota(jnp.int32, (step, step), 0)
    return i >= lax.broadcasted_iota(jnp.int32, (step, step), 1)


def attend(query, key, value, parts, deps=()):
    tokens, half = query.shape
    pairs, step = half // LANES, tokens // 2

    def kernel(q_ref, k_ref, v_ref, *refs):
        mixed_ref, low_ref, denom_ref, state_ref, token_ref = refs[len(parts) :]
        token_ref[...] = jnp.zeros_like(token_ref)
        state_ref[...] = total_state(refs[: len(parts)])
        lower = causal_mask(step)
        first = low_lanes(step)
        top = low_lanes(HEAD_DIM)
        diagonal = eye(LANES, LANES).astype(WIDE)
        @pl.loop(0, pairs)
        def _(p):
            lanes = at_block(p, LANES)
            packed = state_ref[at_block(p, HEAD_DIM), :]
            sums = state_ref[pl.ds(pairs * HEAD_DIM + p, 1), :]
            column = jnp.sum(diagonal * sums, axis=1, keepdims=True)
            zero = jnp.zeros((HEAD_DIM, LANES), WIDE)
            ext = (
                jnp.concatenate([jnp.where(top, packed, column[:HEAD_DIM]), zero]).astype(LOW),
                jnp.concatenate([zero, jnp.where(top, column[HEAD_DIM:], packed)]).astype(LOW),
            )
            wide = v_ref[:, lanes].astype(WIDE)
            full = low_lanes(tokens)
            value_ext = (jnp.where(full, wide, 1.0).astype(LOW), jnp.where(full, 1.0, wide).astype(LOW))
            queries = by_head(q_ref[:, lanes])
            for i in range(2):
                at = slice(i * step, (i + 1) * step)
                got = []
                for h in range(2):
                    rows = queries[h][at]
                    total = dot(rows, ext[h])
                    for j in range(i + 1):
                        to = slice(j * step, (j + 1) * step)
                        scores = dot_cols(rows, k_ref[to, lanes])
                        if j == i:
                            scores = jnp.where(lower, scores, 0.0)
                        total = total + dot(scores.astype(LOW), value_ext[h][to])
                    got.append(total)
                denom = pltpu.roll(jnp.where(first, got[1], got[0]), HEAD_DIM, 1)
                mixed = jnp.where(first, got[0], got[1]) / denom
                mixed_ref[at, lanes] = mixed
                low_ref[at, lanes] = mixed.astype(LOW)
                denom_ref[at, lanes] = denom

    outs = [((tokens, half), WIDE), ((tokens, half), LOW), ((tokens, half), WIDE), (parts[0].shape, WIDE)]
    outs += [((8, LANES), WIDE)]
    return run(kernel, outs, query, key, value, *parts, scalars=False, deps=deps)


def out_project(mixed, out_w):
    def kernel(mixed_ref, w_ref, part_ref, low_ref):
        part = dot(mixed_ref[...], w_ref[...])
        part_ref[...] = part
        low_ref[...] = part.astype(LOW)

    shape = (mixed.shape[0], out_w.shape[1])
    return run(kernel, [(shape, WIDE), (shape, LOW)], mixed, out_w, scalars=False)


def feed(x, part, got, rows, up_w):
    tokens, width = x.shape
    units, step, cut = up_w.shape[1], tokens // 2, 512

    def kernel(x_ref, part_ref, got_ref, rows_ref, w_ref, resid_ref, normed_ref, act_ref, slope_ref):
        @pl.loop(0, 2)
        def _(i):
            at = at_block(i, step)
            resid = x_ref[at, :].astype(WIDE) + part_ref[at, :] + got_ref[at, :].astype(WIDE)
            resid_ref[at, :] = resid
            normed_ref[at, :] = (normalise(resid)[0] * rows_ref[2:3, :] + rows_ref[3:4, :]).astype(LOW)

        @pl.loop(0, units // cut)
        def _(j):
            to = at_block(j, cut)
            v = dot(normed_ref[...], w_ref[:, to])
            root = (2.0 / 3.141592653589793) ** 0.5
            square = v * v
            bend = jnp.tanh(root * v * (1.0 + 0.044715 * square))
            cdf = 0.5 * (1.0 + bend)
            act_ref[:, to] = (v * cdf).astype(LOW)
            slope_ref[:, to] = cdf + 0.5 * v * (1.0 - bend * bend) * (root * (1.0 + 3.0 * 0.044715 * square))

    outs = [((tokens, width), WIDE), ((tokens, width), LOW), ((tokens, units), LOW), ((tokens, units), WIDE)]
    return run(kernel, outs, x, part, got, rows, up_w, scalars=False)


def feed_back(grad_out, down_w, slope, up_w):
    tokens, width = grad_out.shape
    units, cut = up_w.shape[1], 512

    def kernel(g_ref, down_ref, slope_ref, up_ref, hidden_ref, part_ref, low_ref):
        @pl.loop(0, units // cut)
        def _(j):
            to = at_block(j, cut)
            hidden_ref[:, to] = (dot_cols(g_ref[...], down_ref[to, :]) * slope_ref[:, to]).astype(LOW)

        @pl.loop(0, width // cut)
        def _(j):
            to = at_block(j, cut)
            part = dot_cols(hidden_ref[...], up_ref[to, :])
            part_ref[:, to] = part
            low_ref[:, to] = part.astype(LOW)

    outs = [((tokens, units), LOW), ((tokens, width), WIDE), ((tokens, width), LOW)]
    return run(kernel, outs, grad_out, down_w, slope, up_w, scalars=False)


def down_project(activated, down_w, resid, deps):
    tokens, width = resid.shape
    group, cut = tokens // 2, width // 2

    def kernel(coords, act_ref, w_ref, resid_ref, own_ref, give_ref):
        own = pl.ds(pl.multiple_of(coords[3] * group, 16), group)
        mate = pl.ds(pl.multiple_of((1 - coords[3]) * group, 16), group)

        @pl.loop(0, 2)
        def _(j):
            to = at_block(j, cut)
            own_ref[:, to] = resid_ref[own, to] + dot(act_ref[own, :], w_ref[:, to])
            give_ref[:, to] = dot(act_ref[mate, :], w_ref[:, to]).astype(LOW)

    outs = [((group, width), WIDE), ((group, width), LOW)]
    return run(kernel, outs, activated, down_w, resid, deps=deps)


def weight_grad(rows, grad, deps=()):
    tokens, width = rows.shape
    units, cut = grad.shape[1], 512

    def kernel(rows_ref, grad_ref, out_ref):
        @pl.loop(0, units // cut)
        def _(j):
            to = at_block(j, cut)
            out_ref[:, to] = dot_rows(rows_ref[...], grad_ref[:, to]).astype(LOW)

    return run(kernel, [((width, units), LOW)], rows, grad, scalars=False, deps=deps)[0]


def attend_turn(part, got, resid, rows, grad_out, out_w, mixed, denom, query, deps):
    tokens, width = resid.shape
    half = mixed.shape[1]
    pairs, step = half // LANES, tokens // 2

    def kernel(
        part_ref, got_ref, resid_ref, rows_ref, g_ref, w_ref, mixed_ref, denom_ref, q_ref,
        grad_ref, low_ref, a_ref, b_ref, state_ref, norm_ref, sums,
    ):
        gain = rows_ref[2:3, :]
        first = low_lanes(step)
        norm_ref[...] = jnp.zeros_like(norm_ref)

        @pl.loop(0, 2)
        def _(i):
            at = at_block(i, step)
            normed, rate = normalise(resid_ref[at, :])
            own = part_ref[at, :]
            norm_ref[0:1, :] += jnp.sum(own * normed, axis=0, keepdims=True)
            norm_ref[1:2, :] += jnp.sum(own, axis=0, keepdims=True)
            grad = g_ref[at, :].astype(WIDE) + norm_back(normed, rate, own + got_ref[at, :].astype(WIDE), gain)
            grad_ref[at, :] = grad
            low_ref[at, :] = grad.astype(LOW)
            turned = dot_cols(low_ref[at, :], w_ref[...]) / denom_ref[at, :]
            a_ref[at, :] = turned.astype(LOW)
            along = turned * mixed_ref[at, :]
            for p in range(pairs):
                lanes = slice(p * LANES, (p + 1) * LANES)
                piece = along[:, lanes]
                low = jnp.sum(jnp.where(first, piece, 0.0), axis=1, keepdims=True)
                high = jnp.sum(jnp.where(first, 0.0, piece), axis=1, keepdims=True)
                b_ref[at, lanes] = -jnp.where(first, low, high)
        sums[...] = jnp.zeros_like(sums)
        for p in range(pairs):
            lanes = slice(p * LANES, (p + 1) * LANES)
            packed = pack_state(dot_rows(q_ref[:, lanes], a_ref[:, lanes]))
            state_ref[p * HEAD_DIM : (p + 1) * HEAD_DIM, :] = packed.astype(LOW)
            sums[p : p + 1, :] = jnp.sum(q_ref[:, lanes].astype(WIDE) * b_ref[:, lanes], axis=0, keepdims=True)
        state_ref[pairs * HEAD_DIM :, :] = sums[...].astype(LOW)

    outs = [((tokens, width), WIDE), ((tokens, width), LOW), ((tokens, half), LOW), ((tokens, half), WIDE)]
    outs += [((pairs * HEAD_DIM + 16, LANES), LOW), ((2, width), WIDE)]
    ins = (part, got, resid, rows, grad_out, out_w, mixed, denom, query)
    scratch = [pltpu.VMEM((16, LANES), WIDE)]
    return run(kernel, outs, *ins, scalars=False, scratch=scratch, deps=deps)


def attend_back(query, key, value, qk, a_low, b_rows, state, parts, deps=()):
    tokens, half = query.shape
    pairs, step = half // LANES, tokens // 2

    def kernel(q_ref, k_ref, v_ref, qk_ref, a_ref, b_ref, state_ref, *refs):
        out_ref, later = refs[len(parts) :]
        later[...] = total_state(refs[: len(parts)])
        lower = causal_mask(step)
        @pl.loop(0, pairs)
        def _(p):
            lanes, rows = at_block(p, LANES), at_block(p, HEAD_DIM)
            sums = pl.ds(pairs * HEAD_DIM + p, 1)
            before, after_it = open_state(state_ref[rows, :]).astype(LOW), open_state(later[rows, :]).astype(LOW)
            queries, keys, pulls = by_head(q_ref[:, lanes]), by_head(k_ref[:, lanes]), by_head(a_ref[:, lanes])
            cuts = [slice(i * step, (i + 1) * step) for i in range(2)]
            grad_q = [dot_cols(a_ref[c, lanes], before) + b_ref[c, lanes] * state_ref[sums, :] for c in cuts]
            grad_k = [dot_cols(v_ref[c, lanes], after_it) + later[sums, :] for c in cuts]
            shifts = b_ref[:, lanes]
            grad_v = [dot(k_ref[c, lanes], after_it) for c in cuts]
            for i in range(2):
                for j in range(i + 1):
                    for h in range(2):
                        q, a = queries[h][cuts[i]], pulls[h][cuts[i]]
                        b = shifts[cuts[i], h * HEAD_DIM : h * HEAD_DIM + 1]
                        scores = dot_cols(q, k_ref[cuts[j], lanes])
                        pull = dot_cols(a, v_ref[cuts[j], lanes]) + b
                        if j == i:
                            scores, pull = jnp.where(lower, scores, 0.0), jnp.where(lower, pull, 0.0)
                        scores, pull = scores.astype(LOW), pull.astype(LOW)
                        grad_q[i] = grad_q[i] + dot(pull, keys[h][cuts[j]])
                        grad_k[j] = grad_k[j] + dot_rows(pull, q)
                        grad_v[j] = grad_v[j] + dot_rows(scores, a)
            for i, c in enumerate(cuts):
                for n, grad in enumerate((grad_q[i], grad_k[i])):
                    at = at_block(n * pairs + p, LANES)
                    raw = qk_ref[c, at]
                    out_ref[c, at] = (grad * jnp.where(raw > 0.0, 1.0, jnp.exp(jnp.minimum(raw, 0.0)))).astype(LOW)
                out_ref[c, at_block(2 * pairs + p, LANES)] = grad_v[i].astype(LOW)

    ins = (query, key, value, qk, a_low, b_rows, state, *parts)
    scratch = [pltpu.VMEM(parts[0].shape, WIDE)]
    return run(kernel, [((tokens, 3 * half), LOW)], *ins, scalars=False, scratch=scratch, deps=deps)[0]


def project_back(grad, qkv_w, x, norm_two):
    tokens, width = x.shape
    step = tokens // 2

    def kernel(grad_ref, w_ref, x_ref, two_ref, part_ref, low_ref, cols_ref, rows):
        rows[...] = jnp.zeros_like(rows)

        @pl.loop(0, 2)
        def _(i):
            at = at_block(i, step)
            part = dot_cols(grad_ref[at, :], w_ref[...])
            part_ref[at, :] = part
            low_ref[at, :] = part.astype(LOW)
            rows[0:1, :] += jnp.sum(part * normalise(x_ref[at, :].astype(WIDE))[0], axis=0, keepdims=True)
            rows[1:2, :] += jnp.sum(part, axis=0, keepdims=True)

        rows[2:4, :] = two_ref[...]
        cols_ref[...] = dot_rows(rows[...].astype(LOW), eye(8, LANES)).astype(LOW)

    outs = [((tokens, width), WIDE), ((tokens, width), LOW), ((width, LANES), LOW)]
    scratch = [pltpu.VMEM((8, width), WIDE)]
    return run(kernel, outs, grad, qkv_w, x, norm_two, scalars=False, scratch=scratch)


def input_back(part, got, grad_resid, own_x, rows):
    group, width = own_x.shape

    def kernel(coords, part_ref, got_ref, resid_ref, x_ref, rows_ref, out_ref):
        at = pl.ds(pl.multiple_of(coords[3] * group, 16), group)
        normed, rate = normalise(x_ref[...].astype(WIDE))
        grad = part_ref[at, :] + got_ref[...].astype(WIDE)
        out_ref[...] = (resid_ref[at, :] + norm_back(normed, rate, grad, rows_ref[0:1, :])).astype(LOW)

    return run(kernel, [((group, width), LOW)], part, got, grad_resid, own_x, rows)[0]


def adam_update(weight, first, second, grad, rate, decay):
    first_new = BETA_ONE * first + (1.0 - BETA_ONE) * grad
    second_new = BETA_TWO * second + (1.0 - BETA_TWO) * grad * grad
    first_hat = first_new / (1.0 - BETA_ONE**STEP)
    second_hat = second_new / (1.0 - BETA_TWO**STEP)
    weight_new = weight - rate * (first_hat / (jnp.sqrt(second_hat) + ADAM_EPS) + decay * weight)
    return (weight_new, first_new, second_new)


def from_others(low, step):
    if lax.axis_size("z") == 4 and step == 1:
        near = shift(low, step, wrap=False)
        pair = (low.astype(WIDE) + near.astype(WIDE)).astype(LOW)
        return [near, shift(pair, 2 * step, wrap=False)]
    return [shift(low, step * k, wrap=False) for k in range(1, lax.axis_size("z"))]


def body(
    images,
    cotangent,
    qkv_weight,
    out_weight,
    up_weight,
    down_weight,
    norm_params,
    qkv_first,
    out_first,
    up_first,
    down_first,
    norm_first,
    qkv_second,
    out_second,
    up_second,
    down_second,
    norm_second,
):
    depth, core = lax.axis_size("z"), lax.axis_index("c")
    count, group, width = images.shape
    hidden_units = up_weight.shape[1]
    own_rows = qkv_weight.shape[0]
    own_units = down_weight.shape[0]
    chips = lax.axis_size("y") * lax.axis_size("x")
    block, ff_block = width // (2 * depth), hidden_units // (2 * depth)
    half_qkv, half_ff, half_d = 3 * width // 2, hidden_units // 2, width // 2
    ring = lax.axis_size("y") == 2 and lax.axis_size("x") == 2 and depth == 4 and own_rows % 32 == 0
    heads = half_d // HEAD_DIM
    tokens = 2 * group

    own_x, own_g = images.reshape(group, width), cotangent.reshape(group, width)
    split_qkv = lambda w: jnp.moveaxis(w.reshape(-1, 3 * depth, 2, block), 2, 0).reshape(2, -1, half_qkv)
    split_up = lambda w: jnp.moveaxis(w.reshape(-1, depth, 2, ff_block), 2, 0).reshape(2, -1, half_ff)

    thin, small, last = own_units // 2, own_rows // 2, 3 * own_units // 8
    if ring:
        qkv_mine, qkv_give = cast_qkv(qkv_weight, norm_params, 3 * depth)
        qkv_part = join_rows(qkv_mine, swap(qkv_give, "c"))
        down_one, down_two = cast_down(down_weight, last)
        down_two = after(down_two, qkv_part)
        along = swap(down_two, "x"), swap(down_two, "y")
        up_mine, up_give, out_part = cast_rest(after(up_weight, along[0]), out_weight, depth)
        inputs = join_rows(own_x, swap(own_x, "c"))
        up_part = join_rows(up_mine, swap(up_give, "c"), out_part)
        qkv_column = column_first(qkv_part)
        two_plane = plane_first(down_two, *along, qkv_column[1])
        qkv_column = [after(part, two_plane, up_part, inputs) for part in qkv_column]
        up_column = column_first(after(up_part, *qkv_column))
        qkv_parts = plane_last(jnp.stack(qkv_column))
        g_mate = swap(after(own_g, *up_column), "c")
        two_parts = [two_plane, shift(after(two_plane, *up_column), 1)]
        one_column = column_first(after(down_one, two_parts[1]))

        def qkv_moves(zz, plane, piece):
            row = lambda h: ((zz * 2 + h) * chips + plane) * own_rows
            moves = [(0, h * own_rows, 0, own_rows, half_qkv, row(h), 0) for h in (0, 1)]
            return moves + [(1, h * own_rows, half_qkv, own_rows, LANES, row(h), 0) for h in (0, 1)]

        def up_moves(zz, plane, piece):
            row = lambda h: ((zz * 2 + h) * chips + plane) * own_rows
            moves = [(0, h * own_rows, 0, own_rows, half_ff, row(h), 0) for h in (0, 1)]
            to = zz * block + plane * own_rows
            return moves + [(1, h * own_rows, half_ff, own_rows, half_d, to, h * half_d) for h in (0, 1)]

        def down_moves(zz, plane, piece):
            rows = own_units - last if piece else last
            return [(0, 0, 0, rows, width, zz * ff_block + plane * own_units + piece * last, 0)]

        spots = column_first_spots(depth)
        qkv_w, norm_w = place(qkv_parts, depth, [(width, half_qkv), (width, LANES)], spots, qkv_moves)
    else:
        qkv_low, out_low = qkv_weight.astype(LOW), out_weight.astype(LOW)
        up_low, down_low = up_weight.astype(LOW), down_weight.astype(LOW)
        norm_low = norm_params.astype(LOW)
        x_mate, g_mate = swap(own_x, "c"), swap(own_g, "c")
        whole = lambda w, axis=0: lax.all_gather(w, ALL, axis=axis, tiled=True)
        qkv_w, up_w = mine(split_qkv(whole(qkv_low))), mine(split_up(whole(up_low)))
        rows_half = lambda w, b: mine(jnp.moveaxis(w.reshape(depth, 2, b, width), 1, 0)).reshape(-1, width)
        out_w, down_w = rows_half(whole(out_low), block), rows_half(whole(down_low), ff_block)
        norm_w = jnp.pad(whole(norm_low, 1).T, ((0, 0), (0, LANES - 4)))

        inputs = join_rows(own_x, x_mate)
    grad_out = join_rows(own_g, g_mate)
    halves = lambda a: a.reshape(2, group, -1)
    rows, normed_one, qk, query, key, value, state = project(inputs, norm_w, qkv_w)
    earlier = from_others(state, 1)
    mixed, mixed_low, denom, state_in, attended = attend(query, key, value, earlier, (grad_out,))
    if ring:
        gate = (*earlier, *one_column[1:])
        up_parts = plane_last(after(jnp.stack(up_column), *qkv_parts[3:]), gate)
        two_parts.append(shift(after(two_parts[-1], *gate), 1))
        for _ in range(3, depth):
            two_parts.append(shift(two_parts[-1], 1))
        up_w, out_w = place(
            up_parts, depth, [(width, half_ff), (half_d, width)], spots, up_moves, two_parts[2:3]
        )
    out_part, out_low = out_project(mixed_low, out_w)
    out_got = swap(out_low, "c")
    resid, normed_two, activated, slope = feed(inputs, out_part, out_got, rows, up_w)
    down_grad = dot_rows(activated, grad_out).astype(LOW)
    if ring:
        def down_cuts(zz, plane, half):
            return [(0, zz * ff_block + plane * own_units + half * thin, 0, thin, width, 0, 0)]

        down_cut = unplace([down_grad], depth, (thin, width), down_cuts)
        one_parts = plane_last(after(jnp.stack(one_column), *up_parts[3:]), (down_cut[0][0, 0, :16, :LANES],))
        down_hop = first_hop(*down_cut, one_parts[3:])
        spots = spots + plane_first_spots(depth, own_units - last, 5)
        down_parts = [*one_parts, *two_parts]
        (down_w,) = place(down_parts, depth, [(half_ff, width)], spots, down_moves, (down_cut[0],))

    grad_hidden, two_part, two_low = feed_back(grad_out, down_w, slope, up_w)
    down_own, down_give = down_project(activated, down_w, resid, (two_low,))
    down_got = swap(down_give, "c")
    activations = (down_own + down_got.astype(WIDE)).astype(LOW)
    up_grad = weight_grad(normed_two, grad_hidden)
    two_got = swap(two_low, "c")
    deps = (up_grad,)
    if ring:
        down_turn = second_hop_of(*down_hop, (up_grad,))
        deps = (up_grad, down_turn[0])
    grad_resid, grad_resid_low, a_low, b_rows, state_grad, norm_two = attend_turn(
        two_part, two_got, resid, rows, grad_out, out_w, mixed, denom, query, deps
    )
    later = from_others(state_grad, -1)
    out_grad = dot_rows(mixed_low, grad_resid_low).astype(LOW)
    deps = ()
    if ring:

        def up_cuts(zz, plane, half):
            cuts = [(0, ((zz * 2 + half) * chips + plane) * own_rows, 0, own_rows, half_ff, 0, 0)]
            row = zz * block + plane * own_rows + half * small
            return cuts + [(1, row, p * half_d, small, half_d, p * small, half_ff) for p in (0, 1)]

        up_cut = unplace([up_grad, out_grad], depth, (own_rows, half_ff + half_d), up_cuts)
        deps = (up_cut[0],)
    grad_projected = attend_back(query, key, value, qk, a_low, b_rows, state_in, later, deps)
    qkv_grad = dot_rows(normed_one, grad_projected).astype(LOW)
    one_part, one_low, norm_cols = project_back(grad_projected, qkv_w, inputs, norm_two)
    input_grad = input_back(one_part, swap(other(halves(one_low)), "c"), grad_resid, own_x, rows)

    out_fan = max(1, width * 64 // (tokens * depth))
    rates = (3.0 * width**-0.5, 3.0 * out_fan**-0.5, 3.0 * width**-0.5, 3.0 * hidden_units**-0.5, 1.5)
    decays = (WEIGHT_DECAY, WEIGHT_DECAY, WEIGHT_DECAY, WEIGHT_DECAY, 0.0)
    masters = (qkv_weight, out_weight, up_weight, down_weight, norm_params)
    firsts = (qkv_first, out_first, up_first, down_first, norm_first)
    seconds = (qkv_second, out_second, up_second, down_second, norm_second)
    if ring:

        def qkv_cuts(zz, plane, half):
            row = ((zz * 2 + half) * chips + plane) * own_rows
            return [(0, row, 0, own_rows, half_qkv, 0, 0), (1, row, 0, own_rows, LANES, 0, half_qkv)]

        hop = swap(down_turn[0], "y"), swap(down_turn[1], "x")
        down_sum = third_hop_of(*down_hop, *hop)
        up_hop = first_hop(*up_cut, (*hop, *later))
        turn = second_hop_of(*up_hop, (*down_sum[1:], grad_projected))
        hop = swap(turn[0], "y"), swap(turn[1], "x")
        up_sum = third_hop_of(*up_hop, *hop)
        qkv_cut = unplace([qkv_grad, norm_cols], depth, (own_rows, half_qkv + LANES), qkv_cuts)
        qkv_hop = first_hop(*qkv_cut, hop)
        turn = second_hop_of(*qkv_hop)
        hop = swap(turn[0], "y"), swap(turn[1], "x")
        qkv_sum = third_hop_of(*qkv_hop, *hop, up_sum[1:])
        down_red, squares = finish_down(down_sum, qkv_sum[:1])
        up_mine, up_give, out_red, squares = finish_up(up_sum, squares, own_rows, half_ff)
        up_mate = swap(up_give, "c")
        deps = (input_grad, activations, up_mate)
        qkv_mine, qkv_give, small_mine = finish_qkv(qkv_sum, squares, own_rows, half_qkv, deps)
        small_mate, qkv_mate = swap(small_mine, "c"), swap(qkv_give, "c")
        squares, norm_sum = chip_squares(small_mine, small_mate)
        norm_red = mine(norm_sum.reshape(2, own_rows, LANES))[:, :4].T
        grads = (qkv_mine, qkv_mate, out_red, up_mine, up_mate, down_red, norm_red)
        *news, grad_norm = update_all(
            grads, sum_chips(squares), masters, firsts, seconds, rates, decays, (3 * depth, depth)
        )
        return (
            activations.reshape(count, group, width),
            input_grad.reshape(count, group, width),
            grad_norm.reshape(()),
            *news,
        )
    scatter = lambda g: lax.psum_scatter(g, ALL, scatter_dimension=0, tiled=True)
    both = lambda a, axis: jnp.stack([jnp.where(core == k, a, 0.0) for k in (0, 1)], axis)
    to_all = lambda a: a.astype(WIDE)
    qkv_red = scatter(both(to_all(qkv_grad).reshape(width, 3 * depth, block), 2).reshape(width, -1))
    up_red = scatter(both(to_all(up_grad).reshape(width, depth, ff_block), 2).reshape(width, -1))
    out_red = scatter(both(to_all(out_grad).reshape(depth, block, width), 1).reshape(width, width))
    down_red = scatter(both(to_all(down_grad).reshape(depth, ff_block, width), 1).reshape(hidden_units, width))
    norm_red = scatter(norm_cols.astype(WIDE))[:, :4].T

    reduced = (qkv_red, out_red, up_red, down_red, norm_red)
    local_squares = sum(jnp.sum(grad * grad) for grad in reduced)
    grad_norm = jnp.sqrt(lax.psum(local_squares, ALL))
    clip = jnp.minimum(1.0, CLIP_LIMIT / (grad_norm + 1e-06))
    news = [
        adam_update(masters[k], firsts[k], seconds[k], clip * reduced[k], rates[k], decays[k]) for k in range(5)
    ]
    return (
        activations.reshape(count, group, width),
        input_grad.reshape(count, group, width),
        grad_norm,
        *[new[0] for new in news],
        *[new[1] for new in news],
        *[new[2] for new in news],
    )


def solution(mesh):
    depth, planes = mesh.shape["seq"] // 2, mesh.shape["img"]
    across = max(k for k in range(1, planes + 1) if planes % k == 0 and k * k <= planes)
    grid = jax.sharding.Mesh(mesh.devices.reshape(depth, 2, planes // across, across), ALL)
    tokens = P(("y", "x"), ("z", "c"), None)
    matrix, norm = P(ALL, None), P(None, ALL)
    state = (matrix, matrix, matrix, matrix, norm)
    return jax.shard_map(
        body,
        mesh=grid,
        in_specs=(tokens, tokens) + state * 3,
        out_specs=(tokens, tokens, P()) + state * 3,
        check_vma=False,
    )
```
